32 devices in a mesh: fsdp: 8 (over y, x, core), tp: 4 (over z).
Axes of the slice: x: 2, y: 2, z: 4, core: 2. Of those that a mesh axis runs over, the one named last changes fastest.
Arguments:
- residual_in: float32 [11776, 1152], P(('fsdp', 'tp')), may hold values from -6 to 6
- cotangent: float32 [11776, 1152], P(('fsdp', 'tp')), may hold values from -6 to 6
- slot_tokens: int32 [16], P('fsdp'), may hold values from 0 to 729, as said below
- qkv_weight: float32 [2, 1152, 3456], P(None, 'fsdp', 'tp'), may hold values from -0.1875 to 0.1875
- out_weight: float32 [2, 1152, 1152], P(None, 'tp', 'fsdp'), may hold values from -3 to 3
- up_weight: float32 [2, 1152, 4304], P(None, 'fsdp', 'tp'), may hold values from -0.1875 to 0.1875
- down_weight: float32 [2, 4304, 1152], P(None, 'tp', 'fsdp'), may hold values from -0.09375 to 0.09375
- vectors: float32 [2, 13520], replicated
- qkv_first: float32 [2, 1152, 3456], P(None, 'fsdp', 'tp'), may hold values from -32 to 32
- qkv_second: float32 [2, 1152, 3456], P(None, 'fsdp', 'tp'), may hold values from 2.944 to 11.776
- out_first: float32 [2, 1152, 1152], P(None, 'tp', 'fsdp'), may hold values from -6 to 6
- out_second: float32 [2, 1152, 1152], P(None, 'tp', 'fsdp'), may hold values from 0.0188416 to 0.0753664
- up_first: float32 [2, 1152, 4304], P(None, 'fsdp', 'tp'), may hold values from -6 to 6
- up_second: float32 [2, 1152, 4304], P(None, 'fsdp', 'tp'), may hold values from 0.47104 to 1.88416
- down_first: float32 [2, 4304, 1152], P(None, 'tp', 'fsdp'), may hold values from -32 to 32
- down_second: float32 [2, 4304, 1152], P(None, 'tp', 'fsdp'), may hold values from 2.3552 to 9.4208
- vec_first: float32 [2, 13520], replicated, may hold values from -32 to 32
- vec_second: float32 [2, 13520], replicated, may hold values from 2.944 to 11.776
Outputs:
- output: float32 [11776, 1152], P(('fsdp', 'tp'))
- grad_input: float32 [11776, 1152], P(('fsdp', 'tp'))
- qkv_grad: float32 [2, 1152, 3456], P(None, 'fsdp', 'tp')
- qkv_first_new: float32 [2, 1152, 3456], P(None, 'fsdp', 'tp')
- qkv_second_new: float32 [2, 1152, 3456], P(None, 'fsdp', 'tp')
- qkv_weight_new: float32 [2, 1152, 3456], P(None, 'fsdp', 'tp')
- out_grad: float32 [2, 1152, 1152], P(None, 'tp', 'fsdp')
- out_first_new: float32 [2, 1152, 1152], P(None, 'tp', 'fsdp')
- out_second_new: float32 [2, 1152, 1152], P(None, 'tp', 'fsdp')
- out_weight_new: float32 [2, 1152, 1152], P(None, 'tp', 'fsdp')
- up_grad: float32 [2, 1152, 4304], P(None, 'fsdp', 'tp')
- up_first_new: float32 [2, 1152, 4304], P(None, 'fsdp', 'tp')
- up_second_new: float32 [2, 1152, 4304], P(None, 'fsdp', 'tp')
- up_weight_new: float32 [2, 1152, 4304], P(None, 'fsdp', 'tp')
- down_grad: float32 [2, 4304, 1152], P(None, 'tp', 'fsdp')
- down_first_new: float32 [2, 4304, 1152], P(None, 'tp', 'fsdp')
- down_second_new: float32 [2, 4304, 1152], P(None, 'tp', 'fsdp')
- down_weight_new: float32 [2, 4304, 1152], P(None, 'tp', 'fsdp')
- vec_grad: float32 [2, 13520], replicated
- vec_first_new: float32 [2, 13520], replicated
- vec_second_new: float32 [2, 13520], replicated
- vec_weight_new: float32 [2, 13520], replicated
The draws below stay inside these ranges and needn't reach their ends.
Inputs may be any that keep to these rules, and one draw needn't show every extreme that they name: `slot_tokens`: each slot holds 729 tokens or none; a group's filled slots come first; every group has at least one image; in every draw some group has all 2 slots filled and another exactly one.
All inputs are finite; a program needn't handle non-finite values.
Results may differ from the reference program's by a relative error of at most 0.011.
The reference program's roundings to bfloat16 on the way count: a program that leaves them out, or rounds other values in their place, can miss the bound.
Values may be sent and summed in bfloat16 or wider, within the bound.
No kernel may reach another device: no remote copies, remote signals or barrier semaphores. Data moves between devices by JAX's collectives and lax.ppermute only.
A program may use at most 256 MiB of HBM per device.

```python
import math
import jax
import jax.numpy as jnp
from jax import lax

D = 1152
HEADS = 16
HD = 72
FF = 4304
IMG_TOK = 729
SEQ = 736
SLOTS = 2
LAYERS = 2
STEP = 10
GROUPS = 8
IMAGES = 16
TOKENS = 11776
VEC = 13520


def draw_slot_tokens(key, part):
    key = jax.random.fold_in(key, 7)
    count_key, order_key = jax.random.split(key)
    counts = jax.random.randint(count_key, (GROUPS,), 1, SLOTS + 1)
    ranking = jax.random.permutation(order_key, GROUPS)
    counts = counts.at[ranking[0]].set(SLOTS)
    counts = counts.at[ranking[1]].set(1)
    slot_index = jnp.arange(SLOTS)
    filled = jnp.where(slot_index[None, :] < counts[:, None], IMG_TOK, 0)
    return filled.reshape(GROUPS * SLOTS).astype(jnp.int32)


def draw_vectors(key, part):
    key = jax.random.fold_in(key, 11)
    jitter = jax.random.normal(key, (LAYERS, VEC), jnp.float32) * 0.3
    column = jnp.arange(VEC)
    gain_slot = jnp.logical_or(column < D, jnp.logical_and(column >= 5 * D, column < 6 * D))
    return jnp.where(gain_slot[None, :], 1.0 + 0.5 * jitter, jitter).astype(jnp.float32)


def raised(drawn, key, source, target, parts, factor):
    owner, partner = [(jnp.arange(drawn.shape[axis_at]) // (drawn.shape[axis_at] // parts)).reshape([-1 if axis == axis_at else 1 for axis in range(drawn.ndim)]) for axis_at in (source, target)]
    chosen = jax.random.permutation(key, parts)[partner]
    strong = (owner == chosen) | (owner == (partner + parts // 2) % parts)
    return jnp.where(strong, factor * drawn, drawn)


def levels(own_key, shape, shards, low, top_value):
    gain, own = 1.0, jax.random.fold_in(own_key, 6)
    for dim, blocks in shards:
        heights = jnp.exp(jax.random.uniform(jax.random.fold_in(own, dim), (blocks,), jnp.float32, low / len(shards), top_value / len(shards)))
        gain = gain * jnp.repeat(heights, shape[dim] // blocks).reshape([-1 if axis == dim else 1 for axis in range(len(shape))])
    return gain


def gaussian(rng, dims, spread, reach, cuts=(), kind=jnp.bfloat16):
    factor_of = levels(rng, dims, cuts, -0.22, 0.18) if cuts else 1.0
    entries = jax.random.normal(rng, dims, jnp.float32) * spread * factor_of
    return jnp.minimum(jnp.maximum(entries, -reach), reach).astype(kind)


def gaussian_with(key, shape, width, most, cuts, heavy, kind=jnp.bfloat16):
    drawn = width * jax.random.normal(key, shape, jnp.float32)
    if cuts:
        drawn = drawn * levels(key, shape, cuts, -0.22, 0.18)
    return jnp.clip(raised(drawn, jax.random.fold_in(key, 3), *heavy), -most, most).astype(kind)


def setup_inputs(seed: int = 0) -> dict:
    keys = jax.random.split(jax.random.key(seed), 19)
    residual_in = gaussian(keys[0], (TOKENS, D), 1.0, 6.0, ((0, 32),), jnp.float32)
    cotangent = gaussian_with(keys[1], (TOKENS, D), 1.0, 6.0, ((0, 32),), (0, 1, 32, 2.75), jnp.float32)
    slot_tokens = draw_slot_tokens(jax.random.fold_in(keys[18], 71), 0)
    qkv_weight = gaussian(keys[3], (LAYERS, D, 3 * D), D ** -0.5, 0.1875, ((1, 8), (2, 4)), jnp.float32)
    out_weight = gaussian(keys[4], (LAYERS, D, D), (max(3 * D // IMG_TOK, 1)) ** -0.5, 3.0, ((1, 4), (2, 8)), jnp.float32)
    up_weight = gaussian(keys[5], (LAYERS, D, FF), D ** -0.5, 0.1875, ((1, 8), (2, 4)), jnp.float32)
    down_weight = gaussian(keys[6], (LAYERS, FF, D), FF ** -0.5, 0.09375, ((1, 4), (2, 8)), jnp.float32)
    vectors = draw_vectors(jax.random.fold_in(keys[18], 71), 0)
    qkv_first = gaussian(keys[8], (LAYERS, D, 3 * D), (0.055 * TOKENS ** 0.5), 32.0, ((1, 8), (2, 4)), jnp.float32)
    qkv_second = jnp.clip(jnp.exp(math.log(11.776) - 1.3862944 * jax.random.uniform(keys[9], (LAYERS, D, 3 * D), jnp.float32) ** levels(keys[9], (LAYERS, D, 3 * D), ((1, 8), (2, 4)), -0.2, 0.2)), 2.944, 11.776)
    out_first = gaussian(keys[10], (LAYERS, D, D), (0.0044 * TOKENS ** 0.5), 6.0, ((1, 4), (2, 8)), jnp.float32)
    out_second = jnp.clip(jnp.exp(math.log(0.0753664) - 1.3862944 * jax.random.uniform(keys[11], (LAYERS, D, D), jnp.float32) ** levels(keys[11], (LAYERS, D, D), ((1, 4), (2, 8)), -0.2, 0.2)), 0.0188416, 0.0753664)
    up_first = gaussian(keys[12], (LAYERS, D, FF), (0.022 * TOKENS ** 0.5), 6.0, ((1, 8), (2, 4)), jnp.float32)
    up_second = jnp.clip(jnp.exp(math.log(1.88416) - 1.3862944 * jax.random.uniform(keys[13], (LAYERS, D, FF), jnp.float32) ** levels(keys[13], (LAYERS, D, FF), ((1, 8), (2, 4)), -0.2, 0.2)), 0.47104, 1.88416)
    down_first = gaussian(keys[14], (LAYERS, FF, D), (0.05 * TOKENS ** 0.5), 32.0, ((1, 4), (2, 8)), jnp.float32)
    down_second = jnp.clip(jnp.exp(math.log(9.4208) - 1.3862944 * jax.random.uniform(keys[15], (LAYERS, FF, D), jnp.float32) ** levels(keys[15], (LAYERS, FF, D), ((1, 4), (2, 8)), -0.2, 0.2)), 2.3552, 9.4208)
    vec_first = gaussian(keys[16], (LAYERS, VEC), (0.055 * TOKENS ** 0.5), 32.0, (), jnp.float32)
    vec_second = jnp.clip(jnp.exp(jax.random.uniform(keys[17], (LAYERS, VEC), jnp.float32, math.log(2.944), math.log(11.776))), 2.944, 11.776)
    return dict(residual_in=residual_in, cotangent=cotangent, slot_tokens=slot_tokens, qkv_weight=qkv_weight, out_weight=out_weight, up_weight=up_weight, down_weight=down_weight, vectors=vectors, qkv_first=qkv_first, qkv_second=qkv_second, out_first=out_first, out_second=out_second, up_first=up_first, up_second=up_second, down_first=down_first, down_second=down_second, vec_first=vec_first, vec_second=vec_second)


EPS_NORM = 1e-06
MASKED = -30000.0
BETA_ONE = 0.9
BETA_TWO = 0.999
ADAM_EPS = 1e-08
DECAY = 0.1
RATES = (0.05, 1.0, 0.05, 0.03, 0.3)
HIGH = lax.Precision.HIGHEST

@jax.custom_vjp
def low(v):
    return lax.optimization_barrier(v.astype(jnp.bfloat16)).astype(jnp.float32)

@jax.custom_vjp
def low_back(v):
    return v

def low_keep(v):
    return (low(v), None)

def low_pass(kept, grad):
    return (grad,)

def back_keep(v):
    return (v, None)

def back_low(kept, grad):
    return (low(grad),)
low.defvjp(low_keep, low_pass)
low_back.defvjp(back_keep, back_low)

def layer_norm(inputs, scale_row, shift_row):
    feature_mean = lax.optimization_barrier(jnp.mean(inputs, axis=-1, keepdims=True))
    centred = inputs - feature_mean
    variance = lax.optimization_barrier(jnp.mean(centred * centred, axis=-1, keepdims=True))
    return centred * lax.rsqrt(variance + EPS_NORM) * scale_row + shift_row

def gelu_tanh(inputs):
    return jax.nn.gelu(inputs, approximate=True)

def feature_piece(vector_row, number):
    return vector_row[number * D:(number + 1) * D]

def matmul(left_rows, right_matrix):
    return jnp.dot(left_rows, right_matrix, precision=HIGH, preferred_element_type=jnp.float32)

def attend(slot_item):
    slot_block, usable = slot_item
    query_rows = slot_block[:, :, 0]
    key_rows = slot_block[:, :, 1]
    value_rows = slot_block[:, :, 2]
    score_scale = slot_block.shape[-1] ** (-0.5)
    scores = jnp.einsum('qhd,khd->hqk', query_rows, key_rows, precision=HIGH) * score_scale
    scores = low_back(scores)
    scores = jnp.where(usable[None, None, :], scores, MASKED)
    softmax_out = low(jax.nn.softmax(scores, axis=-1))
    return jnp.einsum('hqk,khd->qhd', softmax_out, value_rows, precision=HIGH)

def adam_step(weight, gradient, first_moment, second_moment, step_rate, decay_rate):
    first_new = BETA_ONE * first_moment + (1.0 - BETA_ONE) * gradient
    second_new = BETA_TWO * second_moment + (1.0 - BETA_TWO) * gradient * gradient
    first_hat = first_new / (1.0 - BETA_ONE ** STEP)
    second_hat = second_new / (1.0 - BETA_TWO ** STEP)
    weight_new = weight - step_rate * (first_hat / (jnp.sqrt(second_hat) + ADAM_EPS) + decay_rate * weight)
    return (weight_new, first_new, second_new)

def reference(residual_in, cotangent, slot_tokens, qkv_weight, out_weight, up_weight, down_weight, vectors, qkv_first, qkv_second, out_first, out_second, up_first, up_second, down_first, down_second, vec_first, vec_second):
    position = jnp.arange(SEQ, dtype=jnp.int32)
    usable = position[None, :] < slot_tokens[:, None]
    row_mask = usable.reshape(TOKENS, 1).astype(jnp.float32)

    def forward(stream, qkv_all, out_all, up_all, down_all, vector_all):
        for layer_index in range(LAYERS):
            vector_row = vector_all[layer_index]
            normed = low(layer_norm(stream, feature_piece(vector_row, 0), feature_piece(vector_row, 1)))
            head_bias = jnp.stack([feature_piece(vector_row, 2).reshape(HEADS, HD), jnp.zeros((HEADS, HD), jnp.float32), feature_piece(vector_row, 3).reshape(HEADS, HD)], axis=1).reshape(3 * D)
            qkv_rows = low(low_back(matmul(normed, low(qkv_all[layer_index]))) + head_bias)
            mixed = lax.map(jax.checkpoint(attend), (qkv_rows.reshape(IMAGES, SEQ, HEADS, 3, HD), usable))
            mixed_rows = low(low_back(mixed.reshape(TOKENS, D)))
            middle = stream + low_back(matmul(mixed_rows, low(out_all[layer_index]))) + feature_piece(vector_row, 4)
            normed_two = low(layer_norm(middle, feature_piece(vector_row, 5), feature_piece(vector_row, 6)))
            hidden_pre = low_back(matmul(normed_two, low(up_all[layer_index]))) + vector_row[8 * D:]
            activated = low(gelu_tanh(hidden_pre))
            stream = middle + low_back(matmul(activated, low(down_all[layer_index]))) + feature_piece(vector_row, 7)
        return stream * row_mask
    output, pull_back = jax.vjp(forward, residual_in, qkv_weight, out_weight, up_weight, down_weight, vectors)
    grad_input, qkv_grad, out_grad, up_grad, down_grad, vec_grad = pull_back(cotangent)
    qkv_new = adam_step(qkv_weight, qkv_grad, qkv_first, qkv_second, RATES[0], DECAY)
    out_new = adam_step(out_weight, out_grad, out_first, out_second, RATES[1], DECAY)
    up_new = adam_step(up_weight, up_grad, up_first, up_second, RATES[2], DECAY)
    down_new = adam_step(down_weight, down_grad, down_first, down_second, RATES[3], DECAY)
    vec_new = adam_step(vectors, vec_grad, vec_first, vec_second, RATES[4], 0.0)
    return (output, grad_input, qkv_grad, qkv_new[1], qkv_new[2], qkv_new[0], out_grad, out_new[1], out_new[2], out_new[0], up_grad, up_new[1], up_new[2], up_new[0], down_grad, down_new[1], down_new[2], down_new[0], vec_grad, vec_new[1], vec_new[2], vec_new[0])
```

```python
import math

import jax
import jax.numpy as jnp
from jax import lax
from jax.sharding import PartitionSpec as P

HD = 72
STEP = 10


EPS_NORM = 1e-06
MASKED = -30000.0
BETA_ONE = 0.9
BETA_TWO = 0.999
ADAM_EPS = 1e-08
DECAY = 0.1
RATES = (0.05, 1.0, 0.05, 0.03, 0.3)
LOW = jnp.bfloat16
F32 = jnp.float32


def layer_norm(inputs, scale_row, shift_row):
    feature_mean = jnp.mean(inputs, axis=-1, keepdims=True)
    centred = inputs - feature_mean
    variance = jnp.mean(centred * centred, axis=-1, keepdims=True)
    return centred * lax.rsqrt(variance + EPS_NORM) * scale_row + shift_row


def gelu_tanh(inputs):
    return jax.nn.gelu(inputs, approximate=True)


def adam_step(weight, gradient, first_moment, second_moment, step_rate, decay_rate):
    first_new = BETA_ONE * first_moment + (1.0 - BETA_ONE) * gradient
    second_new = BETA_TWO * second_moment + (1.0 - BETA_TWO) * gradient * gradient
    first_hat = first_new / (1.0 - BETA_ONE**STEP)
    second_hat = second_new / (1.0 - BETA_TWO**STEP)
    weight_new = weight - step_rate * (
        first_hat / (jnp.sqrt(second_hat) + ADAM_EPS) + decay_rate * weight
    )
    return (weight_new, first_new, second_new)


def dot(left, right, left_dim, right_dim):
    return lax.dot_general(
        left, right, (((left_dim,), (right_dim,)), ((), ())), preferred_element_type=F32
    )


def plane_sides(chips):
    side = math.isqrt(chips)
    while chips % side:
        side -= 1
    return side, chips // side


class Place:
    def __init__(self):
        self.nf = lax.axis_size("fsdp")
        self.nt = lax.axis_size("tp")
        self.na, self.nb = plane_sides(self.nf // 2)
        fi = lax.axis_index("fsdp")
        self.core = fi % 2
        self.a = (fi // 2) // self.nb
        self.b = (fi // 2) % self.nb
        self.t = lax.axis_index("tp")
        self.size = {"a": self.na, "b": self.nb, "t": self.nt}
        self.at = {"a": self.a, "b": self.b, "t": self.t}

    def pairs(self, axis, move):
        if axis == "t":
            return [(i, move(i)) for i in range(self.nt)]
        found = []
        for f in range(self.nf):
            place = {"a": f // 2 // self.nb, "b": f // 2 % self.nb, "core": f % 2}
            place[axis] = move(place[axis])
            found.append((f, (place["a"] * self.nb + place["b"]) * 2 + place["core"]))
        return found

    def send(self, values, axis, move):
        return lax.ppermute(values, "tp" if axis == "t" else "fsdp", self.pairs(axis, move))

    def sibling(self, values):
        return self.send(values, "core", lambda i: 1 - i)

    def receive_next(self, values, axis):
        n = self.size[axis]
        return self.send(values, axis, lambda i: (i - 1) % n)

    def pass_on(self, values, axis):
        n = self.size[axis]
        return self.send(values, axis, lambda i: (i + 1) % n)

    def swap_rows(self, values):
        pairs = []
        for f in range(self.nf):
            for t in range(self.nt):
                if f % 2 == 0 and t % 2 == 1:
                    target = (f + 1) * self.nt + t - 1
                elif f % 2 == 1 and t % 2 == 0:
                    target = (f - 1) * self.nt + t + 1
                else:
                    target = f * self.nt + t
                pairs.append((f * self.nt + t, target))
        return lax.ppermute(values, ("fsdp", "tp"), pairs)

    def gather_axis(self, block, axis):
        blocks = [block]
        for _ in range(self.size[axis] - 1):
            blocks.append(self.receive_next(blocks[-1], axis))
        return blocks

    def reduce_axis(self, parts, axis):
        total = parts[-1]
        for part in reversed(parts[:-1]):
            total = self.pass_on(total.astype(LOW), axis).astype(F32) + part
        return total

    def rotate(self, values, axis, back=False):
        n = self.size[axis]
        start = self.at[axis]
        if back:
            start = (n - start) % n
        return lax.dynamic_slice_in_dim(jnp.concatenate([values, values]), start, n)


def in_pair(place, own, other, axis):
    return jnp.where(
        place.core == 0,
        jnp.concatenate([own, other], axis=axis),
        jnp.concatenate([other, own], axis=axis),
    )


def half_of(place, values, axis, sibling=False):
    half = values.shape[axis] // 2
    at = (1 - place.core) if sibling else place.core
    return lax.dynamic_slice_in_dim(values, at * half, half, axis)


def gather_weight(place, shard, order):
    own = half_of(place, shard, 1)
    block = in_pair(place, own, place.sibling(half_of(place, shard, 1, True)), 0)
    block = jnp.concatenate(place.gather_axis(block, "t"), axis=1)
    rows = block.shape[0]
    if order == "ba":
        block = jnp.concatenate(place.gather_axis(block, "b"), axis=0)
        return jnp.concatenate(place.gather_axis(block, "a"), axis=0)
    block = jnp.concatenate(place.gather_axis(block, "a"), axis=0)
    by_b = place.gather_axis(block, "b")
    return jnp.concatenate(
        [piece[a * rows : (a + 1) * rows] for a in range(place.na) for piece in by_b], axis=0
    )


def reduce_weight(place, grad, order):
    rows = grad.shape[0] // (place.na * place.nb)
    if order == "ba":
        wide = rows * place.nb
        grad = place.reduce_axis([grad[a * wide : (a + 1) * wide] for a in range(place.na)], "a")
        grad = place.reduce_axis([grad[b * rows : (b + 1) * rows] for b in range(place.nb)], "b")
    else:
        grad = grad.reshape(place.na, place.nb, rows, -1)
        grad = place.reduce_axis([grad[:, b] for b in range(place.nb)], "b")
        grad = place.reduce_axis([grad[a] for a in range(place.na)], "a")
    columns = grad.shape[1] // place.nt
    grad = place.reduce_axis(
        [grad[:, t * columns : (t + 1) * columns] for t in range(place.nt)], "t"
    )
    other = place.sibling(half_of(place, grad, 0, True))
    return in_pair(place, half_of(place, grad, 0), other, 1)


def attend_forward(heads, usable):
    scale = heads.shape[-1] ** (-0.5)
    query, key, value = heads[:, :, 0], heads[:, :, 1], heads[:, :, 2]
    scores = jnp.einsum("qhd,khd->hqk", query, key, preferred_element_type=F32) * scale
    scores = jnp.where(usable[None, None, :], scores, MASKED)
    row_max = jnp.max(scores, axis=-1, keepdims=True)
    exponent = jnp.exp(scores - row_max)
    row_sum = jnp.sum(exponent, axis=-1, keepdims=True)
    probs_low = (exponent / row_sum).astype(LOW)
    mixed = jnp.einsum("hqk,khd->qhd", probs_low, value, preferred_element_type=F32)
    return mixed.astype(LOW), (row_max + jnp.log(row_sum))[:, :, 0]


def attend_backward(heads, usable, log_sums, grad_mixed):
    scale = heads.shape[-1] ** (-0.5)
    query, key, value = heads[:, :, 0], heads[:, :, 1], heads[:, :, 2]
    scores = jnp.einsum("qhd,khd->hqk", query, key, preferred_element_type=F32) * scale
    scores = jnp.where(usable[None, None, :], scores, MASKED)
    probs = jnp.exp(scores - log_sums[:, :, None])
    grad_probs = jnp.einsum("qhd,khd->hqk", grad_mixed, value, preferred_element_type=F32)
    row_dot = jnp.sum(grad_probs * probs, axis=-1, keepdims=True)
    grad_scores = (probs * (grad_probs - row_dot)).astype(LOW)
    grad_query = jnp.einsum("hqk,khd->qhd", grad_scores, key, preferred_element_type=F32) * scale
    grad_key = jnp.einsum("hqk,qhd->khd", grad_scores, query, preferred_element_type=F32) * scale
    grad_value = jnp.einsum(
        "hqk,qhd->khd", probs.astype(LOW), grad_mixed, preferred_element_type=F32
    )
    return jnp.stack([grad_query, grad_key, grad_value], axis=2)


def body(
    residual_in,
    cotangent,
    slot_tokens,
    qkv_weight,
    out_weight,
    up_weight,
    down_weight,
    vectors,
    qkv_first,
    qkv_second,
    out_first,
    out_second,
    up_first,
    up_second,
    down_first,
    down_second,
    vec_first,
    vec_second,
):
    place = Place()
    layer_count = qkv_weight.shape[0]
    half_rows, width = residual_in.shape
    rows = 2 * half_rows
    nt, na, nb = place.nt, place.na, place.nb
    hidden_total = vectors.shape[1] - 8 * width
    local_heads = out_weight.shape[1] * nt // (2 * HD)

    tokens_pair = in_pair(place, slot_tokens, place.sibling(slot_tokens), 0)
    slots = slot_tokens.shape[0]
    slot_at = (place.t % 2) * slots + place.t // 2
    token_count = lax.dynamic_slice_in_dim(tokens_pair, slot_at, 1)[0]
    usable = jnp.arange(rows, dtype=jnp.int32) < token_count
    row_mask = usable.astype(F32)[:, None]
    counted = (place.core == 0).astype(F32)

    def features_in(values):
        lead = values.shape[:-1]
        wide = width // na
        block = wide // nb
        pieces = []
        for a in range(na):
            for b in range(nb):
                start = ((place.a + a) % na) * wide + ((place.b + b) % nb) * block
                pieces.append(lax.dynamic_slice_in_dim(values, start, block, len(lead)))
        return jnp.concatenate(pieces, axis=-1)

    def features_out(values):
        lead = values.shape[:-1]
        wide = width // na
        block = wide // nb
        pieces = []
        for a in range(na):
            for b in range(nb):
                start = ((a - place.a) % na) * wide + ((b - place.b) % nb) * block
                pieces.append(lax.dynamic_slice_in_dim(values, start, block, len(lead)))
        return jnp.concatenate(pieces, axis=-1)

    def columns_in(values):
        blocks = values.reshape(nt, 2, -1)
        blocks = lax.dynamic_slice_in_dim(blocks, place.core, 1, 1)
        return place.rotate(blocks, "t").reshape(-1)

    def columns_out(values):
        blocks = place.rotate(values.reshape(nt, 1, -1), "t", back=True)
        empty = jnp.zeros((nt, 2, blocks.shape[2]), F32)
        return lax.dynamic_update_slice_in_dim(empty, blocks, place.core, 1).reshape(-1)

    def rows_in(values):
        mine = features_in(place.swap_rows(values))
        return in_pair(place, mine, place.sibling(mine), 0)

    def rows_out(values):
        mine = lax.dynamic_slice_in_dim(values, place.core * half_rows, half_rows)
        return place.swap_rows(features_out(mine))

    def both_cores(partial):
        return partial + place.sibling(partial.astype(LOW)).astype(F32)

    def feature_piece(vector_row, number):
        return vector_row[number * width : (number + 1) * width]

    def shards(layer):
        return (
            qkv_weight[layer].astype(LOW),
            out_weight[layer].astype(LOW).T,
            up_weight[layer].astype(LOW),
            down_weight[layer].astype(LOW).T,
        )

    orders = ("ba", "ab", "ba", "ab"), ("ab", "ba", "ab", "ba")
    gathered = []
    for layer in range(layer_count):
        gathered.append(
            [
                gather_weight(place, shard, order)
                for shard, order in zip(shards(layer), orders[layer % 2])
            ]
        )

    stream = rows_in(residual_in)
    grad_stream = rows_in(cotangent) * row_mask
    saved = []
    for layer in range(layer_count):
        vector_row = vectors[layer]
        qkv_full, out_full, up_full, down_full = gathered[layer]
        normal = [features_in(feature_piece(vector_row, n)) for n in (0, 1, 4, 5, 6, 7)]
        query_bias = columns_in(feature_piece(vector_row, 2)).reshape(local_heads, HD)
        value_bias = columns_in(feature_piece(vector_row, 3)).reshape(local_heads, HD)
        head_bias = jnp.stack([query_bias, jnp.zeros_like(query_bias), value_bias], axis=1)
        hidden_bias = columns_in(vector_row[8 * width :])
        normed = layer_norm(stream, normal[0], normal[1]).astype(LOW)
        qkv = (dot(normed, qkv_full, 1, 0) + head_bias.reshape(-1)).astype(LOW)
        heads = qkv.reshape(rows, local_heads, 3, HD)
        mixed, log_sums = attend_forward(heads, usable)
        mixed = mixed.reshape(rows, local_heads * HD)
        middle = stream + both_cores(dot(mixed, out_full, 1, 1)) + normal[2]
        normed_two = layer_norm(middle, normal[3], normal[4]).astype(LOW)
        hidden_pre = dot(normed_two, up_full, 1, 0) + hidden_bias
        activated = gelu_tanh(hidden_pre).astype(LOW)
        new_stream = middle + both_cores(dot(activated, down_full, 1, 1)) + normal[5]
        saved.append(
            (stream, normed, heads, log_sums, mixed, middle, normed_two, hidden_pre, activated, normal)
        )
        stream = new_stream
    output = rows_out(stream * row_mask)

    shard_grads = [None] * layer_count
    vector_grads = [None] * layer_count
    for layer in reversed(range(layer_count)):
        stream_in, normed, heads, log_sums, mixed, middle, normed_two, hidden_pre, activated, normal = (
            saved[layer]
        )
        qkv_full, out_full, up_full, down_full = gathered[layer]
        order = orders[layer % 2]
        dz = grad_stream.astype(LOW)
        down_grad = reduce_weight(place, dot(dz, activated, 0, 0), order[3])
        grad_act = dot(dz, down_full, 1, 0)
        grad_hidden = jax.vjp(gelu_tanh, hidden_pre)[1](grad_act)[0]
        hidden_low = grad_hidden.astype(LOW)
        up_grad = reduce_weight(place, dot(normed_two, hidden_low, 0, 0), order[2])
        grad_normed = both_cores(dot(hidden_low, up_full, 1, 1))
        pull = jax.vjp(layer_norm, middle, normal[3], normal[4])[1]
        grad_inner, scale_two, shift_two = pull(grad_normed)
        down_bias = jnp.sum(grad_stream, axis=0)
        grad_stream = grad_stream + grad_inner
        dm = grad_stream.astype(LOW)
        out_grad = reduce_weight(place, dot(dm, mixed, 0, 0), order[1])
        grad_mixed = dot(dm, out_full, 1, 0).astype(LOW)
        grad_heads = attend_backward(
            heads, usable, log_sums, grad_mixed.reshape(rows, local_heads, HD)
        )
        head_sums = jnp.sum(grad_heads, axis=0)
        qkv_low = grad_heads.reshape(rows, -1).astype(LOW)
        qkv_grad = reduce_weight(place, dot(normed, qkv_low, 0, 0), order[0])
        grad_normed = both_cores(dot(qkv_low, qkv_full, 1, 1))
        pull = jax.vjp(layer_norm, stream_in, normal[0], normal[1])[1]
        grad_inner, scale_one, shift_one = pull(grad_normed)
        out_bias = jnp.sum(grad_stream, axis=0)
        grad_stream = grad_stream + grad_inner
        flat = [
            features_out(piece) * counted
            for piece in (scale_one, shift_one, out_bias, scale_two, shift_two, down_bias)
        ]
        vector_grads[layer] = jnp.concatenate(
            [
                flat[0],
                flat[1],
                columns_out(head_sums[:, 0].reshape(-1)),
                columns_out(head_sums[:, 2].reshape(-1)),
                flat[2],
                flat[3],
                flat[4],
                flat[5],
                columns_out(jnp.sum(grad_hidden, axis=0)),
            ]
        )
        shard_grads[layer] = (qkv_grad, out_grad.T, up_grad, down_grad.T)
    grad_input = rows_out(grad_stream)

    vector_total = jnp.stack(vector_grads)
    vector_total = vector_total + place.sibling(vector_total)
    for axis in ("b", "a", "t"):
        step = 1
        while step < place.size[axis]:
            vector_total = vector_total + place.send(vector_total, axis, lambda i: i ^ step)
            step *= 2

    reduced = tuple(jnp.stack([grads[member] for grads in shard_grads]) for member in range(4))
    qkv_new = adam_step(qkv_weight, reduced[0], qkv_first, qkv_second, RATES[0], DECAY)
    out_new = adam_step(out_weight, reduced[1], out_first, out_second, RATES[1], DECAY)
    up_new = adam_step(up_weight, reduced[2], up_first, up_second, RATES[2], DECAY)
    down_new = adam_step(down_weight, reduced[3], down_first, down_second, RATES[3], DECAY)
    vec_new = adam_step(vectors, vector_total, vec_first, vec_second, RATES[4], 0.0)
    return (
        output,
        grad_input,
        reduced[0],
        qkv_new[1],
        qkv_new[2],
        qkv_new[0],
        reduced[1],
        out_new[1],
        out_new[2],
        out_new[0],
        reduced[2],
        up_new[1],
        up_new[2],
        up_new[0],
        reduced[3],
        down_new[1],
        down_new[2],
        down_new[0],
        vector_total,
        vec_new[1],
        vec_new[2],
        vec_new[0],
    )


def solution(mesh):
    rows = P(("fsdp", "tp"), None)
    wide = P(None, "fsdp", "tp")
    tall = P(None, "tp", "fsdp")
    moments = (wide, wide, tall, tall, wide, wide, tall, tall, P(), P())
    return jax.shard_map(
        body,
        mesh=mesh,
        in_specs=(rows, rows, P("fsdp"), wide, tall, wide, tall, P(), *moments),
        out_specs=(rows, rows, *[wide] * 4, *[tall] * 4, *[wide] * 4, *[tall] * 4, *[P()] * 4),
        check_vma=False,
    )
```

```python
import math

import jax
import jax.numpy as jnp
from jax import lax
from jax.sharding import PartitionSpec as P

HD = 72
STEP = 10


EPS_NORM = 1e-06
MASKED = -30000.0
BETA_ONE = 0.9
BETA_TWO = 0.999
ADAM_EPS = 1e-08
DECAY = 0.1
RATES = (0.05, 1.0, 0.05, 0.03, 0.3)
LOW = jnp.bfloat16
F32 = jnp.float32


def layer_norm(inputs, scale_row, shift_row):
    feature_mean = jnp.mean(inputs, axis=-1, keepdims=True)
    centred = inputs - feature_mean
    variance = jnp.mean(centred * centred, axis=-1, keepdims=True)
    return centred * lax.rsqrt(variance + EPS_NORM) * scale_row + shift_row


def gelu_tanh(inputs):
    return jax.nn.gelu(inputs, approximate=True)


def adam_step(weight, gradient, first_moment, second_moment, step_rate, decay_rate):
    first_new = BETA_ONE * first_moment + (1.0 - BETA_ONE) * gradient
    second_new = BETA_TWO * second_moment + (1.0 - BETA_TWO) * gradient * gradient
    first_hat = first_new / (1.0 - BETA_ONE**STEP)
    second_hat = second_new / (1.0 - BETA_TWO**STEP)
    weight_new = weight - step_rate * (
        first_hat / (jnp.sqrt(second_hat) + ADAM_EPS) + decay_rate * weight
    )
    return (weight_new, first_new, second_new)


def dot(left, right, left_dim, right_dim):
    return lax.dot_general(
        left, right, (((left_dim,), (right_dim,)), ((), ())), preferred_element_type=F32
    )


def plane_sides(chips):
    side = math.isqrt(chips)
    while chips % side:
        side -= 1
    return side, chips // side


class Place:
    def __init__(self):
        self.nf = lax.axis_size("fsdp")
        self.nt = lax.axis_size("tp")
        self.na, self.nb = plane_sides(self.nf // 2)
        fi = lax.axis_index("fsdp")
        self.core = fi % 2
        self.a = (fi // 2) // self.nb
        self.b = (fi // 2) % self.nb
        self.t = lax.axis_index("tp")
        self.size = {"a": self.na, "b": self.nb, "t": self.nt}
        self.at = {"a": self.a, "b": self.b, "t": self.t}

    def pairs(self, axis, move):
        if axis == "t":
            return [(i, move(i)) for i in range(self.nt)]
        found = []
        for f in range(self.nf):
            place = {"a": f // 2 // self.nb, "b": f // 2 % self.nb, "core": f % 2}
            place[axis] = move(place[axis])
            found.append((f, (place["a"] * self.nb + place["b"]) * 2 + place["core"]))
        return found

    def send(self, values, axis, move):
        return lax.ppermute(values, "tp" if axis == "t" else "fsdp", self.pairs(axis, move))

    def sibling(self, values):
        return self.send(values, "core", lambda i: 1 - i)

    def receive_next(self, values, axis):
        n = self.size[axis]
        return self.send(values, axis, lambda i: (i - 1) % n)

    def pass_on(self, values, axis):
        n = self.size[axis]
        return self.send(values, axis, lambda i: (i + 1) % n)

    def swap_rows(self, values):
        pairs = []
        for f in range(self.nf):
            for t in range(self.nt):
                if f % 2 == 0 and t % 2 == 1:
                    target = (f + 1) * self.nt + t - 1
                elif f % 2 == 1 and t % 2 == 0:
                    target = (f - 1) * self.nt + t + 1
                else:
                    target = f * self.nt + t
                pairs.append((f * self.nt + t, target))
        return lax.ppermute(values, ("fsdp", "tp"), pairs)

    def gather_axis(self, block, axis):
        blocks = [block]
        for _ in range(self.size[axis] - 1):
            blocks.append(self.receive_next(blocks[-1], axis))
        return blocks

    def reduce_axis(self, parts, axis):
        total = parts[-1]
        for part in reversed(parts[:-1]):
            total = self.pass_on(total.astype(LOW), axis).astype(F32) + part
        return total

    def rotate(self, values, axis, back=False):
        n = self.size[axis]
        start = self.at[axis]
        if back:
            start = (n - start) % n
        return lax.dynamic_slice_in_dim(jnp.concatenate([values, values]), start, n)


def in_pair(place, own, other, axis):
    return jnp.where(
        place.core == 0,
        jnp.concatenate([own, other], axis=axis),
        jnp.concatenate([other, own], axis=axis),
    )


def half_of(place, values, axis, sibling=False):
    half = values.shape[axis] // 2
    at = (1 - place.core) if sibling else place.core
    return lax.dynamic_slice_in_dim(values, at * half, half, axis)


def gather_weight(place, shard, order):
    own = half_of(place, shard, 1)
    block = in_pair(place, own, place.sibling(half_of(place, shard, 1, True)), 0)
    rows, columns = block.shape
    groups = [
        [f * place.nt + t for f in range(core, place.nf, 2) for t in range(place.nt)]
        for core in range(2)
    ]
    full = lax.all_gather(block, ("fsdp", "tp"), axis_index_groups=groups)
    full = full.reshape(place.na, place.nb, place.nt, rows, columns)
    full = place.rotate(full, "a")
    full = jnp.moveaxis(place.rotate(jnp.moveaxis(full, 1, 0), "b"), 1, 0)
    full = jnp.moveaxis(place.rotate(jnp.moveaxis(full, 2, 0), "t"), 0, 3)
    return full.reshape(place.na * place.nb * rows, place.nt * columns)


def reduce_weight(place, grad, order):
    rows = grad.shape[0] // (place.na * place.nb)
    if order == "ba":
        wide = rows * place.nb
        grad = place.reduce_axis([grad[a * wide : (a + 1) * wide] for a in range(place.na)], "a")
        grad = place.reduce_axis([grad[b * rows : (b + 1) * rows] for b in range(place.nb)], "b")
    else:
        grad = grad.reshape(place.na, place.nb, rows, -1)
        grad = place.reduce_axis([grad[:, b] for b in range(place.nb)], "b")
        grad = place.reduce_axis([grad[a] for a in range(place.na)], "a")
    columns = grad.shape[1] // place.nt
    grad = place.reduce_axis(
        [grad[:, t * columns : (t + 1) * columns] for t in range(place.nt)], "t"
    )
    other = place.sibling(half_of(place, grad, 0, True))
    return in_pair(place, half_of(place, grad, 0), other, 1)


def attend_forward(heads, usable):
    scale = heads.shape[-1] ** (-0.5)
    query, key, value = heads[:, :, 0], heads[:, :, 1], heads[:, :, 2]
    scores = jnp.einsum("qhd,khd->hqk", query, key, preferred_element_type=F32) * scale
    scores = jnp.where(usable[None, None, :], scores, MASKED)
    row_max = jnp.max(scores, axis=-1, keepdims=True)
    exponent = jnp.exp(scores - row_max)
    row_sum = jnp.sum(exponent, axis=-1, keepdims=True)
    probs_low = (exponent / row_sum).astype(LOW)
    mixed = jnp.einsum("hqk,khd->qhd", probs_low, value, preferred_element_type=F32)
    return mixed.astype(LOW), (row_max + jnp.log(row_sum))[:, :, 0]


def attend_backward(heads, usable, log_sums, grad_mixed):
    scale = heads.shape[-1] ** (-0.5)
    query, key, value = heads[:, :, 0], heads[:, :, 1], heads[:, :, 2]
    scores = jnp.einsum("qhd,khd->hqk", query, key, preferred_element_type=F32) * scale
    scores = jnp.where(usable[None, None, :], scores, MASKED)
    probs = jnp.exp(scores - log_sums[:, :, None])
    grad_probs = jnp.einsum("qhd,khd->hqk", grad_mixed, value, preferred_element_type=F32)
    row_dot = jnp.sum(grad_probs * probs, axis=-1, keepdims=True)
    grad_scores = (probs * (grad_probs - row_dot)).astype(LOW)
    grad_query = jnp.einsum("hqk,khd->qhd", grad_scores, key, preferred_element_type=F32) * scale
    grad_key = jnp.einsum("hqk,qhd->khd", grad_scores, query, preferred_element_type=F32) * scale
    grad_value = jnp.einsum(
        "hqk,qhd->khd", probs.astype(LOW), grad_mixed, preferred_element_type=F32
    )
    return jnp.stack([grad_query, grad_key, grad_value], axis=2)


def body(
    residual_in,
    cotangent,
    slot_tokens,
    qkv_weight,
    out_weight,
    up_weight,
    down_weight,
    vectors,
    qkv_first,
    qkv_second,
    out_first,
    out_second,
    up_first,
    up_second,
    down_first,
    down_second,
    vec_first,
    vec_second,
):
    place = Place()
    layer_count = qkv_weight.shape[0]
    half_rows, width = residual_in.shape
    rows = 2 * half_rows
    nt, na, nb = place.nt, place.na, place.nb
    hidden_total = vectors.shape[1] - 8 * width
    local_heads = out_weight.shape[1] * nt // (2 * HD)

    tokens_pair = in_pair(place, slot_tokens, place.sibling(slot_tokens), 0)
    slots = slot_tokens.shape[0]
    slot_at = (place.t % 2) * slots + place.t // 2
    token_count = lax.dynamic_slice_in_dim(tokens_pair, slot_at, 1)[0]
    usable = jnp.arange(rows, dtype=jnp.int32) < token_count
    row_mask = usable.astype(F32)[:, None]
    counted = (place.core == 0).astype(F32)

    def features_in(values):
        lead = values.shape[:-1]
        wide = width // na
        block = wide // nb
        pieces = []
        for a in range(na):
            for b in range(nb):
                start = ((place.a + a) % na) * wide + ((place.b + b) % nb) * block
                pieces.append(lax.dynamic_slice_in_dim(values, start, block, len(lead)))
        return jnp.concatenate(pieces, axis=-1)

    def features_out(values):
        lead = values.shape[:-1]
        wide = width // na
        block = wide // nb
        pieces = []
        for a in range(na):
            for b in range(nb):
                start = ((a - place.a) % na) * wide + ((b - place.b) % nb) * block
                pieces.append(lax.dynamic_slice_in_dim(values, start, block, len(lead)))
        return jnp.concatenate(pieces, axis=-1)

    def columns_in(values):
        blocks = values.reshape(nt, 2, -1)
        blocks = lax.dynamic_slice_in_dim(blocks, place.core, 1, 1)
        return place.rotate(blocks, "t").reshape(-1)

    def columns_out(values):
        blocks = place.rotate(values.reshape(nt, 1, -1), "t", back=True)
        empty = jnp.zeros((nt, 2, blocks.shape[2]), F32)
        return lax.dynamic_update_slice_in_dim(empty, blocks, place.core, 1).reshape(-1)

    def rows_in(values):
        mine = features_in(place.swap_rows(values))
        return in_pair(place, mine, place.sibling(mine), 0)

    def rows_out(values):
        mine = lax.dynamic_slice_in_dim(values, place.core * half_rows, half_rows)
        return place.swap_rows(features_out(mine))

    def both_cores(partial):
        return partial + place.sibling(partial.astype(LOW)).astype(F32)

    def feature_piece(vector_row, number):
        return vector_row[number * width : (number + 1) * width]

    def shards(layer):
        return (
            qkv_weight[layer].astype(LOW),
            out_weight[layer].astype(LOW).T,
            up_weight[layer].astype(LOW),
            down_weight[layer].astype(LOW).T,
        )

    orders = ("ba", "ab", "ba", "ab"), ("ab", "ba", "ab", "ba")
    gathered = []
    for layer in range(layer_count):
        gathered.append(
            [
                gather_weight(place, shard, order)
                for shard, order in zip(shards(layer), orders[layer % 2])
            ]
        )

    stream = rows_in(residual_in)
    grad_stream = rows_in(cotangent) * row_mask
    saved = []
    for layer in range(layer_count):
        vector_row = vectors[layer]
        qkv_full, out_full, up_full, down_full = gathered[layer]
        normal = [features_in(feature_piece(vector_row, n)) for n in (0, 1, 4, 5, 6, 7)]
        query_bias = columns_in(feature_piece(vector_row, 2)).reshape(local_heads, HD)
        value_bias = columns_in(feature_piece(vector_row, 3)).reshape(local_heads, HD)
        head_bias = jnp.stack([query_bias, jnp.zeros_like(query_bias), value_bias], axis=1)
        hidden_bias = columns_in(vector_row[8 * width :])
        normed = layer_norm(stream, normal[0], normal[1]).astype(LOW)
        qkv = (dot(normed, qkv_full, 1, 0) + head_bias.reshape(-1)).astype(LOW)
        heads = qkv.reshape(rows, local_heads, 3, HD)
        mixed, log_sums = attend_forward(heads, usable)
        mixed = mixed.reshape(rows, local_heads * HD)
        middle = stream + both_cores(dot(mixed, out_full, 1, 1)) + normal[2]
        normed_two = layer_norm(middle, normal[3], normal[4]).astype(LOW)
        hidden_pre = dot(normed_two, up_full, 1, 0) + hidden_bias
        activated = gelu_tanh(hidden_pre).astype(LOW)
        new_stream = middle + both_cores(dot(activated, down_full, 1, 1)) + normal[5]
        saved.append(
            (stream, normed, heads, log_sums, mixed, middle, normed_two, hidden_pre, activated, normal)
        )
        stream = new_stream
    output = rows_out(stream * row_mask)

    shard_grads = [None] * layer_count
    vector_grads = [None] * layer_count
    for layer in reversed(range(layer_count)):
        stream_in, normed, heads, log_sums, mixed, middle, normed_two, hidden_pre, activated, normal = (
            saved[layer]
        )
        qkv_full, out_full, up_full, down_full = gathered[layer]
        order = orders[layer % 2]
        dz = grad_stream.astype(LOW)
        down_grad = reduce_weight(place, dot(dz, activated, 0, 0), order[3])
        grad_act = dot(dz, down_full, 1, 0)
        grad_hidden = jax.vjp(gelu_tanh, hidden_pre)[1](grad_act)[0]
        hidden_low = grad_hidden.astype(LOW)
        up_grad = reduce_weight(place, dot(normed_two, hidden_low, 0, 0), order[2])
        grad_normed = both_cores(dot(hidden_low, up_full, 1, 1))
        pull = jax.vjp(layer_norm, middle, normal[3], normal[4])[1]
        grad_inner, scale_two, shift_two = pull(grad_normed)
        down_bias = jnp.sum(grad_stream, axis=0)
        grad_stream = grad_stream + grad_inner
        dm = grad_stream.astype(LOW)
        out_grad = reduce_weight(place, dot(dm, mixed, 0, 0), order[1])
        grad_mixed = dot(dm, out_full, 1, 0).astype(LOW)
        grad_heads = attend_backward(
            heads, usable, log_sums, grad_mixed.reshape(rows, local_heads, HD)
        )
        head_sums = jnp.sum(grad_heads, axis=0)
        qkv_low = grad_heads.reshape(rows, -1).astype(LOW)
        qkv_grad = reduce_weight(place, dot(normed, qkv_low, 0, 0), order[0])
        grad_normed = both_cores(dot(qkv_low, qkv_full, 1, 1))
        pull = jax.vjp(layer_norm, stream_in, normal[0], normal[1])[1]
        grad_inner, scale_one, shift_one = pull(grad_normed)
        out_bias = jnp.sum(grad_stream, axis=0)
        grad_stream = grad_stream + grad_inner
        flat = [
            features_out(piece) * counted
            for piece in (scale_one, shift_one, out_bias, scale_two, shift_two, down_bias)
        ]
        vector_grads[layer] = jnp.concatenate(
            [
                flat[0],
                flat[1],
                columns_out(head_sums[:, 0].reshape(-1)),
                columns_out(head_sums[:, 2].reshape(-1)),
                flat[2],
                flat[3],
                flat[4],
                flat[5],
                columns_out(jnp.sum(grad_hidden, axis=0)),
            ]
        )
        shard_grads[layer] = (qkv_grad, out_grad.T, up_grad, down_grad.T)
    grad_input = rows_out(grad_stream)

    vector_total = jnp.stack(vector_grads)
    vector_total = vector_total + place.sibling(vector_total)
    for axis in ("b", "a", "t"):
        step = 1
        while step < place.size[axis]:
            vector_total = vector_total + place.send(vector_total, axis, lambda i: i ^ step)
            step *= 2

    reduced = tuple(jnp.stack([grads[member] for grads in shard_grads]) for member in range(4))
    qkv_new = adam_step(qkv_weight, reduced[0], qkv_first, qkv_second, RATES[0], DECAY)
    out_new = adam_step(out_weight, reduced[1], out_first, out_second, RATES[1], DECAY)
    up_new = adam_step(up_weight, reduced[2], up_first, up_second, RATES[2], DECAY)
    down_new = adam_step(down_weight, reduced[3], down_first, down_second, RATES[3], DECAY)
    vec_new = adam_step(vectors, vector_total, vec_first, vec_second, RATES[4], 0.0)
    return (
        output,
        grad_input,
        reduced[0],
        qkv_new[1],
        qkv_new[2],
        qkv_new[0],
        reduced[1],
        out_new[1],
        out_new[2],
        out_new[0],
        reduced[2],
        up_new[1],
        up_new[2],
        up_new[0],
        reduced[3],
        down_new[1],
        down_new[2],
        down_new[0],
        vector_total,
        vec_new[1],
        vec_new[2],
        vec_new[0],
    )


def solution(mesh):
    rows = P(("fsdp", "tp"), None)
    wide = P(None, "fsdp", "tp")
    tall = P(None, "tp", "fsdp")
    moments = (wide, wide, tall, tall, wide, wide, tall, tall, P(), P())
    return jax.shard_map(
        body,
        mesh=mesh,
        in_specs=(rows, rows, P("fsdp"), wide, tall, wide, tall, P(), *moments),
        out_specs=(rows, rows, *[wide] * 4, *[tall] * 4, *[wide] * 4, *[tall] * 4, *[P()] * 4),
        check_vma=False,
    )
```

```python
import functools
import math

import jax
import jax.numpy as jnp
from jax import lax
from jax.experimental import pallas as pl
from jax.experimental.pallas import tpu as pltpu
from jax.sharding import PartitionSpec as P

HD = 72
IMG_TOK = 729
STEP = 10


EPS_NORM = 1e-06
MASKED = -30000.0
BETA_ONE = 0.9
BETA_TWO = 0.999
ADAM_EPS = 1e-08
DECAY = 0.1
RATES = (0.05, 1.0, 0.05, 0.03, 0.3)
LOW = jnp.bfloat16
F32 = jnp.float32
GELU = math.sqrt(2.0 / math.pi)
VMEM = 56 * 1024 * 1024


def adam_step(weight, gradient, first_moment, second_moment, step_rate, decay_rate):
    first_new = BETA_ONE * first_moment + (1.0 - BETA_ONE) * gradient
    second_new = BETA_TWO * second_moment + (1.0 - BETA_TWO) * gradient * gradient
    first_hat = first_new / (1.0 - BETA_ONE**STEP)
    second_hat = second_new / (1.0 - BETA_TWO**STEP)
    weight_new = weight - step_rate * (
        first_hat / (jnp.sqrt(second_hat) + ADAM_EPS) + decay_rate * weight
    )
    return (weight_new, first_new, second_new)


def cdot(left, right, left_dim=1, right_dim=0):
    return lax.dot_general(
        left, right, (((left_dim,), (right_dim,)), ((), ())), preferred_element_type=F32
    )


def norm_parts(values):
    centred = values - jnp.mean(values, axis=-1, keepdims=True)
    inverse = lax.rsqrt(jnp.mean(centred * centred, axis=-1, keepdims=True) + EPS_NORM)
    return centred * inverse, inverse


def norm_backward(grad_out, values, gain):
    unit, inverse = norm_parts(values)
    scaled = grad_out * gain
    mean_one = jnp.mean(scaled, axis=-1, keepdims=True)
    mean_two = jnp.mean(scaled * unit, axis=-1, keepdims=True)
    grad_in = inverse * (scaled - mean_one - unit * mean_two)
    gain_sum = jnp.sum(grad_out * unit, axis=0, keepdims=True)
    return grad_in, gain_sum, jnp.sum(grad_out, axis=0, keepdims=True)


def gelu_both(inputs):
    cubic = 0.044715 * inputs * inputs
    tanh = jnp.tanh(GELU * inputs * (1.0 + cubic))
    half = 0.5 * (1.0 + tanh)
    slope = half + 0.5 * GELU * inputs * (1.0 - tanh * tanh) * (1.0 + 3.0 * cubic)
    return inputs * half, slope


def mask_keys(scores, tokens):
    rows = scores.shape[0]
    whole = IMG_TOK // 8 * 8
    position = whole + lax.broadcasted_iota(jnp.int32, (rows - whole, 1), 0)
    return jnp.concatenate(
        [scores[:whole], jnp.where(position < tokens, scores[whole:], MASKED)], axis=0
    )


def attn_forward_kernel(
    joined, tokens_ref, *refs
):
    if joined:
        (base_ref, own_ref, other_ref, bias_row_ref, gain_ref, shift_ref, w_ref, bias_ref,
         stream_ref, normed_ref, qkv_ref, mixed_ref, sums_ref, part_ref, total) = refs
    else:
        (base_ref, gain_ref, shift_ref, w_ref, bias_ref,
         normed_ref, qkv_ref, mixed_ref, sums_ref, part_ref, total) = refs
    step = pl.program_id(0)

    @pl.when(step == 0)
    def _():
        stream = base_ref[...]
        if joined:
            stream = (
                stream + (own_ref[...].astype(F32) + other_ref[...].astype(F32)) + bias_row_ref[...]
            )
            stream_ref[...] = stream
        unit, _ = norm_parts(stream)
        normed_ref[...] = (unit * gain_ref[...] + shift_ref[...]).astype(LOW)
        total[...] = jnp.zeros_like(total)

    tokens = tokens_ref[0]
    head_columns = 3 * HD
    local = qkv_ref.shape[2]
    scale = HD ** (-0.5)
    weight = w_ref[0]
    qkv = (cdot(normed_ref[...], weight[:, :local]) + bias_ref[0]).astype(LOW)
    qkv_ref[0] = qkv
    mixed = []
    for head in range(local // head_columns):
        at = head * head_columns
        query = qkv[:, at : at + HD]
        key = qkv[:, at + HD : at + 2 * HD]
        value = qkv[:, at + 2 * HD : at + 3 * HD]
        scores = mask_keys(cdot(key, query, 1, 1) * scale, tokens)
        top = jnp.max(scores, axis=0, keepdims=True)
        raised = jnp.exp(scores - top)
        weight_sum = jnp.sum(raised, axis=0, keepdims=True)
        probs = (raised * (1.0 / weight_sum)).astype(LOW)
        mixed.append(cdot(value, probs, 0, 0))
        sums_ref[0, head : head + 1, :] = top + jnp.log(weight_sum)
    mixed = jnp.concatenate(mixed, axis=0).T.astype(LOW)
    mixed_ref[0] = mixed
    total[...] += cdot(mixed, weight[:, local : local + mixed.shape[1]], 1, 1)

    @pl.when(step == pl.num_programs(0) - 1)
    def _():
        part_ref[...] = total[...].astype(LOW)


def mlp_forward_kernel(
    base_ref, own_ref, other_ref, bias_row_ref, gain_ref, shift_ref,
    w_ref, bias_ref, up_tail_ref, down_tail_ref, tail_bias_ref,
    middle_ref, normed_ref, act_ref, slope_ref, act_tail_ref, slope_tail_ref, part_ref, total,
):
    step = pl.program_id(0)

    @pl.when(step == 0)
    def _():
        middle = (
            base_ref[...] + (own_ref[...].astype(F32) + other_ref[...].astype(F32)) + bias_row_ref[...]
        )
        middle_ref[...] = middle
        unit, _ = norm_parts(middle)
        normed_ref[...] = (unit * gain_ref[...] + shift_ref[...]).astype(LOW)
        act, slope = gelu_both(cdot(normed_ref[...], up_tail_ref[...]) + tail_bias_ref[...])
        act = act.astype(LOW)
        act_tail_ref[...] = act
        slope_tail_ref[...] = slope.astype(LOW)
        total[...] = cdot(act, down_tail_ref[...], 1, 1)

    weight = w_ref[0]
    units = act_ref.shape[2]
    act, slope = gelu_both(cdot(normed_ref[...], weight[:, :units]) + bias_ref[0])
    act = act.astype(LOW)
    act_ref[0] = act
    slope_ref[0] = slope.astype(LOW)
    total[...] += cdot(act, weight[:, units:], 1, 1)

    @pl.when(step == pl.num_programs(0) - 1)
    def _():
        part_ref[...] = total[...].astype(LOW)


def mlp_backward_kernel(
    grad_ref, w_ref, slope_ref, up_tail_ref, down_tail_ref, slope_tail_ref,
    hidden_ref, hidden_tail_ref, sums_ref, sums_tail_ref, part_ref, low, total,
):
    step = pl.program_id(0)

    @pl.when(step == 0)
    def _():
        low[...] = grad_ref[...].astype(LOW)
        hidden = cdot(low[...], down_tail_ref[...]) * slope_tail_ref[...].astype(F32)
        sums_tail_ref[...] = jnp.sum(hidden, axis=0, keepdims=True)
        hidden = hidden.astype(LOW)
        hidden_tail_ref[...] = hidden
        total[...] = cdot(hidden, up_tail_ref[...], 1, 1)

    weight = w_ref[0]
    units = hidden_ref.shape[2]
    hidden = cdot(low[...], weight[:, units:]) * slope_ref[0].astype(F32)
    sums_ref[0] = jnp.sum(hidden, axis=0, keepdims=True)
    hidden = hidden.astype(LOW)
    hidden_ref[0] = hidden
    total[...] += cdot(hidden, weight[:, :units], 1, 1)

    @pl.when(step == pl.num_programs(0) - 1)
    def _():
        part_ref[...] = total[...].astype(LOW)


def mlp_grads_kernel(
    grad_ref, normed_ref, hidden_ref, act_ref, hidden_tail_ref, act_tail_ref,
    out_ref, up_tail_ref, down_tail_ref, grad_turned, normed_turned,
):
    step = pl.program_id(0)

    @pl.when(step == 0)
    def _():
        grad_turned[...] = grad_ref[...].astype(LOW).T
        normed_turned[...] = normed_ref[...].T
        up_tail_ref[...] = cdot(normed_turned[...], hidden_tail_ref[...]).astype(LOW)
        down_tail_ref[...] = cdot(grad_turned[...], act_tail_ref[...]).astype(LOW)

    units = hidden_ref.shape[2]
    out_ref[0, :, :units] = cdot(normed_turned[...], hidden_ref[0]).astype(LOW)
    out_ref[0, :, units:] = cdot(grad_turned[...], act_ref[0]).astype(LOW)


def attn_backward_kernel(
    tokens_ref, grad_ref, own_ref, other_ref, middle_ref, gain_ref, w_ref, qkv_ref, sums_ref,
    dmiddle_ref, norm_sums_ref, dqkv_ref, head_sums_ref, part_ref, low, total,
):
    step = pl.program_id(0)

    @pl.when(step == 0)
    def _():
        grad = grad_ref[...]
        inner, gain_sum, shift_sum = norm_backward(
            own_ref[...].astype(F32) + other_ref[...].astype(F32), middle_ref[...], gain_ref[...]
        )
        dmiddle = grad + inner
        dmiddle_ref[...] = dmiddle
        low[...] = dmiddle.astype(LOW)
        norm_sums_ref[0:1, :] = gain_sum
        norm_sums_ref[1:2, :] = shift_sum
        norm_sums_ref[2:3, :] = jnp.sum(grad, axis=0, keepdims=True)
        norm_sums_ref[3:4, :] = jnp.sum(dmiddle, axis=0, keepdims=True)
        total[...] = jnp.zeros_like(total)

    tokens = tokens_ref[0]
    head_columns = 3 * HD
    local = qkv_ref.shape[2]
    heads = local // head_columns
    scale = HD ** (-0.5)
    weight = w_ref[0]
    qkv = qkv_ref[0]
    dmixed = cdot(low[...], weight[:, local : local + heads * HD]).astype(LOW)
    pieces = []
    for head in range(heads):
        at = head * head_columns
        query = qkv[:, at : at + HD]
        key = qkv[:, at + HD : at + 2 * HD]
        value = qkv[:, at + 2 * HD : at + 3 * HD]
        grad = dmixed[:, head * HD : (head + 1) * HD]
        scores = mask_keys(cdot(key, query, 1, 1) * scale, tokens)
        probs = jnp.exp(scores - sums_ref[0, head : head + 1, :])
        dprobs = cdot(value, grad, 1, 1)
        row_dot = jnp.sum(dprobs * probs, axis=0, keepdims=True)
        dscores = (probs * (dprobs - row_dot)).astype(LOW)
        pieces.append(cdot(key, dscores, 0, 0).T * scale)
        pieces.append(cdot(dscores, query) * scale)
        pieces.append(cdot(probs.astype(LOW), grad))
    dqkv = jnp.concatenate(pieces, axis=1)
    head_sums_ref[0] = jnp.sum(dqkv, axis=0, keepdims=True)
    dqkv = dqkv.astype(LOW)
    dqkv_ref[0] = dqkv
    total[...] += cdot(dqkv, weight[:, :local], 1, 1)

    @pl.when(step == pl.num_programs(0) - 1)
    def _():
        part_ref[...] = total[...].astype(LOW)


def attn_grads_kernel(
    dmiddle_ref, normed_ref, dqkv_ref, mixed_ref, qkv_out_ref, out_out_ref, grad_turned, normed_turned,
):
    @pl.when(pl.program_id(0) == 0)
    def _():
        grad_turned[...] = dmiddle_ref[...].astype(LOW).T
        normed_turned[...] = normed_ref[...].T

    qkv_out_ref[0] = cdot(normed_turned[...], dqkv_ref[0]).astype(LOW)
    out_out_ref[0] = cdot(grad_turned[...], mixed_ref[0]).astype(LOW)


def norm_backward_kernel(dmiddle_ref, own_ref, other_ref, stream_ref, gain_ref, out_ref, sums_ref):
    inner, gain_sum, shift_sum = norm_backward(
        own_ref[...].astype(F32) + other_ref[...].astype(F32), stream_ref[...], gain_ref[...]
    )
    out_ref[...] = dmiddle_ref[...] + inner
    sums_ref[0:1, :] = gain_sum
    sums_ref[1:2, :] = shift_sum


def whole(shape):
    return pl.BlockSpec(shape, lambda t: (0,) * len(shape), pipeline_mode=pl.Buffered(1))


def held(shape):
    return pl.BlockSpec(shape, lambda t: (0,) * len(shape))


def stepped(shape):
    return pl.BlockSpec((1,) + shape, lambda t: (t,) + (0,) * len(shape))


def low_of(*shape):
    return jax.ShapeDtypeStruct(shape, LOW)


def f32_of(*shape):
    return jax.ShapeDtypeStruct(shape, F32)


def call(kernel, steps, in_specs, outs, scratch, flops, bytes_accessed, transcendentals=0):
    return pl.pallas_call(
        kernel,
        grid=(steps,),
        in_specs=in_specs,
        out_specs=[spec for spec, _ in outs],
        out_shape=[shape for _, shape in outs],
        scratch_shapes=scratch,
        compiler_params=pltpu.CompilerParams(vmem_limit_bytes=VMEM),
        cost_estimate=pl.CostEstimate(
            flops=flops, bytes_accessed=bytes_accessed, transcendentals=transcendentals
        ),
    )


def attn_forward(tokens, base, branch, norm, weight, bias):
    rows, width = base.shape
    steps, _, columns = weight.shape
    local = bias.shape[2]
    heads = local // (3 * HD)
    joined = branch is not None
    row = whole((1, width))
    full = whole((rows, width))
    in_specs = [pl.BlockSpec(memory_space=pltpu.SMEM), full]
    args = [tokens, base]
    outs = []
    if joined:
        in_specs += [full, full, row]
        args += list(branch)
        outs.append((held((rows, width)), f32_of(rows, width)))
    in_specs += [row, row, stepped((width, columns)), stepped((1, local))]
    args += [*norm, weight, bias]
    outs += [
        (held((rows, width)), low_of(rows, width)),
        (stepped((rows, local)), low_of(steps, rows, local)),
        (stepped((rows, heads * HD)), low_of(steps, rows, heads * HD)),
        (stepped((heads, rows)), f32_of(steps, heads, rows)),
        (held((rows, width)), low_of(rows, width)),
    ]
    flops = 2 * rows * steps * (width * (local + heads * HD) + heads * 2 * rows * HD)
    result = call(
        functools.partial(attn_forward_kernel, joined),
        steps, in_specs, outs, [pltpu.VMEM((rows, width), F32)],
        flops, rows * width * 12 + weight.size * 2, steps * heads * rows * rows,
    )(*args)
    return result if joined else [base, *result]


def mlp_forward(base, branch, norm, weight, bias, tails, tail_bias):
    rows, width = base.shape
    steps, _, columns = weight.shape
    units = columns // 2
    tail = tail_bias.shape[1]
    row = whole((1, width))
    full = whole((rows, width))
    outs = [
        (held((rows, width)), f32_of(rows, width)),
        (held((rows, width)), low_of(rows, width)),
        (stepped((rows, units)), low_of(steps, rows, units)),
        (stepped((rows, units)), low_of(steps, rows, units)),
        (held((rows, tail)), low_of(rows, tail)),
        (held((rows, tail)), low_of(rows, tail)),
        (held((rows, width)), low_of(rows, width)),
    ]
    return call(
        mlp_forward_kernel,
        steps,
        [full, full, full, row, row, row, stepped((width, columns)), stepped((1, units)),
         whole((width, tail)), whole((width, tail)), whole((1, tail))],
        outs, [pltpu.VMEM((rows, width), F32)],
        4 * rows * width * (steps * units + tail),
        rows * width * 16 + weight.size * 2 + rows * steps * units * 4,
        rows * steps * units,
    )(base, *branch, *norm, weight, bias, *tails, tail_bias)


def mlp_backward(grad, weight, slope, tails, slope_tail):
    rows, width = grad.shape
    steps, _, columns = weight.shape
    units = columns // 2
    tail = slope_tail.shape[1]
    outs = [
        (stepped((rows, units)), low_of(steps, rows, units)),
        (held((rows, tail)), low_of(rows, tail)),
        (stepped((1, units)), f32_of(steps, 1, units)),
        (held((1, tail)), f32_of(1, tail)),
        (held((rows, width)), low_of(rows, width)),
    ]
    return call(
        mlp_backward_kernel,
        steps,
        [whole((rows, width)), stepped((width, columns)), stepped((rows, units)),
         whole((width, tail)), whole((width, tail)), whole((rows, tail))],
        outs, [pltpu.VMEM((rows, width), LOW), pltpu.VMEM((rows, width), F32)],
        4 * rows * width * (steps * units + tail),
        rows * width * 6 + weight.size * 2 + rows * steps * units * 4,
    )(grad, weight, slope, *tails, slope_tail)


def mlp_grads(grad, normed, hidden, act, hidden_tail, act_tail):
    rows, width = grad.shape
    steps, _, units = hidden.shape
    tail = hidden_tail.shape[1]
    outs = [
        (stepped((width, 2 * units)), low_of(steps, width, 2 * units)),
        (held((width, tail)), low_of(width, tail)),
        (held((width, tail)), low_of(width, tail)),
    ]
    return call(
        mlp_grads_kernel,
        steps,
        [whole((rows, width)), whole((rows, width)), stepped((rows, units)), stepped((rows, units)),
         whole((rows, tail)), whole((rows, tail))],
        outs, [pltpu.VMEM((width, rows), LOW), pltpu.VMEM((width, rows), LOW)],
        4 * rows * width * (steps * units + tail),
        rows * width * 6 + steps * units * (rows + width) * 4,
    )(grad, normed, hidden, act, hidden_tail, act_tail)


def attn_backward(tokens, grad, parts, middle, gain, weight, qkv, sums):
    rows, width = grad.shape
    steps, _, columns = weight.shape
    local = qkv.shape[2]
    heads = local // (3 * HD)
    full = whole((rows, width))
    outs = [
        (held((rows, width)), f32_of(rows, width)),
        (held((8, width)), f32_of(8, width)),
        (stepped((rows, local)), low_of(steps, rows, local)),
        (stepped((1, local)), f32_of(steps, 1, local)),
        (held((rows, width)), low_of(rows, width)),
    ]
    flops = 2 * rows * steps * (width * (local + heads * HD) + heads * 5 * rows * HD)
    return call(
        attn_backward_kernel,
        steps,
        [pl.BlockSpec(memory_space=pltpu.SMEM), full, full, full, full, whole((1, width)),
         stepped((width, columns)), stepped((rows, local)), stepped((heads, rows))],
        outs, [pltpu.VMEM((rows, width), LOW), pltpu.VMEM((rows, width), F32)],
        flops, rows * width * 20 + weight.size * 2, steps * heads * rows * rows,
    )(tokens, grad, *parts, middle, gain, weight, qkv, sums)


def attn_grads(dmiddle, normed, dqkv, mixed):
    rows, width = dmiddle.shape
    steps, _, local = dqkv.shape
    own = mixed.shape[2]
    outs = [
        (stepped((width, local)), low_of(steps, width, local)),
        (stepped((width, own)), low_of(steps, width, own)),
    ]
    return call(
        attn_grads_kernel,
        steps,
        [whole((rows, width)), whole((rows, width)), stepped((rows, local)), stepped((rows, own))],
        outs, [pltpu.VMEM((width, rows), LOW), pltpu.VMEM((width, rows), LOW)],
        2 * rows * width * steps * (local + own),
        rows * width * 6 + steps * (local + own) * (rows + width) * 2,
    )(dmiddle, normed, dqkv, mixed)


def norm_backward_call(dmiddle, parts, stream, gain):
    rows, width = dmiddle.shape
    full = whole((rows, width))
    return call(
        norm_backward_kernel,
        1,
        [full, full, full, full, whole((1, width))],
        [(held((rows, width)), f32_of(rows, width)), (held((8, width)), f32_of(8, width))],
        [], rows * width * 20, rows * width * 16,
    )(dmiddle, *parts, stream, gain)


def plane_sides(chips):
    side = math.isqrt(chips)
    while chips % side:
        side -= 1
    return side, chips // side


class Place:
    def __init__(self):
        self.nf = lax.axis_size("fsdp")
        self.nt = lax.axis_size("tp")
        self.na, self.nb = plane_sides(self.nf // 2)
        fi = lax.axis_index("fsdp")
        self.core = fi % 2
        self.a = (fi // 2) // self.nb
        self.b = (fi // 2) % self.nb
        self.t = lax.axis_index("tp")
        self.size = {"a": self.na, "b": self.nb, "t": self.nt}
        self.at = {"a": self.a, "b": self.b, "t": self.t}

    def pairs(self, axis, move):
        if axis == "t":
            return [(i, move(i)) for i in range(self.nt)]
        found = []
        for f in range(self.nf):
            place = {"a": f // 2 // self.nb, "b": f // 2 % self.nb, "core": f % 2}
            place[axis] = move(place[axis])
            found.append((f, (place["a"] * self.nb + place["b"]) * 2 + place["core"]))
        return found

    def send(self, values, axis, move):
        return lax.ppermute(values, "tp" if axis == "t" else "fsdp", self.pairs(axis, move))

    def sibling(self, values):
        return self.send(values, "core", lambda i: 1 - i)

    def receive_next(self, values, axis):
        n = self.size[axis]
        return self.send(values, axis, lambda i: (i - 1) % n)

    def pass_on(self, values, axis):
        n = self.size[axis]
        return self.send(values, axis, lambda i: (i + 1) % n)

    def swap_rows(self, values):
        pairs = []
        for f in range(self.nf):
            for t in range(self.nt):
                if f % 2 != t % 2:
                    sign = 1 if t % 2 else -1
                    pairs.append((f * self.nt + t, (f + sign) * self.nt + t - sign))
        arrived = lax.ppermute(values.astype(LOW), ("fsdp", "tp"), pairs).astype(F32)
        return jnp.where(self.core != self.t % 2, arrived, values)

    def gather_axis(self, block, axis):
        blocks = [block]
        for _ in range(self.size[axis] - 1):
            blocks.append(self.receive_next(blocks[-1], axis))
        return blocks

    def reduce_axis(self, parts, axis):
        total = parts[-1]
        for part in reversed(parts[:-1]):
            total = self.pass_on(total.astype(LOW), axis).astype(F32) + part
        return total

    def rotate(self, values, axis, back=False):
        n = self.size[axis]
        start = self.at[axis]
        if back:
            start = (n - start) % n
        return lax.dynamic_slice_in_dim(jnp.concatenate([values, values]), start, n)


def split_pair(place, first, second):
    return (
        jnp.where(place.core == 0, first, second),
        jnp.where(place.core == 0, second, first),
    )


def pack_weights(place, qkv, out, up, down, units):
    def halves(values):
        half = values.shape[1] // 2
        return values[:, :half], values[:, half:]

    packs = []
    for qkv_h, out_h, up_h, down_h in zip(*[halves(v) for v in (qkv, out, up, down)]):
        rows = qkv_h.shape[0]
        tail = [qkv_h, out_h, up_h[:, units:], down_h[:, units:]]
        used = sum(piece.shape[1] for piece in tail)
        if used % 128:
            tail.append(jnp.zeros((rows, -used % 128), LOW))
        packs.append(
            (
                jnp.concatenate(tail, axis=1),
                jnp.concatenate([up_h[:, :units], down_h[:, :units]], axis=1),
            )
        )
    own_attn, other_attn = split_pair(place, packs[0][0], packs[1][0])
    own_mlp, other_mlp = split_pair(place, packs[0][1], packs[1][1])
    return (own_attn, other_attn), (own_mlp, other_mlp)


def row_halves(place, own, other):
    return split_pair(place, own, place.sibling(other))


ROUTES = {"attn": (("t", "b", "a"), ("t", "a", "b")), "mlp": (("b", "t", "a"), ("a", "t", "b"))}


def gather_weight(place, own, other, kind):
    rows, columns = own.shape
    found = []
    for block, route in zip(row_halves(place, own, other), ROUTES[kind]):
        for axis in route[:-1]:
            block = jnp.stack(place.gather_axis(block, axis))
        blocks = place.gather_axis(block, route[-1])
        found.append((blocks, route))
    pieces = []
    for t in range(place.nt):
        for a in range(place.na):
            for b in range(place.nb):
                at = {"t": t, "a": a, "b": b}
                for blocks, route in found:
                    pieces.append(blocks[at[route[2]]][at[route[1]], at[route[0]]])
    full = jnp.concatenate(pieces, axis=0)
    return full.reshape(place.nt, -1, columns)


def reduce_weight(place, grad, kind):
    nt, _, columns = grad.shape
    grad = grad.reshape(nt, place.na, place.nb, 2, -1, columns)
    done = []
    for half, route in enumerate(ROUTES[kind]):
        dims = {"t": 0, "a": 1, "b": 2}
        values = grad[:, :, :, half]
        parts = [lax.index_in_dim(values, k, dims[route[2]], False) for k in range(place.size[route[2]])]
        values = place.reduce_axis(parts, route[2])
        left = [axis for axis in "tab" if axis != route[2]]
        parts = [
            lax.index_in_dim(values, k, left.index(route[1]), False)
            for k in range(place.size[route[1]])
        ]
        values = place.reduce_axis(parts, route[1])
        done.append(place.reduce_axis([values[k] for k in range(place.size[route[0]])], route[0]))
    mine, other = split_pair(place, *done)
    return split_pair(place, mine, place.sibling(other))


def body(
    residual_in,
    cotangent,
    slot_tokens,
    qkv_weight,
    out_weight,
    up_weight,
    down_weight,
    vectors,
    qkv_first,
    qkv_second,
    out_first,
    out_second,
    up_first,
    up_second,
    down_first,
    down_second,
    vec_first,
    vec_second,
):
    place = Place()
    layer_count = qkv_weight.shape[0]
    half_rows, width = residual_in.shape
    rows = 2 * half_rows
    nt, na, nb = place.nt, place.na, place.nb
    local = qkv_weight.shape[2] // 2
    out_local = out_weight.shape[1] // 2
    hidden_local = up_weight.shape[2] // 2
    units = hidden_local // 128 * 128
    tail_units = hidden_local - units

    first_tokens, second_tokens = split_pair(place, slot_tokens, place.sibling(slot_tokens))
    tokens_pair = jnp.concatenate([first_tokens, second_tokens])
    slot_at = (place.t % 2) * slot_tokens.shape[0] + place.t // 2
    tokens = lax.dynamic_slice_in_dim(tokens_pair, slot_at, 1)
    row_mask = (jnp.arange(rows, dtype=jnp.int32) < tokens[0]).astype(F32)[:, None]
    counted = (place.core == 0).astype(F32)

    def features(values, sign):
        axis = values.ndim - 1
        wide = width // na
        block = wide // nb
        pieces = []
        for a in range(na):
            for b in range(nb):
                start = ((a + sign * place.a) % na) * wide + ((b + sign * place.b) % nb) * block
                pieces.append(lax.dynamic_slice_in_dim(values, start, block, axis))
        return jnp.concatenate(pieces, axis=axis)

    def columns_in(values):
        blocks = values.reshape(nt, 2, -1)
        blocks = lax.dynamic_slice_in_dim(blocks, place.core, 1, 1)
        return place.rotate(blocks, "t")

    def columns_out(values):
        blocks = place.rotate(values.reshape(nt, 1, -1), "t", back=True)
        empty = jnp.zeros((nt, 2, blocks.shape[2]), F32)
        return lax.dynamic_update_slice_in_dim(empty, blocks, place.core, 1).reshape(-1)

    def rows_in(values):
        mine = features(place.swap_rows(values), 1)
        return jnp.concatenate(split_pair(place, mine, place.sibling(mine)), axis=0)

    def own_rows(values):
        return lax.dynamic_slice_in_dim(values, place.core * half_rows, half_rows)

    def rows_out(values):
        return place.swap_rows(features(values, -1))

    def vector_piece(layer, number):
        return vectors[layer, number * width : (number + 1) * width]

    packs = [
        pack_weights(
            place,
            qkv_weight[layer].astype(LOW),
            out_weight[layer].astype(LOW).T,
            up_weight[layer].astype(LOW),
            down_weight[layer].astype(LOW).T,
            units,
        )
        for layer in range(layer_count)
    ]
    weights = []
    for layer in range(layer_count):
        attn_full = gather_weight(place, *packs[layer][0], "attn")
        mlp_full = gather_weight(place, *packs[layer][1], "mlp")
        at = local + out_local
        tails = [
            jnp.moveaxis(attn_full[:, :, at + k * tail_units : at + (k + 1) * tail_units], 0, 1).reshape(
                width, nt * tail_units
            )
            for k in range(2)
        ]
        weights.append((attn_full, mlp_full, tails))

    stream = rows_in(residual_in)
    branch = None
    saved = []
    for layer in range(layer_count):
        attn_full, mlp_full, tails = weights[layer]
        normal = features(jnp.stack([vector_piece(layer, n) for n in (0, 1, 4, 5, 6, 7)]), 1)
        normal = [normal[n : n + 1] for n in range(6)]
        query_bias = columns_in(vector_piece(layer, 2)).reshape(nt, -1, 1, HD)
        value_bias = columns_in(vector_piece(layer, 3)).reshape(nt, -1, 1, HD)
        head_bias = jnp.concatenate(
            [query_bias, jnp.zeros_like(query_bias), value_bias], axis=2
        ).reshape(nt, 1, local)
        hidden_bias = columns_in(vectors[layer, 8 * width :])
        main_bias = hidden_bias[:, :, :units]
        tail_bias = hidden_bias[:, :, units:].reshape(1, nt * tail_units)
        stream, normed, qkv, mixed, log_sums, part = attn_forward(
            tokens, stream, branch, normal[:2], attn_full, head_bias
        )
        middle, normed_two, act, slope, act_tail, slope_tail, part = mlp_forward(
            stream, (part, place.sibling(part), normal[2]), normal[3:5], mlp_full, main_bias, tails, tail_bias
        )
        saved.append(
            (stream, normed, qkv, mixed, log_sums, middle, normed_two, act, slope, act_tail, slope_tail, normal)
        )
        branch = (part, place.sibling(part), normal[5])
        stream = middle
    output = own_rows(stream) + (own_rows(branch[0]).astype(F32) + own_rows(branch[1]).astype(F32))
    output = rows_out((output + branch[2]) * own_rows(row_mask))

    grad_stream = rows_in(cotangent) * row_mask
    shard_grads = [None] * layer_count
    vector_grads = [None] * layer_count
    for layer in reversed(range(layer_count)):
        (stream, normed, qkv, mixed, log_sums, middle, normed_two, act, slope, act_tail, slope_tail, normal) = (
            saved[layer]
        )
        attn_full, mlp_full, tails = weights[layer]
        hidden, hidden_tail, hidden_sums, tail_sums, part = mlp_backward(
            grad_stream, mlp_full, slope, tails, slope_tail
        )
        parts = (part, place.sibling(part))
        mlp_grad, up_tail, down_tail = mlp_grads(
            grad_stream, normed_two, hidden, act, hidden_tail, act_tail
        )
        mlp_pair = reduce_weight(place, mlp_grad, "mlp")
        dmiddle, norm_two_sums, dqkv, head_sums, part = attn_backward(
            tokens, grad_stream, parts, middle, normal[3], attn_full, qkv, log_sums
        )
        parts = (part, place.sibling(part))
        qkv_grad, out_grad = attn_grads(dmiddle, normed, dqkv, mixed)
        tail_grads = [
            jnp.moveaxis(tail.reshape(width, nt, tail_units), 1, 0) for tail in (up_tail, down_tail)
        ]
        attn_grad = jnp.concatenate([qkv_grad, out_grad, *tail_grads], axis=2)
        attn_pair = reduce_weight(place, attn_grad, "attn")
        grad_stream, norm_one_sums = norm_backward_call(dmiddle, parts, stream, normal[0])
        flat = features(jnp.concatenate([norm_one_sums[:2], norm_two_sums[:4]]), -1) * counted
        head_sums = head_sums.reshape(nt, -1, 3, HD)
        hidden_sums = jnp.concatenate([hidden_sums, tail_sums.reshape(nt, 1, tail_units)], axis=2)
        vector_grads[layer] = jnp.concatenate(
            [
                flat[0],
                flat[1],
                columns_out(head_sums[:, :, 0]),
                columns_out(head_sums[:, :, 2]),
                flat[5],
                flat[2],
                flat[3],
                flat[4],
                columns_out(hidden_sums),
            ]
        )
        at = local + out_local
        shard_grads[layer] = (
            jnp.concatenate([pair[:, :local] for pair in attn_pair], axis=1),
            jnp.concatenate([pair[:, local:at] for pair in attn_pair], axis=1).T,
            jnp.concatenate(
                [
                    piece
                    for mlp_half, attn_half in zip(mlp_pair, attn_pair)
                    for piece in (mlp_half[:, :units], attn_half[:, at : at + tail_units])
                ],
                axis=1,
            ),
            jnp.concatenate(
                [
                    piece
                    for mlp_half, attn_half in zip(mlp_pair, attn_pair)
                    for piece in (
                        mlp_half[:, units:],
                        attn_half[:, at + tail_units : at + 2 * tail_units],
                    )
                ],
                axis=1,
            ).T,
        )
    grad_input = rows_out(own_rows(grad_stream))

    vector_total = jnp.stack(vector_grads)
    vector_total = vector_total + place.sibling(vector_total)
    for axis in ("b", "a", "t"):
        step = 1
        while step < place.size[axis]:
            vector_total = vector_total + place.send(vector_total, axis, lambda i: i ^ step)
            step *= 2

    reduced = tuple(jnp.stack([grads[member] for grads in shard_grads]) for member in range(4))
    qkv_new = adam_step(qkv_weight, reduced[0], qkv_first, qkv_second, RATES[0], DECAY)
    out_new = adam_step(out_weight, reduced[1], out_first, out_second, RATES[1], DECAY)
    up_new = adam_step(up_weight, reduced[2], up_first, up_second, RATES[2], DECAY)
    down_new = adam_step(down_weight, reduced[3], down_first, down_second, RATES[3], DECAY)
    vec_new = adam_step(vectors, vector_total, vec_first, vec_second, RATES[4], 0.0)
    return (
        output,
        grad_input,
        reduced[0],
        qkv_new[1],
        qkv_new[2],
        qkv_new[0],
        reduced[1],
        out_new[1],
        out_new[2],
        out_new[0],
        reduced[2],
        up_new[1],
        up_new[2],
        up_new[0],
        reduced[3],
        down_new[1],
        down_new[2],
        down_new[0],
        vector_total,
        vec_new[1],
        vec_new[2],
        vec_new[0],
    )


def solution(mesh):
    rows = P(("fsdp", "tp"), None)
    wide = P(None, "fsdp", "tp")
    tall = P(None, "tp", "fsdp")
    moments = (wide, wide, tall, tall, wide, wide, tall, tall, P(), P())
    return jax.shard_map(
        body,
        mesh=mesh,
        in_specs=(rows, rows, P("fsdp"), wide, tall, wide, tall, P(), *moments),
        out_specs=(rows, rows, *[wide] * 4, *[tall] * 4, *[wide] * 4, *[tall] * 4, *[P()] * 4),
        check_vma=False,
    )
```

```python
import functools
import math

import jax
import jax.numpy as jnp
from jax import lax
from jax.experimental import pallas as pl
from jax.experimental.pallas import tpu as pltpu
from jax.sharding import PartitionSpec as P

HD = 72
IMG_TOK = 729
STEP = 10


EPS_NORM = 1e-06
MASKED = -30000.0
BETA_ONE = 0.9
BETA_TWO = 0.999
ADAM_EPS = 1e-08
DECAY = 0.1
RATES = (0.05, 1.0, 0.05, 0.03, 0.3)
LOW = jnp.bfloat16
F32 = jnp.float32
GELU = math.sqrt(2.0 / math.pi)
VMEM = 56 * 1024 * 1024


def adam_step(weight, gradient, first_moment, second_moment, step_rate, decay_rate):
    first_new = BETA_ONE * first_moment + (1.0 - BETA_ONE) * gradient
    second_new = BETA_TWO * second_moment + (1.0 - BETA_TWO) * gradient * gradient
    first_hat = first_new / (1.0 - BETA_ONE**STEP)
    second_hat = second_new / (1.0 - BETA_TWO**STEP)
    weight_new = weight - step_rate * (
        first_hat / (jnp.sqrt(second_hat) + ADAM_EPS) + decay_rate * weight
    )
    return (weight_new, first_new, second_new)


def cdot(left, right, left_dim=1, right_dim=0):
    return lax.dot_general(
        left, right, (((left_dim,), (right_dim,)), ((), ())), preferred_element_type=F32
    )


def norm_parts(values):
    centred = values - jnp.mean(values, axis=-1, keepdims=True)
    inverse = lax.rsqrt(jnp.mean(centred * centred, axis=-1, keepdims=True) + EPS_NORM)
    return centred * inverse, inverse


def norm_backward(grad_out, values, gain):
    unit, inverse = norm_parts(values)
    scaled = grad_out * gain
    mean_one = jnp.mean(scaled, axis=-1, keepdims=True)
    mean_two = jnp.mean(scaled * unit, axis=-1, keepdims=True)
    grad_in = inverse * (scaled - mean_one - unit * mean_two)
    gain_sum = jnp.sum(grad_out * unit, axis=0, keepdims=True)
    return grad_in, gain_sum, jnp.sum(grad_out, axis=0, keepdims=True)


def gelu_both(inputs):
    cubic = 0.044715 * inputs * inputs
    tanh = jnp.tanh(GELU * inputs * (1.0 + cubic))
    half = 0.5 * (1.0 + tanh)
    slope = half + 0.5 * GELU * inputs * (1.0 - tanh * tanh) * (1.0 + 3.0 * cubic)
    return inputs * half, slope


def mask_keys(scores, tokens):
    rows = scores.shape[0]
    whole = IMG_TOK // 8 * 8
    position = whole + lax.broadcasted_iota(jnp.int32, (rows - whole, 1), 0)
    return jnp.concatenate(
        [scores[:whole], jnp.where(position < tokens, scores[whole:], MASKED)], axis=0
    )


def whole(shape):
    return pl.BlockSpec(shape, lambda i, s: (0,) * len(shape), pipeline_mode=pl.Buffered(1))


def held(shape):
    return pl.BlockSpec(shape, lambda i, s: (0,) * len(shape))


def stepped(shape):
    return pl.BlockSpec((1,) + shape, lambda i, s: (i,) + (0,) * len(shape))


def low_of(*shape):
    return jax.ShapeDtypeStruct(shape, LOW)


def f32_of(*shape):
    return jax.ShapeDtypeStruct(shape, F32)


def call(kernel, where, steps, ins, outs, scratch, flops=0, bytes_accessed=0, transcendentals=0, aliases=None):
    return pl.pallas_call(
        kernel,
        grid_spec=pltpu.PrefetchScalarGridSpec(
            num_scalar_prefetch=1,
            grid=(steps,),
            in_specs=[spec for spec, _ in ins],
            out_specs=[spec for spec, _ in outs],
            scratch_shapes=scratch,
        ),
        out_shape=[shape for _, shape in outs],
        input_output_aliases=aliases or {},
        compiler_params=pltpu.CompilerParams(vmem_limit_bytes=VMEM),
        cost_estimate=pl.CostEstimate(
            flops=flops, bytes_accessed=bytes_accessed, transcendentals=transcendentals
        ),
    )(where, *[array for _, array in ins])


def turned(values, place_t, count):
    block = values.shape[1] // count
    result = values
    for shift in range(1, count):
        moved = jnp.concatenate([values[:, shift * block :], values[:, : shift * block]], axis=1)
        result = jnp.where(place_t == shift, moved, result)
    return result


def pack_kernel(units, where, qkv_ref, out_ref, up_ref, down_ref, own_attn, other_attn, own_mlp, other_mlp):
    qkv, out = qkv_ref[0].astype(LOW), out_ref[0].T.astype(LOW)
    up, down = up_ref[0].astype(LOW), down_ref[0].T.astype(LOW)

    def half(values, number):
        size = values.shape[1] // 2
        return values[:, number * size : (number + 1) * size]

    for number in range(2):
        up_h, down_h = half(up, number), half(down, number)
        attn = [half(qkv, number), half(out, number), up_h[:, units:], down_h[:, units:]]
        used = sum(piece.shape[1] for piece in attn)
        attn.append(jnp.zeros((qkv.shape[0], own_attn.shape[1] - used), LOW))
        attn = jnp.concatenate(attn, axis=1)
        mlp = jnp.concatenate([up_h[:, :units], down_h[:, :units]], axis=1)

        @pl.when(where[3] == number)
        def _():
            own_attn[...] = attn
            own_mlp[...] = mlp

        @pl.when(where[3] != number)
        def _():
            other_attn[...] = attn
            other_mlp[...] = mlp


def attn_forward_kernel(spread, joined, tail_units, where, *refs):
    refs = list(refs)
    count = len(spread.shapes())
    if joined:
        base_ref, own_ref, other_ref, old_ref = refs[:4]
        del refs[:4]
    else:
        own_ref, other_ref = refs[:2]
        del refs[:2]
    vec_ref, bias_ref = refs[:2]
    w_refs = refs[2 : 2 + count]
    (stream_ref, normed_ref, qkv_ref, mixed_ref, sums_ref, tail_ref, part_ref, total, held_weight) = refs[
        2 + count :
    ]
    step = pl.program_id(0)

    @pl.when(step == 0)
    def _():
        if joined:
            stream = (
                base_ref[...] + (own_ref[...].astype(F32) + other_ref[...].astype(F32)) + old_ref[0, 7:8, :]
            )
            stream_ref[...] = stream
        else:
            half = own_ref.shape[0]
            stream_ref[pl.ds(pl.multiple_of(where[3] * half, 8), half), :] = own_ref[...]
            stream_ref[pl.ds(pl.multiple_of((1 - where[3]) * half, 8), half), :] = other_ref[...]
            stream = stream_ref[...]
        unit, _ = norm_parts(stream)
        normed_ref[...] = (unit * vec_ref[0, 0:1, :] + vec_ref[0, 1:2, :]).astype(LOW)
        total[...] = jnp.zeros_like(total)

    weight = spread.load(w_refs, where, held_weight)
    tokens = where[4]
    head_columns = 3 * HD
    local = qkv_ref.shape[2]
    heads = local // head_columns
    scale = HD ** (-0.5)
    bias = []
    for head in range(heads):
        at = head * HD
        query_bias, value_bias = bias_ref[0, 0, 0, :, at : at + HD], bias_ref[0, 1, 0, :, at : at + HD]
        bias += [query_bias, jnp.zeros_like(query_bias), value_bias]
    bias = jnp.concatenate(bias, axis=1)
    qkv = (cdot(normed_ref[...], weight[:, :local]) + bias).astype(LOW)
    qkv_ref[0] = qkv
    mixed = []
    for head in range(heads):
        at = head * head_columns
        query = qkv[:, at : at + HD]
        key = qkv[:, at + HD : at + 2 * HD]
        value = qkv[:, at + 2 * HD : at + 3 * HD]
        scores = mask_keys(cdot(key, query, 1, 1) * scale, tokens)
        top = jnp.max(scores, axis=0, keepdims=True)
        raised = jnp.exp(scores - top)
        weight_sum = jnp.sum(raised, axis=0, keepdims=True)
        probs = (raised * (1.0 / weight_sum)).astype(LOW)
        mixed.append(cdot(value, probs, 0, 0))
        sums_ref[0, head : head + 1, :] = top + jnp.log(weight_sum)
    mixed = jnp.concatenate(mixed, axis=0).T.astype(LOW)
    mixed_ref[0] = mixed
    at = local + mixed.shape[1]
    total[...] += cdot(mixed, weight[:, local:at], 1, 1)
    tail_ref[0] = weight[:, at : at + 2 * tail_units]

    @pl.when(step == pl.num_programs(0) - 1)
    def _():
        part_ref[...] = total[...].astype(LOW)


def mlp_forward_kernel(spread, where, *refs):
    count = len(spread.shapes())
    base_ref, own_ref, other_ref, vec_ref, bias_ref, tail_ref, tail_bias_ref = refs[:7]
    w_refs = refs[7 : 7 + count]
    (middle_ref, normed_ref, act_ref, slope_ref, act_tail_ref, slope_tail_ref, up_tail_ref, down_tail_ref,
     part_ref, total, held_weight) = refs[7 + count :]
    step = pl.program_id(0)

    @pl.when(step == 0)
    def _():
        middle = (
            base_ref[...] + (own_ref[...].astype(F32) + other_ref[...].astype(F32)) + vec_ref[0, 4:5, :]
        )
        middle_ref[...] = middle
        unit, _ = norm_parts(middle)
        normed_ref[...] = (unit * vec_ref[0, 5:6, :] + vec_ref[0, 6:7, :]).astype(LOW)
        steps, _, both = tail_ref.shape
        half = both // 2
        up_tail_ref[...] = jnp.concatenate([tail_ref[t, :, :half] for t in range(steps)], axis=1)
        down_tail_ref[...] = jnp.concatenate([tail_ref[t, :, half:] for t in range(steps)], axis=1)
        tail_bias = turned(tail_bias_ref[0, 0], where[2], steps)
        act, slope = gelu_both(cdot(normed_ref[...], up_tail_ref[...]) + tail_bias)
        act = act.astype(LOW)
        act_tail_ref[...] = act
        slope_tail_ref[...] = slope.astype(LOW)
        total[...] = cdot(act, down_tail_ref[...], 1, 1)

    weight = spread.load(w_refs, where, held_weight)
    units = act_ref.shape[2]
    act, slope = gelu_both(cdot(normed_ref[...], weight[:, :units]) + bias_ref[0, 0, 0])
    act = act.astype(LOW)
    act_ref[0] = act
    slope_ref[0] = slope.astype(LOW)
    total[...] += cdot(act, weight[:, units:], 1, 1)

    @pl.when(step == pl.num_programs(0) - 1)
    def _():
        part_ref[...] = total[...].astype(LOW)


def mlp_backward_kernel(spread, where, *refs):
    count = len(spread.shapes())
    grad_ref, slope_ref, up_tail_ref, down_tail_ref, slope_tail_ref = refs[:5]
    w_refs = refs[5 : 5 + count]
    hidden_ref, hidden_tail_ref, sums_ref, sums_tail_ref, part_ref, low, total, held_weight = refs[5 + count :]
    step = pl.program_id(0)

    @pl.when(step == 0)
    def _():
        low[...] = grad_ref[...].astype(LOW)
        hidden = cdot(low[...], down_tail_ref[...]) * slope_tail_ref[...].astype(F32)
        steps = pl.num_programs(0)
        back = lax.rem(steps - where[2], steps)
        sums_tail_ref[...] = turned(jnp.sum(hidden, axis=0, keepdims=True), back, spread.place.nt)
        hidden = hidden.astype(LOW)
        hidden_tail_ref[...] = hidden
        total[...] = cdot(hidden, up_tail_ref[...], 1, 1)

    weight = spread.load(w_refs, where, held_weight)
    units = hidden_ref.shape[2]
    hidden = cdot(low[...], weight[:, units:]) * slope_ref[0].astype(F32)
    sums_ref[0] = jnp.sum(hidden, axis=0, keepdims=True)
    hidden = hidden.astype(LOW)
    hidden_ref[0] = hidden
    total[...] += cdot(hidden, weight[:, :units], 1, 1)

    @pl.when(step == pl.num_programs(0) - 1)
    def _():
        part_ref[...] = total[...].astype(LOW)


def mlp_grads_kernel(spread, where, *refs):
    count = len(spread.shapes())
    grad_ref, normed_ref, hidden_ref, act_ref, hidden_tail_ref, act_tail_ref = refs[:6]
    out_refs = refs[6 : 6 + count]
    tail_ref, grad_turned, normed_turned, result = refs[6 + count :]
    step = pl.program_id(0)

    @pl.when(step == 0)
    def _():
        grad_turned[...] = grad_ref[...].astype(LOW).T
        normed_turned[...] = normed_ref[...].T
        up_tail = cdot(normed_turned[...], hidden_tail_ref[...]).astype(LOW)
        down_tail = cdot(grad_turned[...], act_tail_ref[...]).astype(LOW)
        steps, _, both = tail_ref.shape
        half = both // 2
        for t in range(steps):
            at = slice(t * half, (t + 1) * half)
            tail_ref[t] = jnp.concatenate([up_tail[:, at], down_tail[:, at]], axis=1)

    units = hidden_ref.shape[2]
    result[:, :units] = cdot(normed_turned[...], hidden_ref[0]).astype(LOW)
    result[:, units:] = cdot(grad_turned[...], act_ref[0]).astype(LOW)
    spread.store(out_refs, where, result)


def attn_backward_kernel(spread, where, *refs):
    count = len(spread.shapes())
    grad_ref, own_ref, other_ref, middle_ref, vec_ref, qkv_ref, sums_ref = refs[:7]
    w_refs = refs[7 : 7 + count]
    dmiddle_ref, norm_sums_ref, dqkv_ref, head_sums_ref, part_ref, low, total, held_weight = refs[7 + count :]
    step = pl.program_id(0)

    @pl.when(step == 0)
    def _():
        grad = grad_ref[...]
        inner, gain_sum, shift_sum = norm_backward(
            own_ref[...].astype(F32) + other_ref[...].astype(F32), middle_ref[...], vec_ref[0, 5:6, :]
        )
        dmiddle = grad + inner
        dmiddle_ref[...] = dmiddle
        low[...] = dmiddle.astype(LOW)
        norm_sums_ref[0:1, :] = gain_sum
        norm_sums_ref[1:2, :] = shift_sum
        norm_sums_ref[2:3, :] = jnp.sum(grad, axis=0, keepdims=True)
        norm_sums_ref[3:4, :] = jnp.sum(dmiddle, axis=0, keepdims=True)
        total[...] = jnp.zeros_like(total)

    weight = spread.load(w_refs, where, held_weight)
    tokens = where[4]
    head_columns = 3 * HD
    local = qkv_ref.shape[2]
    heads = local // head_columns
    scale = HD ** (-0.5)
    qkv = qkv_ref[0]
    dmixed = cdot(low[...], weight[:, local : local + heads * HD]).astype(LOW)
    pieces = []
    for head in range(heads):
        at = head * head_columns
        query = qkv[:, at : at + HD]
        key = qkv[:, at + HD : at + 2 * HD]
        value = qkv[:, at + 2 * HD : at + 3 * HD]
        grad = dmixed[:, head * HD : (head + 1) * HD]
        scores = mask_keys(cdot(key, query, 1, 1) * scale, tokens)
        probs = jnp.exp(scores - sums_ref[0, head : head + 1, :])
        dprobs = cdot(value, grad, 1, 1)
        row_dot = jnp.sum(dprobs * probs, axis=0, keepdims=True)
        dscores = (probs * (dprobs - row_dot)).astype(LOW)
        pieces.append(cdot(key, dscores, 0, 0).T * scale)
        pieces.append(cdot(dscores, query) * scale)
        pieces.append(cdot(probs.astype(LOW), grad))
    dqkv = jnp.concatenate(pieces, axis=1)
    head_sums_ref[0] = jnp.sum(dqkv, axis=0, keepdims=True)
    dqkv = dqkv.astype(LOW)
    dqkv_ref[0] = dqkv
    total[...] += cdot(dqkv, weight[:, :local], 1, 1)

    @pl.when(step == pl.num_programs(0) - 1)
    def _():
        part_ref[...] = total[...].astype(LOW)


def attn_grads_kernel(spread, where, *refs):
    count = len(spread.shapes())
    dmiddle_ref, normed_ref, dqkv_ref, mixed_ref, tail_ref = refs[:5]
    out_refs = refs[5 : 5 + count]
    grad_turned, normed_turned, result = refs[5 + count :]

    @pl.when(pl.program_id(0) == 0)
    def _():
        grad_turned[...] = dmiddle_ref[...].astype(LOW).T
        normed_turned[...] = normed_ref[...].T

    parts = [
        cdot(normed_turned[...], dqkv_ref[0]).astype(LOW),
        cdot(grad_turned[...], mixed_ref[0]).astype(LOW),
        tail_ref[0],
    ]
    used = sum(part.shape[1] for part in parts)
    parts.append(jnp.zeros((result.shape[0], result.shape[1] - used), LOW))
    result[...] = jnp.concatenate(parts, axis=1)
    spread.store(out_refs, where, result)


def norm_backward_kernel(where, dmiddle_ref, own_ref, other_ref, stream_ref, vec_ref, out_ref, sums_ref):
    inner, gain_sum, shift_sum = norm_backward(
        own_ref[...].astype(F32) + other_ref[...].astype(F32), stream_ref[...], vec_ref[0, 0:1, :]
    )
    out_ref[...] = dmiddle_ref[...] + inner
    sums_ref[0:1, :] = gain_sum
    sums_ref[1:2, :] = shift_sum


def adam_kernel(units, local, out_local, tail_units, where, *refs):
    attn_own, attn_other, mlp_own, mlp_other = refs[:4]
    states = [refs[4 + 3 * k : 7 + 3 * k] for k in range(4)]
    outs = refs[len(refs) - 16 :]

    def pair(own, other):
        own, other = own[...], other[...]
        low_core = where[3] == 0
        return jnp.where(low_core, own, other), jnp.where(low_core, other, own)

    attn = pair(attn_own, attn_other)
    mlp = pair(mlp_own, mlp_other)
    at = local + out_local
    grads = [
        jnp.concatenate([half[:, :local] for half in attn], axis=1),
        jnp.concatenate([half[:, local:at] for half in attn], axis=1).T,
        jnp.concatenate(
            [piece for m, n in zip(mlp, attn) for piece in (m[:, :units], n[:, at : at + tail_units])], axis=1
        ),
        jnp.concatenate(
            [
                piece
                for m, n in zip(mlp, attn)
                for piece in (m[:, units:], n[:, at + tail_units : at + 2 * tail_units])
            ],
            axis=1,
        ).T,
    ]
    for number, grad in enumerate(grads):
        weight, first, second = [ref[0] for ref in states[number]]
        new = adam_step(weight, grad, first, second, RATES[number], DECAY)
        for ref, values in zip(outs[4 * number : 4 * number + 4], (grad, new[1], new[2], new[0])):
            ref[0] = values


def vec_pack_kernel(where, *refs):
    out_ref = refs[-1]
    layers = out_ref.shape[0]
    out_ref[...] = jnp.zeros_like(out_ref)
    for layer in range(layers):
        one_ref, two_ref, head_ref, main_ref, tail_ref = refs[5 * layer : 5 * layer + 5]
        out_ref[layer, 0:2, :] = one_ref[0:2, :]
        out_ref[layer, 2:6, :] = two_ref[0:4, :]
        for t in range(head_ref.shape[0]):
            out_ref[layer, 8 + t : 9 + t, : head_ref.shape[2]] = head_ref[t]
            out_ref[layer, 16 + t : 17 + t, : main_ref.shape[2]] = main_ref[t]
        out_ref[layer, 6:7, : tail_ref.shape[1]] = tail_ref[...]


def vec_kernel(steps, local, units, tail_units, where, own_ref, other_ref, vec_ref, first_ref, second_ref,
               grad_out, first_out, second_out, weight_out):
    low_core = where[3] == 0
    for layer in range(vec_ref.shape[0]):
        own, other = own_ref[layer], other_ref[layer]
        cores = jnp.where(low_core, own, other), jnp.where(low_core, other, own)
        norms = cores[0][0:6]
        heads = local // (3 * HD)

        def head_piece(kind):
            return [
                core[8 + t : 9 + t, (3 * head + kind) * HD : (3 * head + kind + 1) * HD]
                for t in range(steps)
                for core in cores
                for head in range(heads)
            ]

        hidden = [
            piece
            for t in range(steps)
            for core in cores
            for piece in (core[16 + t : 17 + t, :units], core[6:7, t * tail_units : (t + 1) * tail_units])
        ]
        grad = jnp.concatenate(
            [norms[0:1], norms[1:2], *head_piece(0), *head_piece(2),
             norms[5:6], norms[2:3], norms[3:4], norms[4:5], *hidden],
            axis=1,
        )
        at = slice(layer, layer + 1)
        new = adam_step(vec_ref[at, :], grad, first_ref[at, :], second_ref[at, :], RATES[4], 0.0)
        grad_out[at, :] = grad
        first_out[at, :] = new[1]
        second_out[at, :] = new[2]
        weight_out[at, :] = new[0]


def plane_sides(chips):
    side = math.isqrt(chips)
    while chips % side:
        side -= 1
    return side, chips // side


class Place:
    def __init__(self):
        self.nf = lax.axis_size("fsdp")
        self.nt = lax.axis_size("tp")
        self.na, self.nb = plane_sides(self.nf // 2)
        fi = lax.axis_index("fsdp")
        self.core = fi % 2
        self.a = (fi // 2) // self.nb
        self.b = (fi // 2) % self.nb
        self.t = lax.axis_index("tp")
        self.size = {"a": self.na, "b": self.nb, "t": self.nt}
        self.at = {"a": self.a, "b": self.b, "t": self.t}

    def pairs(self, axis, move):
        if axis == "t":
            return [(i, move(i)) for i in range(self.nt)]
        found = []
        for f in range(self.nf):
            place = {"a": f // 2 // self.nb, "b": f // 2 % self.nb, "core": f % 2}
            place[axis] = move(place[axis])
            found.append((f, (place["a"] * self.nb + place["b"]) * 2 + place["core"]))
        return found

    def send(self, values, axis, move):
        return lax.ppermute(values, "tp" if axis == "t" else "fsdp", self.pairs(axis, move))

    def sibling(self, values):
        return self.send(values, "core", lambda i: 1 - i)

    def swap_rows(self, values):
        pairs = []
        for f in range(self.nf):
            for t in range(self.nt):
                if f % 2 != t % 2:
                    sign = 1 if t % 2 else -1
                    pairs.append((f * self.nt + t, (f + sign) * self.nt + t - sign))
        arrived = lax.ppermute(values.astype(LOW), ("fsdp", "tp"), pairs).astype(F32)
        return jnp.where(self.core != self.t % 2, arrived, values)

    def gather_axis(self, block, axis):
        n = self.size[axis]
        return [block] + [self.send(block, axis, lambda i, k=k: (i - k) % n) for k in range(1, n)]

    def scatter_axis(self, parts, axis):
        n = self.size[axis]
        sent = [self.send(parts[k], axis, lambda i, k=k: (i + k) % n) for k in range(1, n)]
        return [parts[0], *sent]


def split_pair(place, first, second):
    return (
        jnp.where(place.core == 0, first, second),
        jnp.where(place.core == 0, second, first),
    )


def routes_of(kind, layer):
    if kind == "attn" or layer % 2 == 0:
        return ("t", "b", "a"), ("t", "a", "b")
    return ("b", "t", "a"), ("a", "t", "b")


class Spread:
    def __init__(self, place, kind, layer, rows, columns):
        self.place, self.rows, self.columns = place, rows, columns
        self.routes = routes_of(kind, layer)
        self.direct = rows % 16 == 0
        self.width = place.na * place.nb * 2 * rows

    def lead(self, route):
        return route[1], route[0]

    def shapes(self):
        size = self.place.size
        if not self.direct:
            full = (size["t"], self.width, self.columns)
            return [(full, (1, *full[1:]))]
        found = []
        for route in self.routes:
            lead = self.lead(route)
            shape = (*[size[axis] for axis in lead], self.rows, self.columns)
            block = (*[1 if axis == "t" else size[axis] for axis in lead], self.rows, self.columns)
            found += [(shape, block)] * size[route[2]]
        return found

    def specs(self):
        if not self.direct:
            return [pl.BlockSpec(block, lambda i, s: (i, 0, 0)) for _, block in self.shapes()]
        found = []
        for (shape, block), route in zip(
            self.shapes(), [route for route in self.routes for _ in range(self.place.size[route[2]])]
        ):
            if self.lead(route)[0] == "t":
                found.append(pl.BlockSpec(block, lambda i, s: (i, 0, 0, 0)))
            else:
                found.append(pl.BlockSpec(block, lambda i, s: (0, i, 0, 0)))
        return found

    def pieces(self, where):
        size = self.place.size
        number = 0
        for half, route in enumerate(self.routes):
            plane = [axis for axis in route[:2] if axis != "t"][0]
            for last in range(size[route[2]]):
                for inner in range(size[plane]):
                    at = {route[2]: last, plane: inner}
                    a = lax.rem(where[0] + at["a"], size["a"])
                    b = lax.rem(where[1] + at["b"], size["b"])
                    index = (0, inner) if self.lead(route)[0] == "t" else (inner, 0)
                    yield number, index, ((a * size["b"] + b) * 2 + half) * self.rows
                number += 1

    def load(self, refs, where, scratch):
        if not self.direct:
            return refs[0].at[0]
        for number, index, first in self.pieces(where):
            scratch[pl.ds(pl.multiple_of(first, 16), self.rows), :] = refs[number][index]
        return scratch

    def store(self, refs, where, scratch):
        if not self.direct:
            refs[0][0] = scratch[...]
            return
        for number, index, first in self.pieces(where):
            refs[number][index] = scratch[pl.ds(pl.multiple_of(first, 16), self.rows), :]

    def gather(self, own, other):
        place = self.place
        arrays = []
        for block, route in zip(split_pair(place, own, other), self.routes):
            for axis in route[:2]:
                block = jnp.stack(place.gather_axis(block, axis))
            arrays.append(place.gather_axis(block, route[2]))
        if self.direct:
            return [array for half in arrays for array in half]
        pieces = []
        for t in range(place.nt):
            for a in range(place.na):
                for b in range(place.nb):
                    at = {"t": t, "a": a, "b": b}
                    for blocks, route in zip(arrays, self.routes):
                        pieces.append(blocks[at[route[2]]][at[route[1]], at[route[0]]])
        full = jnp.concatenate(pieces, axis=0).reshape(place.nt, place.na, place.nb, -1, self.columns)
        full = lax.dynamic_slice_in_dim(
            jnp.concatenate([full, full], axis=1), (place.na - place.a) % place.na, place.na, 1
        )
        full = lax.dynamic_slice_in_dim(
            jnp.concatenate([full, full], axis=2), (place.nb - place.b) % place.nb, place.nb, 2
        )
        return [full.reshape(place.nt, -1, self.columns)]

    def scatter(self, arrays):
        place = self.place
        size = place.size
        if not self.direct:
            full = arrays[0].reshape(place.nt, place.na, place.nb, 2, self.rows, self.columns)
            full = lax.dynamic_slice_in_dim(jnp.concatenate([full, full], axis=1), place.a, place.na, 1)
            full = lax.dynamic_slice_in_dim(jnp.concatenate([full, full], axis=2), place.b, place.nb, 2)
            arrays = []
            for half, route in enumerate(self.routes):
                dims = ["tab".index(axis) for axis in (route[2], *self.lead(route))]
                values = full[:, :, :, half].transpose(*dims, 3, 4)
                arrays += [values[k] for k in range(size[route[2]])]
        done = []
        for route in self.routes:
            count = size[route[2]]
            parts, arrays = arrays[:count], arrays[count:]
            terms = place.scatter_axis(parts, route[2])
            for axis in (route[1], route[0]):
                parts = []
                for k in range(size[axis]):
                    total = sum(term[k].astype(F32) for term in terms)
                    parts.append(total if k == 0 else total.astype(LOW))
                terms = place.scatter_axis(parts, axis)
            done.append(sum(term.astype(F32) for term in terms))
        mine, other = split_pair(place, *done)
        return mine, place.sibling(other)


def body(
    residual_in,
    cotangent,
    slot_tokens,
    qkv_weight,
    out_weight,
    up_weight,
    down_weight,
    vectors,
    qkv_first,
    qkv_second,
    out_first,
    out_second,
    up_first,
    up_second,
    down_first,
    down_second,
    vec_first,
    vec_second,
):
    place = Place()
    layer_count, shard_rows, _ = qkv_weight.shape
    half_rows, width = residual_in.shape
    rows = 2 * half_rows
    nt = place.nt
    local = qkv_weight.shape[2] // 2
    out_local = out_weight.shape[1] // 2
    hidden_local = up_weight.shape[2] // 2
    units = hidden_local // 128 * 128
    tail_units = hidden_local - units
    heads = out_local // HD
    attn_columns = -(-(local + out_local + 2 * tail_units) // 128) * 128
    mlp_columns = 2 * units

    tokens_pair = jnp.concatenate(split_pair(place, slot_tokens, place.sibling(slot_tokens)))
    slot_at = (place.t % 2) * slot_tokens.shape[0] + place.t // 2
    tokens = lax.dynamic_slice_in_dim(tokens_pair, slot_at, 1)
    row_mask = (jnp.arange(rows, dtype=jnp.int32) < tokens[0]).astype(F32)[:, None]
    here = jnp.stack([place.a, place.b, place.t, place.core]).astype(jnp.int32)
    where = jnp.concatenate([here, tokens.astype(jnp.int32)])

    def own_rows(values):
        return lax.dynamic_slice_in_dim(values, place.core * half_rows, half_rows)

    spreads = [
        (
            Spread(place, "attn", layer, shard_rows, attn_columns),
            Spread(place, "mlp", layer, shard_rows, mlp_columns),
        )
        for layer in range(layer_count)
    ]

    def layer_block(array, layer):
        block = (1, *array.shape[1:])
        return pl.BlockSpec(block, lambda i, s: (layer, 0, 0), pipeline_mode=pl.Buffered(1))

    def pack(layer):
        attn, mlp = (shard_rows, attn_columns), (shard_rows, mlp_columns)
        return call(
            functools.partial(pack_kernel, units),
            here,
            1,
            [(layer_block(w, layer), w) for w in (qkv_weight, out_weight, up_weight, down_weight)],
            [(held(shape), low_of(*shape)) for shape in (attn, attn, mlp, mlp)],
            [],
            bytes_accessed=6 * shard_rows * 13216 // 4,
        )

    gathered = []
    for layer in range(layer_count):
        own_attn, other_attn, own_mlp, other_mlp = pack(layer)
        gathered.append(
            (
                spreads[layer][0].gather(own_attn, place.sibling(other_attn)),
                spreads[layer][1].gather(own_mlp, place.sibling(other_mlp)),
            )
        )

    wide = vectors[:, : 8 * width].reshape(layer_count, 8, width)
    head_bias = vectors[:, 2 * width : 4 * width].reshape(layer_count, 2, 2 * nt, 1, out_local)
    hidden_bias = vectors[:, 8 * width :].reshape(layer_count, nt, 2, 1, hidden_local)
    main_bias = hidden_bias[..., :units]
    tail_bias = jnp.moveaxis(hidden_bias[..., units:], 1, 3).reshape(layer_count, 2, 1, nt * tail_units)

    full = whole((rows, width))
    weight_scratch = [
        pltpu.VMEM((width, attn_columns), LOW),
        pltpu.VMEM((width, mlp_columns), LOW),
    ]
    flat = pltpu.VMEM((rows, width), F32)
    flat_low = pltpu.VMEM((rows, width), LOW)
    big = 2 * rows * width

    def wide_of(layer):
        spec = pl.BlockSpec((1, 8, width), lambda i, s: (layer, 0, 0), pipeline_mode=pl.Buffered(1))
        return spec, wide

    def block_at(i, s):
        return lax.rem(s[2] + i, nt)

    def attn_forward(layer, base, own, other):
        spread = spreads[layer][0]
        joined = base is not None
        if joined:
            ins = [(full, base), (full, own), (full, other), wide_of(layer - 1)]
        else:
            half = whole((half_rows, width))
            ins = [(half, own), (half, other)]
        ins.append(wide_of(layer))
        ins.append(
            (
                pl.BlockSpec(
                    (1, 2, 1, 1, out_local), lambda i, s: (layer, 0, 2 * block_at(i, s) + s[3], 0, 0)
                ),
                head_bias,
            )
        )
        ins += list(zip(spread.specs(), gathered[layer][0]))
        return call(
            functools.partial(attn_forward_kernel, spread, joined, tail_units),
            where,
            nt,
            ins,
            [
                (held((rows, width)), f32_of(rows, width)),
                (held((rows, width)), low_of(rows, width)),
                (stepped((rows, local)), low_of(nt, rows, local)),
                (stepped((rows, out_local)), low_of(nt, rows, out_local)),
                (stepped((heads, rows)), f32_of(nt, heads, rows)),
                (stepped((width, 2 * tail_units)), low_of(nt, width, 2 * tail_units)),
                (held((rows, width)), low_of(rows, width)),
            ],
            [flat, weight_scratch[0]],
            big * nt * (local + out_local) + 4 * nt * heads * rows * rows * HD,
            rows * width * 12 + nt * width * attn_columns * 2,
            nt * heads * rows * rows,
        )

    def mlp_forward(layer, base, own, other, tails):
        spread = spreads[layer][1]
        tail = nt * tail_units
        tail_shape = (width, tail)
        ins = [
            (full, base),
            (full, own),
            (full, other),
            wide_of(layer),
            (pl.BlockSpec((1, 1, 1, 1, units), lambda i, s: (layer, block_at(i, s), s[3], 0, 0)), main_bias),
            (whole(tails.shape), tails),
            (pl.BlockSpec((1, 1, 1, tail), lambda i, s: (layer, s[3], 0, 0)), tail_bias),
        ]
        ins += list(zip(spread.specs(), gathered[layer][1]))
        return call(
            functools.partial(mlp_forward_kernel, spread),
            where,
            nt,
            ins,
            [
                (held((rows, width)), f32_of(rows, width)),
                (held((rows, width)), low_of(rows, width)),
                (stepped((rows, units)), low_of(nt, rows, units)),
                (stepped((rows, units)), low_of(nt, rows, units)),
                (held((rows, tail)), low_of(rows, tail)),
                (held((rows, tail)), low_of(rows, tail)),
                (held(tail_shape), low_of(*tail_shape)),
                (held(tail_shape), low_of(*tail_shape)),
                (held((rows, width)), low_of(rows, width)),
            ],
            [flat, weight_scratch[1]],
            2 * big * (nt * units + tail),
            rows * width * 16 + nt * (width + rows) * mlp_columns * 2,
            rows * nt * units,
        )

    def mlp_backward(layer, grad, slope, tails, slope_tail):
        spread = spreads[layer][1]
        tail = nt * tail_units
        ins = [(full, grad), (stepped((rows, units)), slope)]
        ins += [(whole(w.shape), w) for w in (*tails, slope_tail)]
        ins += list(zip(spread.specs(), gathered[layer][1]))
        return call(
            functools.partial(mlp_backward_kernel, spread),
            where,
            nt,
            ins,
            [
                (stepped((rows, units)), low_of(nt, rows, units)),
                (held((rows, tail)), low_of(rows, tail)),
                (
                    pl.BlockSpec((1, 1, units), lambda i, s: (block_at(i, s), 0, 0)),
                    f32_of(nt, 1, units),
                ),
                (held((1, tail)), f32_of(1, tail)),
                (held((rows, width)), low_of(rows, width)),
            ],
            [flat_low, flat, weight_scratch[1]],
            2 * big * (nt * units + tail),
            rows * width * 6 + nt * (width + rows) * mlp_columns * 2,
        )

    def mlp_grads(layer, grad, normed, hidden, act, hidden_tail, act_tail):
        spread = spreads[layer][1]
        ins = [(full, grad), (full, normed)]
        ins += [(stepped((rows, units)), hidden), (stepped((rows, units)), act)]
        ins += [(whole(x.shape), x) for x in (hidden_tail, act_tail)]
        tail_shape = (nt, width, 2 * tail_units)
        outs = [(spec, low_of(*shape)) for spec, (shape, _) in zip(spread.specs(), spread.shapes())]
        outs.append((held(tail_shape), low_of(*tail_shape)))
        turned_low = pltpu.VMEM((width, rows), LOW)
        return call(
            functools.partial(mlp_grads_kernel, spread),
            where,
            nt,
            ins,
            outs,
            [turned_low, turned_low, weight_scratch[1]],
            2 * big * nt * (units + tail_units),
            rows * width * 6 + nt * (width + rows) * mlp_columns * 2,
        )

    def attn_backward(layer, grad, own, other, middle, qkv, log_sums):
        spread = spreads[layer][0]
        ins = [(full, grad), (full, own), (full, other), (full, middle), wide_of(layer)]
        ins += [(stepped((rows, local)), qkv), (stepped((heads, rows)), log_sums)]
        ins += list(zip(spread.specs(), gathered[layer][0]))
        return call(
            functools.partial(attn_backward_kernel, spread),
            where,
            nt,
            ins,
            [
                (held((rows, width)), f32_of(rows, width)),
                (held((8, width)), f32_of(8, width)),
                (stepped((rows, local)), low_of(nt, rows, local)),
                (
                    pl.BlockSpec((1, 1, local), lambda i, s: (block_at(i, s), 0, 0)),
                    f32_of(nt, 1, local),
                ),
                (held((rows, width)), low_of(rows, width)),
            ],
            [flat_low, flat, weight_scratch[0]],
            big * nt * (local + out_local) + 10 * nt * heads * rows * rows * HD,
            rows * width * 20 + nt * width * attn_columns * 2,
            nt * heads * rows * rows,
        )

    def attn_grads(layer, dmiddle, normed, dqkv, mixed, tail_grads):
        spread = spreads[layer][0]
        ins = [(full, dmiddle), (full, normed)]
        ins += [(stepped((rows, local)), dqkv), (stepped((rows, out_local)), mixed)]
        ins.append((stepped((width, 2 * tail_units)), tail_grads))
        outs = [(spec, low_of(*shape)) for spec, (shape, _) in zip(spread.specs(), spread.shapes())]
        turned_low = pltpu.VMEM((width, rows), LOW)
        return call(
            functools.partial(attn_grads_kernel, spread),
            where,
            nt,
            ins,
            outs,
            [turned_low, turned_low, weight_scratch[0]],
            big * nt * (local + out_local),
            rows * width * 6 + nt * (width + rows) * attn_columns * 2,
        )

    def norm_one_backward(layer, dmiddle, own, other, stream):
        return call(
            norm_backward_kernel,
            where,
            1,
            [(full, dmiddle), (full, own), (full, other), (full, stream), wide_of(layer)],
            [(held((rows, width)), f32_of(rows, width)), (held((8, width)), f32_of(8, width))],
            [],
            rows * width * 20,
            rows * width * 16,
        )

    mine = place.swap_rows(residual_in)
    base, own, other = None, mine, place.sibling(mine)
    saved = []
    for layer in range(layer_count):
        stream, normed, qkv, mixed, log_sums, tails, part = attn_forward(layer, base, own, other)
        middle, normed_two, act, slope, act_tail, slope_tail, up_tail, down_tail, part = mlp_forward(
            layer, stream, part, place.sibling(part), tails
        )
        saved.append(
            (stream, normed, qkv, mixed, log_sums, middle, normed_two, act, slope, act_tail, slope_tail,
             (up_tail, down_tail))
        )
        base, own, other = middle, part, place.sibling(part)
    output = own_rows(base) + (own_rows(own).astype(F32) + own_rows(other).astype(F32))
    output = place.swap_rows((output + wide[layer_count - 1, 7:8]) * own_rows(row_mask))

    mine = place.swap_rows(cotangent)
    grad_stream = jnp.concatenate(split_pair(place, mine, place.sibling(mine)), axis=0) * row_mask

    weights = (qkv_weight, out_weight, up_weight, down_weight)
    firsts = (qkv_first, out_first, up_first, down_first)
    seconds = (qkv_second, out_second, up_second, down_second)

    def adam(layer, attn_pair, mlp_pair, before):
        ins = [(whole(x.shape), x) for x in (*attn_pair, *mlp_pair)]
        for states in zip(weights, firsts, seconds):
            ins += [(layer_block(x, layer), x) for x in states]
        outs = [
            (layer_block(weight, layer), f32_of(*weight.shape)) for weight in weights for _ in range(4)
        ]
        aliases = None
        if before is not None:
            aliases = {1 + len(ins) + k: k for k in range(16)}
            ins += [(pl.BlockSpec(memory_space=pl.ANY), x) for x in before]
        return call(
            functools.partial(adam_kernel, units, local, out_local, tail_units),
            where,
            1,
            ins,
            outs,
            [],
            bytes_accessed=28 * shard_rows * 13216 // 4,
            aliases=aliases,
        )

    vec_sums = [None] * layer_count
    updated = None
    for layer in reversed(range(layer_count)):
        (stream, normed, qkv, mixed, log_sums, middle, normed_two, act, slope, act_tail, slope_tail, tails) = (
            saved[layer]
        )
        spread_attn, spread_mlp = spreads[layer]
        hidden, hidden_tail, hidden_sums, tail_sums, part = mlp_backward(
            layer, grad_stream, slope, tails, slope_tail
        )
        other = place.sibling(part)
        *mlp_grad, tail_grads = mlp_grads(
            layer, grad_stream, normed_two, hidden, act, hidden_tail, act_tail
        )
        mlp_pair = spread_mlp.scatter(mlp_grad)
        dmiddle, norm_two_sums, dqkv, head_sums, part = attn_backward(
            layer, grad_stream, part, other, middle, qkv, log_sums
        )
        other = place.sibling(part)
        attn_grad = attn_grads(layer, dmiddle, normed, dqkv, mixed, tail_grads)
        attn_pair = spread_attn.scatter(attn_grad)
        grad_stream, norm_one_sums = norm_one_backward(layer, dmiddle, part, other, stream)
        vec_sums[layer] = (norm_one_sums, norm_two_sums, head_sums, hidden_sums, tail_sums)
        updated = adam(layer, attn_pair, mlp_pair, updated)
    grad_input = place.swap_rows(own_rows(grad_stream))

    flat_sums = [x for sums in vec_sums for x in sums]
    vec_shape = (layer_count, 24, width)
    (vec_total,) = call(
        vec_pack_kernel,
        where,
        1,
        [(whole(x.shape), x) for x in flat_sums],
        [(held(vec_shape), f32_of(*vec_shape))],
        [],
    )
    for axis in ("b", "a", "t"):
        step = 1
        while step < place.size[axis]:
            vec_total = vec_total + place.send(vec_total, axis, lambda i: i ^ step)
            step *= 2
    vec_new = call(
        functools.partial(vec_kernel, nt, local, units, tail_units),
        where,
        1,
        [(whole(x.shape), x) for x in (vec_total, place.sibling(vec_total), vectors, vec_first, vec_second)],
        [(held(vectors.shape), f32_of(*vectors.shape)) for _ in range(4)],
        [],
    )
    return (output, grad_input, *updated, *vec_new)


def solution(mesh):
    rows = P(("fsdp", "tp"), None)
    wide = P(None, "fsdp", "tp")
    tall = P(None, "tp", "fsdp")
    moments = (wide, wide, tall, tall, wide, wide, tall, tall, P(), P())
    return jax.shard_map(
        body,
        mesh=mesh,
        in_specs=(rows, rows, P("fsdp"), wide, tall, wide, tall, P(), *moments),
        out_specs=(rows, rows, *[wide] * 4, *[tall] * 4, *[wide] * 4, *[tall] * 4, *[P()] * 4),
        check_vma=False,
    )
```

```python
import functools
import math

import jax
import jax.numpy as jnp
from jax import lax
from jax.experimental import pallas as pl
from jax.experimental.pallas import tpu as pltpu
from jax.sharding import PartitionSpec as P

HD = 72
IMG_TOK = 729
STEP = 10


EPS_NORM = 1e-06
MASKED = -30000.0
BETA_ONE = 0.9
BETA_TWO = 0.999
ADAM_EPS = 1e-08
DECAY = 0.1
RATES = (0.05, 1.0, 0.05, 0.03, 0.3)
LOW = jnp.bfloat16
F32 = jnp.float32
GELU = math.sqrt(2.0 / math.pi)
VMEM = 56 * 1024 * 1024


def adam_step(weight, gradient, first_moment, second_moment, step_rate, decay_rate):
    first_new = BETA_ONE * first_moment + (1.0 - BETA_ONE) * gradient
    second_new = BETA_TWO * second_moment + (1.0 - BETA_TWO) * gradient * gradient
    first_hat = first_new / (1.0 - BETA_ONE**STEP)
    second_hat = second_new / (1.0 - BETA_TWO**STEP)
    weight_new = weight - step_rate * (
        first_hat / (jnp.sqrt(second_hat) + ADAM_EPS) + decay_rate * weight
    )
    return (weight_new, first_new, second_new)


def cdot(left, right, left_dim=1, right_dim=0):
    return lax.dot_general(
        left, right, (((left_dim,), (right_dim,)), ((), ())), preferred_element_type=F32
    )


def norm_parts(values):
    centred = values - jnp.mean(values, axis=-1, keepdims=True)
    inverse = lax.rsqrt(jnp.mean(centred * centred, axis=-1, keepdims=True) + EPS_NORM)
    return centred * inverse, inverse


def norm_backward(grad_out, values, gain):
    unit, inverse = norm_parts(values)
    scaled = grad_out * gain
    mean_one = jnp.mean(scaled, axis=-1, keepdims=True)
    mean_two = jnp.mean(scaled * unit, axis=-1, keepdims=True)
    grad_in = inverse * (scaled - mean_one - unit * mean_two)
    gain_sum = jnp.sum(grad_out * unit, axis=0, keepdims=True)
    return grad_in, gain_sum, jnp.sum(grad_out, axis=0, keepdims=True)


def gelu_both(inputs):
    cubic = 0.044715 * inputs * inputs
    tanh = jnp.tanh(GELU * inputs * (1.0 + cubic))
    half = 0.5 * (1.0 + tanh)
    slope = half + 0.5 * GELU * inputs * (1.0 - tanh * tanh) * (1.0 + 3.0 * cubic)
    return inputs * half, slope


def mask_keys(scores, tokens):
    rows = scores.shape[0]
    whole = IMG_TOK // 8 * 8
    position = whole + lax.broadcasted_iota(jnp.int32, (rows - whole, 1), 0)
    return jnp.concatenate(
        [scores[:whole], jnp.where(position < tokens, scores[whole:], MASKED)], axis=0
    )


def whole(shape):
    return pl.BlockSpec(shape, lambda i, s: (0,) * len(shape), pipeline_mode=pl.Buffered(1))


def held(shape):
    return pl.BlockSpec(shape, lambda i, s: (0,) * len(shape))


def stepped(shape):
    return pl.BlockSpec((1,) + shape, lambda i, s: (i,) + (0,) * len(shape))


def low_of(*shape):
    return jax.ShapeDtypeStruct(shape, LOW)


def f32_of(*shape):
    return jax.ShapeDtypeStruct(shape, F32)


def call(kernel, where, steps, ins, outs, scratch, flops=0, bytes_accessed=0, transcendentals=0, aliases=None,
         after=()):
    given = 1 + len(ins)
    ins = ins + [(pl.BlockSpec(memory_space=pl.ANY), array) for array in after]

    def run(*refs):
        kernel(*refs[:given], *refs[given + len(after) :])

    return pl.pallas_call(
        run,
        grid_spec=pltpu.PrefetchScalarGridSpec(
            num_scalar_prefetch=1,
            grid=(steps,),
            in_specs=[spec for spec, _ in ins],
            out_specs=[spec for spec, _ in outs],
            scratch_shapes=scratch,
        ),
        out_shape=[shape for _, shape in outs],
        input_output_aliases=aliases or {},
        compiler_params=pltpu.CompilerParams(vmem_limit_bytes=VMEM),
        cost_estimate=pl.CostEstimate(
            flops=flops, bytes_accessed=bytes_accessed, transcendentals=transcendentals
        ),
    )(where, *[array for _, array in ins])


def pack_kernel(units, where, qkv_ref, out_ref, up_ref, down_ref, own_attn, other_attn, own_mlp, other_mlp):
    qkv, out = qkv_ref[0].astype(LOW), out_ref[0].T.astype(LOW)
    up, down = up_ref[0].astype(LOW), down_ref[0].T.astype(LOW)

    def half(values, number):
        size = values.shape[1] // 2
        return values[:, number * size : (number + 1) * size]

    for number in range(2):
        up_h, down_h = half(up, number), half(down, number)
        attn = [half(qkv, number), half(out, number), up_h[:, units:], down_h[:, units:]]
        used = sum(piece.shape[1] for piece in attn)
        attn.append(jnp.zeros((qkv.shape[0], own_attn.shape[1] - used), LOW))
        attn = jnp.concatenate(attn, axis=1)
        mlp = jnp.concatenate([up_h[:, :units], down_h[:, :units]], axis=1)

        @pl.when(where[3] == number)
        def _():
            own_attn[...] = attn
            own_mlp[...] = mlp

        @pl.when(where[3] != number)
        def _():
            other_attn[...] = attn
            other_mlp[...] = mlp


def attn_forward_kernel(spread, joined, tail_units, where, *refs):
    refs = list(refs)
    count = spread.count
    if joined:
        base_ref, own_ref, other_ref, old_ref = refs[:4]
        del refs[:4]
    else:
        own_ref, other_ref = refs[:2]
        del refs[:2]
    vec_ref, bias_ref = refs[:2]
    w_refs = refs[2 : 2 + count]
    (stream_ref, normed_ref, qkv_ref, mixed_ref, sums_ref, tail_ref, part_ref, total, held_weight) = refs[
        2 + count :
    ]
    step = pl.program_id(0)

    @pl.when(step == 0)
    def _():
        if joined:
            stream = (
                base_ref[...] + (own_ref[...].astype(F32) + other_ref[...].astype(F32)) + old_ref[0, 7:8, :]
            )
            stream_ref[...] = stream
        else:
            half = own_ref.shape[0]
            stream_ref[pl.ds(pl.multiple_of(where[3] * half, 8), half), :] = own_ref[...]
            stream_ref[pl.ds(pl.multiple_of((1 - where[3]) * half, 8), half), :] = other_ref[...]
            stream = stream_ref[...]
        unit, _ = norm_parts(stream)
        normed_ref[...] = (unit * vec_ref[0, 0:1, :] + vec_ref[0, 1:2, :]).astype(LOW)
        total[...] = jnp.zeros_like(total)

    weight = spread.load(w_refs, where, held_weight)
    tokens = where[4]
    head_columns = 3 * HD
    local = qkv_ref.shape[2]
    heads = local // head_columns
    scale = HD ** (-0.5)
    bias = []
    for head in range(heads):
        at = head * HD
        query_bias, value_bias = bias_ref[0, 0, 0, :, at : at + HD], bias_ref[0, 1, 0, :, at : at + HD]
        bias += [query_bias, jnp.zeros_like(query_bias), value_bias]
    bias = jnp.concatenate(bias, axis=1)
    qkv = (cdot(normed_ref[...], weight[:, :local]) + bias).astype(LOW)
    qkv_ref[0] = qkv
    mixed = []
    for head in range(heads):
        at = head * head_columns
        query = qkv[:, at : at + HD]
        key = qkv[:, at + HD : at + 2 * HD]
        value = qkv[:, at + 2 * HD : at + 3 * HD]
        scores = mask_keys(cdot(key, query, 1, 1) * scale, tokens)
        top = jnp.max(scores, axis=0, keepdims=True)
        raised = jnp.exp(scores - top)
        weight_sum = jnp.sum(raised, axis=0, keepdims=True)
        probs = (raised * (1.0 / weight_sum)).astype(LOW)
        mixed.append(cdot(value, probs, 0, 0))
        sums_ref[0, head : head + 1, :] = top + jnp.log(weight_sum)
    mixed = jnp.concatenate(mixed, axis=0).T.astype(LOW)
    mixed_ref[0] = mixed
    at = local + mixed.shape[1]
    total[...] += cdot(mixed, weight[:, local:at], 1, 1)
    tail_ref[0] = weight[:, at : at + 2 * tail_units]

    @pl.when(step == pl.num_programs(0) - 1)
    def _():
        part_ref[...] = total[...].astype(LOW)


def mlp_forward_kernel(spread, where, *refs):
    count = spread.count
    base_ref, own_ref, other_ref, vec_ref, bias_ref, tail_ref, tail_bias_ref = refs[:7]
    w_refs = refs[7 : 7 + count]
    (middle_ref, normed_ref, act_ref, slope_ref, act_tail_ref, slope_tail_ref, up_tail_ref, down_tail_ref,
     part_ref, total, held_weight) = refs[7 + count :]
    step = pl.program_id(0)

    @pl.when(step == 0)
    def _():
        middle = (
            base_ref[...] + (own_ref[...].astype(F32) + other_ref[...].astype(F32)) + vec_ref[0, 4:5, :]
        )
        middle_ref[...] = middle
        unit, _ = norm_parts(middle)
        normed_ref[...] = (unit * vec_ref[0, 5:6, :] + vec_ref[0, 6:7, :]).astype(LOW)
        steps, _, both = tail_ref.shape
        half = both // 2
        up_tail_ref[...] = jnp.concatenate([tail_ref[t, :, :half] for t in range(steps)], axis=1)
        down_tail_ref[...] = jnp.concatenate([tail_ref[t, :, half:] for t in range(steps)], axis=1)
        act, slope = gelu_both(cdot(normed_ref[...], up_tail_ref[...]) + tail_bias_ref[0, 0])
        act = act.astype(LOW)
        act_tail_ref[...] = act
        slope_tail_ref[...] = slope.astype(LOW)
        total[...] = cdot(act, down_tail_ref[...], 1, 1)

    weight = spread.load(w_refs, where, held_weight)
    units = act_ref.shape[2]
    act, slope = gelu_both(cdot(normed_ref[...], weight[:, :units]) + bias_ref[0, 0, 0])
    act = act.astype(LOW)
    act_ref[0] = act
    slope_ref[0] = slope.astype(LOW)
    total[...] += cdot(act, weight[:, units:], 1, 1)

    @pl.when(step == pl.num_programs(0) - 1)
    def _():
        part_ref[...] = total[...].astype(LOW)


def mlp_backward_kernel(spread, where, *refs):
    count = spread.count
    grad_ref, slope_ref, up_tail_ref, down_tail_ref, slope_tail_ref = refs[:5]
    w_refs = refs[5 : 5 + count]
    hidden_ref, hidden_tail_ref, sums_ref, sums_tail_ref, part_ref, low, total, held_weight = refs[5 + count :]
    step = pl.program_id(0)

    @pl.when(step == 0)
    def _():
        low[...] = grad_ref[...].astype(LOW)
        hidden = cdot(low[...], down_tail_ref[...]) * slope_tail_ref[...].astype(F32)
        sums_tail_ref[...] = jnp.sum(hidden, axis=0, keepdims=True)
        hidden = hidden.astype(LOW)
        hidden_tail_ref[...] = hidden
        total[...] = cdot(hidden, up_tail_ref[...], 1, 1)

    weight = spread.load(w_refs, where, held_weight)
    units = hidden_ref.shape[2]
    hidden = cdot(low[...], weight[:, units:]) * slope_ref[0].astype(F32)
    sums_ref[0] = jnp.sum(hidden, axis=0, keepdims=True)
    hidden = hidden.astype(LOW)
    hidden_ref[0] = hidden
    total[...] += cdot(hidden, weight[:, :units], 1, 1)

    @pl.when(step == pl.num_programs(0) - 1)
    def _():
        part_ref[...] = total[...].astype(LOW)


def mlp_grads_kernel(spread, where, *refs):
    count = spread.count
    grad_ref, normed_ref, hidden_ref, act_ref, hidden_tail_ref, act_tail_ref = refs[:6]
    out_refs = refs[6 : 6 + count]
    tail_ref, grad_turned, normed_turned, result = refs[6 + count :]
    step = pl.program_id(0)

    @pl.when(step == 0)
    def _():
        grad_turned[...] = grad_ref[...].astype(LOW).T
        normed_turned[...] = normed_ref[...].T
        up_tail = cdot(normed_turned[...], hidden_tail_ref[...]).astype(LOW)
        down_tail = cdot(grad_turned[...], act_tail_ref[...]).astype(LOW)
        steps, _, both = tail_ref.shape
        half = both // 2
        for t in range(steps):
            at = slice(t * half, (t + 1) * half)
            tail_ref[t] = jnp.concatenate([up_tail[:, at], down_tail[:, at]], axis=1)

    units = hidden_ref.shape[2]
    result[:, :units] = cdot(normed_turned[...], hidden_ref[0]).astype(LOW)
    result[:, units:] = cdot(grad_turned[...], act_ref[0]).astype(LOW)
    spread.store(out_refs, where, result)


def attn_backward_kernel(spread, where, *refs):
    count = spread.count
    grad_ref, own_ref, other_ref, middle_ref, vec_ref, qkv_ref, sums_ref = refs[:7]
    w_refs = refs[7 : 7 + count]
    dmiddle_ref, norm_sums_ref, dqkv_ref, head_sums_ref, part_ref, low, total, held_weight = refs[7 + count :]
    step = pl.program_id(0)

    @pl.when(step == 0)
    def _():
        grad = grad_ref[...]
        inner, gain_sum, shift_sum = norm_backward(
            own_ref[...].astype(F32) + other_ref[...].astype(F32), middle_ref[...], vec_ref[0, 5:6, :]
        )
        dmiddle = grad + inner
        dmiddle_ref[...] = dmiddle
        low[...] = dmiddle.astype(LOW)
        norm_sums_ref[0:1, :] = gain_sum
        norm_sums_ref[1:2, :] = shift_sum
        norm_sums_ref[2:3, :] = jnp.sum(grad, axis=0, keepdims=True)
        norm_sums_ref[3:4, :] = jnp.sum(dmiddle, axis=0, keepdims=True)
        total[...] = jnp.zeros_like(total)

    weight = spread.load(w_refs, where, held_weight)
    tokens = where[4]
    head_columns = 3 * HD
    local = qkv_ref.shape[2]
    heads = local // head_columns
    scale = HD ** (-0.5)
    qkv = qkv_ref[0]
    dmixed = cdot(low[...], weight[:, local : local + heads * HD]).astype(LOW)
    pieces = []
    for head in range(heads):
        at = head * head_columns
        query = qkv[:, at : at + HD]
        key = qkv[:, at + HD : at + 2 * HD]
        value = qkv[:, at + 2 * HD : at + 3 * HD]
        grad = dmixed[:, head * HD : (head + 1) * HD]
        scores = mask_keys(cdot(key, query, 1, 1) * scale, tokens)
        probs = jnp.exp(scores - sums_ref[0, head : head + 1, :])
        dprobs = cdot(value, grad, 1, 1)
        row_dot = jnp.sum(dprobs * probs, axis=0, keepdims=True)
        dscores = (probs * (dprobs - row_dot)).astype(LOW)
        pieces.append(cdot(key, dscores, 0, 0).T * scale)
        pieces.append(cdot(dscores, query) * scale)
        pieces.append(cdot(probs.astype(LOW), grad))
    dqkv = jnp.concatenate(pieces, axis=1)
    head_sums_ref[0] = jnp.sum(dqkv, axis=0, keepdims=True)
    dqkv = dqkv.astype(LOW)
    dqkv_ref[0] = dqkv
    total[...] += cdot(dqkv, weight[:, :local], 1, 1)

    @pl.when(step == pl.num_programs(0) - 1)
    def _():
        part_ref[...] = total[...].astype(LOW)


def attn_grads_kernel(spread, where, *refs):
    count = spread.count
    dmiddle_ref, normed_ref, dqkv_ref, mixed_ref, tail_ref = refs[:5]
    out_refs = refs[5 : 5 + count]
    grad_turned, normed_turned, result = refs[5 + count :]

    @pl.when(pl.program_id(0) == 0)
    def _():
        grad_turned[...] = dmiddle_ref[...].astype(LOW).T
        normed_turned[...] = normed_ref[...].T

    parts = [
        cdot(normed_turned[...], dqkv_ref[0]).astype(LOW),
        cdot(grad_turned[...], mixed_ref[0]).astype(LOW),
        tail_ref[0],
    ]
    used = sum(part.shape[1] for part in parts)
    parts.append(jnp.zeros((result.shape[0], result.shape[1] - used), LOW))
    result[...] = jnp.concatenate(parts, axis=1)
    spread.store(out_refs, where, result)


def norm_backward_kernel(where, dmiddle_ref, own_ref, other_ref, stream_ref, vec_ref, out_ref, sums_ref):
    inner, gain_sum, shift_sum = norm_backward(
        own_ref[...].astype(F32) + other_ref[...].astype(F32), stream_ref[...], vec_ref[0, 0:1, :]
    )
    out_ref[...] = dmiddle_ref[...] + inner
    sums_ref[0:1, :] = gain_sum
    sums_ref[1:2, :] = shift_sum


def adam_kernel(units, local, out_local, tail_units, where, *refs):
    attn_own, attn_other, mlp_own, mlp_other = refs[:4]
    states = [refs[4 + 3 * k : 7 + 3 * k] for k in range(4)]
    outs = refs[len(refs) - 16 :]

    def pair(own, other):
        own, other = own[...].astype(F32), other[...].astype(F32)
        low_core = where[3] == 0
        return jnp.where(low_core, own, other), jnp.where(low_core, other, own)

    attn = pair(attn_own, attn_other)
    mlp = pair(mlp_own, mlp_other)
    at = local + out_local
    grads = [
        jnp.concatenate([half[:, :local] for half in attn], axis=1),
        jnp.concatenate([half[:, local:at] for half in attn], axis=1).T,
        jnp.concatenate(
            [piece for m, n in zip(mlp, attn) for piece in (m[:, :units], n[:, at : at + tail_units])], axis=1
        ),
        jnp.concatenate(
            [
                piece
                for m, n in zip(mlp, attn)
                for piece in (m[:, units:], n[:, at + tail_units : at + 2 * tail_units])
            ],
            axis=1,
        ).T,
    ]
    for number, grad in enumerate(grads):
        weight, first, second = [ref[0] for ref in states[number]]
        new = adam_step(weight, grad, first, second, RATES[number], DECAY)
        for ref, values in zip(outs[4 * number : 4 * number + 4], (grad, new[1], new[2], new[0])):
            ref[0] = values


def vec_pack_kernel(where, *refs):
    out_ref = refs[-1]
    layers = out_ref.shape[0]
    out_ref[...] = jnp.zeros_like(out_ref)
    for layer in range(layers):
        one_ref, two_ref, head_ref, main_ref, tail_ref = refs[5 * layer : 5 * layer + 5]
        out_ref[layer, 0:2, :] = one_ref[0:2, :]
        out_ref[layer, 2:6, :] = two_ref[0:4, :]
        for t in range(head_ref.shape[0]):
            out_ref[layer, 8 + t : 9 + t, : head_ref.shape[2]] = head_ref[t]
            out_ref[layer, 16 + t : 17 + t, : main_ref.shape[2]] = main_ref[t]
        out_ref[layer, 6:7, : tail_ref.shape[1]] = tail_ref[...]


def vec_kernel(steps, local, units, tail_units, where, own_ref, other_ref, vec_ref, first_ref, second_ref,
               grad_out, first_out, second_out, weight_out):
    low_core = where[3] == 0
    for layer in range(vec_ref.shape[0]):
        own, other = own_ref[layer], other_ref[layer]
        cores = jnp.where(low_core, own, other), jnp.where(low_core, other, own)
        norms = cores[0][0:6]
        heads = local // (3 * HD)

        def head_piece(kind):
            return [
                core[8 + t : 9 + t, (3 * head + kind) * HD : (3 * head + kind + 1) * HD]
                for t in range(steps)
                for core in cores
                for head in range(heads)
            ]

        hidden = [
            piece
            for t in range(steps)
            for core in cores
            for piece in (core[16 + t : 17 + t, :units], core[6:7, t * tail_units : (t + 1) * tail_units])
        ]
        grad = jnp.concatenate(
            [norms[0:1], norms[1:2], *head_piece(0), *head_piece(2),
             norms[5:6], norms[2:3], norms[3:4], norms[4:5], *hidden],
            axis=1,
        )
        at = slice(layer, layer + 1)
        new = adam_step(vec_ref[at, :], grad, first_ref[at, :], second_ref[at, :], RATES[4], 0.0)
        grad_out[at, :] = grad
        first_out[at, :] = new[1]
        second_out[at, :] = new[2]
        weight_out[at, :] = new[0]


def plane_sides(chips):
    side = math.isqrt(chips)
    while chips % side:
        side -= 1
    return side, chips // side


class Place:
    def __init__(self):
        self.nf = lax.axis_size("fsdp")
        self.nt = lax.axis_size("tp")
        self.na, self.nb = plane_sides(self.nf // 2)
        fi = lax.axis_index("fsdp")
        self.core = fi % 2
        self.a = (fi // 2) // self.nb
        self.b = (fi // 2) % self.nb
        self.t = lax.axis_index("tp")
        self.size = {"a": self.na, "b": self.nb, "t": self.nt}
        self.at = {"a": self.a, "b": self.b, "t": self.t}

    def pairs(self, axis, move):
        if axis == "t":
            return [(i, move(i)) for i in range(self.nt)]
        found = []
        for f in range(self.nf):
            place = {"a": f // 2 // self.nb, "b": f // 2 % self.nb, "core": f % 2}
            place[axis] = move(place[axis])
            found.append((f, (place["a"] * self.nb + place["b"]) * 2 + place["core"]))
        return found

    def send(self, values, axis, move):
        return lax.ppermute(values, "tp" if axis == "t" else "fsdp", self.pairs(axis, move))

    def sibling(self, values):
        return self.send(values, "core", lambda i: 1 - i)

    def swap_rows(self, values):
        pairs = []
        for f in range(self.nf):
            for t in range(self.nt):
                if f % 2 != t % 2:
                    sign = 1 if t % 2 else -1
                    pairs.append((f * self.nt + t, (f + sign) * self.nt + t - sign))
        arrived = lax.ppermute(values.astype(LOW), ("fsdp", "tp"), pairs).astype(F32)
        return jnp.where(self.core != self.t % 2, arrived, values)

    def gather_axis(self, block, axis):
        n = self.size[axis]
        return [block] + [self.send(block, axis, lambda i, k=k: (i - k) % n) for k in range(1, n)]

    def scatter_axis(self, parts, axis):
        n = self.size[axis]
        sent = [self.send(parts[k], axis, lambda i, k=k: (i + k) % n) for k in range(1, n)]
        return [parts[0], *sent]


def split_pair(place, first, second):
    return (
        jnp.where(place.core == 0, first, second),
        jnp.where(place.core == 0, second, first),
    )


def sum_kernel(groups, where, *refs):
    ins, outs = refs[: sum(groups)], refs[sum(groups) :]
    for out_ref, size in zip(outs, groups):
        total = ins[0][...].astype(F32)
        for ref in ins[1:size]:
            total += ref[...].astype(F32)
        out_ref[...] = total.astype(LOW)
        ins = ins[size:]


class Spread:
    def __init__(self, place, rows, columns):
        self.place, self.rows, self.columns = place, rows, columns
        self.direct = rows % 16 == 0
        self.width = place.na * place.nb * 2 * rows
        self.keys = [(half, a, b) for half in range(2) for a in range(place.na) for b in range(place.nb)]
        if self.direct:
            self.shape = (place.nt, rows, columns)
            self.count = len(self.keys)
        else:
            self.shape = (place.nt, self.width, columns)
            self.count = 1

    def specs(self):
        return [stepped(self.shape[1:])] * self.count

    def first_row(self, where, key):
        half, a, b = key
        a = lax.rem(where[0] + a, self.place.na)
        b = lax.rem(where[1] + b, self.place.nb)
        return pl.multiple_of(((a * self.place.nb + b) * 2 + half) * self.rows, 16)

    def load(self, refs, where, scratch):
        if not self.direct:
            return refs[0].at[0]
        for ref, key in zip(refs, self.keys):
            scratch[pl.ds(self.first_row(where, key), self.rows), :] = ref[0]
        return scratch

    def store(self, refs, where, scratch):
        if not self.direct:
            refs[0][0] = scratch[...]
            return
        for ref, key in zip(refs, self.keys):
            ref[0] = scratch[pl.ds(self.first_row(where, key), self.rows), :]

    def gather(self, own, other):
        place = self.place
        found = {}
        for half, block in enumerate(split_pair(place, own, other)):
            block = lax.all_gather(block, "tp")
            first, last = ("b", "a") if half == 0 else ("a", "b")
            for i, outer in enumerate(place.gather_axis(block, first)):
                for j, inner in enumerate(place.gather_axis(outer, last)):
                    found[(half, j, i) if half == 0 else (half, i, j)] = inner
        arrays = [found[key] for key in self.keys]
        if self.direct:
            return arrays
        full = jnp.stack(arrays).reshape(2, place.na, place.nb, place.nt, self.rows, self.columns)
        full = full.transpose(3, 1, 2, 0, 4, 5)
        full = self.roll(full, (place.na - place.a) % place.na, (place.nb - place.b) % place.nb)
        return [full.reshape(self.shape)]

    def roll(self, full, a, b):
        full = lax.dynamic_slice_in_dim(jnp.concatenate([full, full], axis=1), a, self.place.na, 1)
        return lax.dynamic_slice_in_dim(jnp.concatenate([full, full], axis=2), b, self.place.nb, 2)

    def split(self, arrays):
        if not self.direct:
            place = self.place
            full = arrays[0].reshape(place.nt, place.na, place.nb, 2, self.rows, self.columns)
            full = self.roll(full, place.a, place.b)
            arrays = [full[:, a, b, half] for half, a, b in self.keys]
        return dict(zip(self.keys, arrays))

    def sums(self, where, groups, after=()):
        shape = (self.place.nt, self.rows, self.columns)
        spec = stepped(shape[1:])
        return call(
            functools.partial(sum_kernel, [len(group) for group in groups]),
            where,
            self.place.nt,
            [(spec, x) for group in groups for x in group],
            [(spec, low_of(*shape))] * len(groups),
            [],
            bytes_accessed=math.prod(shape) * 2 * (sum(len(group) for group in groups) + len(groups)),
            after=after,
        )

    def scatter_last(self, arrays):
        place = self.place
        grads = self.split(arrays)
        terms = {}
        for half in range(2):
            axis, other = ("a", "b") if half == 0 else ("b", "a")
            for i in range(place.size[other]):
                parts = [
                    grads[(half, k, i) if half == 0 else (half, i, k)] for k in range(place.size[axis])
                ]
                terms[half, i] = place.scatter_axis(parts, axis)
        return terms

    def scatter_first(self, where, terms, after=()):
        place = self.place
        axes = ("b", "a")
        keys = [(half, i) for half in range(2) for i in range(1, place.size[axes[half]])]
        sums = dict(zip(keys, self.sums(where, [terms[key] for key in keys], after)))
        result = []
        for half, axis in enumerate(axes):
            sent = [
                place.send(sums[half, k], axis, lambda i, k=k: (i + k) % place.size[axis])
                for k in range(1, place.size[axis])
            ]
            result.append([*terms[half, 0], *sent])
        return result

    def scatter_tp(self, where, groups, after=()):
        place = self.place
        sums = self.sums(where, groups, after)
        done = [lax.psum_scatter(total, "tp", scatter_dimension=0, tiled=True)[0] for total in sums]
        mine, other = split_pair(place, *done)
        return mine, place.sibling(other)


def body(
    residual_in,
    cotangent,
    slot_tokens,
    qkv_weight,
    out_weight,
    up_weight,
    down_weight,
    vectors,
    qkv_first,
    qkv_second,
    out_first,
    out_second,
    up_first,
    up_second,
    down_first,
    down_second,
    vec_first,
    vec_second,
):
    place = Place()
    layer_count, shard_rows, _ = qkv_weight.shape
    half_rows, width = residual_in.shape
    rows = 2 * half_rows
    nt = place.nt
    local = qkv_weight.shape[2] // 2
    out_local = out_weight.shape[1] // 2
    hidden_local = up_weight.shape[2] // 2
    units = hidden_local // 128 * 128
    tail_units = hidden_local - units
    heads = out_local // HD
    attn_columns = -(-(local + out_local + 2 * tail_units) // 128) * 128
    mlp_columns = 2 * units

    tokens_pair = jnp.concatenate(split_pair(place, slot_tokens, place.sibling(slot_tokens)))
    slot_at = (place.t % 2) * slot_tokens.shape[0] + place.t // 2
    tokens = lax.dynamic_slice_in_dim(tokens_pair, slot_at, 1)
    row_mask = (jnp.arange(rows, dtype=jnp.int32) < tokens[0]).astype(F32)[:, None]
    here = jnp.stack([place.a, place.b, place.t, place.core]).astype(jnp.int32)
    where = jnp.concatenate([here, tokens.astype(jnp.int32)])

    def own_rows(values):
        return lax.dynamic_slice_in_dim(values, place.core * half_rows, half_rows)

    spreads = [
        (
            Spread(place, shard_rows, attn_columns),
            Spread(place, shard_rows, mlp_columns),
        )
        for layer in range(layer_count)
    ]

    def layer_block(array, layer):
        block = (1, *array.shape[1:])
        return pl.BlockSpec(block, lambda i, s: (layer, 0, 0), pipeline_mode=pl.Buffered(1))

    def pack(layer):
        attn, mlp = (shard_rows, attn_columns), (shard_rows, mlp_columns)
        return call(
            functools.partial(pack_kernel, units),
            here,
            1,
            [(layer_block(w, layer), w) for w in (qkv_weight, out_weight, up_weight, down_weight)],
            [(held(shape), low_of(*shape)) for shape in (attn, attn, mlp, mlp)],
            [],
            bytes_accessed=6 * shard_rows * 13216 // 4,
        )

    gathered = []
    for layer in range(layer_count):
        own_attn, other_attn, own_mlp, other_mlp = pack(layer)
        gathered.append(
            (
                spreads[layer][0].gather(own_attn, place.sibling(other_attn)),
                spreads[layer][1].gather(own_mlp, place.sibling(other_mlp)),
            )
        )

    wide = vectors[:, : 8 * width].reshape(layer_count, 8, width)
    head_bias = vectors[:, 2 * width : 4 * width].reshape(layer_count, 2, 2 * nt, 1, out_local)
    hidden_bias = vectors[:, 8 * width :].reshape(layer_count, nt, 2, 1, hidden_local)
    main_bias = hidden_bias[..., :units]
    tail_bias = jnp.moveaxis(hidden_bias[..., units:], 1, 3).reshape(layer_count, 2, 1, nt * tail_units)

    full = whole((rows, width))
    weight_scratch = [
        pltpu.VMEM((width, attn_columns), LOW),
        pltpu.VMEM((width, mlp_columns), LOW),
    ]
    flat = pltpu.VMEM((rows, width), F32)
    flat_low = pltpu.VMEM((rows, width), LOW)
    big = 2 * rows * width

    def wide_of(layer):
        spec = pl.BlockSpec((1, 8, width), lambda i, s: (layer, 0, 0), pipeline_mode=pl.Buffered(1))
        return spec, wide

    def attn_forward(layer, base, own, other):
        spread = spreads[layer][0]
        joined = base is not None
        if joined:
            ins = [(full, base), (full, own), (full, other), wide_of(layer - 1)]
        else:
            half = whole((half_rows, width))
            ins = [(half, own), (half, other)]
        ins.append(wide_of(layer))
        ins.append(
            (
                pl.BlockSpec(
                    (1, 2, 1, 1, out_local), lambda i, s: (layer, 0, 2 * i + s[3], 0, 0)
                ),
                head_bias,
            )
        )
        ins += list(zip(spread.specs(), gathered[layer][0]))
        return call(
            functools.partial(attn_forward_kernel, spread, joined, tail_units),
            where,
            nt,
            ins,
            [
                (held((rows, width)), f32_of(rows, width)),
                (held((rows, width)), low_of(rows, width)),
                (stepped((rows, local)), low_of(nt, rows, local)),
                (stepped((rows, out_local)), low_of(nt, rows, out_local)),
                (stepped((heads, rows)), f32_of(nt, heads, rows)),
                (stepped((width, 2 * tail_units)), low_of(nt, width, 2 * tail_units)),
                (held((rows, width)), low_of(rows, width)),
            ],
            [flat, weight_scratch[0]],
            big * nt * (local + out_local) + 4 * nt * heads * rows * rows * HD,
            rows * width * 12 + nt * width * attn_columns * 2,
            nt * heads * rows * rows,
        )

    def mlp_forward(layer, base, own, other, tails):
        spread = spreads[layer][1]
        tail = nt * tail_units
        tail_shape = (width, tail)
        ins = [
            (full, base),
            (full, own),
            (full, other),
            wide_of(layer),
            (pl.BlockSpec((1, 1, 1, 1, units), lambda i, s: (layer, i, s[3], 0, 0)), main_bias),
            (whole(tails.shape), tails),
            (pl.BlockSpec((1, 1, 1, tail), lambda i, s: (layer, s[3], 0, 0)), tail_bias),
        ]
        ins += list(zip(spread.specs(), gathered[layer][1]))
        return call(
            functools.partial(mlp_forward_kernel, spread),
            where,
            nt,
            ins,
            [
                (held((rows, width)), f32_of(rows, width)),
                (held((rows, width)), low_of(rows, width)),
                (stepped((rows, units)), low_of(nt, rows, units)),
                (stepped((rows, units)), low_of(nt, rows, units)),
                (held((rows, tail)), low_of(rows, tail)),
                (held((rows, tail)), low_of(rows, tail)),
                (held(tail_shape), low_of(*tail_shape)),
                (held(tail_shape), low_of(*tail_shape)),
                (held((rows, width)), low_of(rows, width)),
            ],
            [flat, weight_scratch[1]],
            2 * big * (nt * units + tail),
            rows * width * 16 + nt * (width + rows) * mlp_columns * 2,
            rows * nt * units,
        )

    def mlp_backward(layer, grad, slope, tails, slope_tail):
        spread = spreads[layer][1]
        tail = nt * tail_units
        ins = [(full, grad), (stepped((rows, units)), slope)]
        ins += [(whole(w.shape), w) for w in (*tails, slope_tail)]
        ins += list(zip(spread.specs(), gathered[layer][1]))
        return call(
            functools.partial(mlp_backward_kernel, spread),
            where,
            nt,
            ins,
            [
                (stepped((rows, units)), low_of(nt, rows, units)),
                (held((rows, tail)), low_of(rows, tail)),
                (stepped((1, units)), f32_of(nt, 1, units)),
                (held((1, tail)), f32_of(1, tail)),
                (held((rows, width)), low_of(rows, width)),
            ],
            [flat_low, flat, weight_scratch[1]],
            2 * big * (nt * units + tail),
            rows * width * 6 + nt * (width + rows) * mlp_columns * 2,
        )

    def mlp_grads(layer, grad, normed, hidden, act, hidden_tail, act_tail):
        spread = spreads[layer][1]
        ins = [(full, grad), (full, normed)]
        ins += [(stepped((rows, units)), hidden), (stepped((rows, units)), act)]
        ins += [(whole(x.shape), x) for x in (hidden_tail, act_tail)]
        tail_shape = (nt, width, 2 * tail_units)
        outs = [(spec, low_of(*spread.shape)) for spec in spread.specs()]
        outs.append((held(tail_shape), low_of(*tail_shape)))
        turned_low = pltpu.VMEM((width, rows), LOW)
        return call(
            functools.partial(mlp_grads_kernel, spread),
            where,
            nt,
            ins,
            outs,
            [turned_low, turned_low, weight_scratch[1]],
            2 * big * nt * (units + tail_units),
            rows * width * 6 + nt * (width + rows) * mlp_columns * 2,
        )

    def attn_backward(layer, grad, own, other, middle, qkv, log_sums, after=()):
        spread = spreads[layer][0]
        ins = [(full, grad), (full, own), (full, other), (full, middle), wide_of(layer)]
        ins += [(stepped((rows, local)), qkv), (stepped((heads, rows)), log_sums)]
        ins += list(zip(spread.specs(), gathered[layer][0]))
        return call(
            functools.partial(attn_backward_kernel, spread),
            where,
            nt,
            ins,
            [
                (held((rows, width)), f32_of(rows, width)),
                (held((8, width)), f32_of(8, width)),
                (stepped((rows, local)), low_of(nt, rows, local)),
                (stepped((1, local)), f32_of(nt, 1, local)),
                (held((rows, width)), low_of(rows, width)),
            ],
            [flat_low, flat, weight_scratch[0]],
            big * nt * (local + out_local) + 10 * nt * heads * rows * rows * HD,
            rows * width * 20 + nt * width * attn_columns * 2,
            nt * heads * rows * rows,
            after=after,
        )

    def attn_grads(layer, dmiddle, normed, dqkv, mixed, tail_grads):
        spread = spreads[layer][0]
        ins = [(full, dmiddle), (full, normed)]
        ins += [(stepped((rows, local)), dqkv), (stepped((rows, out_local)), mixed)]
        ins.append((stepped((width, 2 * tail_units)), tail_grads))
        outs = [(spec, low_of(*spread.shape)) for spec in spread.specs()]
        turned_low = pltpu.VMEM((width, rows), LOW)
        return call(
            functools.partial(attn_grads_kernel, spread),
            where,
            nt,
            ins,
            outs,
            [turned_low, turned_low, weight_scratch[0]],
            big * nt * (local + out_local),
            rows * width * 6 + nt * (width + rows) * attn_columns * 2,
        )

    def norm_one_backward(layer, dmiddle, own, other, stream, after=()):
        return call(
            norm_backward_kernel,
            where,
            1,
            [(full, dmiddle), (full, own), (full, other), (full, stream), wide_of(layer)],
            [(held((rows, width)), f32_of(rows, width)), (held((8, width)), f32_of(8, width))],
            [],
            rows * width * 20,
            rows * width * 16,
            after=after,
        )

    mine = place.swap_rows(residual_in)
    base, own, other = None, mine, place.sibling(mine)
    saved = []
    for layer in range(layer_count):
        stream, normed, qkv, mixed, log_sums, tails, part = attn_forward(layer, base, own, other)
        middle, normed_two, act, slope, act_tail, slope_tail, up_tail, down_tail, part = mlp_forward(
            layer, stream, part, place.sibling(part), tails
        )
        saved.append(
            (stream, normed, qkv, mixed, log_sums, middle, normed_two, act, slope, act_tail, slope_tail,
             (up_tail, down_tail))
        )
        base, own, other = middle, part, place.sibling(part)
    output = own_rows(base) + (own_rows(own).astype(F32) + own_rows(other).astype(F32))
    output = place.swap_rows((output + wide[layer_count - 1, 7:8]) * own_rows(row_mask))

    mine = place.swap_rows(cotangent)
    grad_stream = jnp.concatenate(split_pair(place, mine, place.sibling(mine)), axis=0) * row_mask

    weights = (qkv_weight, out_weight, up_weight, down_weight)
    firsts = (qkv_first, out_first, up_first, down_first)
    seconds = (qkv_second, out_second, up_second, down_second)

    def adam(layer, attn_pair, mlp_pair, before, after=()):
        ins = [(whole(x.shape), x) for x in (*attn_pair, *mlp_pair)]
        for states in zip(weights, firsts, seconds):
            ins += [(layer_block(x, layer), x) for x in states]
        outs = [
            (layer_block(weight, layer), f32_of(*weight.shape)) for weight in weights for _ in range(4)
        ]
        aliases = None
        if before is not None:
            aliases = {1 + len(ins) + k: k for k in range(16)}
            ins += [(pl.BlockSpec(memory_space=pl.ANY), x) for x in before]
        return call(
            functools.partial(adam_kernel, units, local, out_local, tail_units),
            where,
            1,
            ins,
            outs,
            [],
            bytes_accessed=28 * shard_rows * 13216 // 4,
            aliases=aliases,
            after=after,
        )

    vec_sums = [None] * layer_count
    updated = None
    behind = []
    for layer in reversed(range(layer_count)):
        (stream, normed, qkv, mixed, log_sums, middle, normed_two, act, slope, act_tail, slope_tail, tails) = (
            saved[layer]
        )
        spread_attn, spread_mlp = spreads[layer]
        hidden, hidden_tail, hidden_sums, tail_sums, part = mlp_backward(
            layer, grad_stream, slope, tails, slope_tail
        )
        other = place.sibling(part)
        *mlp_grad, tail_grads = mlp_grads(
            layer, grad_stream, normed_two, hidden, act, hidden_tail, act_tail
        )
        mlp_terms = spread_mlp.scatter_last(mlp_grad)
        if behind:
            above, attn_terms_above, mlp_pair_above = behind
            attn_terms_above = spreads[above][0].scatter_first(where, attn_terms_above, mlp_grad[:1])
        dmiddle, norm_two_sums, dqkv, head_sums, part = attn_backward(
            layer, grad_stream, part, other, middle, qkv, log_sums, mlp_grad[:1]
        )
        other = place.sibling(part)
        attn_grad = attn_grads(layer, dmiddle, normed, dqkv, mixed, tail_grads)
        attn_terms = spread_attn.scatter_last(attn_grad)
        if behind:
            attn_pair_above = spreads[above][0].scatter_tp(where, attn_terms_above, attn_grad[:1])
        grad_stream, norm_one_sums = norm_one_backward(layer, dmiddle, part, other, stream, attn_grad[:1])
        mlp_terms = spread_mlp.scatter_first(where, mlp_terms, [norm_one_sums])
        vec_sums[layer] = (norm_one_sums, norm_two_sums, head_sums, hidden_sums, tail_sums)
        mlp_pair = spread_mlp.scatter_tp(where, mlp_terms)
        if behind:
            updated = adam(above, attn_pair_above, mlp_pair_above, updated)
        behind = layer, attn_terms, mlp_pair
    above, attn_terms_above, mlp_pair_above = behind
    attn_terms_above = spreads[above][0].scatter_first(where, attn_terms_above)
    attn_pair_above = spreads[above][0].scatter_tp(where, attn_terms_above)
    updated = adam(above, attn_pair_above, mlp_pair_above, updated)
    grad_input = place.swap_rows(own_rows(grad_stream))

    flat_sums = [x for sums in vec_sums for x in sums]
    vec_shape = (layer_count, 24, width)
    (vec_total,) = call(
        vec_pack_kernel,
        where,
        1,
        [(whole(x.shape), x) for x in flat_sums],
        [(held(vec_shape), f32_of(*vec_shape))],
        [],
    )
    for axis in ("b", "a", "t"):
        step = 1
        while step < place.size[axis]:
            vec_total = vec_total + place.send(vec_total, axis, lambda i: i ^ step)
            step *= 2
    vec_new = call(
        functools.partial(vec_kernel, nt, local, units, tail_units),
        where,
        1,
        [(whole(x.shape), x) for x in (vec_total, place.sibling(vec_total), vectors, vec_first, vec_second)],
        [(held(vectors.shape), f32_of(*vectors.shape)) for _ in range(4)],
        [],
    )
    return (output, grad_input, *updated, *vec_new)


def solution(mesh):
    rows = P(("fsdp", "tp"), None)
    wide = P(None, "fsdp", "tp")
    tall = P(None, "tp", "fsdp")
    moments = (wide, wide, tall, tall, wide, wide, tall, tall, P(), P())
    return jax.shard_map(
        body,
        mesh=mesh,
        in_specs=(rows, rows, P("fsdp"), wide, tall, wide, tall, P(), *moments),
        out_specs=(rows, rows, *[wide] * 4, *[tall] * 4, *[wide] * 4, *[tall] * 4, *[P()] * 4),
        check_vma=False,
    )
```

```python
import functools
import math

import jax
import jax.numpy as jnp
from jax import lax
from jax.experimental import pallas as pl
from jax.experimental.pallas import tpu as pltpu
from jax.sharding import PartitionSpec as P

HD = 72
IMG_TOK = 729
STEP = 10


EPS_NORM = 1e-06
MASKED = -30000.0
BETA_ONE = 0.9
BETA_TWO = 0.999
ADAM_EPS = 1e-08
DECAY = 0.1
RATES = (0.05, 1.0, 0.05, 0.03, 0.3)
LOW = jnp.bfloat16
F32 = jnp.float32
GELU = math.sqrt(2.0 / math.pi)
VMEM = 56 * 1024 * 1024


def adam_step(weight, gradient, first_moment, second_moment, step_rate, decay_rate):
    first_new = BETA_ONE * first_moment + (1.0 - BETA_ONE) * gradient
    second_new = BETA_TWO * second_moment + (1.0 - BETA_TWO) * gradient * gradient
    first_hat = first_new / (1.0 - BETA_ONE**STEP)
    second_hat = second_new / (1.0 - BETA_TWO**STEP)
    weight_new = weight - step_rate * (
        first_hat / (jnp.sqrt(second_hat) + ADAM_EPS) + decay_rate * weight
    )
    return (weight_new, first_new, second_new)


def cdot(left, right, left_dim=1, right_dim=0):
    return lax.dot_general(
        left, right, (((left_dim,), (right_dim,)), ((), ())), preferred_element_type=F32
    )


def norm_parts(values):
    centred = values - jnp.mean(values, axis=-1, keepdims=True)
    inverse = lax.rsqrt(jnp.mean(centred * centred, axis=-1, keepdims=True) + EPS_NORM)
    return centred * inverse, inverse


def norm_backward(grad_out, values, gain):
    unit, inverse = norm_parts(values)
    scaled = grad_out * gain
    mean_one = jnp.mean(scaled, axis=-1, keepdims=True)
    mean_two = jnp.mean(scaled * unit, axis=-1, keepdims=True)
    grad_in = inverse * (scaled - mean_one - unit * mean_two)
    gain_sum = jnp.sum(grad_out * unit, axis=0, keepdims=True)
    return grad_in, gain_sum, jnp.sum(grad_out, axis=0, keepdims=True)


def gelu_both(inputs):
    cubic = 0.044715 * inputs * inputs
    tanh = jnp.tanh(GELU * inputs * (1.0 + cubic))
    half = 0.5 * (1.0 + tanh)
    slope = half + 0.5 * GELU * inputs * (1.0 - tanh * tanh) * (1.0 + 3.0 * cubic)
    return inputs * half, slope


def mask_keys(scores, tokens):
    rows = scores.shape[0]
    whole = IMG_TOK // 8 * 8
    position = whole + lax.broadcasted_iota(jnp.int32, (rows - whole, 1), 0)
    return jnp.concatenate(
        [scores[:whole], jnp.where(position < tokens, scores[whole:], MASKED)], axis=0
    )


def whole(shape):
    return pl.BlockSpec(shape, lambda i, s: (0,) * len(shape), pipeline_mode=pl.Buffered(1))


def held(shape):
    return pl.BlockSpec(shape, lambda i, s: (0,) * len(shape))


def stepped(shape):
    return pl.BlockSpec((1,) + shape, lambda i, s: (i,) + (0,) * len(shape))


def low_of(*shape):
    return jax.ShapeDtypeStruct(shape, LOW)


def f32_of(*shape):
    return jax.ShapeDtypeStruct(shape, F32)


def call(kernel, where, steps, ins, outs, scratch, flops=0, bytes_accessed=0, transcendentals=0, aliases=None,
         after=()):
    given = 1 + len(ins)
    ins = ins + [(pl.BlockSpec(memory_space=pl.ANY), array) for array in after]

    def run(*refs):
        kernel(*refs[:given], *refs[given + len(after) :])

    return pl.pallas_call(
        run,
        name=getattr(kernel, "func", kernel).__name__.removesuffix("_kernel"),
        grid_spec=pltpu.PrefetchScalarGridSpec(
            num_scalar_prefetch=1,
            grid=(steps,),
            in_specs=[spec for spec, _ in ins],
            out_specs=[spec for spec, _ in outs],
            scratch_shapes=scratch,
        ),
        out_shape=[shape for _, shape in outs],
        input_output_aliases=aliases or {},
        compiler_params=pltpu.CompilerParams(vmem_limit_bytes=VMEM),
        cost_estimate=pl.CostEstimate(flops=1, bytes_accessed=1, transcendentals=0),
    )(where, *[array for _, array in ins])


def pack_kernel(units, where, qkv_ref, out_ref, up_ref, down_ref, own_attn, other_attn, own_mlp, other_mlp):
    qkv, out = qkv_ref[0].astype(LOW), out_ref[0].astype(LOW)
    up, down = up_ref[0].astype(LOW), down_ref[0].astype(LOW)

    def half(values, number):
        size = values.shape[1] // 2
        return values[:, number * size : (number + 1) * size]

    for number in range(2):
        up_h, down_h = half(up, number), half(down, number)
        attn = [half(qkv, number), half(out, number), up_h[:, units:], down_h[:, units:]]
        used = sum(piece.shape[1] for piece in attn)
        attn.append(jnp.zeros((qkv.shape[0], own_attn.shape[1] - used), LOW))
        attn = jnp.concatenate(attn, axis=1)
        mlp = jnp.concatenate([up_h[:, :units], down_h[:, :units]], axis=1)

        @pl.when(where[3] == number)
        def _():
            own_attn[...] = attn
            own_mlp[...] = mlp

        @pl.when(where[3] != number)
        def _():
            other_attn[...] = attn
            other_mlp[...] = mlp


def attn_forward_kernel(spread, joined, tail_units, where, *refs):
    refs = list(refs)
    count = len(spread.weight_keys)
    if joined:
        base_ref, own_ref, other_ref, old_ref = refs[:4]
        del refs[:4]
    else:
        own_ref, other_ref = refs[:2]
        del refs[:2]
    vec_ref, bias_ref = refs[:2]
    w_refs = refs[2 : 2 + count]
    (stream_ref, normed_ref, qkv_ref, mixed_ref, sums_ref, tail_ref, part_ref, total, held_weight) = refs[
        2 + count :
    ]
    step = pl.program_id(0)

    @pl.when(step == 0)
    def _():
        if joined:
            stream = (
                base_ref[...] + (own_ref[...].astype(F32) + other_ref[...].astype(F32)) + old_ref[0, 7:8, :]
            )
            stream_ref[...] = stream
        else:
            half = own_ref.shape[0]
            stream_ref[pl.ds(pl.multiple_of(where[3] * half, 8), half), :] = own_ref[...]
            stream_ref[pl.ds(pl.multiple_of((1 - where[3]) * half, 8), half), :] = other_ref[...]
            stream = stream_ref[...]
        unit, _ = norm_parts(stream)
        normed_ref[...] = (unit * vec_ref[0, 0:1, :] + vec_ref[0, 1:2, :]).astype(LOW)
        total[...] = jnp.zeros_like(total)

    weight = spread.load(w_refs, where, held_weight)
    tokens = where[4]
    head_columns = 3 * HD
    local = qkv_ref.shape[2]
    heads = local // head_columns
    scale = HD ** (-0.5)
    bias = []
    for head in range(heads):
        at = head * HD
        query_bias, value_bias = bias_ref[0, 0, 0, :, at : at + HD], bias_ref[0, 1, 0, :, at : at + HD]
        bias += [query_bias, jnp.zeros_like(query_bias), value_bias]
    bias = jnp.concatenate(bias, axis=1)
    qkv = (cdot(normed_ref[...], weight[:, :local]) + bias).astype(LOW)
    qkv_ref[0] = qkv
    mixed = []
    for head in range(heads):
        at = head * head_columns
        query = qkv[:, at : at + HD]
        key = qkv[:, at + HD : at + 2 * HD]
        value = qkv[:, at + 2 * HD : at + 3 * HD]
        scores = mask_keys(cdot(key, query, 1, 1) * scale, tokens)
        top = jnp.max(scores, axis=0, keepdims=True)
        raised = jnp.exp(scores - top)
        weight_sum = jnp.sum(raised, axis=0, keepdims=True)
        probs = (raised * (1.0 / weight_sum)).astype(LOW)
        mixed.append(cdot(value, probs, 0, 0))
        sums_ref[0, head : head + 1, :] = top + jnp.log(weight_sum)
    mixed = jnp.concatenate(mixed, axis=0).T.astype(LOW)
    mixed_ref[0] = mixed
    at = local + mixed.shape[1]
    total[...] += cdot(mixed, weight[:, local:at], 1, 1)
    tail_ref[0] = weight[:, at : at + 2 * tail_units]

    @pl.when(step == pl.num_programs(0) - 1)
    def _():
        part_ref[...] = total[...].astype(LOW)


def mlp_forward_kernel(spread, where, *refs):
    count = len(spread.weight_keys)
    base_ref, own_ref, other_ref, vec_ref, bias_ref, tail_ref, tail_bias_ref = refs[:7]
    w_refs = refs[7 : 7 + count]
    (middle_ref, normed_ref, act_ref, slope_ref, act_tail_ref, slope_tail_ref, up_tail_ref, down_tail_ref,
     part_ref, total, held_weight) = refs[7 + count :]
    step = pl.program_id(0)

    @pl.when(step == 0)
    def _():
        middle = (
            base_ref[...] + (own_ref[...].astype(F32) + other_ref[...].astype(F32)) + vec_ref[0, 4:5, :]
        )
        middle_ref[...] = middle
        unit, _ = norm_parts(middle)
        normed_ref[...] = (unit * vec_ref[0, 5:6, :] + vec_ref[0, 6:7, :]).astype(LOW)
        steps, _, both = tail_ref.shape
        half = both // 2
        up_tail_ref[...] = jnp.concatenate([tail_ref[t, :, :half] for t in range(steps)], axis=1)
        down_tail_ref[...] = jnp.concatenate([tail_ref[t, :, half:] for t in range(steps)], axis=1)
        act, slope = gelu_both(cdot(normed_ref[...], up_tail_ref[...]) + tail_bias_ref[0, 0])
        act = act.astype(LOW)
        act_tail_ref[...] = act
        slope_tail_ref[...] = slope.astype(LOW)
        total[...] = cdot(act, down_tail_ref[...], 1, 1)

    weight = spread.load(w_refs, where, held_weight)
    units = act_ref.shape[2]
    act, slope = gelu_both(cdot(normed_ref[...], weight[:, :units]) + bias_ref[0, 0, 0])
    act = act.astype(LOW)
    act_ref[0] = act
    slope_ref[0] = slope.astype(LOW)
    total[...] += cdot(act, weight[:, units:], 1, 1)

    @pl.when(step == pl.num_programs(0) - 1)
    def _():
        part_ref[...] = total[...].astype(LOW)


def mlp_backward_kernel(spread, where, *refs):
    count = len(spread.weight_keys)
    grad_ref, slope_ref, up_tail_ref, down_tail_ref, slope_tail_ref = refs[:5]
    w_refs = refs[5 : 5 + count]
    hidden_ref, hidden_tail_ref, sums_ref, sums_tail_ref, part_ref, low, total, held_weight = refs[5 + count :]
    step = pl.program_id(0)

    @pl.when(step == 0)
    def _():
        low[...] = grad_ref[...].astype(LOW)
        hidden = cdot(low[...], down_tail_ref[...]) * slope_tail_ref[...].astype(F32)
        sums_tail_ref[...] = jnp.sum(hidden, axis=0, keepdims=True)
        hidden = hidden.astype(LOW)
        hidden_tail_ref[...] = hidden
        total[...] = cdot(hidden, up_tail_ref[...], 1, 1)

    weight = spread.load(w_refs, where, held_weight)
    units = hidden_ref.shape[2]
    hidden = cdot(low[...], weight[:, units:]) * slope_ref[0].astype(F32)
    sums_ref[0] = jnp.sum(hidden, axis=0, keepdims=True)
    hidden = hidden.astype(LOW)
    hidden_ref[0] = hidden
    total[...] += cdot(hidden, weight[:, :units], 1, 1)

    @pl.when(step == pl.num_programs(0) - 1)
    def _():
        part_ref[...] = total[...].astype(LOW)


def mlp_grads_kernel(spread, where, *refs):
    count = len(spread.grad_keys)
    grad_ref, normed_ref, hidden_ref, act_ref, hidden_tail_ref, act_tail_ref = refs[:6]
    out_refs = refs[6 : 6 + count]
    tail_ref, grad_turned, normed_turned, result = refs[6 + count :]
    step = pl.program_id(0)

    @pl.when(step == 0)
    def _():
        grad_turned[...] = grad_ref[...].astype(LOW).T
        normed_turned[...] = normed_ref[...].T
        up_tail = cdot(normed_turned[...], hidden_tail_ref[...]).astype(LOW)
        down_tail = cdot(grad_turned[...], act_tail_ref[...]).astype(LOW)
        steps, _, both = tail_ref.shape
        half = both // 2
        for t in range(steps):
            at = slice(t * half, (t + 1) * half)
            tail_ref[t] = jnp.concatenate([up_tail[:, at], down_tail[:, at]], axis=1)

    units = hidden_ref.shape[2]
    result[:, :units] = cdot(normed_turned[...], hidden_ref[0]).astype(LOW)
    result[:, units:] = cdot(grad_turned[...], act_ref[0]).astype(LOW)
    spread.store(out_refs, where, result)


def attn_backward_kernel(spread, where, *refs):
    count = len(spread.weight_keys)
    grad_ref, own_ref, other_ref, middle_ref, vec_ref, qkv_ref, sums_ref = refs[:7]
    w_refs = refs[7 : 7 + count]
    dmiddle_ref, norm_sums_ref, dqkv_ref, head_sums_ref, part_ref, low, total, held_weight = refs[7 + count :]
    step = pl.program_id(0)

    @pl.when(step == 0)
    def _():
        grad = grad_ref[...]
        inner, gain_sum, shift_sum = norm_backward(
            own_ref[...].astype(F32) + other_ref[...].astype(F32), middle_ref[...], vec_ref[0, 5:6, :]
        )
        dmiddle = grad + inner
        dmiddle_ref[...] = dmiddle
        low[...] = dmiddle.astype(LOW)
        norm_sums_ref[0:1, :] = gain_sum
        norm_sums_ref[1:2, :] = shift_sum
        norm_sums_ref[2:3, :] = jnp.sum(grad, axis=0, keepdims=True)
        norm_sums_ref[3:4, :] = jnp.sum(dmiddle, axis=0, keepdims=True)
        total[...] = jnp.zeros_like(total)

    weight = spread.load(w_refs, where, held_weight)
    tokens = where[4]
    head_columns = 3 * HD
    local = qkv_ref.shape[2]
    heads = local // head_columns
    scale = HD ** (-0.5)
    qkv = qkv_ref[0]
    dmixed = cdot(low[...], weight[:, local : local + heads * HD]).astype(LOW)
    pieces = []
    for head in range(heads):
        at = head * head_columns
        query = qkv[:, at : at + HD]
        key = qkv[:, at + HD : at + 2 * HD]
        value = qkv[:, at + 2 * HD : at + 3 * HD]
        grad = dmixed[:, head * HD : (head + 1) * HD]
        scores = mask_keys(cdot(key, query, 1, 1) * scale, tokens)
        probs = jnp.exp(scores - sums_ref[0, head : head + 1, :])
        dprobs = cdot(value, grad, 1, 1)
        row_dot = jnp.sum(dprobs * probs, axis=0, keepdims=True)
        dscores = (probs * (dprobs - row_dot)).astype(LOW)
        pieces.append(cdot(key, dscores, 0, 0).T * scale)
        pieces.append(cdot(dscores, query) * scale)
        pieces.append(cdot(probs.astype(LOW), grad))
    dqkv = jnp.concatenate(pieces, axis=1)
    head_sums_ref[0] = jnp.sum(dqkv, axis=0, keepdims=True)
    dqkv = dqkv.astype(LOW)
    dqkv_ref[0] = dqkv
    total[...] += cdot(dqkv, weight[:, :local], 1, 1)

    @pl.when(step == pl.num_programs(0) - 1)
    def _():
        part_ref[...] = total[...].astype(LOW)


def attn_grads_kernel(spread, where, *refs):
    count = len(spread.grad_keys)
    dmiddle_ref, normed_ref, dqkv_ref, mixed_ref, tail_ref = refs[:5]
    out_refs = refs[5 : 5 + count]
    grad_turned, normed_turned, result = refs[5 + count :]

    @pl.when(pl.program_id(0) == 0)
    def _():
        grad_turned[...] = dmiddle_ref[...].astype(LOW).T
        normed_turned[...] = normed_ref[...].T

    parts = [
        cdot(normed_turned[...], dqkv_ref[0]).astype(LOW),
        cdot(grad_turned[...], mixed_ref[0]).astype(LOW),
        tail_ref[0],
    ]
    used = sum(part.shape[1] for part in parts)
    parts.append(jnp.zeros((result.shape[0], result.shape[1] - used), LOW))
    result[...] = jnp.concatenate(parts, axis=1)
    spread.store(out_refs, where, result)


def norm_backward_kernel(where, dmiddle_ref, own_ref, other_ref, stream_ref, vec_ref, out_ref, sums_ref):
    inner, gain_sum, shift_sum = norm_backward(
        own_ref[...].astype(F32) + other_ref[...].astype(F32), stream_ref[...], vec_ref[0, 0:1, :]
    )
    out_ref[...] = dmiddle_ref[...] + inner
    sums_ref[0:1, :] = gain_sum
    sums_ref[1:2, :] = shift_sum


def adam_kernel(units, local, out_local, tail_units, where, *refs):
    attn_own, attn_other, mlp_own, mlp_other = refs[:4]
    states = [refs[4 + 3 * k : 7 + 3 * k] for k in range(4)]
    outs = refs[len(refs) - 16 :]

    def pair(own, other):
        own, other = own[...].astype(F32), other[...].astype(F32)
        low_core = where[3] == 0
        return jnp.where(low_core, own, other), jnp.where(low_core, other, own)

    attn = pair(attn_own, attn_other)
    mlp = pair(mlp_own, mlp_other)
    at = local + out_local
    grads = [
        jnp.concatenate([half[:, :local] for half in attn], axis=1),
        jnp.concatenate([half[:, local:at] for half in attn], axis=1),
        jnp.concatenate(
            [piece for m, n in zip(mlp, attn) for piece in (m[:, :units], n[:, at : at + tail_units])], axis=1
        ),
        jnp.concatenate(
            [
                piece
                for m, n in zip(mlp, attn)
                for piece in (m[:, units:], n[:, at + tail_units : at + 2 * tail_units])
            ],
            axis=1,
        ),
    ]
    for number, grad in enumerate(grads):
        weight, first, second = [ref[0] for ref in states[number]]
        new = adam_step(weight, grad, first, second, RATES[number], DECAY)
        for ref, values in zip(outs[4 * number : 4 * number + 4], (grad, new[1], new[2], new[0])):
            ref[0] = values


def vec_pack_kernel(where, *refs):
    out_ref = refs[-1]
    layers = out_ref.shape[0]
    out_ref[...] = jnp.zeros_like(out_ref)
    for layer in range(layers):
        one_ref, two_ref, head_ref, main_ref, tail_ref = refs[5 * layer : 5 * layer + 5]
        out_ref[layer, 0:2, :] = one_ref[0:2, :]
        out_ref[layer, 2:6, :] = two_ref[0:4, :]
        for t in range(head_ref.shape[0]):
            out_ref[layer, 8 + t : 9 + t, : head_ref.shape[2]] = head_ref[t]
            out_ref[layer, 16 + t : 17 + t, : main_ref.shape[2]] = main_ref[t]
        out_ref[layer, 6:7, : tail_ref.shape[1]] = tail_ref[...]


def vec_kernel(steps, local, units, tail_units, where, own_ref, other_ref, vec_ref, first_ref, second_ref,
               grad_out, first_out, second_out, weight_out):
    low_core = where[3] == 0
    for layer in range(vec_ref.shape[0]):
        own, other = own_ref[layer], other_ref[layer]
        cores = jnp.where(low_core, own, other), jnp.where(low_core, other, own)
        norms = cores[0][0:6]
        heads = local // (3 * HD)

        def head_piece(kind):
            return [
                core[8 + t : 9 + t, (3 * head + kind) * HD : (3 * head + kind + 1) * HD]
                for t in range(steps)
                for core in cores
                for head in range(heads)
            ]

        hidden = [
            piece
            for t in range(steps)
            for core in cores
            for piece in (core[16 + t : 17 + t, :units], core[6:7, t * tail_units : (t + 1) * tail_units])
        ]
        grad = jnp.concatenate(
            [norms[0:1], norms[1:2], *head_piece(0), *head_piece(2),
             norms[5:6], norms[2:3], norms[3:4], norms[4:5], *hidden],
            axis=1,
        )
        at = slice(layer, layer + 1)
        new = adam_step(vec_ref[at, :], grad, first_ref[at, :], second_ref[at, :], RATES[4], 0.0)
        grad_out[at, :] = grad
        first_out[at, :] = new[1]
        second_out[at, :] = new[2]
        weight_out[at, :] = new[0]


def plane_sides(chips):
    side = math.isqrt(chips)
    while chips % side:
        side -= 1
    return side, chips // side


class Place:
    def __init__(self):
        self.nf = lax.axis_size("fsdp")
        self.nt = lax.axis_size("tp")
        self.na, self.nb = plane_sides(self.nf // 2)
        fi = lax.axis_index("fsdp")
        self.core = fi % 2
        self.a = (fi // 2) // self.nb
        self.b = (fi // 2) % self.nb
        self.t = lax.axis_index("tp")
        self.size = {"a": self.na, "b": self.nb, "t": self.nt}
        self.at = {"a": self.a, "b": self.b, "t": self.t}

    def pairs(self, axis, move):
        if axis == "t":
            return [(i, move(i)) for i in range(self.nt)]
        found = []
        for f in range(self.nf):
            place = {"a": f // 2 // self.nb, "b": f // 2 % self.nb, "core": f % 2}
            place[axis] = move(place[axis])
            found.append((f, (place["a"] * self.nb + place["b"]) * 2 + place["core"]))
        return found

    def send(self, values, axis, move):
        return lax.ppermute(values, "tp" if axis == "t" else "fsdp", self.pairs(axis, move))

    def sibling(self, values):
        return self.send(values, "core", lambda i: 1 - i)

    def swap_rows(self, values):
        pairs = []
        for f in range(self.nf):
            for t in range(self.nt):
                if f % 2 != t % 2:
                    sign = 1 if t % 2 else -1
                    pairs.append((f * self.nt + t, (f + sign) * self.nt + t - sign))
        arrived = lax.ppermute(values.astype(LOW), ("fsdp", "tp"), pairs).astype(F32)
        return jnp.where(self.core != self.t % 2, arrived, values)

    def gather_axis(self, block, axis):
        n = self.size[axis]
        return [block] + [self.send(block, axis, lambda i, k=k: (i - k) % n) for k in range(1, n)]

    def scatter_axis(self, parts, axis):
        n = self.size[axis]
        sent = [self.send(parts[k], axis, lambda i, k=k: (i + k) % n) for k in range(1, n)]
        return [parts[0], *sent]


def split_pair(place, first, second):
    return (
        jnp.where(place.core == 0, first, second),
        jnp.where(place.core == 0, second, first),
    )


def sum_kernel(groups, joined, where, *refs):
    ins, outs = refs[: sum(groups)], refs[sum(groups) :]
    for number, size in enumerate(groups):
        total = ins[0][0, 0].astype(F32)
        for ref in ins[1:size]:
            total += ref[0, 0].astype(F32)
        ins = ins[size:]
        if joined:
            outs[0][0, number] = total.astype(LOW)
        else:
            outs[number][0, 0] = total.astype(LOW)


class Spread:
    def __init__(self, place, rows, columns):
        self.place, self.rows, self.columns = place, rows, columns
        self.direct = rows % 16 == 0
        self.width = place.na * place.nb * 2 * rows
        na, nb = place.na, place.nb
        self.weight_keys = [[(0, 0, 0), (1, 0, 0)]]
        self.weight_keys += [[(0, 0, b), (1, 0, b)] for b in range(1, nb)]
        self.weight_keys += [[(0, a, 0), (1, a, 0)] for a in range(1, na)]
        self.weight_keys += [[(half, a, b)] for half in range(2) for a in range(1, na) for b in range(1, nb)]
        self.grad_keys = [[(0, a, b) for b in range(nb)] for a in range(na)]
        self.grad_keys += [[(1, a, b) for a in range(na)] for b in range(nb)]
        if not self.direct:
            self.weight_keys = self.grad_keys = [None]

    def shapes(self, keys):
        if not self.direct:
            return [(self.place.nt, self.width, self.columns)]
        return [(self.place.nt, len(blocks), self.rows, self.columns) for blocks in keys]

    def specs(self, keys):
        return [stepped(shape[1:]) for shape in self.shapes(keys)]

    def first_row(self, where, key):
        half, a, b = key
        a = lax.rem(where[0] + a, self.place.na)
        b = lax.rem(where[1] + b, self.place.nb)
        return pl.multiple_of(((a * self.place.nb + b) * 2 + half) * self.rows, 16)

    def load(self, refs, where, scratch):
        if not self.direct:
            return refs[0].at[0]
        for ref, blocks in zip(refs, self.weight_keys):
            for number, key in enumerate(blocks):
                scratch[pl.ds(self.first_row(where, key), self.rows), :] = ref[0, number]
        return scratch

    def store(self, refs, where, scratch):
        if not self.direct:
            refs[0][0] = scratch[...]
            return
        for ref, blocks in zip(refs, self.grad_keys):
            for number, key in enumerate(blocks):
                ref[0, number] = scratch[pl.ds(self.first_row(where, key), self.rows), :]

    def gather(self, own, other):
        place = self.place
        both = lax.all_gather(jnp.stack(split_pair(place, own, other)), "tp")
        along_b = place.gather_axis(both, "b")
        along_a = place.gather_axis(both, "a")
        first = [place.gather_axis(x[:, :1], "a")[1:] for x in along_b[1:]]
        second = [place.gather_axis(x[:, 1:], "b")[1:] for x in along_a[1:]]
        na, nb = place.na, place.nb
        arrays = along_b + along_a[1:]
        arrays += [first[b][a] for a in range(na - 1) for b in range(nb - 1)]
        arrays += [second[a][b] for a in range(na - 1) for b in range(nb - 1)]
        if self.direct:
            return arrays
        keys = [[(0, 0, 0), (1, 0, 0)]]
        keys += [[(0, 0, b), (1, 0, b)] for b in range(1, nb)] + [[(0, a, 0), (1, a, 0)] for a in range(1, na)]
        keys += [[(half, a, b)] for half in range(2) for a in range(1, na) for b in range(1, nb)]
        found = {
            key: array[:, number] for array, blocks in zip(arrays, keys) for number, key in enumerate(blocks)
        }
        full = jnp.stack([found[half, a, b] for a in range(na) for b in range(nb) for half in range(2)], axis=1)
        full = full.reshape(place.nt, na, nb, 2, self.rows, self.columns)
        full = self.roll(full, (na - place.a) % na, (nb - place.b) % nb)
        return [full.reshape(place.nt, self.width, self.columns)]

    def roll(self, full, a, b):
        full = lax.dynamic_slice_in_dim(jnp.concatenate([full, full], axis=1), a, self.place.na, 1)
        return lax.dynamic_slice_in_dim(jnp.concatenate([full, full], axis=2), b, self.place.nb, 2)

    def sums(self, where, groups, after, joined=False):
        place, rows, columns = self.place, self.rows, self.columns

        def block(number):
            return pl.BlockSpec((1, 1, rows, columns), lambda i, s: (i, number, 0, 0))

        shape = (place.nt, len(groups) if joined else 1, rows, columns)
        out = (stepped(shape[1:]), low_of(*shape))
        return call(
            functools.partial(sum_kernel, [len(group) for group in groups], joined),
            where,
            place.nt,
            [(block(number), x) for group in groups for x, number in group],
            [out] if joined else [out] * len(groups),
            [],
            after=after,
        )

    def scatter_last(self, arrays):
        place = self.place
        if not self.direct:
            full = arrays[0].reshape(place.nt, place.na, place.nb, 2, self.rows, self.columns)
            full = self.roll(full, place.a, place.b)
            arrays = [full[:, a, :, 0] for a in range(place.na)] + [full[:, :, b, 1] for b in range(place.nb)]
        return (
            place.scatter_axis(arrays[: place.na], "a"),
            place.scatter_axis(arrays[place.na :], "b"),
        )

    def scatter_first(self, where, halves, after):
        place = self.place
        axes = ("b", "a")
        keys = [(half, k) for half in range(2) for k in range(1, place.size[axes[half]])]
        results = self.sums(where, [[(x, k) for x in halves[half]] for half, k in keys], after)
        terms = [[(x, 0) for x in arrays] for arrays in halves]
        for (half, k), total in zip(keys, results):
            n = place.size[axes[half]]
            terms[half].append((place.send(total, axes[half], lambda i: (i + k) % n), 0))
        return results[0], terms

    def scatter_tp(self, where, terms, after):
        place = self.place
        (sums,) = self.sums(where, terms, after, joined=True)
        done = lax.psum_scatter(sums, "tp", scatter_dimension=0, tiled=True)[0]
        mine, other = split_pair(place, done[0], done[1])
        return sums, (mine, place.sibling(other))


def body(
    residual_in,
    cotangent,
    slot_tokens,
    qkv_weight,
    out_weight,
    up_weight,
    down_weight,
    vectors,
    qkv_first,
    qkv_second,
    out_first,
    out_second,
    up_first,
    up_second,
    down_first,
    down_second,
    vec_first,
    vec_second,
):
    place = Place()
    layer_count, shard_rows, _ = qkv_weight.shape
    half_rows, width = residual_in.shape
    rows = 2 * half_rows
    nt = place.nt
    local = qkv_weight.shape[2] // 2
    out_local = out_weight.shape[1] // 2
    hidden_local = up_weight.shape[2] // 2
    units = hidden_local // 128 * 128
    tail_units = hidden_local - units
    heads = out_local // HD
    attn_columns = -(-(local + out_local + 2 * tail_units) // 128) * 128
    mlp_columns = 2 * units

    tokens_pair = jnp.concatenate(split_pair(place, slot_tokens, place.sibling(slot_tokens)))
    slot_at = (place.t % 2) * slot_tokens.shape[0] + place.t // 2
    tokens = lax.dynamic_slice_in_dim(tokens_pair, slot_at, 1)
    row_mask = (jnp.arange(rows, dtype=jnp.int32) < tokens[0]).astype(F32)[:, None]
    here = jnp.stack([place.a, place.b, place.t, place.core]).astype(jnp.int32)
    where = jnp.concatenate([here, tokens.astype(jnp.int32)])

    def own_rows(values):
        return lax.dynamic_slice_in_dim(values, place.core * half_rows, half_rows)

    spreads = [
        (
            Spread(place, shard_rows, attn_columns),
            Spread(place, shard_rows, mlp_columns),
        )
        for layer in range(layer_count)
    ]

    def turn(arrays):
        qkv, out, up, down = arrays
        return qkv, jnp.swapaxes(out, 1, 2), up, jnp.swapaxes(down, 1, 2)

    weights = turn((qkv_weight, out_weight, up_weight, down_weight))
    firsts = turn((qkv_first, out_first, up_first, down_first))
    seconds = turn((qkv_second, out_second, up_second, down_second))

    def layer_block(array, layer):
        block = (1, *array.shape[1:])
        return pl.BlockSpec(block, lambda i, s: (layer, 0, 0), pipeline_mode=pl.Buffered(1))

    def pack(layer):
        attn, mlp = (shard_rows, attn_columns), (shard_rows, mlp_columns)
        return call(
            functools.partial(pack_kernel, units),
            here,
            1,
            [(layer_block(w, layer), w) for w in weights],
            [(held(shape), low_of(*shape)) for shape in (attn, attn, mlp, mlp)],
            [],
            bytes_accessed=6 * shard_rows * 13216 // 4,
        )

    gathered = []
    for layer in range(layer_count):
        own_attn, other_attn, own_mlp, other_mlp = pack(layer)
        gathered.append(
            (
                spreads[layer][0].gather(own_attn, place.sibling(other_attn)),
                spreads[layer][1].gather(own_mlp, place.sibling(other_mlp)),
            )
        )

    wide = vectors[:, : 8 * width].reshape(layer_count, 8, width)
    head_bias = vectors[:, 2 * width : 4 * width].reshape(layer_count, 2, 2 * nt, 1, out_local)
    hidden_bias = vectors[:, 8 * width :].reshape(layer_count, nt, 2, 1, hidden_local)
    main_bias = hidden_bias[..., :units]
    tail_bias = jnp.moveaxis(hidden_bias[..., units:], 1, 3).reshape(layer_count, 2, 1, nt * tail_units)

    full = whole((rows, width))
    weight_scratch = [
        pltpu.VMEM((width, attn_columns), LOW),
        pltpu.VMEM((width, mlp_columns), LOW),
    ]
    flat = pltpu.VMEM((rows, width), F32)
    flat_low = pltpu.VMEM((rows, width), LOW)
    big = 2 * rows * width

    def wide_of(layer):
        spec = pl.BlockSpec((1, 8, width), lambda i, s: (layer, 0, 0), pipeline_mode=pl.Buffered(1))
        return spec, wide

    def attn_forward(layer, base, own, other):
        spread = spreads[layer][0]
        joined = base is not None
        if joined:
            ins = [(full, base), (full, own), (full, other), wide_of(layer - 1)]
        else:
            half = whole((half_rows, width))
            ins = [(half, own), (half, other)]
        ins.append(wide_of(layer))
        ins.append(
            (
                pl.BlockSpec(
                    (1, 2, 1, 1, out_local), lambda i, s: (layer, 0, 2 * i + s[3], 0, 0)
                ),
                head_bias,
            )
        )
        ins += list(zip(spread.specs(spread.weight_keys), gathered[layer][0]))
        return call(
            functools.partial(attn_forward_kernel, spread, joined, tail_units),
            where,
            nt,
            ins,
            [
                (held((rows, width)), f32_of(rows, width)),
                (held((rows, width)), low_of(rows, width)),
                (stepped((rows, local)), low_of(nt, rows, local)),
                (stepped((rows, out_local)), low_of(nt, rows, out_local)),
                (stepped((heads, rows)), f32_of(nt, heads, rows)),
                (stepped((width, 2 * tail_units)), low_of(nt, width, 2 * tail_units)),
                (held((rows, width)), low_of(rows, width)),
            ],
            [flat, weight_scratch[0]],
            big * nt * (local + out_local) + 4 * nt * heads * rows * rows * HD,
            rows * width * 12 + nt * width * attn_columns * 2,
            nt * heads * rows * rows,
        )

    def mlp_forward(layer, base, own, other, tails):
        spread = spreads[layer][1]
        tail = nt * tail_units
        tail_shape = (width, tail)
        ins = [
            (full, base),
            (full, own),
            (full, other),
            wide_of(layer),
            (pl.BlockSpec((1, 1, 1, 1, units), lambda i, s: (layer, i, s[3], 0, 0)), main_bias),
            (whole(tails.shape), tails),
            (pl.BlockSpec((1, 1, 1, tail), lambda i, s: (layer, s[3], 0, 0)), tail_bias),
        ]
        ins += list(zip(spread.specs(spread.weight_keys), gathered[layer][1]))
        return call(
            functools.partial(mlp_forward_kernel, spread),
            where,
            nt,
            ins,
            [
                (held((rows, width)), f32_of(rows, width)),
                (held((rows, width)), low_of(rows, width)),
                (stepped((rows, units)), low_of(nt, rows, units)),
                (stepped((rows, units)), low_of(nt, rows, units)),
                (held((rows, tail)), low_of(rows, tail)),
                (held((rows, tail)), low_of(rows, tail)),
                (held(tail_shape), low_of(*tail_shape)),
                (held(tail_shape), low_of(*tail_shape)),
                (held((rows, width)), low_of(rows, width)),
            ],
            [flat, weight_scratch[1]],
            2 * big * (nt * units + tail),
            rows * width * 16 + nt * (width + rows) * mlp_columns * 2,
            rows * nt * units,
        )

    def mlp_backward(layer, grad, slope, tails, slope_tail):
        spread = spreads[layer][1]
        tail = nt * tail_units
        ins = [(full, grad), (stepped((rows, units)), slope)]
        ins += [(whole(w.shape), w) for w in (*tails, slope_tail)]
        ins += list(zip(spread.specs(spread.weight_keys), gathered[layer][1]))
        return call(
            functools.partial(mlp_backward_kernel, spread),
            where,
            nt,
            ins,
            [
                (stepped((rows, units)), low_of(nt, rows, units)),
                (held((rows, tail)), low_of(rows, tail)),
                (stepped((1, units)), f32_of(nt, 1, units)),
                (held((1, tail)), f32_of(1, tail)),
                (held((rows, width)), low_of(rows, width)),
            ],
            [flat_low, flat, weight_scratch[1]],
            2 * big * (nt * units + tail),
            rows * width * 6 + nt * (width + rows) * mlp_columns * 2,
        )

    def mlp_grads(layer, grad, normed, hidden, act, hidden_tail, act_tail):
        spread = spreads[layer][1]
        ins = [(full, grad), (full, normed)]
        ins += [(stepped((rows, units)), hidden), (stepped((rows, units)), act)]
        ins += [(whole(x.shape), x) for x in (hidden_tail, act_tail)]
        tail_shape = (nt, width, 2 * tail_units)
        outs = [
            (spec, low_of(*shape))
            for spec, shape in zip(spread.specs(spread.grad_keys), spread.shapes(spread.grad_keys))
        ]
        outs.append((held(tail_shape), low_of(*tail_shape)))
        turned_low = pltpu.VMEM((width, rows), LOW)
        return call(
            functools.partial(mlp_grads_kernel, spread),
            where,
            nt,
            ins,
            outs,
            [turned_low, turned_low, weight_scratch[1]],
            2 * big * nt * (units + tail_units),
            rows * width * 6 + nt * (width + rows) * mlp_columns * 2,
        )

    def attn_backward(layer, grad, own, other, middle, qkv, log_sums, after=()):
        spread = spreads[layer][0]
        ins = [(full, grad), (full, own), (full, other), (full, middle), wide_of(layer)]
        ins += [(stepped((rows, local)), qkv), (stepped((heads, rows)), log_sums)]
        ins += list(zip(spread.specs(spread.weight_keys), gathered[layer][0]))
        return call(
            functools.partial(attn_backward_kernel, spread),
            where,
            nt,
            ins,
            [
                (held((rows, width)), f32_of(rows, width)),
                (held((8, width)), f32_of(8, width)),
                (stepped((rows, local)), low_of(nt, rows, local)),
                (stepped((1, local)), f32_of(nt, 1, local)),
                (held((rows, width)), low_of(rows, width)),
            ],
            [flat_low, flat, weight_scratch[0]],
            big * nt * (local + out_local) + 10 * nt * heads * rows * rows * HD,
            rows * width * 20 + nt * width * attn_columns * 2,
            nt * heads * rows * rows,
            after=after,
        )

    def attn_grads(layer, dmiddle, normed, dqkv, mixed, tail_grads):
        spread = spreads[layer][0]
        ins = [(full, dmiddle), (full, normed)]
        ins += [(stepped((rows, local)), dqkv), (stepped((rows, out_local)), mixed)]
        ins.append((stepped((width, 2 * tail_units)), tail_grads))
        outs = [
            (spec, low_of(*shape))
            for spec, shape in zip(spread.specs(spread.grad_keys), spread.shapes(spread.grad_keys))
        ]
        turned_low = pltpu.VMEM((width, rows), LOW)
        return call(
            functools.partial(attn_grads_kernel, spread),
            where,
            nt,
            ins,
            outs,
            [turned_low, turned_low, weight_scratch[0]],
            big * nt * (local + out_local),
            rows * width * 6 + nt * (width + rows) * attn_columns * 2,
        )

    def norm_one_backward(layer, dmiddle, own, other, stream, after=()):
        return call(
            norm_backward_kernel,
            where,
            1,
            [(full, dmiddle), (full, own), (full, other), (full, stream), wide_of(layer)],
            [(held((rows, width)), f32_of(rows, width)), (held((8, width)), f32_of(8, width))],
            [],
            rows * width * 20,
            rows * width * 16,
            after=after,
        )

    mine = place.swap_rows(residual_in)
    base, own, other = None, mine, place.sibling(mine)
    saved = []
    for layer in range(layer_count):
        stream, normed, qkv, mixed, log_sums, tails, part = attn_forward(layer, base, own, other)
        middle, normed_two, act, slope, act_tail, slope_tail, up_tail, down_tail, part = mlp_forward(
            layer, stream, part, place.sibling(part), tails
        )
        saved.append(
            (stream, normed, qkv, mixed, log_sums, middle, normed_two, act, slope, act_tail, slope_tail,
             (up_tail, down_tail))
        )
        base, own, other = middle, part, place.sibling(part)
    output = own_rows(base) + (own_rows(own).astype(F32) + own_rows(other).astype(F32))
    output = place.swap_rows((output + wide[layer_count - 1, 7:8]) * own_rows(row_mask))

    mine = place.swap_rows(cotangent)
    grad_stream = jnp.concatenate(split_pair(place, mine, place.sibling(mine)), axis=0) * row_mask


    def adam(layer, attn_pair, mlp_pair, before, after=()):
        ins = [(whole(x.shape), x) for x in (*attn_pair, *mlp_pair)]
        for states in zip(weights, firsts, seconds):
            ins += [(layer_block(x, layer), x) for x in states]
        outs = [
            (layer_block(weight, layer), f32_of(*weight.shape)) for weight in weights for _ in range(4)
        ]
        aliases = None
        if before is not None:
            aliases = {1 + len(ins) + k: k for k in range(16)}
            ins += [(pl.BlockSpec(memory_space=pl.ANY), x) for x in before]
        return call(
            functools.partial(adam_kernel, units, local, out_local, tail_units),
            where,
            1,
            ins,
            outs,
            [],
            bytes_accessed=28 * shard_rows * 13216 // 4,
            aliases=aliases,
            after=after,
        )

    vec_sums = [None] * layer_count
    last = grad_stream
    above = None
    for layer in reversed(range(layer_count)):
        (stream, normed, qkv, mixed, log_sums, middle, normed_two, act, slope, act_tail, slope_tail, tails) = (
            saved[layer]
        )
        spread_attn, spread_mlp = spreads[layer]
        hidden, hidden_tail, hidden_sums, tail_sums, part = mlp_backward(
            layer, grad_stream, slope, tails, slope_tail
        )
        other = place.sibling(part)
        *mlp_grad, tail_grads = mlp_grads(
            layer, grad_stream, normed_two, hidden, act, hidden_tail, act_tail
        )
        last = tail_grads
        mlp_terms = spread_mlp.scatter_last(mlp_grad)
        if above:
            last, attn_terms_above = spreads[above][0].scatter_first(where, attn_terms_above, [last])
        dmiddle, norm_two_sums, dqkv, head_sums, part = attn_backward(
            layer, grad_stream, part, other, middle, qkv, log_sums, [last]
        )
        other = place.sibling(part)
        attn_grad = attn_grads(layer, dmiddle, normed, dqkv, mixed, tail_grads)
        last = attn_grad[0]
        attn_terms = spread_attn.scatter_last(attn_grad)
        if above:
            last, mlp_pair_above = spreads[above][1].scatter_tp(where, mlp_terms_above, [last])
        grad_stream, norm_one_sums = norm_one_backward(layer, dmiddle, part, other, stream, [last])
        last, mlp_terms = spread_mlp.scatter_first(where, mlp_terms, [norm_one_sums])
        vec_sums[layer] = (norm_one_sums, norm_two_sums, head_sums, hidden_sums, tail_sums)
        if above:
            last, attn_pair_above = spreads[above][0].scatter_tp(where, attn_terms_above, [last])
            pairs_above = attn_pair_above, mlp_pair_above
        above, mlp_terms_above, attn_terms_above = layer, mlp_terms, attn_terms
        if layer:
            grad_stream, last = lax.optimization_barrier((grad_stream, last))
    last, attn_terms_above = spreads[above][0].scatter_first(where, attn_terms_above, [last])
    last, mlp_pair_above = spreads[above][1].scatter_tp(where, mlp_terms_above, [last])
    last, attn_pair_above = spreads[above][0].scatter_tp(where, attn_terms_above, [last])
    grad_input = place.swap_rows(own_rows(grad_stream))
    updated = adam(1, *pairs_above, None, [last])

    flat_sums = [x for sums in vec_sums for x in sums]
    vec_shape = (layer_count, 24, width)
    (vec_total,) = call(
        vec_pack_kernel,
        where,
        1,
        [(whole(x.shape), x) for x in flat_sums],
        [(held(vec_shape), f32_of(*vec_shape))],
        [],
        after=[last],
    )
    for axis in ("b", "a", "t"):
        step = 1
        while step < place.size[axis]:
            vec_total = vec_total + place.send(vec_total, axis, lambda i: i ^ step)
            step *= 2
    vec_new = call(
        functools.partial(vec_kernel, nt, local, units, tail_units),
        where,
        1,
        [(whole(x.shape), x) for x in (vec_total, place.sibling(vec_total), vectors, vec_first, vec_second)],
        [(held(vectors.shape), f32_of(*vectors.shape)) for _ in range(4)],
        [],
    )
    updated = adam(above, attn_pair_above, mlp_pair_above, updated)
    updated = [
        jnp.swapaxes(x, 1, 2) if number // 4 % 2 else x for number, x in enumerate(updated)
    ]
    return (output, grad_input, *updated, *vec_new)


def solution(mesh):
    rows = P(("fsdp", "tp"), None)
    wide = P(None, "fsdp", "tp")
    tall = P(None, "tp", "fsdp")
    moments = (wide, wide, tall, tall, wide, wide, tall, tall, P(), P())
    return jax.shard_map(
        body,
        mesh=mesh,
        in_specs=(rows, rows, P("fsdp"), wide, tall, wide, tall, P(), *moments),
        out_specs=(rows, rows, *[wide] * 4, *[tall] * 4, *[wide] * 4, *[tall] * 4, *[P()] * 4),
        check_vma=False,
    )
```

```python
import functools
import math

import jax
import jax.numpy as jnp
from jax import lax
from jax.experimental import pallas as pl
from jax.experimental.pallas import tpu as pltpu
from jax.sharding import PartitionSpec as P

HD = 72
IMG_TOK = 729
STEP = 10


EPS_NORM = 1e-06
MASKED = -30000.0
BETA_ONE = 0.9
BETA_TWO = 0.999
ADAM_EPS = 1e-08
DECAY = 0.1
RATES = (0.05, 1.0, 0.05, 0.03, 0.3)
LOW = jnp.bfloat16
F32 = jnp.float32
GELU = math.sqrt(2.0 / math.pi)
VMEM = 56 * 1024 * 1024
COST = {
    "pack_kernel": 4,
    "attn_forward_kernel": 26,
    "mlp_forward_kernel": 24,
    "mlp_backward_kernel": 17,
    "mlp_grads_kernel": 16,
    "attn_backward_kernel": 33,
    "attn_grads_kernel": 13,
    "norm_backward_kernel": 9,
    "sum_kernel": 5,
    "vec_pack_kernel": 0.3,
    "vec_kernel": 0.3,
    "adam_kernel": 1,
    "tie_kernel": 1,
}
SCALE = 2e9


def adam_step(weight, gradient, first_moment, second_moment, step_rate, decay_rate):
    first_new = BETA_ONE * first_moment + (1.0 - BETA_ONE) * gradient
    second_new = BETA_TWO * second_moment + (1.0 - BETA_TWO) * gradient * gradient
    first_hat = first_new / (1.0 - BETA_ONE**STEP)
    second_hat = second_new / (1.0 - BETA_TWO**STEP)
    weight_new = weight - step_rate * (
        first_hat / (jnp.sqrt(second_hat) + ADAM_EPS) + decay_rate * weight
    )
    return (weight_new, first_new, second_new)


def cdot(left, right, left_dim=1, right_dim=0):
    return lax.dot_general(
        left, right, (((left_dim,), (right_dim,)), ((), ())), preferred_element_type=F32
    )


def norm_parts(values):
    centred = values - jnp.mean(values, axis=-1, keepdims=True)
    inverse = lax.rsqrt(jnp.mean(centred * centred, axis=-1, keepdims=True) + EPS_NORM)
    return centred * inverse, inverse


def norm_backward(grad_out, values, gain):
    unit, inverse = norm_parts(values)
    scaled = grad_out * gain
    mean_one = jnp.mean(scaled, axis=-1, keepdims=True)
    mean_two = jnp.mean(scaled * unit, axis=-1, keepdims=True)
    grad_in = inverse * (scaled - mean_one - unit * mean_two)
    gain_sum = jnp.sum(grad_out * unit, axis=0, keepdims=True)
    return grad_in, gain_sum, jnp.sum(grad_out, axis=0, keepdims=True)


def gelu_both(inputs):
    cubic = 0.044715 * inputs * inputs
    tanh = jnp.tanh(GELU * inputs * (1.0 + cubic))
    half = 0.5 * (1.0 + tanh)
    slope = half + 0.5 * GELU * inputs * (1.0 - tanh * tanh) * (1.0 + 3.0 * cubic)
    return inputs * half, slope


def mask_keys(scores, tokens):
    rows = scores.shape[0]
    whole = IMG_TOK // 8 * 8
    position = whole + lax.broadcasted_iota(jnp.int32, (rows - whole, 1), 0)
    return jnp.concatenate(
        [scores[:whole], jnp.where(position < tokens, scores[whole:], MASKED)], axis=0
    )


def whole(shape):
    return pl.BlockSpec(shape, lambda i, s: (0,) * len(shape), pipeline_mode=pl.Buffered(1))


def held(shape):
    return pl.BlockSpec(shape, lambda i, s: (0,) * len(shape))


def stepped(shape):
    return pl.BlockSpec((1,) + shape, lambda i, s: (i,) + (0,) * len(shape))


def low_of(*shape):
    return jax.ShapeDtypeStruct(shape, LOW)


def f32_of(*shape):
    return jax.ShapeDtypeStruct(shape, F32)


def call(kernel, where, steps, ins, outs, scratch, flops=0, bytes_accessed=0, transcendentals=0, aliases=None,
         after=()):
    given = 1 + len(ins)
    ins = ins + [(pl.BlockSpec(memory_space=pl.ANY), array) for array in after]

    def run(*refs):
        kernel(*refs[:given], *refs[given + len(after) :])

    return pl.pallas_call(
        run,
        name=getattr(kernel, "func", kernel).__name__.removesuffix("_kernel"),
        grid_spec=pltpu.PrefetchScalarGridSpec(
            num_scalar_prefetch=1,
            grid=(steps,),
            in_specs=[spec for spec, _ in ins],
            out_specs=[spec for spec, _ in outs],
            scratch_shapes=scratch,
        ),
        out_shape=[shape for _, shape in outs],
        input_output_aliases=aliases or {},
        compiler_params=pltpu.CompilerParams(vmem_limit_bytes=VMEM),
        cost_estimate=pl.CostEstimate(
            flops=int(COST[getattr(kernel, "func", kernel).__name__] * SCALE), bytes_accessed=1, transcendentals=0
        ),
    )(where, *[array for _, array in ins])


def pack_kernel(units, where, qkv_ref, out_ref, up_ref, down_ref, own_attn, other_attn, own_mlp, other_mlp):
    qkv, out = qkv_ref[0].astype(LOW), out_ref[0].astype(LOW)
    up, down = up_ref[0].astype(LOW), down_ref[0].astype(LOW)

    def half(values, number):
        size = values.shape[1] // 2
        return values[:, number * size : (number + 1) * size]

    for number in range(2):
        up_h, down_h = half(up, number), half(down, number)
        attn = [half(qkv, number), half(out, number), up_h[:, units:], down_h[:, units:]]
        used = sum(piece.shape[1] for piece in attn)
        attn.append(jnp.zeros((qkv.shape[0], own_attn.shape[1] - used), LOW))
        attn = jnp.concatenate(attn, axis=1)
        mlp = jnp.concatenate([up_h[:, :units], down_h[:, :units]], axis=1)

        @pl.when(where[3] == number)
        def _():
            own_attn[...] = attn
            own_mlp[...] = mlp

        @pl.when(where[3] != number)
        def _():
            other_attn[...] = attn
            other_mlp[...] = mlp


def attn_forward_kernel(spread, joined, tail_units, where, *refs):
    refs = list(refs)
    count = len(spread.weight_keys)
    if joined:
        base_ref, own_ref, other_ref, old_ref = refs[:4]
        del refs[:4]
    else:
        own_ref, other_ref = refs[:2]
        del refs[:2]
    vec_ref, bias_ref = refs[:2]
    w_refs = refs[2 : 2 + count]
    (stream_ref, normed_ref, qkv_ref, mixed_ref, sums_ref, tail_ref, part_ref, total, held_weight) = refs[
        2 + count :
    ]
    step = pl.program_id(0)

    @pl.when(step == 0)
    def _():
        if joined:
            stream = (
                base_ref[...] + (own_ref[...].astype(F32) + other_ref[...].astype(F32)) + old_ref[0, 7:8, :]
            )
            stream_ref[...] = stream
        else:
            half = own_ref.shape[0]
            stream_ref[pl.ds(pl.multiple_of(where[3] * half, 8), half), :] = own_ref[...]
            stream_ref[pl.ds(pl.multiple_of((1 - where[3]) * half, 8), half), :] = other_ref[...]
            stream = stream_ref[...]
        unit, _ = norm_parts(stream)
        normed_ref[...] = (unit * vec_ref[0, 0:1, :] + vec_ref[0, 1:2, :]).astype(LOW)
        total[...] = jnp.zeros_like(total)

    weight = spread.load(w_refs, where, held_weight)
    tokens = where[4]
    head_columns = 3 * HD
    local = qkv_ref.shape[2]
    heads = local // head_columns
    scale = HD ** (-0.5)
    bias = []
    for head in range(heads):
        at = head * HD
        query_bias, value_bias = bias_ref[0, 0, 0, :, at : at + HD], bias_ref[0, 1, 0, :, at : at + HD]
        bias += [query_bias, jnp.zeros_like(query_bias), value_bias]
    bias = jnp.concatenate(bias, axis=1)
    qkv = (cdot(normed_ref[...], weight[:, :local]) + bias).astype(LOW)
    qkv_ref[0] = qkv
    mixed = []
    for head in range(heads):
        at = head * head_columns
        query = qkv[:, at : at + HD]
        key = qkv[:, at + HD : at + 2 * HD]
        value = qkv[:, at + 2 * HD : at + 3 * HD]
        scores = mask_keys(cdot(key, query, 1, 1) * scale, tokens)
        top = jnp.max(scores, axis=0, keepdims=True)
        raised = jnp.exp(scores - top)
        weight_sum = jnp.sum(raised, axis=0, keepdims=True)
        probs = (raised * (1.0 / weight_sum)).astype(LOW)
        mixed.append(cdot(value, probs, 0, 0))
        sums_ref[0, head : head + 1, :] = top + jnp.log(weight_sum)
    mixed = jnp.concatenate(mixed, axis=0).T.astype(LOW)
    mixed_ref[0] = mixed
    at = local + mixed.shape[1]
    total[...] += cdot(mixed, weight[:, local:at], 1, 1)
    tail_ref[0] = weight[:, at : at + 2 * tail_units]

    @pl.when(step == pl.num_programs(0) - 1)
    def _():
        part_ref[...] = total[...].astype(LOW)


def mlp_forward_kernel(spread, where, *refs):
    count = len(spread.weight_keys)
    base_ref, own_ref, other_ref, vec_ref, bias_ref, tail_ref, tail_bias_ref = refs[:7]
    w_refs = refs[7 : 7 + count]
    (middle_ref, normed_ref, act_ref, slope_ref, act_tail_ref, slope_tail_ref, up_tail_ref, down_tail_ref,
     part_ref, total, held_weight) = refs[7 + count :]
    step = pl.program_id(0)

    @pl.when(step == 0)
    def _():
        middle = (
            base_ref[...] + (own_ref[...].astype(F32) + other_ref[...].astype(F32)) + vec_ref[0, 4:5, :]
        )
        middle_ref[...] = middle
        unit, _ = norm_parts(middle)
        normed_ref[...] = (unit * vec_ref[0, 5:6, :] + vec_ref[0, 6:7, :]).astype(LOW)
        steps, _, both = tail_ref.shape
        half = both // 2
        up_tail_ref[...] = jnp.concatenate([tail_ref[t, :, :half] for t in range(steps)], axis=1)
        down_tail_ref[...] = jnp.concatenate([tail_ref[t, :, half:] for t in range(steps)], axis=1)
        act, slope = gelu_both(cdot(normed_ref[...], up_tail_ref[...]) + tail_bias_ref[0, 0])
        act = act.astype(LOW)
        act_tail_ref[...] = act
        slope_tail_ref[...] = slope.astype(LOW)
        total[...] = cdot(act, down_tail_ref[...], 1, 1)

    weight = spread.load(w_refs, where, held_weight)
    units = act_ref.shape[2]
    act, slope = gelu_both(cdot(normed_ref[...], weight[:, :units]) + bias_ref[0, 0, 0])
    act = act.astype(LOW)
    act_ref[0] = act
    slope_ref[0] = slope.astype(LOW)
    total[...] += cdot(act, weight[:, units:], 1, 1)

    @pl.when(step == pl.num_programs(0) - 1)
    def _():
        part_ref[...] = total[...].astype(LOW)


def mlp_backward_kernel(spread, where, *refs):
    count = len(spread.weight_keys)
    grad_ref, slope_ref, up_tail_ref, down_tail_ref, slope_tail_ref = refs[:5]
    w_refs = refs[5 : 5 + count]
    hidden_ref, hidden_tail_ref, sums_ref, sums_tail_ref, part_ref, low, total, held_weight = refs[5 + count :]
    step = pl.program_id(0)

    @pl.when(step == 0)
    def _():
        low[...] = grad_ref[...].astype(LOW)
        hidden = cdot(low[...], down_tail_ref[...]) * slope_tail_ref[...].astype(F32)
        sums_tail_ref[...] = jnp.sum(hidden, axis=0, keepdims=True)
        hidden = hidden.astype(LOW)
        hidden_tail_ref[...] = hidden
        total[...] = cdot(hidden, up_tail_ref[...], 1, 1)

    weight = spread.load(w_refs, where, held_weight)
    units = hidden_ref.shape[2]
    hidden = cdot(low[...], weight[:, units:]) * slope_ref[0].astype(F32)
    sums_ref[0] = jnp.sum(hidden, axis=0, keepdims=True)
    hidden = hidden.astype(LOW)
    hidden_ref[0] = hidden
    total[...] += cdot(hidden, weight[:, :units], 1, 1)

    @pl.when(step == pl.num_programs(0) - 1)
    def _():
        part_ref[...] = total[...].astype(LOW)


def mlp_grads_kernel(spread, where, *refs):
    count = len(spread.grad_keys)
    grad_ref, normed_ref, hidden_ref, act_ref, hidden_tail_ref, act_tail_ref = refs[:6]
    out_refs = refs[6 : 6 + count]
    tail_ref, grad_turned, normed_turned, result = refs[6 + count :]
    step = pl.program_id(0)

    @pl.when(step == 0)
    def _():
        grad_turned[...] = grad_ref[...].astype(LOW).T
        normed_turned[...] = normed_ref[...].T
        up_tail = cdot(normed_turned[...], hidden_tail_ref[...]).astype(LOW)
        down_tail = cdot(grad_turned[...], act_tail_ref[...]).astype(LOW)
        steps, _, both = tail_ref.shape
        half = both // 2
        for t in range(steps):
            at = slice(t * half, (t + 1) * half)
            tail_ref[t] = jnp.concatenate([up_tail[:, at], down_tail[:, at]], axis=1)

    units = hidden_ref.shape[2]
    result[:, :units] = cdot(normed_turned[...], hidden_ref[0]).astype(LOW)
    result[:, units:] = cdot(grad_turned[...], act_ref[0]).astype(LOW)
    spread.store(out_refs, where, result)


def attn_backward_kernel(spread, where, *refs):
    count = len(spread.weight_keys)
    grad_ref, own_ref, other_ref, middle_ref, vec_ref, qkv_ref, sums_ref = refs[:7]
    w_refs = refs[7 : 7 + count]
    dmiddle_ref, norm_sums_ref, dqkv_ref, head_sums_ref, part_ref, low, total, held_weight = refs[7 + count :]
    step = pl.program_id(0)

    @pl.when(step == 0)
    def _():
        grad = grad_ref[...]
        inner, gain_sum, shift_sum = norm_backward(
            own_ref[...].astype(F32) + other_ref[...].astype(F32), middle_ref[...], vec_ref[0, 5:6, :]
        )
        dmiddle = grad + inner
        dmiddle_ref[...] = dmiddle
        low[...] = dmiddle.astype(LOW)
        norm_sums_ref[0:1, :] = gain_sum
        norm_sums_ref[1:2, :] = shift_sum
        norm_sums_ref[2:3, :] = jnp.sum(grad, axis=0, keepdims=True)
        norm_sums_ref[3:4, :] = jnp.sum(dmiddle, axis=0, keepdims=True)
        total[...] = jnp.zeros_like(total)

    weight = spread.load(w_refs, where, held_weight)
    tokens = where[4]
    head_columns = 3 * HD
    local = qkv_ref.shape[2]
    heads = local // head_columns
    scale = HD ** (-0.5)
    qkv = qkv_ref[0]
    dmixed = cdot(low[...], weight[:, local : local + heads * HD]).astype(LOW)
    pieces = []
    for head in range(heads):
        at = head * head_columns
        query = qkv[:, at : at + HD]
        key = qkv[:, at + HD : at + 2 * HD]
        value = qkv[:, at + 2 * HD : at + 3 * HD]
        grad = dmixed[:, head * HD : (head + 1) * HD]
        scores = mask_keys(cdot(key, query, 1, 1) * scale, tokens)
        probs = jnp.exp(scores - sums_ref[0, head : head + 1, :])
        dprobs = cdot(value, grad, 1, 1)
        row_dot = jnp.sum(dprobs * probs, axis=0, keepdims=True)
        dscores = (probs * (dprobs - row_dot)).astype(LOW)
        pieces.append(cdot(key, dscores, 0, 0).T * scale)
        pieces.append(cdot(dscores, query) * scale)
        pieces.append(cdot(probs.astype(LOW), grad))
    dqkv = jnp.concatenate(pieces, axis=1)
    head_sums_ref[0] = jnp.sum(dqkv, axis=0, keepdims=True)
    dqkv = dqkv.astype(LOW)
    dqkv_ref[0] = dqkv
    total[...] += cdot(dqkv, weight[:, :local], 1, 1)

    @pl.when(step == pl.num_programs(0) - 1)
    def _():
        part_ref[...] = total[...].astype(LOW)


def attn_grads_kernel(spread, where, *refs):
    count = len(spread.grad_keys)
    dmiddle_ref, normed_ref, dqkv_ref, mixed_ref, tail_ref = refs[:5]
    out_refs = refs[5 : 5 + count]
    grad_turned, normed_turned, result = refs[5 + count :]

    @pl.when(pl.program_id(0) == 0)
    def _():
        grad_turned[...] = dmiddle_ref[...].astype(LOW).T
        normed_turned[...] = normed_ref[...].T

    parts = [
        cdot(normed_turned[...], dqkv_ref[0]).astype(LOW),
        cdot(grad_turned[...], mixed_ref[0]).astype(LOW),
        tail_ref[0],
    ]
    used = sum(part.shape[1] for part in parts)
    parts.append(jnp.zeros((result.shape[0], result.shape[1] - used), LOW))
    result[...] = jnp.concatenate(parts, axis=1)
    spread.store(out_refs, where, result)


def norm_backward_kernel(where, dmiddle_ref, own_ref, other_ref, stream_ref, vec_ref, out_ref, sums_ref):
    inner, gain_sum, shift_sum = norm_backward(
        own_ref[...].astype(F32) + other_ref[...].astype(F32), stream_ref[...], vec_ref[0, 0:1, :]
    )
    out_ref[...] = dmiddle_ref[...] + inner
    sums_ref[0:1, :] = gain_sum
    sums_ref[1:2, :] = shift_sum


def adam_kernel(units, local, out_local, tail_units, where, *refs):
    attn_own, attn_other, mlp_own, mlp_other = refs[:4]
    states = [refs[4 + 3 * k : 7 + 3 * k] for k in range(4)]
    outs = refs[len(refs) - 16 :]

    def pair(own, other):
        own, other = own[...].astype(F32), other[...].astype(F32)
        low_core = where[3] == 0
        return jnp.where(low_core, own, other), jnp.where(low_core, other, own)

    attn = pair(attn_own, attn_other)
    mlp = pair(mlp_own, mlp_other)
    at = local + out_local
    grads = [
        jnp.concatenate([half[:, :local] for half in attn], axis=1),
        jnp.concatenate([half[:, local:at] for half in attn], axis=1),
        jnp.concatenate(
            [piece for m, n in zip(mlp, attn) for piece in (m[:, :units], n[:, at : at + tail_units])], axis=1
        ),
        jnp.concatenate(
            [
                piece
                for m, n in zip(mlp, attn)
                for piece in (m[:, units:], n[:, at + tail_units : at + 2 * tail_units])
            ],
            axis=1,
        ),
    ]
    for number, grad in enumerate(grads):
        weight, first, second = [ref[0] for ref in states[number]]
        new = adam_step(weight, grad, first, second, RATES[number], DECAY)
        for ref, values in zip(outs[4 * number : 4 * number + 4], (grad, new[1], new[2], new[0])):
            ref[0] = values


def vec_pack_kernel(where, *refs):
    out_ref = refs[-1]
    layers = out_ref.shape[0]
    out_ref[...] = jnp.zeros_like(out_ref)
    for layer in range(layers):
        one_ref, two_ref, head_ref, main_ref, tail_ref = refs[5 * layer : 5 * layer + 5]
        out_ref[layer, 0:2, :] = one_ref[0:2, :]
        out_ref[layer, 2:6, :] = two_ref[0:4, :]
        for t in range(head_ref.shape[0]):
            out_ref[layer, 8 + t : 9 + t, : head_ref.shape[2]] = head_ref[t]
            out_ref[layer, 16 + t : 17 + t, : main_ref.shape[2]] = main_ref[t]
        out_ref[layer, 6:7, : tail_ref.shape[1]] = tail_ref[...]


def vec_kernel(steps, local, units, tail_units, where, own_ref, other_ref, vec_ref, first_ref, second_ref,
               grad_out, first_out, second_out, weight_out):
    low_core = where[3] == 0
    for layer in range(vec_ref.shape[0]):
        own, other = own_ref[layer], other_ref[layer]
        cores = jnp.where(low_core, own, other), jnp.where(low_core, other, own)
        norms = cores[0][0:6]
        heads = local // (3 * HD)

        def head_piece(kind):
            return [
                core[8 + t : 9 + t, (3 * head + kind) * HD : (3 * head + kind + 1) * HD]
                for t in range(steps)
                for core in cores
                for head in range(heads)
            ]

        hidden = [
            piece
            for t in range(steps)
            for core in cores
            for piece in (core[16 + t : 17 + t, :units], core[6:7, t * tail_units : (t + 1) * tail_units])
        ]
        grad = jnp.concatenate(
            [norms[0:1], norms[1:2], *head_piece(0), *head_piece(2),
             norms[5:6], norms[2:3], norms[3:4], norms[4:5], *hidden],
            axis=1,
        )
        at = slice(layer, layer + 1)
        new = adam_step(vec_ref[at, :], grad, first_ref[at, :], second_ref[at, :], RATES[4], 0.0)
        grad_out[at, :] = grad
        first_out[at, :] = new[1]
        second_out[at, :] = new[2]
        weight_out[at, :] = new[0]


def plane_sides(chips):
    side = math.isqrt(chips)
    while chips % side:
        side -= 1
    return side, chips // side


class Place:
    def __init__(self):
        self.nf = lax.axis_size("fsdp")
        self.nt = lax.axis_size("tp")
        self.na, self.nb = plane_sides(self.nf // 2)
        fi = lax.axis_index("fsdp")
        self.core = fi % 2
        self.a = (fi // 2) // self.nb
        self.b = (fi // 2) % self.nb
        self.t = lax.axis_index("tp")
        self.size = {"a": self.na, "b": self.nb, "t": self.nt}
        self.at = {"a": self.a, "b": self.b, "t": self.t}

    def pairs(self, axis, move):
        if axis == "t":
            return [(i, move(i)) for i in range(self.nt)]
        found = []
        for f in range(self.nf):
            place = {"a": f // 2 // self.nb, "b": f // 2 % self.nb, "core": f % 2}
            place[axis] = move(place[axis])
            found.append((f, (place["a"] * self.nb + place["b"]) * 2 + place["core"]))
        return found

    def send(self, values, axis, move):
        return lax.ppermute(values, "tp" if axis == "t" else "fsdp", self.pairs(axis, move))

    def sibling(self, values):
        return self.send(values, "core", lambda i: 1 - i)

    def swap_rows(self, values):
        pairs = []
        for f in range(self.nf):
            for t in range(self.nt):
                if f % 2 != t % 2:
                    sign = 1 if t % 2 else -1
                    pairs.append((f * self.nt + t, (f + sign) * self.nt + t - sign))
        arrived = lax.ppermute(values.astype(LOW), ("fsdp", "tp"), pairs).astype(F32)
        return jnp.where(self.core != self.t % 2, arrived, values)

    def gather_axis(self, block, axis):
        n = self.size[axis]
        return [block] + [self.send(block, axis, lambda i, k=k: (i - k) % n) for k in range(1, n)]

    def scatter_axis(self, parts, axis):
        n = self.size[axis]
        sent = [self.send(parts[k], axis, lambda i, k=k: (i + k) % n) for k in range(1, n)]
        return [parts[0], *sent]


def split_pair(place, first, second):
    return (
        jnp.where(place.core == 0, first, second),
        jnp.where(place.core == 0, second, first),
    )


def sum_kernel(outputs, where, *refs):
    count = sum(size for sizes in outputs for size in sizes)
    ins, outs = refs[:count], refs[count:]
    for out_ref, sizes in zip(outs, outputs):
        for number, size in enumerate(sizes):
            total = ins[0][0, 0].astype(F32)
            for ref in ins[1:size]:
                total += ref[0, 0].astype(F32)
            ins = ins[size:]
            out_ref[0, number] = total.astype(LOW)


def tie_kernel(where, *refs):
    pass


def tie(where, arrays, after):
    space = pl.BlockSpec(memory_space=pl.ANY)
    return call(
        tie_kernel,
        where,
        1,
        [(space, x) for x in arrays],
        [(space, jax.ShapeDtypeStruct(x.shape, x.dtype)) for x in arrays],
        [],
        aliases={1 + k: k for k in range(len(arrays))},
        after=after,
    )


class Spread:
    def __init__(self, place, rows, columns, middle):
        self.place, self.rows, self.columns = place, rows, columns
        self.middle = middle
        self.direct = rows % 16 == 0
        self.width = place.na * place.nb * 2 * rows
        na, nb = place.na, place.nb
        self.grad_keys = [[(0, a, b) for b in range(nb)] for a in range(na)]
        self.grad_keys += [[(1, a, b) for a in range(na)] for b in range(nb)]
        self.gather_keys = [[(0, 0, 0), (1, 0, 0)]]
        self.gather_keys += [[(0, 0, b), (1, 0, b)] for b in range(1, nb)]
        self.gather_keys += [[(0, a, 0), (1, a, 0)] for a in range(1, na)]
        self.gather_keys += [[(half, a, b)] for half in range(2) for a in range(1, na) for b in range(1, nb)]
        if middle:
            self.gather_keys = self.grad_keys
        self.weight_keys = self.gather_keys
        if not self.direct:
            self.weight_keys = self.grad_keys = [None]

    def shapes(self, keys):
        if not self.direct:
            return [(self.place.nt, self.width, self.columns)]
        return [(self.place.nt, len(blocks), self.rows, self.columns) for blocks in keys]

    def specs(self, keys):
        return [stepped(shape[1:]) for shape in self.shapes(keys)]

    def first_row(self, where, key):
        half, a, b = key
        a = lax.rem(where[0] + a, self.place.na)
        b = lax.rem(where[1] + b, self.place.nb)
        return pl.multiple_of(((a * self.place.nb + b) * 2 + half) * self.rows, 16)

    def load(self, refs, where, scratch):
        if not self.direct:
            return refs[0].at[0]
        for ref, blocks in zip(refs, self.weight_keys):
            for number, key in enumerate(blocks):
                scratch[pl.ds(self.first_row(where, key), self.rows), :] = ref[0, number]
        return scratch

    def store(self, refs, where, scratch):
        if not self.direct:
            refs[0][0] = scratch[...]
            return
        for ref, blocks in zip(refs, self.grad_keys):
            for number, key in enumerate(blocks):
                ref[0, number] = scratch[pl.ds(self.first_row(where, key), self.rows), :]

    def start(self, own, other):
        place = self.place
        halves = split_pair(place, own, other)
        if self.middle:
            return [jnp.stack(place.gather_axis(half, axis)) for half, axis in zip(halves, "ba")]
        return [jnp.stack(halves)]

    def gather(self, where, blocks, after=()):
        place = self.place
        na, nb = place.na, place.nb
        blocks = [lax.all_gather(block, "tp") for block in blocks]
        if self.direct and len(after):
            blocks = tie(where, blocks, after)
        if self.middle:
            arrays = [array for block, axis in zip(blocks, "ab") for array in place.gather_axis(block, axis)]
        else:
            along_b = place.gather_axis(blocks[0], "b")
            along_a = place.gather_axis(blocks[0], "a")
            first = [place.gather_axis(x[:, :1], "a")[1:] for x in along_b[1:]]
            second = [place.gather_axis(x[:, 1:], "b")[1:] for x in along_a[1:]]
            arrays = along_b + along_a[1:]
            arrays += [first[b][a] for a in range(na - 1) for b in range(nb - 1)]
            arrays += [second[a][b] for a in range(na - 1) for b in range(nb - 1)]
        if self.direct:
            return arrays
        found = {
            key: array[:, number]
            for array, keys in zip(arrays, self.gather_keys)
            for number, key in enumerate(keys)
        }
        full = jnp.stack([found[half, a, b] for a in range(na) for b in range(nb) for half in range(2)], axis=1)
        full = full.reshape(place.nt, na, nb, 2, self.rows, self.columns)
        full = self.roll(full, (na - place.a) % na, (nb - place.b) % nb)
        return [full.reshape(place.nt, self.width, self.columns)]

    def roll(self, full, a, b):
        full = lax.dynamic_slice_in_dim(jnp.concatenate([full, full], axis=1), a, self.place.na, 1)
        return lax.dynamic_slice_in_dim(jnp.concatenate([full, full], axis=2), b, self.place.nb, 2)

    def sums(self, where, outputs, after):
        place, rows, columns = self.place, self.rows, self.columns

        def block(number):
            return pl.BlockSpec((1, 1, rows, columns), lambda i, s: (i, number, 0, 0))

        shapes = [(place.nt, len(groups), rows, columns) for groups in outputs]
        return call(
            functools.partial(sum_kernel, [[len(group) for group in groups] for groups in outputs]),
            where,
            place.nt,
            [(block(number), x) for groups in outputs for group in groups for x, number in group],
            [(stepped(shape[1:]), low_of(*shape)) for shape in shapes],
            [],
            after=after,
        )

    def scatter_last(self, arrays):
        place = self.place
        if not self.direct:
            full = arrays[0].reshape(place.nt, place.na, place.nb, 2, self.rows, self.columns)
            full = self.roll(full, place.a, place.b)
            arrays = [full[:, a, :, 0] for a in range(place.na)] + [full[:, :, b, 1] for b in range(place.nb)]
        return (
            place.scatter_axis(arrays[: place.na], "a"),
            place.scatter_axis(arrays[place.na :], "b"),
        )

    def scatter_first(self, where, halves, after):
        place = self.place
        if self.middle:
            outputs = [[[(x, k) for x in half] for k in range(half[0].shape[1])] for half in halves]
            results = self.sums(where, outputs, after)
            return results[0], [lax.psum_scatter(x, "tp", scatter_dimension=0, tiled=True)[0] for x in results]
        axes = ("b", "a")
        keys = [(half, k) for half in range(2) for k in range(1, place.size[axes[half]])]
        results = self.sums(where, [[[(x, k) for x in halves[half]]] for half, k in keys], after)
        terms = [[(x, 0) for x in arrays] for arrays in halves]
        for (half, k), total in zip(keys, results):
            n = place.size[axes[half]]
            terms[half].append((place.send(total, axes[half], lambda i: (i + k) % n), 0))
        return results[0], terms

    def scatter_tp(self, where, terms, after):
        place = self.place
        if self.middle:
            done = [
                sum(x.astype(F32) for x in place.scatter_axis(list(half), axis)).astype(LOW)
                for half, axis in zip(terms, "ba")
            ]
            last = after[0]
        else:
            (last,) = self.sums(where, [terms], after)
            done = lax.psum_scatter(last, "tp", scatter_dimension=0, tiled=True)[0]
        mine, other = split_pair(place, done[0], done[1])
        return last, (mine, place.sibling(other))


def body(
    residual_in,
    cotangent,
    slot_tokens,
    qkv_weight,
    out_weight,
    up_weight,
    down_weight,
    vectors,
    qkv_first,
    qkv_second,
    out_first,
    out_second,
    up_first,
    up_second,
    down_first,
    down_second,
    vec_first,
    vec_second,
):
    place = Place()
    layer_count, shard_rows, _ = qkv_weight.shape
    half_rows, width = residual_in.shape
    rows = 2 * half_rows
    nt = place.nt
    local = qkv_weight.shape[2] // 2
    out_local = out_weight.shape[1] // 2
    hidden_local = up_weight.shape[2] // 2
    units = hidden_local // 128 * 128
    tail_units = hidden_local - units
    heads = out_local // HD
    attn_columns = -(-(local + out_local + 2 * tail_units) // 128) * 128
    mlp_columns = 2 * units

    tokens_pair = jnp.concatenate(split_pair(place, slot_tokens, place.sibling(slot_tokens)))
    slot_at = (place.t % 2) * slot_tokens.shape[0] + place.t // 2
    tokens = lax.dynamic_slice_in_dim(tokens_pair, slot_at, 1)
    row_mask = (jnp.arange(rows, dtype=jnp.int32) < tokens[0]).astype(F32)[:, None]
    here = jnp.stack([place.a, place.b, place.t, place.core]).astype(jnp.int32)
    where = jnp.concatenate([here, tokens.astype(jnp.int32)])

    def own_rows(values):
        return lax.dynamic_slice_in_dim(values, place.core * half_rows, half_rows)

    spreads = [
        (
            Spread(place, shard_rows, attn_columns, False),
            Spread(place, shard_rows, mlp_columns, layer > 0),
        )
        for layer in range(layer_count)
    ]

    def turn(arrays):
        qkv, out, up, down = arrays
        return qkv, jnp.swapaxes(out, 1, 2), up, jnp.swapaxes(down, 1, 2)

    weights = turn((qkv_weight, out_weight, up_weight, down_weight))
    firsts = turn((qkv_first, out_first, up_first, down_first))
    seconds = turn((qkv_second, out_second, up_second, down_second))

    def layer_block(array, layer):
        block = (1, *array.shape[1:])
        return pl.BlockSpec(block, lambda i, s: (layer, 0, 0), pipeline_mode=pl.Buffered(1))

    def pack(layer):
        attn, mlp = (shard_rows, attn_columns), (shard_rows, mlp_columns)
        return call(
            functools.partial(pack_kernel, units),
            here,
            1,
            [(layer_block(w, layer), w) for w in weights],
            [(held(shape), low_of(*shape)) for shape in (attn, attn, mlp, mlp)],
            [],
            bytes_accessed=6 * shard_rows * 13216 // 4,
        )

    starts = []
    for layer in range(layer_count):
        own_attn, other_attn, own_mlp, other_mlp = pack(layer)
        starts.append(
            (
                spreads[layer][0].start(own_attn, place.sibling(other_attn)),
                spreads[layer][1].start(own_mlp, place.sibling(other_mlp)),
            )
        )
    gathered = []
    before = [x for pair in starts[1:] for blocks in pair for x in blocks]
    for layer in range(layer_count):
        attn_full = spreads[layer][0].gather(where, starts[layer][0], before)
        mlp_full = spreads[layer][1].gather(where, starts[layer][1], attn_full[1:3])
        before = mlp_full[1:3]
        gathered.append((attn_full, mlp_full))

    wide = vectors[:, : 8 * width].reshape(layer_count, 8, width)
    head_bias = vectors[:, 2 * width : 4 * width].reshape(layer_count, 2, 2 * nt, 1, out_local)
    hidden_bias = vectors[:, 8 * width :].reshape(layer_count, nt, 2, 1, hidden_local)
    main_bias = hidden_bias[..., :units]
    tail_bias = jnp.moveaxis(hidden_bias[..., units:], 1, 3).reshape(layer_count, 2, 1, nt * tail_units)

    full = whole((rows, width))
    weight_scratch = [
        pltpu.VMEM((width, attn_columns), LOW),
        pltpu.VMEM((width, mlp_columns), LOW),
    ]
    flat = pltpu.VMEM((rows, width), F32)
    flat_low = pltpu.VMEM((rows, width), LOW)
    big = 2 * rows * width

    def wide_of(layer):
        spec = pl.BlockSpec((1, 8, width), lambda i, s: (layer, 0, 0), pipeline_mode=pl.Buffered(1))
        return spec, wide

    def attn_forward(layer, base, own, other):
        spread = spreads[layer][0]
        joined = base is not None
        if joined:
            ins = [(full, base), (full, own), (full, other), wide_of(layer - 1)]
        else:
            half = whole((half_rows, width))
            ins = [(half, own), (half, other)]
        ins.append(wide_of(layer))
        ins.append(
            (
                pl.BlockSpec(
                    (1, 2, 1, 1, out_local), lambda i, s: (layer, 0, 2 * i + s[3], 0, 0)
                ),
                head_bias,
            )
        )
        ins += list(zip(spread.specs(spread.weight_keys), gathered[layer][0]))
        return call(
            functools.partial(attn_forward_kernel, spread, joined, tail_units),
            where,
            nt,
            ins,
            [
                (held((rows, width)), f32_of(rows, width)),
                (held((rows, width)), low_of(rows, width)),
                (stepped((rows, local)), low_of(nt, rows, local)),
                (stepped((rows, out_local)), low_of(nt, rows, out_local)),
                (stepped((heads, rows)), f32_of(nt, heads, rows)),
                (stepped((width, 2 * tail_units)), low_of(nt, width, 2 * tail_units)),
                (held((rows, width)), low_of(rows, width)),
            ],
            [flat, weight_scratch[0]],
            big * nt * (local + out_local) + 4 * nt * heads * rows * rows * HD,
            rows * width * 12 + nt * width * attn_columns * 2,
            nt * heads * rows * rows,
        )

    def mlp_forward(layer, base, own, other, tails):
        spread = spreads[layer][1]
        tail = nt * tail_units
        tail_shape = (width, tail)
        ins = [
            (full, base),
            (full, own),
            (full, other),
            wide_of(layer),
            (pl.BlockSpec((1, 1, 1, 1, units), lambda i, s: (layer, i, s[3], 0, 0)), main_bias),
            (whole(tails.shape), tails),
            (pl.BlockSpec((1, 1, 1, tail), lambda i, s: (layer, s[3], 0, 0)), tail_bias),
        ]
        ins += list(zip(spread.specs(spread.weight_keys), gathered[layer][1]))
        return call(
            functools.partial(mlp_forward_kernel, spread),
            where,
            nt,
            ins,
            [
                (held((rows, width)), f32_of(rows, width)),
                (held((rows, width)), low_of(rows, width)),
                (stepped((rows, units)), low_of(nt, rows, units)),
                (stepped((rows, units)), low_of(nt, rows, units)),
                (held((rows, tail)), low_of(rows, tail)),
                (held((rows, tail)), low_of(rows, tail)),
                (held(tail_shape), low_of(*tail_shape)),
                (held(tail_shape), low_of(*tail_shape)),
                (held((rows, width)), low_of(rows, width)),
            ],
            [flat, weight_scratch[1]],
            2 * big * (nt * units + tail),
            rows * width * 16 + nt * (width + rows) * mlp_columns * 2,
            rows * nt * units,
        )

    def mlp_backward(layer, grad, slope, tails, slope_tail):
        spread = spreads[layer][1]
        tail = nt * tail_units
        ins = [(full, grad), (stepped((rows, units)), slope)]
        ins += [(whole(w.shape), w) for w in (*tails, slope_tail)]
        ins += list(zip(spread.specs(spread.weight_keys), gathered[layer][1]))
        return call(
            functools.partial(mlp_backward_kernel, spread),
            where,
            nt,
            ins,
            [
                (stepped((rows, units)), low_of(nt, rows, units)),
                (held((rows, tail)), low_of(rows, tail)),
                (stepped((1, units)), f32_of(nt, 1, units)),
                (held((1, tail)), f32_of(1, tail)),
                (held((rows, width)), low_of(rows, width)),
            ],
            [flat_low, flat, weight_scratch[1]],
            2 * big * (nt * units + tail),
            rows * width * 6 + nt * (width + rows) * mlp_columns * 2,
        )

    def mlp_grads(layer, grad, normed, hidden, act, hidden_tail, act_tail):
        spread = spreads[layer][1]
        ins = [(full, grad), (full, normed)]
        ins += [(stepped((rows, units)), hidden), (stepped((rows, units)), act)]
        ins += [(whole(x.shape), x) for x in (hidden_tail, act_tail)]
        tail_shape = (nt, width, 2 * tail_units)
        outs = [
            (spec, low_of(*shape))
            for spec, shape in zip(spread.specs(spread.grad_keys), spread.shapes(spread.grad_keys))
        ]
        outs.append((held(tail_shape), low_of(*tail_shape)))
        turned_low = pltpu.VMEM((width, rows), LOW)
        return call(
            functools.partial(mlp_grads_kernel, spread),
            where,
            nt,
            ins,
            outs,
            [turned_low, turned_low, weight_scratch[1]],
            2 * big * nt * (units + tail_units),
            rows * width * 6 + nt * (width + rows) * mlp_columns * 2,
        )

    def attn_backward(layer, grad, own, other, middle, qkv, log_sums, after=()):
        spread = spreads[layer][0]
        ins = [(full, grad), (full, own), (full, other), (full, middle), wide_of(layer)]
        ins += [(stepped((rows, local)), qkv), (stepped((heads, rows)), log_sums)]
        ins += list(zip(spread.specs(spread.weight_keys), gathered[layer][0]))
        return call(
            functools.partial(attn_backward_kernel, spread),
            where,
            nt,
            ins,
            [
                (held((rows, width)), f32_of(rows, width)),
                (held((8, width)), f32_of(8, width)),
                (stepped((rows, local)), low_of(nt, rows, local)),
                (stepped((1, local)), f32_of(nt, 1, local)),
                (held((rows, width)), low_of(rows, width)),
            ],
            [flat_low, flat, weight_scratch[0]],
            big * nt * (local + out_local) + 10 * nt * heads * rows * rows * HD,
            rows * width * 20 + nt * width * attn_columns * 2,
            nt * heads * rows * rows,
            after=after,
        )

    def attn_grads(layer, dmiddle, normed, dqkv, mixed, tail_grads):
        spread = spreads[layer][0]
        ins = [(full, dmiddle), (full, normed)]
        ins += [(stepped((rows, local)), dqkv), (stepped((rows, out_local)), mixed)]
        ins.append((stepped((width, 2 * tail_units)), tail_grads))
        outs = [
            (spec, low_of(*shape))
            for spec, shape in zip(spread.specs(spread.grad_keys), spread.shapes(spread.grad_keys))
        ]
        turned_low = pltpu.VMEM((width, rows), LOW)
        return call(
            functools.partial(attn_grads_kernel, spread),
            where,
            nt,
            ins,
            outs,
            [turned_low, turned_low, weight_scratch[0]],
            big * nt * (local + out_local),
            rows * width * 6 + nt * (width + rows) * attn_columns * 2,
        )

    def norm_one_backward(layer, dmiddle, own, other, stream, after=()):
        return call(
            norm_backward_kernel,
            where,
            1,
            [(full, dmiddle), (full, own), (full, other), (full, stream), wide_of(layer)],
            [(held((rows, width)), f32_of(rows, width)), (held((8, width)), f32_of(8, width))],
            [],
            rows * width * 20,
            rows * width * 16,
            after=after,
        )

    mine = place.swap_rows(residual_in)
    base, own, other = None, mine, place.sibling(mine)
    saved = []
    for layer in range(layer_count):
        stream, normed, qkv, mixed, log_sums, tails, part = attn_forward(layer, base, own, other)
        middle, normed_two, act, slope, act_tail, slope_tail, up_tail, down_tail, part = mlp_forward(
            layer, stream, part, place.sibling(part), tails
        )
        saved.append(
            (stream, normed, qkv, mixed, log_sums, middle, normed_two, act, slope, act_tail, slope_tail,
             (up_tail, down_tail))
        )
        base, own, other = middle, part, place.sibling(part)
    output = own_rows(base) + (own_rows(own).astype(F32) + own_rows(other).astype(F32))
    output = place.swap_rows((output + wide[layer_count - 1, 7:8]) * own_rows(row_mask))

    mine = place.swap_rows(cotangent)
    grad_stream = jnp.concatenate(split_pair(place, mine, place.sibling(mine)), axis=0) * row_mask


    def adam(layer, attn_pair, mlp_pair, before, after=()):
        ins = [(whole(x.shape), x) for x in (*attn_pair, *mlp_pair)]
        for states in zip(weights, firsts, seconds):
            ins += [(layer_block(x, layer), x) for x in states]
        outs = [
            (layer_block(weight, layer), f32_of(*weight.shape)) for weight in weights for _ in range(4)
        ]
        aliases = None
        if before is not None:
            aliases = {1 + len(ins) + k: k for k in range(16)}
            ins += [(pl.BlockSpec(memory_space=pl.ANY), x) for x in before]
        return call(
            functools.partial(adam_kernel, units, local, out_local, tail_units),
            where,
            1,
            ins,
            outs,
            [],
            bytes_accessed=28 * shard_rows * 13216 // 4,
            aliases=aliases,
            after=after,
        )

    vec_sums = [None] * layer_count
    last = grad_stream
    above = None
    for layer in reversed(range(layer_count)):
        (stream, normed, qkv, mixed, log_sums, middle, normed_two, act, slope, act_tail, slope_tail, tails) = (
            saved[layer]
        )
        spread_attn, spread_mlp = spreads[layer]
        hidden, hidden_tail, hidden_sums, tail_sums, part = mlp_backward(
            layer, grad_stream, slope, tails, slope_tail
        )
        other = place.sibling(part)
        *mlp_grad, tail_grads = mlp_grads(
            layer, grad_stream, normed_two, hidden, act, hidden_tail, act_tail
        )
        last = tail_grads
        mlp_terms = spread_mlp.scatter_last(mlp_grad)
        if above:
            last, attn_terms_above = spreads[above][0].scatter_first(where, attn_terms_above, [last])
        dmiddle, norm_two_sums, dqkv, head_sums, part = attn_backward(
            layer, grad_stream, part, other, middle, qkv, log_sums, [last]
        )
        other = place.sibling(part)
        attn_grad = attn_grads(layer, dmiddle, normed, dqkv, mixed, tail_grads)
        last = attn_grad[0]
        if above:
            last, mlp_pair_above = spreads[above][1].scatter_tp(where, mlp_terms_above, [last])
        grad_stream, norm_one_sums = norm_one_backward(layer, dmiddle, part, other, stream, [last])
        if layer:
            attn_terms = spread_attn.scatter_last(attn_grad)
        last, mlp_terms = spread_mlp.scatter_first(where, mlp_terms, [norm_one_sums])
        if not layer:
            if spread_attn.direct:
                attn_grad = tie(where, attn_grad, [last])
            attn_terms = spread_attn.scatter_last(attn_grad)
        vec_sums[layer] = (norm_one_sums, norm_two_sums, head_sums, hidden_sums, tail_sums)
        if above:
            last, attn_pair_above = spreads[above][0].scatter_tp(where, attn_terms_above, [last])
            pairs_above = attn_pair_above, mlp_pair_above
        above, mlp_terms_above, attn_terms_above = layer, mlp_terms, attn_terms
        if layer:
            grad_stream, last = lax.optimization_barrier((grad_stream, last))
    last, attn_terms_above = spreads[above][0].scatter_first(where, attn_terms_above, [last, *pairs_above[1]])
    updated = adam(1, *pairs_above, None, [last])
    last, mlp_pair_above = spreads[above][1].scatter_tp(where, mlp_terms_above, [last])
    last, attn_pair_above = spreads[above][0].scatter_tp(where, attn_terms_above, [last])
    grad_input = place.swap_rows(own_rows(grad_stream))

    flat_sums = [x for sums in vec_sums for x in sums]
    vec_shape = (layer_count, 24, width)
    (vec_total,) = call(
        vec_pack_kernel,
        where,
        1,
        [(whole(x.shape), x) for x in flat_sums],
        [(held(vec_shape), f32_of(*vec_shape))],
        [],
        after=[last],
    )
    for axis in ("b", "a", "t"):
        step = 1
        while step < place.size[axis]:
            vec_total = vec_total + place.send(vec_total, axis, lambda i: i ^ step)
            step *= 2
    vec_new = call(
        functools.partial(vec_kernel, nt, local, units, tail_units),
        where,
        1,
        [(whole(x.shape), x) for x in (vec_total, place.sibling(vec_total), vectors, vec_first, vec_second)],
        [(held(vectors.shape), f32_of(*vectors.shape)) for _ in range(4)],
        [],
    )
    updated = adam(above, attn_pair_above, mlp_pair_above, updated)
    updated = [
        jnp.swapaxes(x, 1, 2) if number // 4 % 2 else x for number, x in enumerate(updated)
    ]
    return (output, grad_input, *updated, *vec_new)


def solution(mesh):
    rows = P(("fsdp", "tp"), None)
    wide = P(None, "fsdp", "tp")
    tall = P(None, "tp", "fsdp")
    moments = (wide, wide, tall, tall, wide, wide, tall, tall, P(), P())
    return jax.shard_map(
        body,
        mesh=mesh,
        in_specs=(rows, rows, P("fsdp"), wide, tall, wide, tall, P(), *moments),
        out_specs=(rows, rows, *[wide] * 4, *[tall] * 4, *[wide] * 4, *[tall] * 4, *[P()] * 4),
        check_vma=False,
    )
```

```python
import functools
import math

import jax
import jax.numpy as jnp
from jax import lax
from jax.experimental import pallas as pl
from jax.experimental.pallas import tpu as pltpu
from jax.sharding import PartitionSpec as P

HD = 72
IMG_TOK = 729
STEP = 10


EPS_NORM = 1e-06
MASKED = -30000.0
BETA_ONE = 0.9
BETA_TWO = 0.999
ADAM_EPS = 1e-08
DECAY = 0.1
RATES = (0.05, 1.0, 0.05, 0.03, 0.3)
LOW = jnp.bfloat16
F32 = jnp.float32
GELU = math.sqrt(2.0 / math.pi)
SCORE = HD ** (-0.5)
POWER = SCORE / math.log(2.0)
VMEM = 56 * 1024 * 1024
COST = {
    "pack_kernel": 4,
    "attn_forward_kernel": 26,
    "mlp_forward_kernel": 24,
    "mlp_backward_kernel": 17,
    "mlp_grads_kernel": 16,
    "attn_backward_kernel": 33,
    "attn_grads_kernel": 13,
    "norm_backward_kernel": 9,
    "sum_kernel": 5,
    "vec_pack_kernel": 0.3,
    "vec_kernel": 0.3,
    "adam_kernel": 1,
    "tie_kernel": 1,
}
SCALE = 2e9


def adam_step(weight, gradient, first_moment, second_moment, step_rate, decay_rate):
    first_new = BETA_ONE * first_moment + (1.0 - BETA_ONE) * gradient
    second_new = BETA_TWO * second_moment + (1.0 - BETA_TWO) * gradient * gradient
    first_hat = first_new / (1.0 - BETA_ONE**STEP)
    second_hat = second_new / (1.0 - BETA_TWO**STEP)
    weight_new = weight - step_rate * (
        first_hat / (jnp.sqrt(second_hat) + ADAM_EPS) + decay_rate * weight
    )
    return (weight_new, first_new, second_new)


def cdot(left, right, left_dim=1, right_dim=0):
    return lax.dot_general(
        left, right, (((left_dim,), (right_dim,)), ((), ())), preferred_element_type=F32
    )


def norm_parts(values):
    centred = values - jnp.mean(values, axis=-1, keepdims=True)
    inverse = lax.rsqrt(jnp.mean(centred * centred, axis=-1, keepdims=True) + EPS_NORM)
    return centred * inverse, inverse


def over_rows(rows, step, body):
    def run(i, carry):
        body(pl.ds(pl.multiple_of(i * step, step), step))
        return carry

    lax.fori_loop(0, rows // step, run, 0, unroll=2)


def fold(values):
    return jnp.sum(values.reshape(-1, 8, values.shape[1]), axis=0)


def norm_backward(grad_out, values, gain):
    unit, inverse = norm_parts(values)
    scaled = grad_out * gain
    mean_one = jnp.mean(scaled, axis=-1, keepdims=True)
    mean_two = jnp.mean(scaled * unit, axis=-1, keepdims=True)
    return inverse * (scaled - mean_one - unit * mean_two), grad_out * unit


def gelu_both(inputs):
    square = inputs * inputs
    tanh = jnp.tanh(inputs * (GELU + (0.044715 * GELU) * square))
    half = 0.5 + 0.5 * tanh
    act = inputs * half
    return act, half + act * ((1.0 - tanh) * (GELU + (3 * 0.044715 * GELU) * square))


def mask_keys(scores, tokens):
    rows = scores.shape[0]
    whole = IMG_TOK // 8 * 8
    position = whole + lax.broadcasted_iota(jnp.int32, (rows - whole, 1), 0)
    return jnp.concatenate(
        [scores[:whole], jnp.where(position < tokens, scores[whole:], MASKED / SCORE)], axis=0
    )


def whole(shape):
    return pl.BlockSpec(shape, lambda i, s: (0,) * len(shape), pipeline_mode=pl.Buffered(1))


def held(shape):
    return pl.BlockSpec(shape, lambda i, s: (0,) * len(shape))


def stepped(shape):
    return pl.BlockSpec((1,) + shape, lambda i, s: (i,) + (0,) * len(shape))


def low_of(*shape):
    return jax.ShapeDtypeStruct(shape, LOW)


def f32_of(*shape):
    return jax.ShapeDtypeStruct(shape, F32)


def call(kernel, where, steps, ins, outs, scratch, flops=0, bytes_accessed=0, transcendentals=0, aliases=None,
         after=()):
    given = 1 + len(ins)
    ins = ins + [(pl.BlockSpec(memory_space=pl.ANY), array) for array in after]

    def run(*refs):
        kernel(*refs[:given], *refs[given + len(after) :])

    return pl.pallas_call(
        run,
        name=getattr(kernel, "func", kernel).__name__.removesuffix("_kernel"),
        grid_spec=pltpu.PrefetchScalarGridSpec(
            num_scalar_prefetch=1,
            grid=(steps,),
            in_specs=[spec for spec, _ in ins],
            out_specs=[spec for spec, _ in outs],
            scratch_shapes=scratch,
        ),
        out_shape=[shape for _, shape in outs],
        input_output_aliases=aliases or {},
        compiler_params=pltpu.CompilerParams(vmem_limit_bytes=VMEM),
        cost_estimate=pl.CostEstimate(
            flops=int(COST[getattr(kernel, "func", kernel).__name__] * SCALE), bytes_accessed=1, transcendentals=0
        ),
    )(where, *[array for _, array in ins])


def pack_kernel(units, where, qkv_ref, out_ref, up_ref, down_ref, own_attn, other_attn, own_mlp, other_mlp):
    qkv, out = qkv_ref[0].astype(LOW), out_ref[0].astype(LOW)
    up, down = up_ref[0].astype(LOW), down_ref[0].astype(LOW)

    def half(values, number):
        size = values.shape[1] // 2
        return values[:, number * size : (number + 1) * size]

    for number in range(2):
        up_h, down_h = half(up, number), half(down, number)
        attn = [half(qkv, number), half(out, number), up_h[:, units:], down_h[:, units:]]
        used = sum(piece.shape[1] for piece in attn)
        attn.append(jnp.zeros((qkv.shape[0], own_attn.shape[1] - used), LOW))
        attn = jnp.concatenate(attn, axis=1)
        mlp = jnp.concatenate([up_h[:, :units], down_h[:, :units]], axis=1)

        @pl.when(where[3] == number)
        def _():
            own_attn[...] = attn
            own_mlp[...] = mlp

        @pl.when(where[3] != number)
        def _():
            other_attn[...] = attn
            other_mlp[...] = mlp


def attn_forward_kernel(spread, joined, tail_units, where, *refs):
    refs = list(refs)
    count = len(spread.weight_keys)
    if joined:
        base_ref, own_ref, other_ref, old_ref = refs[:4]
        del refs[:4]
    else:
        own_ref, other_ref = refs[:2]
        del refs[:2]
    vec_ref, bias_ref = refs[:2]
    w_refs = refs[2 : 2 + count]
    (stream_ref, normed_ref, qkv_ref, mixed_ref, sums_ref, tail_ref, part_ref, total, held_weight) = refs[
        2 + count :
    ]
    step = pl.program_id(0)

    @pl.when(step == 0)
    def _():
        if not joined:
            half = own_ref.shape[0]
            stream_ref[pl.ds(pl.multiple_of(where[3] * half, 8), half), :] = own_ref[...]
            stream_ref[pl.ds(pl.multiple_of((1 - where[3]) * half, 8), half), :] = other_ref[...]

        def normalize(at):
            if joined:
                branch = own_ref[at, :].astype(F32) + other_ref[at, :].astype(F32)
                stream = base_ref[at, :] + branch + old_ref[0, 7:8, :]
                stream_ref[at, :] = stream
            else:
                stream = stream_ref[at, :]
            unit, _ = norm_parts(stream)
            normed_ref[at, :] = (unit * vec_ref[0, 0:1, :] + vec_ref[0, 1:2, :]).astype(LOW)

        over_rows(stream_ref.shape[0], 16, normalize)

    weight = spread.load(w_refs, where, held_weight)
    tokens = where[4]
    head_columns = 3 * HD
    local = qkv_ref.shape[2]
    heads = local // head_columns
    bias = []
    for head in range(heads):
        at = head * HD
        query_bias, value_bias = bias_ref[0, 0, 0, :, at : at + HD], bias_ref[0, 1, 0, :, at : at + HD]
        bias += [query_bias, jnp.zeros_like(query_bias), value_bias]
    bias = jnp.concatenate(bias, axis=1)
    qkv = (cdot(normed_ref[...], weight[:, :local]) + bias).astype(LOW)
    qkv_ref[0] = qkv
    mixed = []
    for head in range(heads):
        at = head * head_columns
        query = qkv[:, at : at + HD]
        key = qkv[:, at + HD : at + 2 * HD]
        value = qkv[:, at + 2 * HD : at + 3 * HD]
        scores = mask_keys(cdot(key, query, 1, 1), tokens)
        top = jnp.max(scores, axis=0, keepdims=True)
        raised = jnp.exp2((scores - top) * POWER)
        weight_sum = jnp.sum(raised, axis=0, keepdims=True)
        mixed.append(cdot(value, raised.astype(LOW), 0, 0) * (1.0 / weight_sum))
        sums_ref[0, head : head + 1, :] = top * POWER + jnp.log2(weight_sum)
    mixed = jnp.concatenate(mixed, axis=0).T.astype(LOW)
    mixed_ref[0] = mixed
    at = local + mixed.shape[1]
    part = cdot(mixed, weight[:, local:at], 1, 1)

    @pl.when(step == 0)
    def _():
        total[...] = part

    @pl.when(step > 0)
    def _():
        total[...] += part

    tail_ref[0] = weight[:, at : at + 2 * tail_units]

    @pl.when(step == pl.num_programs(0) - 1)
    def _():
        part_ref[...] = total[...].astype(LOW)


def mlp_forward_kernel(spread, where, *refs):
    count = len(spread.weight_keys)
    base_ref, own_ref, other_ref, vec_ref, bias_ref, tail_ref, tail_bias_ref = refs[:7]
    w_refs = refs[7 : 7 + count]
    (middle_ref, normed_ref, act_ref, slope_ref, act_tail_ref, slope_tail_ref, up_tail_ref, down_tail_ref,
     part_ref, total, held_weight) = refs[7 + count :]
    step = pl.program_id(0)

    @pl.when(step == 0)
    def _():
        def normalize(at):
            branch = own_ref[at, :].astype(F32) + other_ref[at, :].astype(F32)
            middle = base_ref[at, :] + branch + vec_ref[0, 4:5, :]
            middle_ref[at, :] = middle
            unit, _ = norm_parts(middle)
            normed_ref[at, :] = (unit * vec_ref[0, 5:6, :] + vec_ref[0, 6:7, :]).astype(LOW)

        over_rows(middle_ref.shape[0], 16, normalize)
        steps, _, both = tail_ref.shape
        half = both // 2
        up_tail_ref[...] = jnp.concatenate([tail_ref[t, :, :half] for t in range(steps)], axis=1)
        down_tail_ref[...] = jnp.concatenate([tail_ref[t, :, half:] for t in range(steps)], axis=1)
        act, slope = gelu_both(cdot(normed_ref[...], up_tail_ref[...]) + tail_bias_ref[0, 0])
        act = act.astype(LOW)
        act_tail_ref[...] = act
        slope_tail_ref[...] = slope.astype(LOW)
        total[...] = cdot(act, down_tail_ref[...], 1, 1)

    weight = spread.load(w_refs, where, held_weight)
    units = act_ref.shape[2]
    act, slope = gelu_both(cdot(normed_ref[...], weight[:, :units]) + bias_ref[0, 0, 0])
    act = act.astype(LOW)
    act_ref[0] = act
    slope_ref[0] = slope.astype(LOW)
    total[...] += cdot(act, weight[:, units:], 1, 1)

    @pl.when(step == pl.num_programs(0) - 1)
    def _():
        part_ref[...] = total[...].astype(LOW)


def mlp_backward_kernel(spread, where, *refs):
    count = len(spread.weight_keys)
    grad_ref, slope_ref, up_tail_ref, down_tail_ref, slope_tail_ref = refs[:5]
    w_refs = refs[5 : 5 + count]
    hidden_ref, hidden_tail_ref, sums_ref, sums_tail_ref, part_ref, low, total, held_weight = refs[5 + count :]
    step = pl.program_id(0)

    @pl.when(step == 0)
    def _():
        low[...] = grad_ref[...].astype(LOW)
        hidden = cdot(low[...], down_tail_ref[...]) * slope_tail_ref[...].astype(F32)
        sums_tail_ref[...] = jnp.sum(hidden, axis=0, keepdims=True)
        hidden = hidden.astype(LOW)
        hidden_tail_ref[...] = hidden
        total[...] = cdot(hidden, up_tail_ref[...], 1, 1)

    weight = spread.load(w_refs, where, held_weight)
    units = hidden_ref.shape[2]
    hidden = cdot(low[...], weight[:, units:]) * slope_ref[0].astype(F32)
    sums_ref[0] = jnp.sum(hidden, axis=0, keepdims=True)
    hidden = hidden.astype(LOW)
    hidden_ref[0] = hidden
    total[...] += cdot(hidden, weight[:, :units], 1, 1)

    @pl.when(step == pl.num_programs(0) - 1)
    def _():
        part_ref[...] = total[...].astype(LOW)


def mlp_grads_kernel(spread, where, *refs):
    count = len(spread.grad_keys)
    grad_ref, normed_ref, hidden_ref, act_ref, hidden_tail_ref, act_tail_ref = refs[:6]
    out_refs = refs[6 : 6 + count]
    tail_ref, grad_turned, normed_turned, result = refs[6 + count :]
    step = pl.program_id(0)

    @pl.when(step == 0)
    def _():
        grad_turned[...] = grad_ref[...].astype(LOW).T
        normed_turned[...] = normed_ref[...].T
        up_tail = cdot(normed_turned[...], hidden_tail_ref[...]).astype(LOW)
        down_tail = cdot(grad_turned[...], act_tail_ref[...]).astype(LOW)
        steps, _, both = tail_ref.shape
        half = both // 2
        for t in range(steps):
            at = slice(t * half, (t + 1) * half)
            tail_ref[t] = jnp.concatenate([up_tail[:, at], down_tail[:, at]], axis=1)

    units = hidden_ref.shape[2]
    result[:, :units] = cdot(normed_turned[...], hidden_ref[0]).astype(LOW)
    result[:, units:] = cdot(grad_turned[...], act_ref[0]).astype(LOW)
    spread.store(out_refs, where, result)


def attn_backward_kernel(spread, where, *refs):
    count = len(spread.weight_keys)
    grad_ref, own_ref, other_ref, middle_ref, vec_ref, qkv_ref, sums_ref = refs[:7]
    w_refs = refs[7 : 7 + count]
    dmiddle_ref, norm_sums_ref, dqkv_ref, head_sums_ref, part_ref, low, total, held_weight, folds = refs[7 + count :]
    step = pl.program_id(0)

    @pl.when(step == 0)
    def _():
        folds[...] = jnp.zeros_like(folds)

        def backward(at):
            grad = grad_ref[at, :]
            dnormed = own_ref[at, :].astype(F32) + other_ref[at, :].astype(F32)
            inner, gain_terms = norm_backward(dnormed, middle_ref[at, :], vec_ref[0, 5:6, :])
            dmiddle = grad + inner
            dmiddle_ref[at, :] = dmiddle
            low[at, :] = dmiddle.astype(LOW)
            for number, terms in enumerate((gain_terms, dnormed, grad, dmiddle)):
                folds[number] += fold(terms)

        over_rows(dmiddle_ref.shape[0], 16, backward)
        for number in range(4):
            norm_sums_ref[number : number + 1, :] = jnp.sum(folds[number], axis=0, keepdims=True)

    weight = spread.load(w_refs, where, held_weight)
    tokens = where[4]
    head_columns = 3 * HD
    local = qkv_ref.shape[2]
    heads = local // head_columns
    qkv = qkv_ref[0]
    dmixed = cdot(low[...], weight[:, local : local + heads * HD]).astype(LOW)
    pieces = []
    for head in range(heads):
        at = head * head_columns
        query = qkv[:, at : at + HD]
        key = qkv[:, at + HD : at + 2 * HD]
        value = qkv[:, at + 2 * HD : at + 3 * HD]
        grad = dmixed[:, head * HD : (head + 1) * HD]
        scores = mask_keys(cdot(key, query, 1, 1), tokens)
        probs = jnp.exp2(scores * POWER - sums_ref[0, head : head + 1, :])
        dprobs = cdot(value, grad, 1, 1)
        row_dot = jnp.sum(dprobs * probs, axis=0, keepdims=True)
        dscores = (probs * (dprobs - row_dot)).astype(LOW)
        pieces.append(cdot(key, dscores, 0, 0).T * SCORE)
        pieces.append(cdot(dscores, query) * SCORE)
        pieces.append(cdot(probs.astype(LOW), grad))
    dqkv = jnp.concatenate(pieces, axis=1)
    head_sums_ref[0] = jnp.sum(dqkv, axis=0, keepdims=True)
    dqkv = dqkv.astype(LOW)
    dqkv_ref[0] = dqkv
    part = cdot(dqkv, weight[:, :local], 1, 1)

    @pl.when(step == 0)
    def _():
        total[...] = part

    @pl.when(step > 0)
    def _():
        total[...] += part

    @pl.when(step == pl.num_programs(0) - 1)
    def _():
        part_ref[...] = total[...].astype(LOW)


def attn_grads_kernel(spread, where, *refs):
    count = len(spread.grad_keys)
    dmiddle_ref, normed_ref, dqkv_ref, mixed_ref, tail_ref = refs[:5]
    out_refs = refs[5 : 5 + count]
    grad_turned, normed_turned, result = refs[5 + count :]

    @pl.when(pl.program_id(0) == 0)
    def _():
        grad_turned[...] = dmiddle_ref[...].astype(LOW).T
        normed_turned[...] = normed_ref[...].T

    parts = [
        cdot(normed_turned[...], dqkv_ref[0]).astype(LOW),
        cdot(grad_turned[...], mixed_ref[0]).astype(LOW),
        tail_ref[0],
    ]
    used = sum(part.shape[1] for part in parts)
    parts.append(jnp.zeros((result.shape[0], result.shape[1] - used), LOW))
    result[...] = jnp.concatenate(parts, axis=1)
    spread.store(out_refs, where, result)


def norm_backward_kernel(where, dmiddle_ref, own_ref, other_ref, stream_ref, vec_ref, out_ref, sums_ref, folds):
    step = pl.program_id(0)

    @pl.when(step == 0)
    def _():
        folds[...] = jnp.zeros_like(folds)

    def backward(at):
        dnormed = own_ref[at, :].astype(F32) + other_ref[at, :].astype(F32)
        inner, gain_terms = norm_backward(dnormed, stream_ref[at, :], vec_ref[0, 0:1, :])
        out_ref[at, :] = dmiddle_ref[at, :] + inner
        folds[0] += fold(gain_terms)
        folds[1] += fold(dnormed)

    over_rows(out_ref.shape[0], 16, backward)

    @pl.when(step == pl.num_programs(0) - 1)
    def _():
        for number in range(2):
            sums_ref[number : number + 1, :] = jnp.sum(folds[number], axis=0, keepdims=True)


def adam_kernel(units, local, out_local, tail_units, where, *refs):
    attn_own, attn_other, mlp_own, mlp_other = refs[:4]
    states = [refs[4 + 3 * k : 7 + 3 * k] for k in range(4)]
    outs = refs[len(refs) - 16 :]

    def pair(own, other):
        own, other = own[...].astype(F32), other[...].astype(F32)
        low_core = where[3] == 0
        return jnp.where(low_core, own, other), jnp.where(low_core, other, own)

    attn = pair(attn_own, attn_other)
    mlp = pair(mlp_own, mlp_other)
    at = local + out_local
    grads = [
        jnp.concatenate([half[:, :local] for half in attn], axis=1),
        jnp.concatenate([half[:, local:at] for half in attn], axis=1),
        jnp.concatenate(
            [piece for m, n in zip(mlp, attn) for piece in (m[:, :units], n[:, at : at + tail_units])], axis=1
        ),
        jnp.concatenate(
            [
                piece
                for m, n in zip(mlp, attn)
                for piece in (m[:, units:], n[:, at + tail_units : at + 2 * tail_units])
            ],
            axis=1,
        ),
    ]
    for number, grad in enumerate(grads):
        weight, first, second = [ref[0] for ref in states[number]]
        new = adam_step(weight, grad, first, second, RATES[number], DECAY)
        for ref, values in zip(outs[4 * number : 4 * number + 4], (grad, new[1], new[2], new[0])):
            ref[0] = values


def vec_pack_kernel(where, *refs):
    out_ref = refs[-1]
    layers = out_ref.shape[0]
    out_ref[...] = jnp.zeros_like(out_ref)
    for layer in range(layers):
        one_ref, two_ref, head_ref, main_ref, tail_ref = refs[5 * layer : 5 * layer + 5]
        out_ref[layer, 0:2, :] = one_ref[0:2, :]
        out_ref[layer, 2:6, :] = two_ref[0:4, :]
        for t in range(head_ref.shape[0]):
            out_ref[layer, 8 + t : 9 + t, : head_ref.shape[2]] = head_ref[t]
            out_ref[layer, 16 + t : 17 + t, : main_ref.shape[2]] = main_ref[t]
        out_ref[layer, 6:7, : tail_ref.shape[1]] = tail_ref[...]


def vec_kernel(steps, local, units, tail_units, where, own_ref, other_ref, vec_ref, first_ref, second_ref,
               grad_out, first_out, second_out, weight_out):
    low_core = where[3] == 0
    for layer in range(vec_ref.shape[0]):
        own, other = own_ref[layer], other_ref[layer]
        cores = jnp.where(low_core, own, other), jnp.where(low_core, other, own)
        norms = cores[0][0:6]
        heads = local // (3 * HD)

        def head_piece(kind):
            return [
                core[8 + t : 9 + t, (3 * head + kind) * HD : (3 * head + kind + 1) * HD]
                for t in range(steps)
                for core in cores
                for head in range(heads)
            ]

        hidden = [
            piece
            for t in range(steps)
            for core in cores
            for piece in (core[16 + t : 17 + t, :units], core[6:7, t * tail_units : (t + 1) * tail_units])
        ]
        grad = jnp.concatenate(
            [norms[0:1], norms[1:2], *head_piece(0), *head_piece(2),
             norms[5:6], norms[2:3], norms[3:4], norms[4:5], *hidden],
            axis=1,
        )
        at = slice(layer, layer + 1)
        new = adam_step(vec_ref[at, :], grad, first_ref[at, :], second_ref[at, :], RATES[4], 0.0)
        grad_out[at, :] = grad
        first_out[at, :] = new[1]
        second_out[at, :] = new[2]
        weight_out[at, :] = new[0]


def plane_sides(chips):
    side = math.isqrt(chips)
    while chips % side:
        side -= 1
    return side, chips // side


class Place:
    def __init__(self):
        self.nf = lax.axis_size("fsdp")
        self.nt = lax.axis_size("tp")
        self.na, self.nb = plane_sides(self.nf // 2)
        fi = lax.axis_index("fsdp")
        self.core = fi % 2
        self.a = (fi // 2) // self.nb
        self.b = (fi // 2) % self.nb
        self.t = lax.axis_index("tp")
        self.size = {"a": self.na, "b": self.nb, "t": self.nt}
        self.at = {"a": self.a, "b": self.b, "t": self.t}

    def pairs(self, axis, move):
        if axis == "t":
            return [(i, move(i)) for i in range(self.nt)]
        found = []
        for f in range(self.nf):
            place = {"a": f // 2 // self.nb, "b": f // 2 % self.nb, "core": f % 2}
            place[axis] = move(place[axis])
            found.append((f, (place["a"] * self.nb + place["b"]) * 2 + place["core"]))
        return found

    def send(self, values, axis, move):
        return lax.ppermute(values, "tp" if axis == "t" else "fsdp", self.pairs(axis, move))

    def sibling(self, values):
        return self.send(values, "core", lambda i: 1 - i)

    def swap_rows(self, values):
        pairs = []
        for f in range(self.nf):
            for t in range(self.nt):
                if f % 2 != t % 2:
                    sign = 1 if t % 2 else -1
                    pairs.append((f * self.nt + t, (f + sign) * self.nt + t - sign))
        arrived = lax.ppermute(values.astype(LOW), ("fsdp", "tp"), pairs).astype(F32)
        return jnp.where(self.core != self.t % 2, arrived, values)

    def gather_axis(self, block, axis):
        n = self.size[axis]
        return [block] + [self.send(block, axis, lambda i, k=k: (i - k) % n) for k in range(1, n)]

    def scatter_axis(self, parts, axis):
        n = self.size[axis]
        sent = [self.send(parts[k], axis, lambda i, k=k: (i + k) % n) for k in range(1, n)]
        return [parts[0], *sent]


def split_pair(place, first, second):
    return (
        jnp.where(place.core == 0, first, second),
        jnp.where(place.core == 0, second, first),
    )


def sum_kernel(outputs, where, *refs):
    count = sum(size for sizes in outputs for size in sizes)
    ins, outs = refs[:count], refs[count:]
    for out_ref, sizes in zip(outs, outputs):
        for number, size in enumerate(sizes):
            total = ins[0][0, 0].astype(F32)
            for ref in ins[1:size]:
                total += ref[0, 0].astype(F32)
            ins = ins[size:]
            out_ref[0, number] = total.astype(LOW)


def tie_kernel(where, *refs):
    pass


def tie(where, arrays, after):
    space = pl.BlockSpec(memory_space=pl.ANY)
    return call(
        tie_kernel,
        where,
        1,
        [(space, x) for x in arrays],
        [(space, jax.ShapeDtypeStruct(x.shape, x.dtype)) for x in arrays],
        [],
        aliases={1 + k: k for k in range(len(arrays))},
        after=after,
    )


class Spread:
    def __init__(self, place, rows, columns, middle):
        self.place, self.rows, self.columns = place, rows, columns
        self.middle = middle
        self.direct = rows % 16 == 0
        self.width = place.na * place.nb * 2 * rows
        na, nb = place.na, place.nb
        self.grad_keys = [[(0, a, b) for b in range(nb)] for a in range(na)]
        self.grad_keys += [[(1, a, b) for a in range(na)] for b in range(nb)]
        self.gather_keys = [[(0, 0, 0), (1, 0, 0)]]
        self.gather_keys += [[(0, 0, b), (1, 0, b)] for b in range(1, nb)]
        self.gather_keys += [[(0, a, 0), (1, a, 0)] for a in range(1, na)]
        self.gather_keys += [[(half, a, b)] for half in range(2) for a in range(1, na) for b in range(1, nb)]
        if middle:
            self.gather_keys = self.grad_keys
        self.weight_keys = self.gather_keys
        if not self.direct:
            self.weight_keys = self.grad_keys = [None]

    def shapes(self, keys):
        if not self.direct:
            return [(self.place.nt, self.width, self.columns)]
        return [(self.place.nt, len(blocks), self.rows, self.columns) for blocks in keys]

    def specs(self, keys):
        return [stepped(shape[1:]) for shape in self.shapes(keys)]

    def first_row(self, where, key):
        half, a, b = key
        a = lax.rem(where[0] + a, self.place.na)
        b = lax.rem(where[1] + b, self.place.nb)
        return pl.multiple_of(((a * self.place.nb + b) * 2 + half) * self.rows, 16)

    def load(self, refs, where, scratch):
        if not self.direct:
            return refs[0].at[0]
        for ref, blocks in zip(refs, self.weight_keys):
            for number, key in enumerate(blocks):
                scratch[pl.ds(self.first_row(where, key), self.rows), :] = ref[0, number]
        return scratch

    def store(self, refs, where, scratch):
        if not self.direct:
            refs[0][0] = scratch[...]
            return
        for ref, blocks in zip(refs, self.grad_keys):
            for number, key in enumerate(blocks):
                ref[0, number] = scratch[pl.ds(self.first_row(where, key), self.rows), :]

    def start(self, own, other):
        place = self.place
        halves = split_pair(place, own, other)
        if self.middle:
            return [jnp.stack(place.gather_axis(half, axis)) for half, axis in zip(halves, "ba")]
        return [jnp.stack(halves)]

    def gather(self, where, blocks, after=()):
        place = self.place
        na, nb = place.na, place.nb
        blocks = [lax.all_gather(block, "tp") for block in blocks]
        if self.direct and len(after):
            blocks = tie(where, blocks, after)
        if self.middle:
            arrays = [array for block, axis in zip(blocks, "ab") for array in place.gather_axis(block, axis)]
        else:
            along_b = place.gather_axis(blocks[0], "b")
            along_a = place.gather_axis(blocks[0], "a")
            first = [place.gather_axis(x[:, :1], "a")[1:] for x in along_b[1:]]
            second = [place.gather_axis(x[:, 1:], "b")[1:] for x in along_a[1:]]
            arrays = along_b + along_a[1:]
            arrays += [first[b][a] for a in range(na - 1) for b in range(nb - 1)]
            arrays += [second[a][b] for a in range(na - 1) for b in range(nb - 1)]
        if self.direct:
            return arrays
        found = {
            key: array[:, number]
            for array, keys in zip(arrays, self.gather_keys)
            for number, key in enumerate(keys)
        }
        full = jnp.stack([found[half, a, b] for a in range(na) for b in range(nb) for half in range(2)], axis=1)
        full = full.reshape(place.nt, na, nb, 2, self.rows, self.columns)
        full = self.roll(full, (na - place.a) % na, (nb - place.b) % nb)
        return [full.reshape(place.nt, self.width, self.columns)]

    def roll(self, full, a, b):
        full = lax.dynamic_slice_in_dim(jnp.concatenate([full, full], axis=1), a, self.place.na, 1)
        return lax.dynamic_slice_in_dim(jnp.concatenate([full, full], axis=2), b, self.place.nb, 2)

    def sums(self, where, outputs, after):
        place, rows, columns = self.place, self.rows, self.columns

        def block(number):
            return pl.BlockSpec((1, 1, rows, columns), lambda i, s: (i, number, 0, 0))

        shapes = [(place.nt, len(groups), rows, columns) for groups in outputs]
        return call(
            functools.partial(sum_kernel, [[len(group) for group in groups] for groups in outputs]),
            where,
            place.nt,
            [(block(number), x) for groups in outputs for group in groups for x, number in group],
            [(stepped(shape[1:]), low_of(*shape)) for shape in shapes],
            [],
            after=after,
        )

    def scatter_last(self, arrays):
        place = self.place
        if not self.direct:
            full = arrays[0].reshape(place.nt, place.na, place.nb, 2, self.rows, self.columns)
            full = self.roll(full, place.a, place.b)
            arrays = [full[:, a, :, 0] for a in range(place.na)] + [full[:, :, b, 1] for b in range(place.nb)]
        return (
            place.scatter_axis(arrays[: place.na], "a"),
            place.scatter_axis(arrays[place.na :], "b"),
        )

    def scatter_first(self, where, halves, after):
        place = self.place
        if self.middle:
            outputs = [[[(x, k) for x in half] for k in range(half[0].shape[1])] for half in halves]
            results = self.sums(where, outputs, after)
            return results[0], [lax.psum_scatter(x, "tp", scatter_dimension=0, tiled=True)[0] for x in results]
        axes = ("b", "a")
        keys = [(half, k) for half in range(2) for k in range(1, place.size[axes[half]])]
        results = self.sums(where, [[[(x, k) for x in halves[half]]] for half, k in keys], after)
        terms = [[(x, 0) for x in arrays] for arrays in halves]
        for (half, k), total in zip(keys, results):
            n = place.size[axes[half]]
            terms[half].append((place.send(total, axes[half], lambda i: (i + k) % n), 0))
        return results[0], terms

    def scatter_tp(self, where, terms, after):
        place = self.place
        if self.middle:
            done = [
                sum(x.astype(F32) for x in place.scatter_axis(list(half), axis)).astype(LOW)
                for half, axis in zip(terms, "ba")
            ]
            last = after[0]
        else:
            (last,) = self.sums(where, [terms], after)
            done = lax.psum_scatter(last, "tp", scatter_dimension=0, tiled=True)[0]
        mine, other = split_pair(place, done[0], done[1])
        return last, (mine, place.sibling(other))


def body(
    residual_in,
    cotangent,
    slot_tokens,
    qkv_weight,
    out_weight,
    up_weight,
    down_weight,
    vectors,
    qkv_first,
    qkv_second,
    out_first,
    out_second,
    up_first,
    up_second,
    down_first,
    down_second,
    vec_first,
    vec_second,
):
    place = Place()
    layer_count, shard_rows, _ = qkv_weight.shape
    half_rows, width = residual_in.shape
    rows = 2 * half_rows
    nt = place.nt
    local = qkv_weight.shape[2] // 2
    out_local = out_weight.shape[1] // 2
    hidden_local = up_weight.shape[2] // 2
    units = hidden_local // 128 * 128
    tail_units = hidden_local - units
    heads = out_local // HD
    attn_columns = -(-(local + out_local + 2 * tail_units) // 128) * 128
    mlp_columns = 2 * units

    tokens_pair = jnp.concatenate(split_pair(place, slot_tokens, place.sibling(slot_tokens)))
    slot_at = (place.t % 2) * slot_tokens.shape[0] + place.t // 2
    tokens = lax.dynamic_slice_in_dim(tokens_pair, slot_at, 1)
    row_mask = (jnp.arange(rows, dtype=jnp.int32) < tokens[0]).astype(F32)[:, None]
    here = jnp.stack([place.a, place.b, place.t, place.core]).astype(jnp.int32)
    where = jnp.concatenate([here, tokens.astype(jnp.int32)])

    def own_rows(values):
        return lax.dynamic_slice_in_dim(values, place.core * half_rows, half_rows)

    spreads = [
        (
            Spread(place, shard_rows, attn_columns, False),
            Spread(place, shard_rows, mlp_columns, layer > 0),
        )
        for layer in range(layer_count)
    ]

    def turn(arrays):
        qkv, out, up, down = arrays
        return qkv, jnp.swapaxes(out, 1, 2), up, jnp.swapaxes(down, 1, 2)

    weights = turn((qkv_weight, out_weight, up_weight, down_weight))
    firsts = turn((qkv_first, out_first, up_first, down_first))
    seconds = turn((qkv_second, out_second, up_second, down_second))

    def layer_block(array, layer, steps=1):
        block = (1, array.shape[1] // steps, array.shape[2])
        return pl.BlockSpec(block, lambda i, s: (layer, i, 0))

    def pack(layer):
        attn, mlp = (shard_rows, attn_columns), (shard_rows, mlp_columns)
        return call(
            functools.partial(pack_kernel, units),
            here,
            1,
            [(layer_block(w, layer), w) for w in weights],
            [(held(shape), low_of(*shape)) for shape in (attn, attn, mlp, mlp)],
            [],
            bytes_accessed=6 * shard_rows * 13216 // 4,
        )

    starts = []
    for layer in range(layer_count):
        own_attn, other_attn, own_mlp, other_mlp = pack(layer)
        starts.append(
            (
                spreads[layer][0].start(own_attn, place.sibling(other_attn)),
                spreads[layer][1].start(own_mlp, place.sibling(other_mlp)),
            )
        )
    gathered = []
    before = [x for pair in starts[1:] for blocks in pair for x in blocks]
    for layer in range(layer_count):
        attn_full = spreads[layer][0].gather(where, starts[layer][0], before)
        mlp_full = spreads[layer][1].gather(where, starts[layer][1], attn_full[1:3])
        before = mlp_full[1:3]
        gathered.append((attn_full, mlp_full))

    wide = vectors[:, : 8 * width].reshape(layer_count, 8, width)
    head_bias = vectors[:, 2 * width : 4 * width].reshape(layer_count, 2, 2 * nt, 1, out_local)
    hidden_bias = vectors[:, 8 * width :].reshape(layer_count, nt, 2, 1, hidden_local)
    main_bias = hidden_bias[..., :units]
    tail_bias = jnp.moveaxis(hidden_bias[..., units:], 1, 3).reshape(layer_count, 2, 1, nt * tail_units)

    full = whole((rows, width))
    weight_scratch = [
        pltpu.VMEM((width, attn_columns), LOW),
        pltpu.VMEM((width, mlp_columns), LOW),
    ]
    flat = pltpu.VMEM((rows, width), F32)
    flat_low = pltpu.VMEM((rows, width), LOW)
    big = 2 * rows * width

    def wide_of(layer):
        spec = pl.BlockSpec((1, 8, width), lambda i, s: (layer, 0, 0), pipeline_mode=pl.Buffered(1))
        return spec, wide

    def attn_forward(layer, base, own, other):
        spread = spreads[layer][0]
        joined = base is not None
        if joined:
            ins = [(full, base), (full, own), (full, other), wide_of(layer - 1)]
        else:
            half = whole((half_rows, width))
            ins = [(half, own), (half, other)]
        ins.append(wide_of(layer))
        ins.append(
            (
                pl.BlockSpec(
                    (1, 2, 1, 1, out_local), lambda i, s: (layer, 0, 2 * i + s[3], 0, 0)
                ),
                head_bias,
            )
        )
        ins += list(zip(spread.specs(spread.weight_keys), gathered[layer][0]))
        return call(
            functools.partial(attn_forward_kernel, spread, joined, tail_units),
            where,
            nt,
            ins,
            [
                (held((rows, width)), f32_of(rows, width)),
                (held((rows, width)), low_of(rows, width)),
                (stepped((rows, local)), low_of(nt, rows, local)),
                (stepped((rows, out_local)), low_of(nt, rows, out_local)),
                (stepped((heads, rows)), f32_of(nt, heads, rows)),
                (stepped((width, 2 * tail_units)), low_of(nt, width, 2 * tail_units)),
                (held((rows, width)), low_of(rows, width)),
            ],
            [flat, weight_scratch[0]],
            big * nt * (local + out_local) + 4 * nt * heads * rows * rows * HD,
            rows * width * 12 + nt * width * attn_columns * 2,
            nt * heads * rows * rows,
        )

    def mlp_forward(layer, base, own, other, tails):
        spread = spreads[layer][1]
        tail = nt * tail_units
        tail_shape = (width, tail)
        ins = [
            (full, base),
            (full, own),
            (full, other),
            wide_of(layer),
            (pl.BlockSpec((1, 1, 1, 1, units), lambda i, s: (layer, i, s[3], 0, 0)), main_bias),
            (whole(tails.shape), tails),
            (pl.BlockSpec((1, 1, 1, tail), lambda i, s: (layer, s[3], 0, 0)), tail_bias),
        ]
        ins += list(zip(spread.specs(spread.weight_keys), gathered[layer][1]))
        return call(
            functools.partial(mlp_forward_kernel, spread),
            where,
            nt,
            ins,
            [
                (held((rows, width)), f32_of(rows, width)),
                (held((rows, width)), low_of(rows, width)),
                (stepped((rows, units)), low_of(nt, rows, units)),
                (stepped((rows, units)), low_of(nt, rows, units)),
                (held((rows, tail)), low_of(rows, tail)),
                (held((rows, tail)), low_of(rows, tail)),
                (held(tail_shape), low_of(*tail_shape)),
                (held(tail_shape), low_of(*tail_shape)),
                (held((rows, width)), low_of(rows, width)),
            ],
            [flat, weight_scratch[1]],
            2 * big * (nt * units + tail),
            rows * width * 16 + nt * (width + rows) * mlp_columns * 2,
            rows * nt * units,
        )

    def mlp_backward(layer, grad, slope, tails, slope_tail):
        spread = spreads[layer][1]
        tail = nt * tail_units
        ins = [(full, grad), (stepped((rows, units)), slope)]
        ins += [(whole(w.shape), w) for w in (*tails, slope_tail)]
        ins += list(zip(spread.specs(spread.weight_keys), gathered[layer][1]))
        return call(
            functools.partial(mlp_backward_kernel, spread),
            where,
            nt,
            ins,
            [
                (stepped((rows, units)), low_of(nt, rows, units)),
                (held((rows, tail)), low_of(rows, tail)),
                (stepped((1, units)), f32_of(nt, 1, units)),
                (held((1, tail)), f32_of(1, tail)),
                (held((rows, width)), low_of(rows, width)),
            ],
            [flat_low, flat, weight_scratch[1]],
            2 * big * (nt * units + tail),
            rows * width * 6 + nt * (width + rows) * mlp_columns * 2,
        )

    def mlp_grads(layer, grad, normed, hidden, act, hidden_tail, act_tail):
        spread = spreads[layer][1]
        ins = [(full, grad), (full, normed)]
        ins += [(stepped((rows, units)), hidden), (stepped((rows, units)), act)]
        ins += [(whole(x.shape), x) for x in (hidden_tail, act_tail)]
        tail_shape = (nt, width, 2 * tail_units)
        outs = [
            (spec, low_of(*shape))
            for spec, shape in zip(spread.specs(spread.grad_keys), spread.shapes(spread.grad_keys))
        ]
        outs.append((held(tail_shape), low_of(*tail_shape)))
        turned_low = pltpu.VMEM((width, rows), LOW)
        return call(
            functools.partial(mlp_grads_kernel, spread),
            where,
            nt,
            ins,
            outs,
            [turned_low, turned_low, weight_scratch[1]],
            2 * big * nt * (units + tail_units),
            rows * width * 6 + nt * (width + rows) * mlp_columns * 2,
        )

    def attn_backward(layer, grad, own, other, middle, qkv, log_sums, after=()):
        spread = spreads[layer][0]
        ins = [(full, grad), (full, own), (full, other), (full, middle), wide_of(layer)]
        ins += [(stepped((rows, local)), qkv), (stepped((heads, rows)), log_sums)]
        ins += list(zip(spread.specs(spread.weight_keys), gathered[layer][0]))
        return call(
            functools.partial(attn_backward_kernel, spread),
            where,
            nt,
            ins,
            [
                (held((rows, width)), f32_of(rows, width)),
                (held((8, width)), f32_of(8, width)),
                (stepped((rows, local)), low_of(nt, rows, local)),
                (stepped((1, local)), f32_of(nt, 1, local)),
                (held((rows, width)), low_of(rows, width)),
            ],
            [flat_low, flat, weight_scratch[0], pltpu.VMEM((4, 8, width), F32)],
            big * nt * (local + out_local) + 10 * nt * heads * rows * rows * HD,
            rows * width * 20 + nt * width * attn_columns * 2,
            nt * heads * rows * rows,
            after=after,
        )

    def attn_grads(layer, dmiddle, normed, dqkv, mixed, tail_grads):
        spread = spreads[layer][0]
        ins = [(full, dmiddle), (full, normed)]
        ins += [(stepped((rows, local)), dqkv), (stepped((rows, out_local)), mixed)]
        ins.append((stepped((width, 2 * tail_units)), tail_grads))
        outs = [
            (spec, low_of(*shape))
            for spec, shape in zip(spread.specs(spread.grad_keys), spread.shapes(spread.grad_keys))
        ]
        turned_low = pltpu.VMEM((width, rows), LOW)
        return call(
            functools.partial(attn_grads_kernel, spread),
            where,
            nt,
            ins,
            outs,
            [turned_low, turned_low, weight_scratch[0]],
            big * nt * (local + out_local),
            rows * width * 6 + nt * (width + rows) * attn_columns * 2,
        )

    def norm_one_backward(layer, dmiddle, own, other, stream, after=()):
        part = pl.BlockSpec((half_rows, width), lambda i, s: (i, 0))
        return call(
            norm_backward_kernel,
            where,
            2,
            [(part, dmiddle), (part, own), (part, other), (part, stream), wide_of(layer)],
            [(part, f32_of(rows, width)), (held((8, width)), f32_of(8, width))],
            [pltpu.VMEM((2, 8, width), F32)],
            rows * width * 20,
            rows * width * 16,
            after=after,
        )

    mine = place.swap_rows(residual_in)
    base, own, other = None, mine, place.sibling(mine)
    saved = []
    for layer in range(layer_count):
        stream, normed, qkv, mixed, log_sums, tails, part = attn_forward(layer, base, own, other)
        middle, normed_two, act, slope, act_tail, slope_tail, up_tail, down_tail, part = mlp_forward(
            layer, stream, part, place.sibling(part), tails
        )
        saved.append(
            (stream, normed, qkv, mixed, log_sums, middle, normed_two, act, slope, act_tail, slope_tail,
             (up_tail, down_tail))
        )
        base, own, other = middle, part, place.sibling(part)
    output = own_rows(base) + (own_rows(own).astype(F32) + own_rows(other).astype(F32))
    output = place.swap_rows((output + wide[layer_count - 1, 7:8]) * own_rows(row_mask))

    mine = place.swap_rows(cotangent)
    grad_stream = jnp.concatenate(split_pair(place, mine, place.sibling(mine)), axis=0) * row_mask


    def adam(layer, attn_pair, mlp_pair, before, after=()):
        steps = 3 if shard_rows % 48 == 0 else 1
        ins = [
            (pl.BlockSpec((shard_rows // steps, x.shape[1]), lambda i, s: (i, 0)), x)
            for x in (*attn_pair, *mlp_pair)
        ]
        for states in zip(weights, firsts, seconds):
            ins += [(layer_block(x, layer, steps), x) for x in states]
        outs = [
            (layer_block(weight, layer, steps), f32_of(*weight.shape)) for weight in weights for _ in range(4)
        ]
        aliases = None
        if before is not None:
            aliases = {1 + len(ins) + k: k for k in range(16)}
            ins += [(pl.BlockSpec(memory_space=pl.ANY), x) for x in before]
        return call(
            functools.partial(adam_kernel, units, local, out_local, tail_units),
            where,
            steps,
            ins,
            outs,
            [],
            bytes_accessed=28 * shard_rows * 13216 // 4,
            aliases=aliases,
            after=after,
        )

    vec_sums = [None] * layer_count
    last = grad_stream
    above = None
    for layer in reversed(range(layer_count)):
        (stream, normed, qkv, mixed, log_sums, middle, normed_two, act, slope, act_tail, slope_tail, tails) = (
            saved[layer]
        )
        spread_attn, spread_mlp = spreads[layer]
        hidden, hidden_tail, hidden_sums, tail_sums, part = mlp_backward(
            layer, grad_stream, slope, tails, slope_tail
        )
        other = place.sibling(part)
        *mlp_grad, tail_grads = mlp_grads(
            layer, grad_stream, normed_two, hidden, act, hidden_tail, act_tail
        )
        last = tail_grads
        mlp_terms = spread_mlp.scatter_last(mlp_grad)
        if above:
            last, attn_terms_above = spreads[above][0].scatter_first(where, attn_terms_above, [last])
        dmiddle, norm_two_sums, dqkv, head_sums, part = attn_backward(
            layer, grad_stream, part, other, middle, qkv, log_sums, [last]
        )
        other = place.sibling(part)
        attn_grad = attn_grads(layer, dmiddle, normed, dqkv, mixed, tail_grads)
        last = attn_grad[0]
        if above:
            last, mlp_pair_above = spreads[above][1].scatter_tp(where, mlp_terms_above, [last])
        grad_stream, norm_one_sums = norm_one_backward(layer, dmiddle, part, other, stream, [last])
        if layer:
            attn_terms = spread_attn.scatter_last(attn_grad)
        last, mlp_terms = spread_mlp.scatter_first(where, mlp_terms, [norm_one_sums])
        vec_sums[layer] = (norm_one_sums, norm_two_sums, head_sums, hidden_sums, tail_sums)
        if above:
            last, attn_pair_above = spreads[above][0].scatter_tp(where, attn_terms_above, [last])
            pairs_above = attn_pair_above, mlp_pair_above
        if not layer:
            if spread_attn.direct:
                attn_grad = tie(where, attn_grad, [last])
            attn_terms = spread_attn.scatter_last(attn_grad)
        above, mlp_terms_above, attn_terms_above = layer, mlp_terms, attn_terms
        if layer:
            grad_stream, last = lax.optimization_barrier((grad_stream, last))
    last, mlp_pair_above = spreads[above][1].scatter_tp(where, mlp_terms_above, [last])
    last, attn_terms_above = spreads[above][0].scatter_first(where, attn_terms_above, [last, *pairs_above[1]])
    updated = adam(1, *pairs_above, None, [last])
    last, attn_pair_above = spreads[above][0].scatter_tp(where, attn_terms_above, [last, updated[0]])
    grad_input = place.swap_rows(own_rows(grad_stream))

    flat_sums = [x for sums in vec_sums for x in sums]
    vec_shape = (layer_count, 24, width)
    (vec_total,) = call(
        vec_pack_kernel,
        where,
        1,
        [(whole(x.shape), x) for x in flat_sums],
        [(held(vec_shape), f32_of(*vec_shape))],
        [],
        after=[last],
    )
    for axis in ("b", "a", "t"):
        step = 1
        while step < place.size[axis]:
            vec_total = vec_total + place.send(vec_total, axis, lambda i: i ^ step)
            step *= 2
    vec_new = call(
        functools.partial(vec_kernel, nt, local, units, tail_units),
        where,
        1,
        [(whole(x.shape), x) for x in (vec_total, place.sibling(vec_total), vectors, vec_first, vec_second)],
        [(held(vectors.shape), f32_of(*vectors.shape)) for _ in range(4)],
        [],
    )
    updated = adam(above, attn_pair_above, mlp_pair_above, updated)
    updated = [
        jnp.swapaxes(x, 1, 2) if number // 4 % 2 else x for number, x in enumerate(updated)
    ]
    return (output, grad_input, *updated, *vec_new)


def solution(mesh):
    rows = P(("fsdp", "tp"), None)
    wide = P(None, "fsdp", "tp")
    tall = P(None, "tp", "fsdp")
    moments = (wide, wide, tall, tall, wide, wide, tall, tall, P(), P())
    return jax.shard_map(
        body,
        mesh=mesh,
        in_specs=(rows, rows, P("fsdp"), wide, tall, wide, tall, P(), *moments),
        out_specs=(rows, rows, *[wide] * 4, *[tall] * 4, *[wide] * 4, *[tall] * 4, *[P()] * 4),
        check_vma=False,
    )
```

```python
import functools
import math

import jax
import jax.numpy as jnp
from jax import lax
from jax.experimental import pallas as pl
from jax.experimental.pallas import tpu as pltpu
from jax.sharding import PartitionSpec as P

HD = 72
IMG_TOK = 729
STEP = 10


EPS_NORM = 1e-06
MASKED = -30000.0
BETA_ONE = 0.9
BETA_TWO = 0.999
ADAM_EPS = 1e-08
DECAY = 0.1
RATES = (0.05, 1.0, 0.05, 0.03, 0.3)
LOW = jnp.bfloat16
F32 = jnp.float32
GELU = math.sqrt(2.0 / math.pi)
SCORE = HD ** (-0.5)
POWER = SCORE / math.log(2.0)
VMEM = 56 * 1024 * 1024
COST = {
    "pack_kernel": 4,
    "attn_forward_kernel": 26,
    "mlp_forward_kernel": 24,
    "mlp_backward_kernel": 17,
    "mlp_grads_kernel": 16,
    "attn_backward_kernel": 33,
    "attn_grads_kernel": 13,
    "norm_backward_kernel": 9,
    "sum_kernel": 5,
    "vec_pack_kernel": 0.3,
    "vec_kernel": 0.3,
    "adam_kernel": 1,
    "tie_kernel": 1,
}
SCALE = 2e9


def adam_step(weight, gradient, first_moment, second_moment, step_rate, decay_rate):
    first_new = BETA_ONE * first_moment + (1.0 - BETA_ONE) * gradient
    second_new = BETA_TWO * second_moment + (1.0 - BETA_TWO) * gradient * gradient
    first_hat = first_new / (1.0 - BETA_ONE**STEP)
    second_hat = second_new / (1.0 - BETA_TWO**STEP)
    weight_new = weight - step_rate * (
        first_hat / (jnp.sqrt(second_hat) + ADAM_EPS) + decay_rate * weight
    )
    return (weight_new, first_new, second_new)


def cdot(left, right, left_dim=1, right_dim=0):
    return lax.dot_general(
        left, right, (((left_dim,), (right_dim,)), ((), ())), preferred_element_type=F32
    )


def norm_parts(values):
    centred = values - jnp.mean(values, axis=-1, keepdims=True)
    inverse = lax.rsqrt(jnp.mean(centred * centred, axis=-1, keepdims=True) + EPS_NORM)
    return centred * inverse, inverse


def norm_backward(grad_out, values, gain):
    unit, inverse = norm_parts(values)
    scaled = grad_out * gain
    mean_one = jnp.mean(scaled, axis=-1, keepdims=True)
    mean_two = jnp.mean(scaled * unit, axis=-1, keepdims=True)
    return inverse * (scaled - mean_one - unit * mean_two), grad_out * unit


def gelu_both(inputs):
    square = inputs * inputs
    tanh = jnp.tanh(inputs * (GELU + (0.044715 * GELU) * square))
    half = 0.5 + 0.5 * tanh
    act = inputs * half
    return act, half + act * ((1.0 - tanh) * (GELU + (3 * 0.044715 * GELU) * square))


def mask_keys(scores, tokens):
    rows = scores.shape[0]
    whole = IMG_TOK // 8 * 8
    position = whole + lax.broadcasted_iota(jnp.int32, (rows - whole, 1), 0)
    return jnp.concatenate(
        [scores[:whole], jnp.where(position < tokens, scores[whole:], MASKED / SCORE)], axis=0
    )


def whole(shape):
    return pl.BlockSpec(shape, lambda i, s: (0,) * len(shape), pipeline_mode=pl.Buffered(1))


def held(shape):
    return pl.BlockSpec(shape, lambda i, s: (0,) * len(shape))


def stepped(shape):
    return pl.BlockSpec((1,) + shape, lambda i, s: (i,) + (0,) * len(shape))


def low_of(*shape):
    return jax.ShapeDtypeStruct(shape, LOW)


def f32_of(*shape):
    return jax.ShapeDtypeStruct(shape, F32)


def call(kernel, where, steps, ins, outs, scratch, flops=0, bytes_accessed=0, transcendentals=0, aliases=None,
         after=()):
    given = 1 + len(ins)
    ins = ins + [(pl.BlockSpec(memory_space=pl.ANY), array) for array in after]

    def run(*refs):
        kernel(*refs[:given], *refs[given + len(after) :])

    return pl.pallas_call(
        run,
        name=getattr(kernel, "func", kernel).__name__.removesuffix("_kernel"),
        grid_spec=pltpu.PrefetchScalarGridSpec(
            num_scalar_prefetch=1,
            grid=(steps,),
            in_specs=[spec for spec, _ in ins],
            out_specs=[spec for spec, _ in outs],
            scratch_shapes=scratch,
        ),
        out_shape=[shape for _, shape in outs],
        input_output_aliases=aliases or {},
        compiler_params=pltpu.CompilerParams(vmem_limit_bytes=VMEM),
        cost_estimate=pl.CostEstimate(
            flops=int(COST[getattr(kernel, "func", kernel).__name__] * SCALE), bytes_accessed=1, transcendentals=0
        ),
    )(where, *[array for _, array in ins])


def turn_part(values, turned, step):
    size = values.shape[1] // 3
    at = pl.ds(pl.multiple_of(jnp.minimum(step, 2) * size, 128), size)
    turned[at, :] = values[:, at].T


def pack_kernel(units, where, qkv_ref, out_ref, up_ref, down_ref, own_attn, other_attn, own_mlp, other_mlp):
    qkv, out = qkv_ref[0].astype(LOW), out_ref[0].astype(LOW)
    up, down = up_ref[0].astype(LOW), down_ref[0].astype(LOW)

    def half(values, number):
        size = values.shape[1] // 2
        return values[:, number * size : (number + 1) * size]

    for number in range(2):
        up_h, down_h = half(up, number), half(down, number)
        attn = [half(qkv, number), half(out, number), up_h[:, units:], down_h[:, units:]]
        used = sum(piece.shape[1] for piece in attn)
        attn.append(jnp.zeros((qkv.shape[0], own_attn.shape[1] - used), LOW))
        attn = jnp.concatenate(attn, axis=1)
        mlp = jnp.concatenate([up_h[:, :units], down_h[:, :units]], axis=1)

        @pl.when(where[3] == number)
        def _():
            own_attn[...] = attn
            own_mlp[...] = mlp

        @pl.when(where[3] != number)
        def _():
            other_attn[...] = attn
            other_mlp[...] = mlp


def attn_forward_kernel(spread, joined, tail_units, where, *refs):
    refs = list(refs)
    count = len(spread.weight_keys)
    if joined:
        base_ref, own_ref, other_ref, old_ref = refs[:4]
        del refs[:4]
    else:
        own_ref, other_ref = refs[:2]
        del refs[:2]
    vec_ref, bias_ref = refs[:2]
    w_refs = refs[2 : 2 + count]
    (stream_ref, turned_ref, qkv_ref, mixed_ref, sums_ref, tail_ref, part_ref, total, held_weight, normed) = refs[
        2 + count :
    ]
    step = pl.program_id(0)

    @pl.when(step == 0)
    def _():
        if not joined:
            half = own_ref.shape[0]
            stream_ref[pl.ds(pl.multiple_of(where[3] * half, 8), half), :] = own_ref[...]
            stream_ref[pl.ds(pl.multiple_of((1 - where[3]) * half, 8), half), :] = other_ref[...]

        if joined:
            branch = own_ref[...].astype(F32) + other_ref[...].astype(F32)
            stream_ref[...] = base_ref[...] + branch + old_ref[0, 7:8, :]
        unit, _ = norm_parts(stream_ref[...])
        normed[...] = (unit * vec_ref[0, 0:1, :] + vec_ref[0, 1:2, :]).astype(LOW)

    weight = spread.load(w_refs, where, held_weight)
    tokens = where[4]
    head_columns = 3 * HD
    local = qkv_ref.shape[2]
    heads = local // head_columns
    bias = []
    for head in range(heads):
        at = head * HD
        query_bias, value_bias = bias_ref[0, 0, 0, :, at : at + HD], bias_ref[0, 1, 0, :, at : at + HD]
        bias += [query_bias, jnp.zeros_like(query_bias), value_bias]
    bias = jnp.concatenate(bias, axis=1)
    qkv = (cdot(normed[...], weight[:, :local]) + bias).astype(LOW)
    qkv_ref[0] = qkv
    mixed = []
    for head in range(heads):
        at = head * head_columns
        query = qkv[:, at : at + HD]
        key = qkv[:, at + HD : at + 2 * HD]
        value = qkv[:, at + 2 * HD : at + 3 * HD]
        scores = mask_keys(cdot(key, query, 1, 1), tokens)
        top = jnp.max(scores, axis=0, keepdims=True)
        raised = jnp.exp2((scores - top) * POWER)
        weight_sum = jnp.sum(raised, axis=0, keepdims=True)
        mixed.append(cdot(value, raised.astype(LOW), 0, 0) * (1.0 / weight_sum))
        sums_ref[0, head : head + 1, :] = top * POWER + jnp.log2(weight_sum)
    mixed = jnp.concatenate(mixed, axis=0).T.astype(LOW)
    mixed_ref[0] = mixed
    at = local + mixed.shape[1]
    part = cdot(mixed, weight[:, local:at], 1, 1)

    @pl.when(step == 0)
    def _():
        total[...] = part

    @pl.when(step > 0)
    def _():
        total[...] += part

    tail_ref[0] = weight[:, at : at + 2 * tail_units]

    @pl.when(step == pl.num_programs(0) - 1)
    def _():
        part_ref[...] = total[...].astype(LOW)
        turned_ref[...] = normed[...].T


def mlp_forward_kernel(spread, where, *refs):
    count = len(spread.weight_keys)
    base_ref, own_ref, other_ref, vec_ref, bias_ref, tail_ref, tail_bias_ref = refs[:7]
    w_refs = refs[7 : 7 + count]
    (middle_ref, turned_ref, act_ref, slope_ref, act_tail_ref, slope_tail_ref, up_tail_ref, down_tail_ref,
     part_ref, total, held_weight, normed) = refs[7 + count :]
    step = pl.program_id(0)

    @pl.when(step == 0)
    def _():
        branch = own_ref[...].astype(F32) + other_ref[...].astype(F32)
        middle = base_ref[...] + branch + vec_ref[0, 4:5, :]
        middle_ref[...] = middle
        unit, _ = norm_parts(middle)
        normed[...] = (unit * vec_ref[0, 5:6, :] + vec_ref[0, 6:7, :]).astype(LOW)
        steps, _, both = tail_ref.shape
        half = both // 2
        up_tail_ref[...] = jnp.concatenate([tail_ref[t, :, :half] for t in range(steps)], axis=1)
        down_tail_ref[...] = jnp.concatenate([tail_ref[t, :, half:] for t in range(steps)], axis=1)
        act, slope = gelu_both(cdot(normed[...], up_tail_ref[...]) + tail_bias_ref[0, 0])
        act = act.astype(LOW)
        act_tail_ref[...] = act
        slope_tail_ref[...] = slope.astype(LOW)
        total[...] = cdot(act, down_tail_ref[...], 1, 1)

    weight = spread.load(w_refs, where, held_weight)
    units = act_ref.shape[2]
    act, slope = gelu_both(cdot(normed[...], weight[:, :units]) + bias_ref[0, 0, 0])
    act = act.astype(LOW)
    act_ref[0] = act
    slope_ref[0] = slope.astype(LOW)
    total[...] += cdot(act, weight[:, units:], 1, 1)

    @pl.when(step == pl.num_programs(0) - 1)
    def _():
        part_ref[...] = total[...].astype(LOW)
        turned_ref[...] = normed[...].T


def mlp_backward_kernel(spread, where, *refs):
    count = len(spread.weight_keys)
    grad_ref, slope_ref, up_tail_ref, down_tail_ref, slope_tail_ref = refs[:5]
    w_refs = refs[5 : 5 + count]
    (hidden_ref, hidden_tail_ref, sums_ref, sums_tail_ref, part_ref, turned_ref, low, total, held_weight) = refs[
        5 + count :
    ]
    step = pl.program_id(0)

    @pl.when(step == 0)
    def _():
        low[...] = grad_ref[...].astype(LOW)
        hidden = cdot(low[...], down_tail_ref[...]) * slope_tail_ref[...].astype(F32)
        sums_tail_ref[...] = jnp.sum(hidden, axis=0, keepdims=True)
        hidden = hidden.astype(LOW)
        hidden_tail_ref[...] = hidden
        total[...] = cdot(hidden, up_tail_ref[...], 1, 1)

    weight = spread.load(w_refs, where, held_weight)
    units = hidden_ref.shape[2]
    turn_part(low, turned_ref, step)
    hidden = cdot(low[...], weight[:, units:]) * slope_ref[0].astype(F32)
    sums_ref[0] = jnp.sum(hidden, axis=0, keepdims=True)
    hidden = hidden.astype(LOW)
    hidden_ref[0] = hidden
    total[...] += cdot(hidden, weight[:, :units], 1, 1)

    @pl.when(step == pl.num_programs(0) - 1)
    def _():
        part_ref[...] = total[...].astype(LOW)


def mlp_grads_kernel(spread, where, *refs):
    count = len(spread.grad_keys)
    grad_turned, normed_turned, hidden_ref, act_ref, hidden_tail_ref, act_tail_ref = refs[:6]
    out_refs = refs[6 : 6 + count]
    tail_ref, result = refs[6 + count :]
    step = pl.program_id(0)

    @pl.when(step == 0)
    def _():
        up_tail = cdot(normed_turned[...], hidden_tail_ref[...]).astype(LOW)
        down_tail = cdot(grad_turned[...], act_tail_ref[...]).astype(LOW)
        steps, _, both = tail_ref.shape
        half = both // 2
        for t in range(steps):
            at = slice(t * half, (t + 1) * half)
            tail_ref[t] = jnp.concatenate([up_tail[:, at], down_tail[:, at]], axis=1)

    units = hidden_ref.shape[2]
    result[:, :units] = cdot(normed_turned[...], hidden_ref[0]).astype(LOW)
    result[:, units:] = cdot(grad_turned[...], act_ref[0]).astype(LOW)
    spread.store(out_refs, where, result)


def attn_backward_kernel(spread, where, *refs):
    count = len(spread.weight_keys)
    grad_ref, own_ref, other_ref, middle_ref, vec_ref, qkv_ref, sums_ref = refs[:7]
    w_refs = refs[7 : 7 + count]
    (dmiddle_ref, norm_sums_ref, dqkv_ref, head_sums_ref, part_ref, turned_ref, low, total, held_weight) = refs[
        7 + count :
    ]
    step = pl.program_id(0)

    @pl.when(step == 0)
    def _():
        grad = grad_ref[...]
        dnormed = own_ref[...].astype(F32) + other_ref[...].astype(F32)
        inner, gain_terms = norm_backward(dnormed, middle_ref[...], vec_ref[0, 5:6, :])
        dmiddle = grad + inner
        dmiddle_ref[...] = dmiddle
        low[...] = dmiddle.astype(LOW)
        for number, terms in enumerate((gain_terms, dnormed, grad, dmiddle)):
            norm_sums_ref[number : number + 1, :] = jnp.sum(terms, axis=0, keepdims=True)

    weight = spread.load(w_refs, where, held_weight)
    tokens = where[4]
    head_columns = 3 * HD
    local = qkv_ref.shape[2]
    heads = local // head_columns
    qkv = qkv_ref[0]
    turn_part(low, turned_ref, step)
    dmixed = cdot(low[...], weight[:, local : local + heads * HD]).astype(LOW)
    pieces = []
    for head in range(heads):
        at = head * head_columns
        query = qkv[:, at : at + HD]
        key = qkv[:, at + HD : at + 2 * HD]
        value = qkv[:, at + 2 * HD : at + 3 * HD]
        grad = dmixed[:, head * HD : (head + 1) * HD]
        scores = mask_keys(cdot(key, query, 1, 1), tokens)
        probs = jnp.exp2(scores * POWER - sums_ref[0, head : head + 1, :])
        dprobs = cdot(value, grad, 1, 1)
        row_dot = jnp.sum(dprobs * probs, axis=0, keepdims=True)
        dscores = (probs * (dprobs - row_dot)).astype(LOW)
        pieces.append(cdot(key, dscores, 0, 0).T * SCORE)
        pieces.append(cdot(dscores, query) * SCORE)
        pieces.append(cdot(probs.astype(LOW), grad))
    dqkv = jnp.concatenate(pieces, axis=1)
    head_sums_ref[0] = jnp.sum(dqkv, axis=0, keepdims=True)
    dqkv = dqkv.astype(LOW)
    dqkv_ref[0] = dqkv
    part = cdot(dqkv, weight[:, :local], 1, 1)

    @pl.when(step == 0)
    def _():
        total[...] = part

    @pl.when(step > 0)
    def _():
        total[...] += part

    @pl.when(step == pl.num_programs(0) - 1)
    def _():
        part_ref[...] = total[...].astype(LOW)


def attn_grads_kernel(spread, where, *refs):
    count = len(spread.grad_keys)
    grad_turned, normed_turned, dqkv_ref, mixed_ref, tail_ref = refs[:5]
    out_refs = refs[5 : 5 + count]
    (result,) = refs[5 + count :]
    parts = [
        cdot(normed_turned[...], dqkv_ref[0]).astype(LOW),
        cdot(grad_turned[...], mixed_ref[0]).astype(LOW),
        tail_ref[0],
    ]
    used = sum(part.shape[1] for part in parts)
    parts.append(jnp.zeros((result.shape[0], result.shape[1] - used), LOW))
    result[...] = jnp.concatenate(parts, axis=1)
    spread.store(out_refs, where, result)


def norm_backward_kernel(where, dmiddle_ref, own_ref, other_ref, stream_ref, vec_ref, out_ref, sums_ref):
    dnormed = own_ref[...].astype(F32) + other_ref[...].astype(F32)
    inner, gain_terms = norm_backward(dnormed, stream_ref[...], vec_ref[0, 0:1, :])
    out_ref[...] = dmiddle_ref[...] + inner

    @pl.when(pl.program_id(0) == 0)
    def _():
        sums_ref[...] = jnp.zeros_like(sums_ref)

    sums_ref[0:1, :] += jnp.sum(gain_terms, axis=0, keepdims=True)
    sums_ref[1:2, :] += jnp.sum(dnormed, axis=0, keepdims=True)


def adam_kernel(units, local, out_local, tail_units, where, *refs):
    attn_own, attn_other, mlp_own, mlp_other = refs[:4]
    states = [refs[4 + 3 * k : 7 + 3 * k] for k in range(4)]
    outs = refs[len(refs) - 16 :]

    def pair(own, other):
        own, other = own[...].astype(F32), other[...].astype(F32)
        low_core = where[3] == 0
        return jnp.where(low_core, own, other), jnp.where(low_core, other, own)

    attn = pair(attn_own, attn_other)
    mlp = pair(mlp_own, mlp_other)
    at = local + out_local
    grads = [
        jnp.concatenate([half[:, :local] for half in attn], axis=1),
        jnp.concatenate([half[:, local:at] for half in attn], axis=1),
        jnp.concatenate(
            [piece for m, n in zip(mlp, attn) for piece in (m[:, :units], n[:, at : at + tail_units])], axis=1
        ),
        jnp.concatenate(
            [
                piece
                for m, n in zip(mlp, attn)
                for piece in (m[:, units:], n[:, at + tail_units : at + 2 * tail_units])
            ],
            axis=1,
        ),
    ]
    for number, grad in enumerate(grads):
        weight, first, second = [ref[0] for ref in states[number]]
        new = adam_step(weight, grad, first, second, RATES[number], DECAY)
        for ref, values in zip(outs[4 * number : 4 * number + 4], (grad, new[1], new[2], new[0])):
            ref[0] = values


def vec_pack_kernel(where, *refs):
    out_ref = refs[-1]
    layers = out_ref.shape[0]
    out_ref[...] = jnp.zeros_like(out_ref)
    for layer in range(layers):
        one_ref, two_ref, head_ref, main_ref, tail_ref = refs[5 * layer : 5 * layer + 5]
        out_ref[layer, 0:2, :] = one_ref[0:2, :]
        out_ref[layer, 2:6, :] = two_ref[0:4, :]
        for t in range(head_ref.shape[0]):
            out_ref[layer, 8 + t : 9 + t, : head_ref.shape[2]] = head_ref[t]
            out_ref[layer, 16 + t : 17 + t, : main_ref.shape[2]] = main_ref[t]
        out_ref[layer, 6:7, : tail_ref.shape[1]] = tail_ref[...]


def vec_kernel(steps, local, units, tail_units, where, own_ref, other_ref, vec_ref, first_ref, second_ref,
               grad_out, first_out, second_out, weight_out):
    low_core = where[3] == 0
    for layer in range(vec_ref.shape[0]):
        own, other = own_ref[layer], other_ref[layer]
        cores = jnp.where(low_core, own, other), jnp.where(low_core, other, own)
        norms = cores[0][0:6]
        heads = local // (3 * HD)

        def head_piece(kind):
            return [
                core[8 + t : 9 + t, (3 * head + kind) * HD : (3 * head + kind + 1) * HD]
                for t in range(steps)
                for core in cores
                for head in range(heads)
            ]

        hidden = [
            piece
            for t in range(steps)
            for core in cores
            for piece in (core[16 + t : 17 + t, :units], core[6:7, t * tail_units : (t + 1) * tail_units])
        ]
        grad = jnp.concatenate(
            [norms[0:1], norms[1:2], *head_piece(0), *head_piece(2),
             norms[5:6], norms[2:3], norms[3:4], norms[4:5], *hidden],
            axis=1,
        )
        at = slice(layer, layer + 1)
        new = adam_step(vec_ref[at, :], grad, first_ref[at, :], second_ref[at, :], RATES[4], 0.0)
        grad_out[at, :] = grad
        first_out[at, :] = new[1]
        second_out[at, :] = new[2]
        weight_out[at, :] = new[0]


def plane_sides(chips):
    side = math.isqrt(chips)
    while chips % side:
        side -= 1
    return side, chips // side


class Place:
    def __init__(self):
        self.nf = lax.axis_size("fsdp")
        self.nt = lax.axis_size("tp")
        self.na, self.nb = plane_sides(self.nf // 2)
        fi = lax.axis_index("fsdp")
        self.core = fi % 2
        self.a = (fi // 2) // self.nb
        self.b = (fi // 2) % self.nb
        self.t = lax.axis_index("tp")
        self.size = {"a": self.na, "b": self.nb, "t": self.nt}
        self.at = {"a": self.a, "b": self.b, "t": self.t}

    def pairs(self, axis, move):
        if axis == "t":
            return [(i, move(i)) for i in range(self.nt)]
        found = []
        for f in range(self.nf):
            place = {"a": f // 2 // self.nb, "b": f // 2 % self.nb, "core": f % 2}
            place[axis] = move(place[axis])
            found.append((f, (place["a"] * self.nb + place["b"]) * 2 + place["core"]))
        return found

    def send(self, values, axis, move):
        return lax.ppermute(values, "tp" if axis == "t" else "fsdp", self.pairs(axis, move))

    def sibling(self, values):
        return self.send(values, "core", lambda i: 1 - i)

    def swap_rows(self, values):
        pairs = []
        for f in range(self.nf):
            for t in range(self.nt):
                if f % 2 != t % 2:
                    sign = 1 if t % 2 else -1
                    pairs.append((f * self.nt + t, (f + sign) * self.nt + t - sign))
        arrived = lax.ppermute(values.astype(LOW), ("fsdp", "tp"), pairs).astype(F32)
        return jnp.where(self.core != self.t % 2, arrived, values)

    def gather_axis(self, block, axis):
        n = self.size[axis]
        return [block] + [self.send(block, axis, lambda i, k=k: (i - k) % n) for k in range(1, n)]

    def scatter_axis(self, parts, axis):
        n = self.size[axis]
        sent = [self.send(parts[k], axis, lambda i, k=k: (i + k) % n) for k in range(1, n)]
        return [parts[0], *sent]


def split_pair(place, first, second):
    return (
        jnp.where(place.core == 0, first, second),
        jnp.where(place.core == 0, second, first),
    )


def sum_kernel(outputs, where, *refs):
    count = sum(size for sizes in outputs for size in sizes)
    ins, outs = refs[:count], refs[count:]
    for out_ref, sizes in zip(outs, outputs):
        for number, size in enumerate(sizes):
            total = ins[0][0, 0].astype(F32)
            for ref in ins[1:size]:
                total += ref[0, 0].astype(F32)
            ins = ins[size:]
            out_ref[0, number] = total.astype(LOW)


def tie_kernel(where, *refs):
    pass


def tie(where, arrays, after):
    space = pl.BlockSpec(memory_space=pl.ANY)
    return call(
        tie_kernel,
        where,
        1,
        [(space, x) for x in arrays],
        [(space, jax.ShapeDtypeStruct(x.shape, x.dtype)) for x in arrays],
        [],
        aliases={1 + k: k for k in range(len(arrays))},
        after=after,
    )


class Spread:
    def __init__(self, place, rows, columns, middle):
        self.place, self.rows, self.columns = place, rows, columns
        self.middle = middle
        self.direct = rows % 16 == 0
        self.width = place.na * place.nb * 2 * rows
        na, nb = place.na, place.nb
        self.grad_keys = [[(0, a, b) for b in range(nb)] for a in range(na)]
        self.grad_keys += [[(1, a, b) for a in range(na)] for b in range(nb)]
        self.gather_keys = [[(0, 0, 0), (1, 0, 0)]]
        self.gather_keys += [[(0, 0, b), (1, 0, b)] for b in range(1, nb)]
        self.gather_keys += [[(0, a, 0), (1, a, 0)] for a in range(1, na)]
        self.gather_keys += [[(half, a, b)] for half in range(2) for a in range(1, na) for b in range(1, nb)]
        if middle:
            self.gather_keys = self.grad_keys
        self.weight_keys = self.gather_keys
        if not self.direct:
            self.weight_keys = self.grad_keys = [None]

    def shapes(self, keys):
        if not self.direct:
            return [(self.place.nt, self.width, self.columns)]
        return [(self.place.nt, len(blocks), self.rows, self.columns) for blocks in keys]

    def specs(self, keys):
        return [stepped(shape[1:]) for shape in self.shapes(keys)]

    def first_row(self, where, key):
        half, a, b = key
        a = lax.rem(where[0] + a, self.place.na)
        b = lax.rem(where[1] + b, self.place.nb)
        return pl.multiple_of(((a * self.place.nb + b) * 2 + half) * self.rows, 16)

    def load(self, refs, where, scratch):
        if not self.direct:
            return refs[0].at[0]
        for ref, blocks in zip(refs, self.weight_keys):
            for number, key in enumerate(blocks):
                scratch[pl.ds(self.first_row(where, key), self.rows), :] = ref[0, number]
        return scratch

    def store(self, refs, where, scratch):
        if not self.direct:
            refs[0][0] = scratch[...]
            return
        for ref, blocks in zip(refs, self.grad_keys):
            for number, key in enumerate(blocks):
                ref[0, number] = scratch[pl.ds(self.first_row(where, key), self.rows), :]

    def start(self, own, other):
        place = self.place
        halves = split_pair(place, own, other)
        if self.middle:
            return [jnp.stack(place.gather_axis(half, axis)) for half, axis in zip(halves, "ba")]
        return [jnp.stack(halves)]

    def gather(self, where, blocks, after=()):
        place = self.place
        na, nb = place.na, place.nb
        blocks = [lax.all_gather(block, "tp") for block in blocks]
        if self.direct and len(after):
            blocks = tie(where, blocks, after)
        if self.middle:
            arrays = [array for block, axis in zip(blocks, "ab") for array in place.gather_axis(block, axis)]
        else:
            along_b = place.gather_axis(blocks[0], "b")
            along_a = place.gather_axis(blocks[0], "a")
            first = [place.gather_axis(x[:, :1], "a")[1:] for x in along_b[1:]]
            second = [place.gather_axis(x[:, 1:], "b")[1:] for x in along_a[1:]]
            arrays = along_b + along_a[1:]
            arrays += [first[b][a] for a in range(na - 1) for b in range(nb - 1)]
            arrays += [second[a][b] for a in range(na - 1) for b in range(nb - 1)]
        if self.direct:
            return arrays
        found = {
            key: array[:, number]
            for array, keys in zip(arrays, self.gather_keys)
            for number, key in enumerate(keys)
        }
        full = jnp.stack([found[half, a, b] for a in range(na) for b in range(nb) for half in range(2)], axis=1)
        full = full.reshape(place.nt, na, nb, 2, self.rows, self.columns)
        full = self.roll(full, (na - place.a) % na, (nb - place.b) % nb)
        return [full.reshape(place.nt, self.width, self.columns)]

    def roll(self, full, a, b):
        full = lax.dynamic_slice_in_dim(jnp.concatenate([full, full], axis=1), a, self.place.na, 1)
        return lax.dynamic_slice_in_dim(jnp.concatenate([full, full], axis=2), b, self.place.nb, 2)

    def sums(self, where, outputs, after):
        place, rows, columns = self.place, self.rows, self.columns

        def block(number):
            return pl.BlockSpec((1, 1, rows, columns), lambda i, s: (i, number, 0, 0))

        shapes = [(place.nt, len(groups), rows, columns) for groups in outputs]
        return call(
            functools.partial(sum_kernel, [[len(group) for group in groups] for groups in outputs]),
            where,
            place.nt,
            [(block(number), x) for groups in outputs for group in groups for x, number in group],
            [(stepped(shape[1:]), low_of(*shape)) for shape in shapes],
            [],
            after=after,
        )

    def scatter_last(self, arrays):
        place = self.place
        if not self.direct:
            full = arrays[0].reshape(place.nt, place.na, place.nb, 2, self.rows, self.columns)
            full = self.roll(full, place.a, place.b)
            arrays = [full[:, a, :, 0] for a in range(place.na)] + [full[:, :, b, 1] for b in range(place.nb)]
        return (
            place.scatter_axis(arrays[: place.na], "a"),
            place.scatter_axis(arrays[place.na :], "b"),
        )

    def scatter_first(self, where, halves, after):
        place = self.place
        if self.middle:
            outputs = [[[(x, k) for x in half] for k in range(half[0].shape[1])] for half in halves]
            results = self.sums(where, outputs, after)
            return results[0], [lax.psum_scatter(x, "tp", scatter_dimension=0, tiled=True)[0] for x in results]
        axes = ("b", "a")
        keys = [(half, k) for half in range(2) for k in range(1, place.size[axes[half]])]
        results = self.sums(where, [[[(x, k) for x in halves[half]]] for half, k in keys], after)
        terms = [[(x, 0) for x in arrays] for arrays in halves]
        for (half, k), total in zip(keys, results):
            n = place.size[axes[half]]
            terms[half].append((place.send(total, axes[half], lambda i: (i + k) % n), 0))
        return results[0], terms

    def scatter_tp(self, where, terms, after):
        place = self.place
        if self.middle:
            if self.direct:
                terms = tie(where, terms, after)
            done = [
                sum(x.astype(F32) for x in place.scatter_axis(list(half), axis)).astype(LOW)
                for half, axis in zip(terms, "ba")
            ]
            last = after[0]
        else:
            (last,) = self.sums(where, [terms], after)
            done = lax.psum_scatter(last, "tp", scatter_dimension=0, tiled=True)[0]
        mine, other = split_pair(place, done[0], done[1])
        return last, (mine, place.sibling(other))


def body(
    residual_in,
    cotangent,
    slot_tokens,
    qkv_weight,
    out_weight,
    up_weight,
    down_weight,
    vectors,
    qkv_first,
    qkv_second,
    out_first,
    out_second,
    up_first,
    up_second,
    down_first,
    down_second,
    vec_first,
    vec_second,
):
    place = Place()
    layer_count, shard_rows, _ = qkv_weight.shape
    half_rows, width = residual_in.shape
    rows = 2 * half_rows
    nt = place.nt
    local = qkv_weight.shape[2] // 2
    out_local = out_weight.shape[1] // 2
    hidden_local = up_weight.shape[2] // 2
    units = hidden_local // 128 * 128
    tail_units = hidden_local - units
    heads = out_local // HD
    attn_columns = -(-(local + out_local + 2 * tail_units) // 128) * 128
    mlp_columns = 2 * units

    tokens_pair = jnp.concatenate(split_pair(place, slot_tokens, place.sibling(slot_tokens)))
    slot_at = (place.t % 2) * slot_tokens.shape[0] + place.t // 2
    tokens = lax.dynamic_slice_in_dim(tokens_pair, slot_at, 1)
    row_mask = (jnp.arange(rows, dtype=jnp.int32) < tokens[0]).astype(F32)[:, None]
    here = jnp.stack([place.a, place.b, place.t, place.core]).astype(jnp.int32)
    where = jnp.concatenate([here, tokens.astype(jnp.int32)])

    def own_rows(values):
        return lax.dynamic_slice_in_dim(values, place.core * half_rows, half_rows)

    spreads = [
        (
            Spread(place, shard_rows, attn_columns, False),
            Spread(place, shard_rows, mlp_columns, layer > 0),
        )
        for layer in range(layer_count)
    ]

    def turn(arrays):
        qkv, out, up, down = arrays
        return qkv, jnp.swapaxes(out, 1, 2), up, jnp.swapaxes(down, 1, 2)

    weights = turn((qkv_weight, out_weight, up_weight, down_weight))
    firsts = turn((qkv_first, out_first, up_first, down_first))
    seconds = turn((qkv_second, out_second, up_second, down_second))

    def layer_block(array, layer, steps=1):
        block = (1, array.shape[1] // steps, array.shape[2])
        return pl.BlockSpec(block, lambda i, s: (layer, i, 0))

    def pack(layer):
        attn, mlp = (shard_rows, attn_columns), (shard_rows, mlp_columns)
        return call(
            functools.partial(pack_kernel, units),
            here,
            1,
            [(layer_block(w, layer), w) for w in weights],
            [(held(shape), low_of(*shape)) for shape in (attn, attn, mlp, mlp)],
            [],
            bytes_accessed=6 * shard_rows * 13216 // 4,
        )

    starts = []
    for layer in range(layer_count):
        own_attn, other_attn, own_mlp, other_mlp = pack(layer)
        starts.append(
            (
                spreads[layer][0].start(own_attn, place.sibling(other_attn)),
                spreads[layer][1].start(own_mlp, place.sibling(other_mlp)),
            )
        )
    gathered = []
    before = [x for pair in starts[1:] for blocks in pair for x in blocks]
    for layer in range(layer_count):
        attn_full = spreads[layer][0].gather(where, starts[layer][0], before)
        mlp_full = spreads[layer][1].gather(where, starts[layer][1], attn_full[1:3])
        before = mlp_full[1:3]
        gathered.append((attn_full, mlp_full))

    wide = vectors[:, : 8 * width].reshape(layer_count, 8, width)
    head_bias = vectors[:, 2 * width : 4 * width].reshape(layer_count, 2, 2 * nt, 1, out_local)
    hidden_bias = vectors[:, 8 * width :].reshape(layer_count, nt, 2, 1, hidden_local)
    main_bias = hidden_bias[..., :units]
    tail_bias = jnp.moveaxis(hidden_bias[..., units:], 1, 3).reshape(layer_count, 2, 1, nt * tail_units)

    full = whole((rows, width))
    weight_scratch = [
        pltpu.VMEM((width, attn_columns), LOW),
        pltpu.VMEM((width, mlp_columns), LOW),
    ]
    flat = pltpu.VMEM((rows, width), F32)
    flat_low = pltpu.VMEM((rows, width), LOW)
    big = 2 * rows * width

    def wide_of(layer):
        spec = pl.BlockSpec((1, 8, width), lambda i, s: (layer, 0, 0), pipeline_mode=pl.Buffered(1))
        return spec, wide

    def attn_forward(layer, base, own, other):
        spread = spreads[layer][0]
        joined = base is not None
        if joined:
            ins = [(full, base), (full, own), (full, other), wide_of(layer - 1)]
        else:
            half = whole((half_rows, width))
            ins = [(half, own), (half, other)]
        ins.append(wide_of(layer))
        ins.append(
            (
                pl.BlockSpec(
                    (1, 2, 1, 1, out_local), lambda i, s: (layer, 0, 2 * i + s[3], 0, 0)
                ),
                head_bias,
            )
        )
        ins += list(zip(spread.specs(spread.weight_keys), gathered[layer][0]))
        return call(
            functools.partial(attn_forward_kernel, spread, joined, tail_units),
            where,
            nt,
            ins,
            [
                (held((rows, width)), f32_of(rows, width)),
                (held((width, rows)), low_of(width, rows)),
                (stepped((rows, local)), low_of(nt, rows, local)),
                (stepped((rows, out_local)), low_of(nt, rows, out_local)),
                (stepped((heads, rows)), f32_of(nt, heads, rows)),
                (stepped((width, 2 * tail_units)), low_of(nt, width, 2 * tail_units)),
                (held((rows, width)), low_of(rows, width)),
            ],
            [flat, weight_scratch[0], flat_low],
            big * nt * (local + out_local) + 4 * nt * heads * rows * rows * HD,
            rows * width * 12 + nt * width * attn_columns * 2,
            nt * heads * rows * rows,
        )

    def mlp_forward(layer, base, own, other, tails):
        spread = spreads[layer][1]
        tail = nt * tail_units
        tail_shape = (width, tail)
        ins = [
            (full, base),
            (full, own),
            (full, other),
            wide_of(layer),
            (pl.BlockSpec((1, 1, 1, 1, units), lambda i, s: (layer, i, s[3], 0, 0)), main_bias),
            (whole(tails.shape), tails),
            (pl.BlockSpec((1, 1, 1, tail), lambda i, s: (layer, s[3], 0, 0)), tail_bias),
        ]
        ins += list(zip(spread.specs(spread.weight_keys), gathered[layer][1]))
        return call(
            functools.partial(mlp_forward_kernel, spread),
            where,
            nt,
            ins,
            [
                (held((rows, width)), f32_of(rows, width)),
                (held((width, rows)), low_of(width, rows)),
                (stepped((rows, units)), low_of(nt, rows, units)),
                (stepped((rows, units)), low_of(nt, rows, units)),
                (held((rows, tail)), low_of(rows, tail)),
                (held((rows, tail)), low_of(rows, tail)),
                (held(tail_shape), low_of(*tail_shape)),
                (held(tail_shape), low_of(*tail_shape)),
                (held((rows, width)), low_of(rows, width)),
            ],
            [flat, weight_scratch[1], flat_low],
            2 * big * (nt * units + tail),
            rows * width * 16 + nt * (width + rows) * mlp_columns * 2,
            rows * nt * units,
        )

    def mlp_backward(layer, grad, slope, tails, slope_tail):
        spread = spreads[layer][1]
        tail = nt * tail_units
        ins = [(full, grad), (stepped((rows, units)), slope)]
        ins += [(whole(w.shape), w) for w in (*tails, slope_tail)]
        ins += list(zip(spread.specs(spread.weight_keys), gathered[layer][1]))
        return call(
            functools.partial(mlp_backward_kernel, spread),
            where,
            nt,
            ins,
            [
                (stepped((rows, units)), low_of(nt, rows, units)),
                (held((rows, tail)), low_of(rows, tail)),
                (stepped((1, units)), f32_of(nt, 1, units)),
                (held((1, tail)), f32_of(1, tail)),
                (held((rows, width)), low_of(rows, width)),
                (held((width, rows)), low_of(width, rows)),
            ],
            [flat_low, flat, weight_scratch[1]],
            2 * big * (nt * units + tail),
            rows * width * 6 + nt * (width + rows) * mlp_columns * 2,
        )

    def mlp_grads(layer, grad, normed, hidden, act, hidden_tail, act_tail):
        spread = spreads[layer][1]
        ins = [(whole((width, rows)), grad), (whole((width, rows)), normed)]
        ins += [(stepped((rows, units)), hidden), (stepped((rows, units)), act)]
        ins += [(whole(x.shape), x) for x in (hidden_tail, act_tail)]
        tail_shape = (nt, width, 2 * tail_units)
        outs = [
            (spec, low_of(*shape))
            for spec, shape in zip(spread.specs(spread.grad_keys), spread.shapes(spread.grad_keys))
        ]
        outs.append((held(tail_shape), low_of(*tail_shape)))
        return call(
            functools.partial(mlp_grads_kernel, spread),
            where,
            nt,
            ins,
            outs,
            [weight_scratch[1]],
            2 * big * nt * (units + tail_units),
            rows * width * 6 + nt * (width + rows) * mlp_columns * 2,
        )

    def attn_backward(layer, grad, own, other, middle, qkv, log_sums, after=()):
        spread = spreads[layer][0]
        ins = [(full, grad), (full, own), (full, other), (full, middle), wide_of(layer)]
        ins += [(stepped((rows, local)), qkv), (stepped((heads, rows)), log_sums)]
        ins += list(zip(spread.specs(spread.weight_keys), gathered[layer][0]))
        return call(
            functools.partial(attn_backward_kernel, spread),
            where,
            nt,
            ins,
            [
                (held((rows, width)), f32_of(rows, width)),
                (held((8, width)), f32_of(8, width)),
                (stepped((rows, local)), low_of(nt, rows, local)),
                (stepped((1, local)), f32_of(nt, 1, local)),
                (held((rows, width)), low_of(rows, width)),
                (held((width, rows)), low_of(width, rows)),
            ],
            [flat_low, flat, weight_scratch[0]],
            big * nt * (local + out_local) + 10 * nt * heads * rows * rows * HD,
            rows * width * 20 + nt * width * attn_columns * 2,
            nt * heads * rows * rows,
            after=after,
        )

    def attn_grads(layer, dmiddle, normed, dqkv, mixed, tail_grads):
        spread = spreads[layer][0]
        ins = [(whole((width, rows)), dmiddle), (whole((width, rows)), normed)]
        ins += [(stepped((rows, local)), dqkv), (stepped((rows, out_local)), mixed)]
        ins.append((stepped((width, 2 * tail_units)), tail_grads))
        outs = [
            (spec, low_of(*shape))
            for spec, shape in zip(spread.specs(spread.grad_keys), spread.shapes(spread.grad_keys))
        ]
        return call(
            functools.partial(attn_grads_kernel, spread),
            where,
            nt,
            ins,
            outs,
            [weight_scratch[0]],
            big * nt * (local + out_local),
            rows * width * 6 + nt * (width + rows) * attn_columns * 2,
        )

    def norm_one_backward(layer, dmiddle, own, other, stream, after=()):
        part = pl.BlockSpec((half_rows, width), lambda i, s: (i, 0))
        return call(
            norm_backward_kernel,
            where,
            2,
            [(part, dmiddle), (part, own), (part, other), (part, stream), wide_of(layer)],
            [(part, f32_of(rows, width)), (held((8, width)), f32_of(8, width))],
            [],
            rows * width * 20,
            rows * width * 16,
            after=after,
        )

    mine = place.swap_rows(residual_in)
    base, own, other = None, mine, place.sibling(mine)
    saved = []
    for layer in range(layer_count):
        stream, normed, qkv, mixed, log_sums, tails, part = attn_forward(layer, base, own, other)
        last_attn = qkv
        middle, normed_two, act, slope, act_tail, slope_tail, up_tail, down_tail, part = mlp_forward(
            layer, stream, part, place.sibling(part), tails
        )
        saved.append(
            (stream, normed, qkv, mixed, log_sums, middle, normed_two, act, slope, act_tail, slope_tail,
             (up_tail, down_tail))
        )
        base, own, other = middle, part, place.sibling(part)
    output = own_rows(base) + (own_rows(own).astype(F32) + own_rows(other).astype(F32))
    output = place.swap_rows((output + wide[layer_count - 1, 7:8]) * own_rows(row_mask))

    (mine,) = tie(where, [place.swap_rows(cotangent)], [last_attn])
    grad_stream = jnp.concatenate(split_pair(place, mine, place.sibling(mine)), axis=0) * row_mask


    def adam(layer, attn_pair, mlp_pair, before, after=()):
        steps = 1
        ins = [
            (pl.BlockSpec((shard_rows // steps, x.shape[1]), lambda i, s: (i, 0)), x)
            for x in (*attn_pair, *mlp_pair)
        ]
        for states in zip(weights, firsts, seconds):
            ins += [(layer_block(x, layer, steps), x) for x in states]
        outs = [
            (layer_block(weight, layer, steps), f32_of(*weight.shape)) for weight in weights for _ in range(4)
        ]
        aliases = None
        if before is not None:
            aliases = {1 + len(ins) + k: k for k in range(16)}
            ins += [(pl.BlockSpec(memory_space=pl.ANY), x) for x in before]
        return call(
            functools.partial(adam_kernel, units, local, out_local, tail_units),
            where,
            steps,
            ins,
            outs,
            [],
            bytes_accessed=28 * shard_rows * 13216 // 4,
            aliases=aliases,
            after=after,
        )

    vec_sums = [None] * layer_count
    last = grad_stream
    above = None
    for layer in reversed(range(layer_count)):
        (stream, normed, qkv, mixed, log_sums, middle, normed_two, act, slope, act_tail, slope_tail, tails) = (
            saved[layer]
        )
        spread_attn, spread_mlp = spreads[layer]
        hidden, hidden_tail, hidden_sums, tail_sums, part, grad_turned = mlp_backward(
            layer, grad_stream, slope, tails, slope_tail
        )
        other = place.sibling(part)
        *mlp_grad, tail_grads = mlp_grads(
            layer, grad_turned, normed_two, hidden, act, hidden_tail, act_tail
        )
        last = tail_grads
        mlp_terms = spread_mlp.scatter_last(mlp_grad)
        if above:
            last, attn_terms_above = spreads[above][0].scatter_first(where, attn_terms_above, [last, output])
        dmiddle, norm_two_sums, dqkv, head_sums, part, grad_turned = attn_backward(
            layer, grad_stream, part, other, middle, qkv, log_sums, [last]
        )
        other = place.sibling(part)
        attn_grad = attn_grads(layer, grad_turned, normed, dqkv, mixed, tail_grads)
        last = attn_grad[0]
        grad_stream, norm_one_sums = norm_one_backward(layer, dmiddle, part, other, stream, [last])
        if layer:
            attn_terms = spread_attn.scatter_last(attn_grad)
        if above:
            _, mlp_pair_above = spreads[above][1].scatter_tp(where, mlp_terms_above, [norm_one_sums])
        last, mlp_terms = spread_mlp.scatter_first(where, mlp_terms, [norm_one_sums])
        vec_sums[layer] = (norm_one_sums, norm_two_sums, head_sums, hidden_sums, tail_sums)
        if above:
            last, attn_pair_above = spreads[above][0].scatter_tp(where, attn_terms_above, [last])
            pairs_above = attn_pair_above, mlp_pair_above
        if not layer:
            if spread_attn.direct:
                attn_grad = tie(where, attn_grad, [last])
            attn_terms = spread_attn.scatter_last(attn_grad)
        above, mlp_terms_above, attn_terms_above = layer, mlp_terms, attn_terms
        if layer:
            grad_stream, last = lax.optimization_barrier((grad_stream, last))
    grad_input = place.swap_rows(own_rows(grad_stream))
    last, mlp_pair_above = spreads[above][1].scatter_tp(where, mlp_terms_above, [last])
    last, attn_terms_above = spreads[above][0].scatter_first(
        where, attn_terms_above, [last, *pairs_above[1], grad_input]
    )
    updated = adam(1, *pairs_above, None, [last])
    last, attn_pair_above = spreads[above][0].scatter_tp(where, attn_terms_above, [last, updated[0]])

    flat_sums = [x for sums in vec_sums for x in sums]
    vec_shape = (layer_count, 24, width)
    (vec_total,) = call(
        vec_pack_kernel,
        where,
        1,
        [(whole(x.shape), x) for x in flat_sums],
        [(held(vec_shape), f32_of(*vec_shape))],
        [],
        after=[last],
    )
    for axis in ("b", "a", "t"):
        step = 1
        while step < place.size[axis]:
            vec_total = vec_total + place.send(vec_total, axis, lambda i: i ^ step)
            step *= 2
    vec_new = call(
        functools.partial(vec_kernel, nt, local, units, tail_units),
        where,
        1,
        [(whole(x.shape), x) for x in (vec_total, place.sibling(vec_total), vectors, vec_first, vec_second)],
        [(held(vectors.shape), f32_of(*vectors.shape)) for _ in range(4)],
        [],
    )
    updated = adam(above, attn_pair_above, mlp_pair_above, updated)
    updated = [
        jnp.swapaxes(x, 1, 2) if number // 4 % 2 else x for number, x in enumerate(updated)
    ]
    return (output, grad_input, *updated, *vec_new)


def solution(mesh):
    rows = P(("fsdp", "tp"), None)
    wide = P(None, "fsdp", "tp")
    tall = P(None, "tp", "fsdp")
    moments = (wide, wide, tall, tall, wide, wide, tall, tall, P(), P())
    return jax.shard_map(
        body,
        mesh=mesh,
        in_specs=(rows, rows, P("fsdp"), wide, tall, wide, tall, P(), *moments),
        out_specs=(rows, rows, *[wide] * 4, *[tall] * 4, *[wide] * 4, *[tall] * 4, *[P()] * 4),
        check_vma=False,
    )
```

```python
import functools
import math

import jax
import jax.numpy as jnp
from jax import lax
from jax.experimental import pallas as pl
from jax.experimental.pallas import tpu as pltpu
from jax.sharding import PartitionSpec as P

HD = 72
IMG_TOK = 729
STEP = 10


EPS_NORM = 1e-06
MASKED = -30000.0
BETA_ONE = 0.9
BETA_TWO = 0.999
ADAM_EPS = 1e-08
DECAY = 0.1
RATES = (0.05, 1.0, 0.05, 0.03, 0.3)
LOW = jnp.bfloat16
F32 = jnp.float32
GELU = math.sqrt(2.0 / math.pi)
SCORE = HD ** (-0.5)
POWER = SCORE / math.log(2.0)
VMEM = 56 * 1024 * 1024
COST = {
    "pack_kernel": 4,
    "attn_forward_kernel": 26,
    "mlp_forward_kernel": 24,
    "mlp_backward_kernel": 17,
    "mlp_grads_kernel": 16,
    "attn_backward_kernel": 33,
    "attn_grads_kernel": 13,
    "norm_backward_kernel": 9,
    "sum_kernel": 5,
    "vec_pack_kernel": 0.3,
    "vec_kernel": 0.3,
    "adam_kernel": 1,
    "tie_kernel": 1,
}
SCALE = 2e9


def adam_step(weight, gradient, first_moment, second_moment, step_rate, decay_rate):
    first_new = BETA_ONE * first_moment + (1.0 - BETA_ONE) * gradient
    second_new = BETA_TWO * second_moment + (1.0 - BETA_TWO) * gradient * gradient
    first_hat = first_new / (1.0 - BETA_ONE**STEP)
    second_hat = second_new / (1.0 - BETA_TWO**STEP)
    weight_new = weight - step_rate * (
        first_hat / (jnp.sqrt(second_hat) + ADAM_EPS) + decay_rate * weight
    )
    return (weight_new, first_new, second_new)


def cdot(left, right, left_dim=1, right_dim=0):
    return lax.dot_general(
        left, right, (((left_dim,), (right_dim,)), ((), ())), preferred_element_type=F32
    )


def norm_parts(values):
    centred = values - jnp.mean(values, axis=-1, keepdims=True)
    inverse = lax.rsqrt(jnp.mean(centred * centred, axis=-1, keepdims=True) + EPS_NORM)
    return centred * inverse, inverse


def norm_backward(grad_out, values, gain):
    unit, inverse = norm_parts(values)
    scaled = grad_out * gain
    mean_one = jnp.mean(scaled, axis=-1, keepdims=True)
    mean_two = jnp.mean(scaled * unit, axis=-1, keepdims=True)
    return inverse * (scaled - mean_one - unit * mean_two), grad_out * unit


def gelu_both(inputs):
    square = inputs * inputs
    tanh = jnp.tanh(inputs * (GELU + (0.044715 * GELU) * square))
    half = 0.5 + 0.5 * tanh
    act = inputs * half
    return act, half + act * ((1.0 - tanh) * (GELU + (3 * 0.044715 * GELU) * square))


def mask_keys(scores, tokens):
    rows = scores.shape[0]
    whole = IMG_TOK // 8 * 8
    position = whole + lax.broadcasted_iota(jnp.int32, (rows - whole, 1), 0)
    return jnp.concatenate(
        [scores[:whole], jnp.where(position < tokens, scores[whole:], MASKED / SCORE)], axis=0
    )


def whole(shape):
    return pl.BlockSpec(shape, lambda i, s: (0,) * len(shape), pipeline_mode=pl.Buffered(1))


def held(shape):
    return pl.BlockSpec(shape, lambda i, s: (0,) * len(shape))


def stepped(shape):
    return pl.BlockSpec((1,) + shape, lambda i, s: (i,) + (0,) * len(shape))


def low_of(*shape):
    return jax.ShapeDtypeStruct(shape, LOW)


def f32_of(*shape):
    return jax.ShapeDtypeStruct(shape, F32)


def call(kernel, where, steps, ins, outs, scratch, flops=0, bytes_accessed=0, transcendentals=0, aliases=None,
         after=()):
    given = 1 + len(ins)
    ins = ins + [(pl.BlockSpec(memory_space=pl.ANY), array) for array in after]

    def run(*refs):
        kernel(*refs[:given], *refs[given + len(after) :])

    return pl.pallas_call(
        run,
        name=getattr(kernel, "func", kernel).__name__.removesuffix("_kernel"),
        grid_spec=pltpu.PrefetchScalarGridSpec(
            num_scalar_prefetch=1,
            grid=(steps,),
            in_specs=[spec for spec, _ in ins],
            out_specs=[spec for spec, _ in outs],
            scratch_shapes=scratch,
        ),
        out_shape=[shape for _, shape in outs],
        input_output_aliases=aliases or {},
        compiler_params=pltpu.CompilerParams(vmem_limit_bytes=VMEM),
        cost_estimate=pl.CostEstimate(
            flops=int(COST[getattr(kernel, "func", kernel).__name__] * SCALE), bytes_accessed=1, transcendentals=0
        ),
    )(where, *[array for _, array in ins])


def turn_part(values, turned, step):
    size = values.shape[1] // 3
    at = pl.ds(pl.multiple_of(jnp.minimum(step, 2) * size, 128), size)
    turned[at, :] = values[:, at].T


def pack_kernel(units, where, qkv_ref, out_ref, up_ref, down_ref, own_attn, other_attn, own_mlp, other_mlp):
    qkv, out = qkv_ref[0].astype(LOW), out_ref[0].astype(LOW)
    up, down = up_ref[0].astype(LOW), down_ref[0].astype(LOW)

    def half(values, number):
        size = values.shape[1] // 2
        return values[:, number * size : (number + 1) * size]

    for number in range(2):
        up_h, down_h = half(up, number), half(down, number)
        attn = [half(qkv, number), half(out, number), up_h[:, units:], down_h[:, units:]]
        used = sum(piece.shape[1] for piece in attn)
        attn.append(jnp.zeros((qkv.shape[0], own_attn.shape[1] - used), LOW))
        attn = jnp.concatenate(attn, axis=1)
        mlp = jnp.concatenate([up_h[:, :units], down_h[:, :units]], axis=1)

        @pl.when(where[3] == number)
        def _():
            own_attn[...] = attn
            own_mlp[...] = mlp

        @pl.when(where[3] != number)
        def _():
            other_attn[...] = attn
            other_mlp[...] = mlp


def attn_forward_kernel(spread, joined, tail_units, where, *refs):
    refs = list(refs)
    count = len(spread.weight_keys)
    if joined:
        base_ref, own_ref, other_ref, old_ref = refs[:4]
        del refs[:4]
    else:
        own_ref, other_ref = refs[:2]
        del refs[:2]
    vec_ref, bias_ref = refs[:2]
    w_refs = refs[2 : 2 + count]
    (stream_ref, turned_ref, qkv_ref, mixed_ref, sums_ref, tail_ref, part_ref, total, held_weight, normed) = refs[
        2 + count :
    ]
    step = pl.program_id(0)

    @pl.when(step == 0)
    def _():
        if not joined:
            half = own_ref.shape[0]
            stream_ref[pl.ds(pl.multiple_of(where[3] * half, 8), half), :] = own_ref[...]
            stream_ref[pl.ds(pl.multiple_of((1 - where[3]) * half, 8), half), :] = other_ref[...]

        if joined:
            branch = own_ref[...].astype(F32) + other_ref[...].astype(F32)
            stream_ref[...] = base_ref[...] + branch + old_ref[0, 7:8, :]
        unit, _ = norm_parts(stream_ref[...])
        normed[...] = (unit * vec_ref[0, 0:1, :] + vec_ref[0, 1:2, :]).astype(LOW)

    weight = spread.load(w_refs, where, held_weight)
    tokens = where[4]
    head_columns = 3 * HD
    local = qkv_ref.shape[2]
    heads = local // head_columns
    bias = []
    for head in range(heads):
        at = head * HD
        query_bias, value_bias = bias_ref[0, 0, 0, :, at : at + HD], bias_ref[0, 1, 0, :, at : at + HD]
        bias += [query_bias, jnp.zeros_like(query_bias), value_bias]
    bias = jnp.concatenate(bias, axis=1)
    qkv = (cdot(normed[...], weight[:, :local]) + bias).astype(LOW)
    qkv_ref[0] = qkv
    mixed = []
    for head in range(heads):
        at = head * head_columns
        query = qkv[:, at : at + HD]
        key = qkv[:, at + HD : at + 2 * HD]
        value = qkv[:, at + 2 * HD : at + 3 * HD]
        scores = mask_keys(cdot(key, query, 1, 1), tokens)
        top = jnp.max(scores, axis=0, keepdims=True)
        raised = jnp.exp2((scores - top) * POWER)
        weight_sum = jnp.sum(raised, axis=0, keepdims=True)
        mixed.append(cdot(value, raised.astype(LOW), 0, 0) * (1.0 / weight_sum))
        sums_ref[0, head : head + 1, :] = top * POWER + jnp.log2(weight_sum)
    mixed = jnp.concatenate(mixed, axis=0).T.astype(LOW)
    mixed_ref[0] = mixed
    at = local + mixed.shape[1]
    part = cdot(mixed, weight[:, local:at], 1, 1)

    @pl.when(step == 0)
    def _():
        total[...] = part

    @pl.when(step > 0)
    def _():
        total[...] += part

    tail_ref[0] = weight[:, at : at + 2 * tail_units]

    @pl.when(step == pl.num_programs(0) - 1)
    def _():
        part_ref[...] = total[...].astype(LOW)
        turned_ref[...] = normed[...].T


def mlp_forward_kernel(spread, where, *refs):
    count = len(spread.weight_keys)
    base_ref, own_ref, other_ref, vec_ref, bias_ref, tail_ref, tail_bias_ref = refs[:7]
    w_refs = refs[7 : 7 + count]
    (middle_ref, turned_ref, act_ref, slope_ref, act_tail_ref, slope_tail_ref, up_tail_ref, down_tail_ref,
     part_ref, total, held_weight, normed) = refs[7 + count :]
    step = pl.program_id(0)

    @pl.when(step == 0)
    def _():
        branch = own_ref[...].astype(F32) + other_ref[...].astype(F32)
        middle = base_ref[...] + branch + vec_ref[0, 4:5, :]
        middle_ref[...] = middle
        unit, _ = norm_parts(middle)
        normed[...] = (unit * vec_ref[0, 5:6, :] + vec_ref[0, 6:7, :]).astype(LOW)
        steps, _, both = tail_ref.shape
        half = both // 2
        up_tail_ref[...] = jnp.concatenate([tail_ref[t, :, :half] for t in range(steps)], axis=1)
        down_tail_ref[...] = jnp.concatenate([tail_ref[t, :, half:] for t in range(steps)], axis=1)
        act, slope = gelu_both(cdot(normed[...], up_tail_ref[...]) + tail_bias_ref[0, 0])
        act = act.astype(LOW)
        act_tail_ref[...] = act
        slope_tail_ref[...] = slope.astype(LOW)
        total[...] = cdot(act, down_tail_ref[...], 1, 1)

    weight = spread.load(w_refs, where, held_weight)
    units = act_ref.shape[2]
    act, slope = gelu_both(cdot(normed[...], weight[:, :units]) + bias_ref[0, 0, 0])
    act = act.astype(LOW)
    act_ref[0] = act
    slope_ref[0] = slope.astype(LOW)
    total[...] += cdot(act, weight[:, units:], 1, 1)

    @pl.when(step == pl.num_programs(0) - 1)
    def _():
        part_ref[...] = total[...].astype(LOW)
        turned_ref[...] = normed[...].T


def mlp_backward_kernel(spread, where, *refs):
    count = len(spread.weight_keys)
    grad_ref, slope_ref, up_tail_ref, down_tail_ref, slope_tail_ref = refs[:5]
    w_refs = refs[5 : 5 + count]
    (hidden_ref, hidden_tail_ref, sums_ref, sums_tail_ref, part_ref, turned_ref, low, total, held_weight) = refs[
        5 + count :
    ]
    step = pl.program_id(0)

    @pl.when(step == 0)
    def _():
        low[...] = grad_ref[...].astype(LOW)
        hidden = cdot(low[...], down_tail_ref[...]) * slope_tail_ref[...].astype(F32)
        sums_tail_ref[...] = jnp.sum(hidden, axis=0, keepdims=True)
        hidden = hidden.astype(LOW)
        hidden_tail_ref[...] = hidden
        total[...] = cdot(hidden, up_tail_ref[...], 1, 1)

    weight = spread.load(w_refs, where, held_weight)
    units = hidden_ref.shape[2]
    turn_part(low, turned_ref, step)
    hidden = cdot(low[...], weight[:, units:]) * slope_ref[0].astype(F32)
    sums_ref[0] = jnp.sum(hidden, axis=0, keepdims=True)
    hidden = hidden.astype(LOW)
    hidden_ref[0] = hidden
    total[...] += cdot(hidden, weight[:, :units], 1, 1)

    @pl.when(step == pl.num_programs(0) - 1)
    def _():
        part_ref[...] = total[...].astype(LOW)


def mlp_grads_kernel(spread, where, *refs):
    count = len(spread.grad_keys)
    grad_turned, normed_turned, hidden_ref, act_ref, hidden_tail_ref, act_tail_ref = refs[:6]
    out_refs = refs[6 : 6 + count]
    tail_ref, result = refs[6 + count :]
    step = pl.program_id(0)

    @pl.when(step == 0)
    def _():
        up_tail = cdot(normed_turned[...], hidden_tail_ref[...]).astype(LOW)
        down_tail = cdot(grad_turned[...], act_tail_ref[...]).astype(LOW)
        steps, _, both = tail_ref.shape
        half = both // 2
        for t in range(steps):
            at = slice(t * half, (t + 1) * half)
            tail_ref[t] = jnp.concatenate([up_tail[:, at], down_tail[:, at]], axis=1)

    units = hidden_ref.shape[2]
    result[:, :units] = cdot(normed_turned[...], hidden_ref[0]).astype(LOW)
    result[:, units:] = cdot(grad_turned[...], act_ref[0]).astype(LOW)
    spread.store(out_refs, where, result)


def attn_backward_kernel(spread, where, *refs):
    count = len(spread.weight_keys)
    grad_ref, own_ref, other_ref, middle_ref, vec_ref, qkv_ref, sums_ref = refs[:7]
    w_refs = refs[7 : 7 + count]
    dmiddle_ref, norm_sums_ref, dqkv_ref, head_sums_ref, part_ref, low, total, held_weight = refs[7 + count :]
    step = pl.program_id(0)

    @pl.when(step == 0)
    def _():
        grad = grad_ref[...]
        dnormed = own_ref[...].astype(F32) + other_ref[...].astype(F32)
        inner, gain_terms = norm_backward(dnormed, middle_ref[...], vec_ref[0, 5:6, :])
        dmiddle = grad + inner
        dmiddle_ref[...] = dmiddle
        low[...] = dmiddle.astype(LOW)
        for number, terms in enumerate((gain_terms, dnormed, grad, dmiddle)):
            norm_sums_ref[number : number + 1, :] = jnp.sum(terms, axis=0, keepdims=True)

    weight = spread.load(w_refs, where, held_weight)
    tokens = where[4]
    head_columns = 3 * HD
    local = qkv_ref.shape[2]
    heads = local // head_columns
    qkv = qkv_ref[0]
    dmixed = cdot(low[...], weight[:, local : local + heads * HD]).astype(LOW)
    pieces = []
    for head in range(heads):
        at = head * head_columns
        query = qkv[:, at : at + HD]
        key = qkv[:, at + HD : at + 2 * HD]
        value = qkv[:, at + 2 * HD : at + 3 * HD]
        grad = dmixed[:, head * HD : (head + 1) * HD]
        scores = mask_keys(cdot(key, query, 1, 1), tokens)
        probs = jnp.exp2(scores * POWER - sums_ref[0, head : head + 1, :])
        dprobs = cdot(value, grad, 1, 1)
        row_dot = jnp.sum(dprobs * probs, axis=0, keepdims=True)
        dscores = (probs * (dprobs - row_dot)).astype(LOW)
        pieces.append(cdot(key, dscores, 0, 0).T * SCORE)
        pieces.append(cdot(dscores, query) * SCORE)
        pieces.append(cdot(probs.astype(LOW), grad))
    dqkv = jnp.concatenate(pieces, axis=1)
    head_sums_ref[0] = jnp.sum(dqkv, axis=0, keepdims=True)
    dqkv = dqkv.astype(LOW)
    dqkv_ref[0] = dqkv
    part = cdot(dqkv, weight[:, :local], 1, 1)

    @pl.when(step == 0)
    def _():
        total[...] = part

    @pl.when(step > 0)
    def _():
        total[...] += part

    @pl.when(step == pl.num_programs(0) - 1)
    def _():
        part_ref[...] = total[...].astype(LOW)


def attn_grads_kernel(spread, where, *refs):
    count = len(spread.grad_keys)
    dmiddle_ref, normed_turned, dqkv_ref, mixed_ref, tail_ref = refs[:5]
    out_refs = refs[5 : 5 + count]
    result, grad_turned = refs[5 + count :]

    @pl.when(pl.program_id(0) == 0)
    def _():
        grad_turned[...] = dmiddle_ref[...].astype(LOW).T

    parts = [
        cdot(normed_turned[...], dqkv_ref[0]).astype(LOW),
        cdot(grad_turned[...], mixed_ref[0]).astype(LOW),
        tail_ref[0],
    ]
    used = sum(part.shape[1] for part in parts)
    parts.append(jnp.zeros((result.shape[0], result.shape[1] - used), LOW))
    result[...] = jnp.concatenate(parts, axis=1)
    spread.store(out_refs, where, result)


def norm_backward_kernel(where, dmiddle_ref, own_ref, other_ref, stream_ref, vec_ref, out_ref, sums_ref):
    dnormed = own_ref[...].astype(F32) + other_ref[...].astype(F32)
    inner, gain_terms = norm_backward(dnormed, stream_ref[...], vec_ref[0, 0:1, :])
    out_ref[...] = dmiddle_ref[...] + inner

    @pl.when(pl.program_id(0) == 0)
    def _():
        sums_ref[...] = jnp.zeros_like(sums_ref)

    sums_ref[0:1, :] += jnp.sum(gain_terms, axis=0, keepdims=True)
    sums_ref[1:2, :] += jnp.sum(dnormed, axis=0, keepdims=True)


def adam_kernel(units, local, out_local, tail_units, where, *refs):
    attn_own, attn_other, mlp_own, mlp_other = refs[:4]
    states = [refs[4 + 3 * k : 7 + 3 * k] for k in range(4)]
    outs = refs[len(refs) - 16 :]

    def pair(own, other):
        own, other = own[...].astype(F32), other[...].astype(F32)
        low_core = where[3] == 0
        return jnp.where(low_core, own, other), jnp.where(low_core, other, own)

    attn = pair(attn_own, attn_other)
    mlp = pair(mlp_own, mlp_other)
    at = local + out_local
    grads = [
        jnp.concatenate([half[:, :local] for half in attn], axis=1),
        jnp.concatenate([half[:, local:at] for half in attn], axis=1),
        jnp.concatenate(
            [piece for m, n in zip(mlp, attn) for piece in (m[:, :units], n[:, at : at + tail_units])], axis=1
        ),
        jnp.concatenate(
            [
                piece
                for m, n in zip(mlp, attn)
                for piece in (m[:, units:], n[:, at + tail_units : at + 2 * tail_units])
            ],
            axis=1,
        ),
    ]
    for number, grad in enumerate(grads):
        weight, first, second = [ref[0] for ref in states[number]]
        new = adam_step(weight, grad, first, second, RATES[number], DECAY)
        for ref, values in zip(outs[4 * number : 4 * number + 4], (grad, new[1], new[2], new[0])):
            ref[0] = values


def vec_pack_kernel(where, *refs):
    out_ref = refs[-1]
    layers = out_ref.shape[0]
    out_ref[...] = jnp.zeros_like(out_ref)
    for layer in range(layers):
        one_ref, two_ref, head_ref, main_ref, tail_ref = refs[5 * layer : 5 * layer + 5]
        out_ref[layer, 0:2, :] = one_ref[0:2, :]
        out_ref[layer, 2:6, :] = two_ref[0:4, :]
        for t in range(head_ref.shape[0]):
            out_ref[layer, 8 + t : 9 + t, : head_ref.shape[2]] = head_ref[t]
            out_ref[layer, 16 + t : 17 + t, : main_ref.shape[2]] = main_ref[t]
        out_ref[layer, 6:7, : tail_ref.shape[1]] = tail_ref[...]


def vec_kernel(steps, local, units, tail_units, where, own_ref, other_ref, vec_ref, first_ref, second_ref,
               grad_out, first_out, second_out, weight_out):
    low_core = where[3] == 0
    for layer in range(vec_ref.shape[0]):
        own, other = own_ref[layer], other_ref[layer]
        cores = jnp.where(low_core, own, other), jnp.where(low_core, other, own)
        norms = cores[0][0:6]
        heads = local // (3 * HD)

        def head_piece(kind):
            return [
                core[8 + t : 9 + t, (3 * head + kind) * HD : (3 * head + kind + 1) * HD]
                for t in range(steps)
                for core in cores
                for head in range(heads)
            ]

        hidden = [
            piece
            for t in range(steps)
            for core in cores
            for piece in (core[16 + t : 17 + t, :units], core[6:7, t * tail_units : (t + 1) * tail_units])
        ]
        grad = jnp.concatenate(
            [norms[0:1], norms[1:2], *head_piece(0), *head_piece(2),
             norms[5:6], norms[2:3], norms[3:4], norms[4:5], *hidden],
            axis=1,
        )
        at = slice(layer, layer + 1)
        new = adam_step(vec_ref[at, :], grad, first_ref[at, :], second_ref[at, :], RATES[4], 0.0)
        grad_out[at, :] = grad
        first_out[at, :] = new[1]
        second_out[at, :] = new[2]
        weight_out[at, :] = new[0]


def plane_sides(chips):
    side = math.isqrt(chips)
    while chips % side:
        side -= 1
    return side, chips // side


class Place:
    def __init__(self):
        self.nf = lax.axis_size("fsdp")
        self.nt = lax.axis_size("tp")
        self.na, self.nb = plane_sides(self.nf // 2)
        fi = lax.axis_index("fsdp")
        self.core = fi % 2
        self.a = (fi // 2) // self.nb
        self.b = (fi // 2) % self.nb
        self.t = lax.axis_index("tp")
        self.size = {"a": self.na, "b": self.nb, "t": self.nt}
        self.at = {"a": self.a, "b": self.b, "t": self.t}

    def pairs(self, axis, move):
        if axis == "t":
            return [(i, move(i)) for i in range(self.nt)]
        found = []
        for f in range(self.nf):
            place = {"a": f // 2 // self.nb, "b": f // 2 % self.nb, "core": f % 2}
            place[axis] = move(place[axis])
            found.append((f, (place["a"] * self.nb + place["b"]) * 2 + place["core"]))
        return found

    def send(self, values, axis, move):
        return lax.ppermute(values, "tp" if axis == "t" else "fsdp", self.pairs(axis, move))

    def sibling(self, values):
        return self.send(values, "core", lambda i: 1 - i)

    def swap_rows(self, values):
        pairs = []
        for f in range(self.nf):
            for t in range(self.nt):
                if f % 2 != t % 2:
                    sign = 1 if t % 2 else -1
                    pairs.append((f * self.nt + t, (f + sign) * self.nt + t - sign))
        arrived = lax.ppermute(values.astype(LOW), ("fsdp", "tp"), pairs).astype(F32)
        return jnp.where(self.core != self.t % 2, arrived, values)

    def gather_axis(self, block, axis):
        n = self.size[axis]
        return [block] + [self.send(block, axis, lambda i, k=k: (i - k) % n) for k in range(1, n)]

    def scatter_axis(self, parts, axis):
        n = self.size[axis]
        sent = [self.send(parts[k], axis, lambda i, k=k: (i + k) % n) for k in range(1, n)]
        return [parts[0], *sent]


def split_pair(place, first, second):
    return (
        jnp.where(place.core == 0, first, second),
        jnp.where(place.core == 0, second, first),
    )


def sum_kernel(outputs, where, *refs):
    count = sum(size for sizes in outputs for size in sizes)
    ins, outs = refs[:count], refs[count:]
    for out_ref, sizes in zip(outs, outputs):
        for number, size in enumerate(sizes):
            total = ins[0][0, 0].astype(F32)
            for ref in ins[1:size]:
                total += ref[0, 0].astype(F32)
            ins = ins[size:]
            out_ref[0, number] = total.astype(LOW)


def tie_kernel(where, *refs):
    pass


def tie(where, arrays, after):
    space = pl.BlockSpec(memory_space=pl.ANY)
    return call(
        tie_kernel,
        where,
        1,
        [(space, x) for x in arrays],
        [(space, jax.ShapeDtypeStruct(x.shape, x.dtype)) for x in arrays],
        [],
        aliases={1 + k: k for k in range(len(arrays))},
        after=after,
    )


class Spread:
    def __init__(self, place, rows, columns, middle):
        self.place, self.rows, self.columns = place, rows, columns
        self.middle = middle
        self.direct = rows % 16 == 0
        self.width = place.na * place.nb * 2 * rows
        na, nb = place.na, place.nb
        self.grad_keys = [[(0, a, b) for b in range(nb)] for a in range(na)]
        self.grad_keys += [[(1, a, b) for a in range(na)] for b in range(nb)]
        self.gather_keys = [[(0, 0, 0), (1, 0, 0)]]
        self.gather_keys += [[(0, 0, b), (1, 0, b)] for b in range(1, nb)]
        self.gather_keys += [[(0, a, 0), (1, a, 0)] for a in range(1, na)]
        self.gather_keys += [[(half, a, b)] for half in range(2) for a in range(1, na) for b in range(1, nb)]
        if middle:
            self.gather_keys = self.grad_keys
        self.weight_keys = self.gather_keys
        if not self.direct:
            self.weight_keys = self.grad_keys = [None]

    def shapes(self, keys):
        if not self.direct:
            return [(self.place.nt, self.width, self.columns)]
        return [(self.place.nt, len(blocks), self.rows, self.columns) for blocks in keys]

    def specs(self, keys):
        return [stepped(shape[1:]) for shape in self.shapes(keys)]

    def first_row(self, where, key):
        half, a, b = key
        a = lax.rem(where[0] + a, self.place.na)
        b = lax.rem(where[1] + b, self.place.nb)
        return pl.multiple_of(((a * self.place.nb + b) * 2 + half) * self.rows, 16)

    def load(self, refs, where, scratch):
        if not self.direct:
            return refs[0].at[0]
        for ref, blocks in zip(refs, self.weight_keys):
            for number, key in enumerate(blocks):
                scratch[pl.ds(self.first_row(where, key), self.rows), :] = ref[0, number]
        return scratch

    def store(self, refs, where, scratch):
        if not self.direct:
            refs[0][0] = scratch[...]
            return
        for ref, blocks in zip(refs, self.grad_keys):
            for number, key in enumerate(blocks):
                ref[0, number] = scratch[pl.ds(self.first_row(where, key), self.rows), :]

    def start(self, own, other):
        place = self.place
        halves = split_pair(place, own, other)
        if self.middle:
            return [jnp.stack(place.gather_axis(half, axis)) for half, axis in zip(halves, "ba")]
        return [jnp.stack(halves)]

    def gather(self, where, blocks, after=()):
        place = self.place
        na, nb = place.na, place.nb
        blocks = [lax.all_gather(block, "tp") for block in blocks]
        if self.direct and len(after):
            blocks = tie(where, blocks, after)
        if self.middle:
            arrays = [array for block, axis in zip(blocks, "ab") for array in place.gather_axis(block, axis)]
        else:
            along_b = place.gather_axis(blocks[0], "b")
            along_a = place.gather_axis(blocks[0], "a")
            first = [place.gather_axis(x[:, :1], "a")[1:] for x in along_b[1:]]
            second = [place.gather_axis(x[:, 1:], "b")[1:] for x in along_a[1:]]
            arrays = along_b + along_a[1:]
            arrays += [first[b][a] for a in range(na - 1) for b in range(nb - 1)]
            arrays += [second[a][b] for a in range(na - 1) for b in range(nb - 1)]
        if self.direct:
            return arrays
        found = {
            key: array[:, number]
            for array, keys in zip(arrays, self.gather_keys)
            for number, key in enumerate(keys)
        }
        full = jnp.stack([found[half, a, b] for a in range(na) for b in range(nb) for half in range(2)], axis=1)
        full = full.reshape(place.nt, na, nb, 2, self.rows, self.columns)
        full = self.roll(full, (na - place.a) % na, (nb - place.b) % nb)
        return [full.reshape(place.nt, self.width, self.columns)]

    def roll(self, full, a, b):
        full = lax.dynamic_slice_in_dim(jnp.concatenate([full, full], axis=1), a, self.place.na, 1)
        return lax.dynamic_slice_in_dim(jnp.concatenate([full, full], axis=2), b, self.place.nb, 2)

    def sums(self, where, outputs, after):
        place, rows, columns = self.place, self.rows, self.columns

        def block(number):
            return pl.BlockSpec((1, 1, rows, columns), lambda i, s: (i, number, 0, 0))

        shapes = [(place.nt, len(groups), rows, columns) for groups in outputs]
        return call(
            functools.partial(sum_kernel, [[len(group) for group in groups] for groups in outputs]),
            where,
            place.nt,
            [(block(number), x) for groups in outputs for group in groups for x, number in group],
            [(stepped(shape[1:]), low_of(*shape)) for shape in shapes],
            [],
            after=after,
        )

    def scatter_last(self, arrays):
        place = self.place
        if not self.direct:
            full = arrays[0].reshape(place.nt, place.na, place.nb, 2, self.rows, self.columns)
            full = self.roll(full, place.a, place.b)
            arrays = [full[:, a, :, 0] for a in range(place.na)] + [full[:, :, b, 1] for b in range(place.nb)]
        return (
            place.scatter_axis(arrays[: place.na], "a"),
            place.scatter_axis(arrays[place.na :], "b"),
        )

    def scatter_first(self, where, halves, after):
        place = self.place
        if self.middle:
            outputs = [[[(x, k) for x in half] for k in range(half[0].shape[1])] for half in halves]
            results = self.sums(where, outputs, after)
            return results[0], [lax.psum_scatter(x, "tp", scatter_dimension=0, tiled=True)[0] for x in results]
        axes = ("b", "a")
        keys = [(half, k) for half in range(2) for k in range(1, place.size[axes[half]])]
        results = self.sums(where, [[[(x, k) for x in halves[half]]] for half, k in keys], after)
        terms = [[(x, 0) for x in arrays] for arrays in halves]
        for (half, k), total in zip(keys, results):
            n = place.size[axes[half]]
            terms[half].append((place.send(total, axes[half], lambda i: (i + k) % n), 0))
        return results[0], terms

    def scatter_tp(self, where, terms, after):
        place = self.place
        if self.middle:
            if self.direct:
                terms = tie(where, terms, after)
            done = [
                sum(x.astype(F32) for x in place.scatter_axis(list(half), axis)).astype(LOW)
                for half, axis in zip(terms, "ba")
            ]
            last = after[0]
        else:
            (last,) = self.sums(where, [terms], after)
            done = lax.psum_scatter(last, "tp", scatter_dimension=0, tiled=True)[0]
        mine, other = split_pair(place, done[0], done[1])
        return last, (mine, place.sibling(other))


def body(
    residual_in,
    cotangent,
    slot_tokens,
    qkv_weight,
    out_weight,
    up_weight,
    down_weight,
    vectors,
    qkv_first,
    qkv_second,
    out_first,
    out_second,
    up_first,
    up_second,
    down_first,
    down_second,
    vec_first,
    vec_second,
):
    place = Place()
    layer_count, shard_rows, _ = qkv_weight.shape
    half_rows, width = residual_in.shape
    rows = 2 * half_rows
    nt = place.nt
    local = qkv_weight.shape[2] // 2
    out_local = out_weight.shape[1] // 2
    hidden_local = up_weight.shape[2] // 2
    units = hidden_local // 128 * 128
    tail_units = hidden_local - units
    heads = out_local // HD
    attn_columns = -(-(local + out_local + 2 * tail_units) // 128) * 128
    mlp_columns = 2 * units

    tokens_pair = jnp.concatenate(split_pair(place, slot_tokens, place.sibling(slot_tokens)))
    slot_at = (place.t % 2) * slot_tokens.shape[0] + place.t // 2
    tokens = lax.dynamic_slice_in_dim(tokens_pair, slot_at, 1)
    row_mask = (jnp.arange(rows, dtype=jnp.int32) < tokens[0]).astype(F32)[:, None]
    here = jnp.stack([place.a, place.b, place.t, place.core]).astype(jnp.int32)
    where = jnp.concatenate([here, tokens.astype(jnp.int32)])

    def own_rows(values):
        return lax.dynamic_slice_in_dim(values, place.core * half_rows, half_rows)

    spreads = [
        (
            Spread(place, shard_rows, attn_columns, False),
            Spread(place, shard_rows, mlp_columns, layer > 0),
        )
        for layer in range(layer_count)
    ]

    def turn(arrays):
        qkv, out, up, down = arrays
        return qkv, jnp.swapaxes(out, 1, 2), up, jnp.swapaxes(down, 1, 2)

    weights = turn((qkv_weight, out_weight, up_weight, down_weight))
    firsts = turn((qkv_first, out_first, up_first, down_first))
    seconds = turn((qkv_second, out_second, up_second, down_second))

    def layer_block(array, layer, steps=1):
        block = (1, array.shape[1] // steps, array.shape[2])
        return pl.BlockSpec(block, lambda i, s: (layer, i, 0))

    def pack(layer):
        attn, mlp = (shard_rows, attn_columns), (shard_rows, mlp_columns)
        return call(
            functools.partial(pack_kernel, units),
            here,
            1,
            [(layer_block(w, layer), w) for w in weights],
            [(held(shape), low_of(*shape)) for shape in (attn, attn, mlp, mlp)],
            [],
            bytes_accessed=6 * shard_rows * 13216 // 4,
        )

    starts = []
    for layer in range(layer_count):
        own_attn, other_attn, own_mlp, other_mlp = pack(layer)
        starts.append(
            (
                spreads[layer][0].start(own_attn, place.sibling(other_attn)),
                spreads[layer][1].start(own_mlp, place.sibling(other_mlp)),
            )
        )
    gathered = []
    before = [x for pair in starts[1:] for blocks in pair for x in blocks]
    for layer in range(layer_count):
        attn_full = spreads[layer][0].gather(where, starts[layer][0], before)
        mlp_full = spreads[layer][1].gather(where, starts[layer][1], attn_full[1:3])
        before = mlp_full[1:3]
        gathered.append((attn_full, mlp_full))

    wide = vectors[:, : 8 * width].reshape(layer_count, 8, width)
    head_bias = vectors[:, 2 * width : 4 * width].reshape(layer_count, 2, 2 * nt, 1, out_local)
    hidden_bias = vectors[:, 8 * width :].reshape(layer_count, nt, 2, 1, hidden_local)
    main_bias = hidden_bias[..., :units]
    tail_bias = jnp.moveaxis(hidden_bias[..., units:], 1, 3).reshape(layer_count, 2, 1, nt * tail_units)

    full = whole((rows, width))
    weight_scratch = [
        pltpu.VMEM((width, attn_columns), LOW),
        pltpu.VMEM((width, mlp_columns), LOW),
    ]
    flat = pltpu.VMEM((rows, width), F32)
    flat_low = pltpu.VMEM((rows, width), LOW)
    big = 2 * rows * width

    def wide_of(layer):
        spec = pl.BlockSpec((1, 8, width), lambda i, s: (layer, 0, 0), pipeline_mode=pl.Buffered(1))
        return spec, wide

    def attn_forward(layer, base, own, other):
        spread = spreads[layer][0]
        joined = base is not None
        if joined:
            ins = [(full, base), (full, own), (full, other), wide_of(layer - 1)]
        else:
            half = whole((half_rows, width))
            ins = [(half, own), (half, other)]
        ins.append(wide_of(layer))
        ins.append(
            (
                pl.BlockSpec(
                    (1, 2, 1, 1, out_local), lambda i, s: (layer, 0, 2 * i + s[3], 0, 0)
                ),
                head_bias,
            )
        )
        ins += list(zip(spread.specs(spread.weight_keys), gathered[layer][0]))
        return call(
            functools.partial(attn_forward_kernel, spread, joined, tail_units),
            where,
            nt,
            ins,
            [
                (held((rows, width)), f32_of(rows, width)),
                (held((width, rows)), low_of(width, rows)),
                (stepped((rows, local)), low_of(nt, rows, local)),
                (stepped((rows, out_local)), low_of(nt, rows, out_local)),
                (stepped((heads, rows)), f32_of(nt, heads, rows)),
                (stepped((width, 2 * tail_units)), low_of(nt, width, 2 * tail_units)),
                (held((rows, width)), low_of(rows, width)),
            ],
            [flat, weight_scratch[0], flat_low],
            big * nt * (local + out_local) + 4 * nt * heads * rows * rows * HD,
            rows * width * 12 + nt * width * attn_columns * 2,
            nt * heads * rows * rows,
        )

    def mlp_forward(layer, base, own, other, tails, after=()):
        spread = spreads[layer][1]
        tail = nt * tail_units
        tail_shape = (width, tail)
        ins = [
            (full, base),
            (full, own),
            (full, other),
            wide_of(layer),
            (pl.BlockSpec((1, 1, 1, 1, units), lambda i, s: (layer, i, s[3], 0, 0)), main_bias),
            (whole(tails.shape), tails),
            (pl.BlockSpec((1, 1, 1, tail), lambda i, s: (layer, s[3], 0, 0)), tail_bias),
        ]
        ins += list(zip(spread.specs(spread.weight_keys), gathered[layer][1]))
        return call(
            functools.partial(mlp_forward_kernel, spread),
            where,
            nt,
            ins,
            [
                (held((rows, width)), f32_of(rows, width)),
                (held((width, rows)), low_of(width, rows)),
                (stepped((rows, units)), low_of(nt, rows, units)),
                (stepped((rows, units)), low_of(nt, rows, units)),
                (held((rows, tail)), low_of(rows, tail)),
                (held((rows, tail)), low_of(rows, tail)),
                (held(tail_shape), low_of(*tail_shape)),
                (held(tail_shape), low_of(*tail_shape)),
                (held((rows, width)), low_of(rows, width)),
            ],
            [flat, weight_scratch[1], flat_low],
            2 * big * (nt * units + tail),
            rows * width * 16 + nt * (width + rows) * mlp_columns * 2,
            rows * nt * units,
            after=after,
        )

    def mlp_backward(layer, grad, slope, tails, slope_tail):
        spread = spreads[layer][1]
        tail = nt * tail_units
        ins = [(full, grad), (stepped((rows, units)), slope)]
        ins += [(whole(w.shape), w) for w in (*tails, slope_tail)]
        ins += list(zip(spread.specs(spread.weight_keys), gathered[layer][1]))
        return call(
            functools.partial(mlp_backward_kernel, spread),
            where,
            nt,
            ins,
            [
                (stepped((rows, units)), low_of(nt, rows, units)),
                (held((rows, tail)), low_of(rows, tail)),
                (stepped((1, units)), f32_of(nt, 1, units)),
                (held((1, tail)), f32_of(1, tail)),
                (held((rows, width)), low_of(rows, width)),
                (held((width, rows)), low_of(width, rows)),
            ],
            [flat_low, flat, weight_scratch[1]],
            2 * big * (nt * units + tail),
            rows * width * 6 + nt * (width + rows) * mlp_columns * 2,
        )

    def mlp_grads(layer, grad, normed, hidden, act, hidden_tail, act_tail):
        spread = spreads[layer][1]
        ins = [(whole((width, rows)), grad), (whole((width, rows)), normed)]
        ins += [(stepped((rows, units)), hidden), (stepped((rows, units)), act)]
        ins += [(whole(x.shape), x) for x in (hidden_tail, act_tail)]
        tail_shape = (nt, width, 2 * tail_units)
        outs = [
            (spec, low_of(*shape))
            for spec, shape in zip(spread.specs(spread.grad_keys), spread.shapes(spread.grad_keys))
        ]
        outs.append((held(tail_shape), low_of(*tail_shape)))
        return call(
            functools.partial(mlp_grads_kernel, spread),
            where,
            nt,
            ins,
            outs,
            [weight_scratch[1]],
            2 * big * nt * (units + tail_units),
            rows * width * 6 + nt * (width + rows) * mlp_columns * 2,
        )

    def attn_backward(layer, grad, own, other, middle, qkv, log_sums, after=()):
        spread = spreads[layer][0]
        ins = [(full, grad), (full, own), (full, other), (full, middle), wide_of(layer)]
        ins += [(stepped((rows, local)), qkv), (stepped((heads, rows)), log_sums)]
        ins += list(zip(spread.specs(spread.weight_keys), gathered[layer][0]))
        return call(
            functools.partial(attn_backward_kernel, spread),
            where,
            nt,
            ins,
            [
                (held((rows, width)), f32_of(rows, width)),
                (held((8, width)), f32_of(8, width)),
                (stepped((rows, local)), low_of(nt, rows, local)),
                (stepped((1, local)), f32_of(nt, 1, local)),
                (held((rows, width)), low_of(rows, width)),
            ],
            [flat_low, flat, weight_scratch[0]],
            big * nt * (local + out_local) + 10 * nt * heads * rows * rows * HD,
            rows * width * 20 + nt * width * attn_columns * 2,
            nt * heads * rows * rows,
            after=after,
        )

    def attn_grads(layer, dmiddle, normed, dqkv, mixed, tail_grads):
        spread = spreads[layer][0]
        ins = [(full, dmiddle), (whole((width, rows)), normed)]
        ins += [(stepped((rows, local)), dqkv), (stepped((rows, out_local)), mixed)]
        ins.append((stepped((width, 2 * tail_units)), tail_grads))
        outs = [
            (spec, low_of(*shape))
            for spec, shape in zip(spread.specs(spread.grad_keys), spread.shapes(spread.grad_keys))
        ]
        return call(
            functools.partial(attn_grads_kernel, spread),
            where,
            nt,
            ins,
            outs,
            [weight_scratch[0], pltpu.VMEM((width, rows), LOW)],
            big * nt * (local + out_local),
            rows * width * 6 + nt * (width + rows) * attn_columns * 2,
        )

    def norm_one_backward(layer, dmiddle, own, other, stream, after=()):
        part = pl.BlockSpec((half_rows, width), lambda i, s: (i, 0))
        return call(
            norm_backward_kernel,
            where,
            2,
            [(part, dmiddle), (part, own), (part, other), (part, stream), wide_of(layer)],
            [(part, f32_of(rows, width)), (held((8, width)), f32_of(8, width))],
            [],
            rows * width * 20,
            rows * width * 16,
            after=after,
        )

    grad_stream = None
    mine = place.swap_rows(residual_in)
    base, own, other = None, mine, place.sibling(mine)
    saved = []
    for layer in range(layer_count):
        stream, normed, qkv, mixed, log_sums, tails, part = attn_forward(layer, base, own, other)
        if layer == layer_count - 1:
            (mine,) = tie(where, [place.swap_rows(cotangent)], [qkv])
            grad_stream = jnp.concatenate(split_pair(place, mine, place.sibling(mine)), axis=0) * row_mask
        middle, normed_two, act, slope, act_tail, slope_tail, up_tail, down_tail, part = mlp_forward(
            layer, stream, part, place.sibling(part), tails
        )
        saved.append(
            (stream, normed, qkv, mixed, log_sums, middle, normed_two, act, slope, act_tail, slope_tail,
             (up_tail, down_tail))
        )
        base, own, other = middle, part, place.sibling(part)
    output = own_rows(base) + (own_rows(own).astype(F32) + own_rows(other).astype(F32))
    output = place.swap_rows((output + wide[layer_count - 1, 7:8]) * own_rows(row_mask))


    def adam(layer, attn_pair, mlp_pair, before, after=()):
        steps = 1
        ins = [
            (pl.BlockSpec((shard_rows // steps, x.shape[1]), lambda i, s: (i, 0)), x)
            for x in (*attn_pair, *mlp_pair)
        ]
        for states in zip(weights, firsts, seconds):
            ins += [(layer_block(x, layer, steps), x) for x in states]
        outs = [
            (layer_block(weight, layer, steps), f32_of(*weight.shape)) for weight in weights for _ in range(4)
        ]
        aliases = None
        if before is not None:
            aliases = {1 + len(ins) + k: k for k in range(16)}
            ins += [(pl.BlockSpec(memory_space=pl.ANY), x) for x in before]
        return call(
            functools.partial(adam_kernel, units, local, out_local, tail_units),
            where,
            steps,
            ins,
            outs,
            [],
            bytes_accessed=28 * shard_rows * 13216 // 4,
            aliases=aliases,
            after=after,
        )

    vec_sums = [None] * layer_count
    last = grad_stream
    above = None
    for layer in reversed(range(layer_count)):
        (stream, normed, qkv, mixed, log_sums, middle, normed_two, act, slope, act_tail, slope_tail, tails) = (
            saved[layer]
        )
        spread_attn, spread_mlp = spreads[layer]
        hidden, hidden_tail, hidden_sums, tail_sums, part, grad_turned = mlp_backward(
            layer, grad_stream, slope, tails, slope_tail
        )
        other = place.sibling(part)
        *mlp_grad, tail_grads = mlp_grads(
            layer, grad_turned, normed_two, hidden, act, hidden_tail, act_tail
        )
        last = tail_grads
        mlp_terms = spread_mlp.scatter_last(mlp_grad)
        dmiddle, norm_two_sums, dqkv, head_sums, part = attn_backward(
            layer, grad_stream, part, other, middle, qkv, log_sums, [last]
        )
        other = place.sibling(part)
        attn_grad = attn_grads(layer, dmiddle, normed, dqkv, mixed, tail_grads)
        last = attn_grad[0]
        if above:
            last, attn_terms_above = spreads[above][0].scatter_first(where, attn_terms_above, [last, output])
        grad_stream, norm_one_sums = norm_one_backward(layer, dmiddle, part, other, stream, [last])
        if layer:
            attn_terms = spread_attn.scatter_last(attn_grad)
        last, mlp_terms = spread_mlp.scatter_first(where, mlp_terms, [norm_one_sums])
        vec_sums[layer] = (norm_one_sums, norm_two_sums, head_sums, hidden_sums, tail_sums)
        if above:
            grad_input = place.swap_rows(own_rows(grad_stream))
            last, attn_pair_one = spreads[above][0].scatter_tp(where, attn_terms_above, [last, grad_input])
            mlp_terms_one = mlp_terms_above
            if spread_attn.direct:
                attn_grad = tie(where, attn_grad, [last])
            attn_terms = spread_attn.scatter_last(attn_grad)
        above, mlp_terms_above, attn_terms_above = layer, mlp_terms, attn_terms
        if layer:
            grad_stream, last = lax.optimization_barrier((grad_stream, last))
    last, mlp_pair_above = spreads[above][1].scatter_tp(where, mlp_terms_above, [last])
    _, mlp_pair_one = spreads[1][1].scatter_tp(where, mlp_terms_one, [last])
    last, attn_terms_above = spreads[above][0].scatter_first(where, attn_terms_above, [last])
    updated = adam(1, attn_pair_one, mlp_pair_one, None, [last])
    last, attn_pair_above = spreads[above][0].scatter_tp(where, attn_terms_above, [last, updated[0]])

    flat_sums = [x for sums in vec_sums for x in sums]
    vec_shape = (layer_count, 24, width)
    (vec_total,) = call(
        vec_pack_kernel,
        where,
        1,
        [(whole(x.shape), x) for x in flat_sums],
        [(held(vec_shape), f32_of(*vec_shape))],
        [],
        after=[last],
    )
    for axis in ("b", "a", "t"):
        step = 1
        while step < place.size[axis]:
            vec_total = vec_total + place.send(vec_total, axis, lambda i: i ^ step)
            step *= 2
    vec_new = call(
        functools.partial(vec_kernel, nt, local, units, tail_units),
        where,
        1,
        [(whole(x.shape), x) for x in (vec_total, place.sibling(vec_total), vectors, vec_first, vec_second)],
        [(held(vectors.shape), f32_of(*vectors.shape)) for _ in range(4)],
        [],
    )
    updated = adam(above, attn_pair_above, mlp_pair_above, updated)
    updated = [
        jnp.swapaxes(x, 1, 2) if number // 4 % 2 else x for number, x in enumerate(updated)
    ]
    return (output, grad_input, *updated, *vec_new)


def solution(mesh):
    rows = P(("fsdp", "tp"), None)
    wide = P(None, "fsdp", "tp")
    tall = P(None, "tp", "fsdp")
    moments = (wide, wide, tall, tall, wide, wide, tall, tall, P(), P())
    return jax.shard_map(
        body,
        mesh=mesh,
        in_specs=(rows, rows, P("fsdp"), wide, tall, wide, tall, P(), *moments),
        out_specs=(rows, rows, *[wide] * 4, *[tall] * 4, *[wide] * 4, *[tall] * 4, *[P()] * 4),
        check_vma=False,
    )
```

```python
import functools
import math

import jax
import jax.numpy as jnp
from jax import lax
from jax.experimental import pallas as pl
from jax.experimental.pallas import tpu as pltpu
from jax.sharding import PartitionSpec as P

HD = 72
IMG_TOK = 729
STEP = 10


EPS_NORM = 1e-06
MASKED = -30000.0
BETA_ONE = 0.9
BETA_TWO = 0.999
ADAM_EPS = 1e-08
DECAY = 0.1
RATES = (0.05, 1.0, 0.05, 0.03, 0.3)
LOW = jnp.bfloat16
F32 = jnp.float32
GELU = math.sqrt(2.0 / math.pi)
SCORE = HD ** (-0.5)
POWER = SCORE / math.log(2.0)
VMEM = 56 * 1024 * 1024
COST = {
    "pack": 4,
    "attn_forward": 26,
    "mlp_forward": 24,
    "mlp_backward": 17,
    "mlp_grads": 16,
    "attn_backward": 33,
    "attn_grads": 13,
    "norm_backward": 9,
    "sum": 5,
    ("sum", 1): 30,
    "vec_pack": 0.3,
    "vec": 0.3,
    "adam": 1,
    "tie": 1,
}
SCALE = 2e9


def adam_step(weight, gradient, first_moment, second_moment, step_rate, decay_rate):
    first_new = BETA_ONE * first_moment + (1.0 - BETA_ONE) * gradient
    second_new = BETA_TWO * second_moment + (1.0 - BETA_TWO) * gradient * gradient
    first_hat = first_new / (1.0 - BETA_ONE**STEP)
    second_hat = second_new / (1.0 - BETA_TWO**STEP)
    weight_new = weight - step_rate * (
        first_hat / (jnp.sqrt(second_hat) + ADAM_EPS) + decay_rate * weight
    )
    return (weight_new, first_new, second_new)


def cdot(left, right, left_dim=1, right_dim=0):
    return lax.dot_general(
        left, right, (((left_dim,), (right_dim,)), ((), ())), preferred_element_type=F32
    )


def norm_parts(values):
    centred = values - jnp.mean(values, axis=-1, keepdims=True)
    inverse = lax.rsqrt(jnp.mean(centred * centred, axis=-1, keepdims=True) + EPS_NORM)
    return centred * inverse, inverse


def norm_backward(grad_out, values, gain):
    unit, inverse = norm_parts(values)
    scaled = grad_out * gain
    mean_one = jnp.mean(scaled, axis=-1, keepdims=True)
    mean_two = jnp.mean(scaled * unit, axis=-1, keepdims=True)
    return inverse * (scaled - mean_one - unit * mean_two), grad_out * unit


def gelu_both(inputs):
    square = inputs * inputs
    tanh = jnp.tanh(inputs * (GELU + (0.044715 * GELU) * square))
    half = 0.5 + 0.5 * tanh
    act = inputs * half
    return act, half + act * ((1.0 - tanh) * (GELU + (3 * 0.044715 * GELU) * square))


def mask_keys(scores, tokens):
    rows = scores.shape[0]
    whole = IMG_TOK // 8 * 8
    position = whole + lax.broadcasted_iota(jnp.int32, (rows - whole, 1), 0)
    return jnp.concatenate(
        [scores[:whole], jnp.where(position < tokens, scores[whole:], MASKED / SCORE)], axis=0
    )


def whole(shape):
    return pl.BlockSpec(shape, lambda i, s: (0,) * len(shape), pipeline_mode=pl.Buffered(1))


def held(shape):
    return pl.BlockSpec(shape, lambda i, s: (0,) * len(shape))


def stepped(shape):
    return pl.BlockSpec((1,) + shape, lambda i, s: (i,) + (0,) * len(shape))


def low_of(*shape):
    return jax.ShapeDtypeStruct(shape, LOW)


def f32_of(*shape):
    return jax.ShapeDtypeStruct(shape, F32)


def call(kernel, where, steps, ins, outs, scratch, flops=0, bytes_accessed=0, transcendentals=0, aliases=None,
         after=(), layer=None):
    given = 1 + len(ins)
    name = getattr(kernel, "func", kernel).__name__.removesuffix("_kernel")
    ins = ins + [(pl.BlockSpec(memory_space=pl.ANY), array) for array in after]

    def run(*refs):
        kernel(*refs[:given], *refs[given + len(after) :])

    return pl.pallas_call(
        run,
        name=name,
        grid_spec=pltpu.PrefetchScalarGridSpec(
            num_scalar_prefetch=1,
            grid=(steps,),
            in_specs=[spec for spec, _ in ins],
            out_specs=[spec for spec, _ in outs],
            scratch_shapes=scratch,
        ),
        out_shape=[shape for _, shape in outs],
        input_output_aliases=aliases or {},
        compiler_params=pltpu.CompilerParams(vmem_limit_bytes=VMEM),
        cost_estimate=pl.CostEstimate(
            flops=int(COST.get((name, layer), COST[name]) * SCALE), bytes_accessed=1, transcendentals=0
        ),
    )(where, *[array for _, array in ins])


def turn_part(values, turned, step):
    size = values.shape[1] // 3
    at = pl.ds(pl.multiple_of(jnp.minimum(step, 2) * size, 128), size)
    turned[at, :] = values[:, at].T


def pack_kernel(units, where, qkv_ref, out_ref, up_ref, down_ref, own_attn, other_attn, own_mlp, other_mlp):
    qkv, out = qkv_ref[0].astype(LOW), out_ref[0].astype(LOW)
    up, down = up_ref[0].astype(LOW), down_ref[0].astype(LOW)

    def half(values, number):
        size = values.shape[1] // 2
        return values[:, number * size : (number + 1) * size]

    for number in range(2):
        up_h, down_h = half(up, number), half(down, number)
        attn = [half(qkv, number), half(out, number), up_h[:, units:], down_h[:, units:]]
        used = sum(piece.shape[1] for piece in attn)
        attn.append(jnp.zeros((qkv.shape[0], own_attn.shape[1] - used), LOW))
        attn = jnp.concatenate(attn, axis=1)
        mlp = jnp.concatenate([up_h[:, :units], down_h[:, :units]], axis=1)

        @pl.when(where[3] == number)
        def _():
            own_attn[...] = attn
            own_mlp[...] = mlp

        @pl.when(where[3] != number)
        def _():
            other_attn[...] = attn
            other_mlp[...] = mlp


def attn_forward_kernel(spread, joined, tail_units, where, *refs):
    refs = list(refs)
    count = len(spread.weight_keys)
    if joined:
        base_ref, own_ref, other_ref, old_ref = refs[:4]
        del refs[:4]
    else:
        own_ref, other_ref = refs[:2]
        del refs[:2]
    vec_ref, bias_ref = refs[:2]
    w_refs = refs[2 : 2 + count]
    (stream_ref, turned_ref, qkv_ref, mixed_ref, sums_ref, tail_ref, part_ref, total, held_weight, normed) = refs[
        2 + count :
    ]
    step = pl.program_id(0)

    @pl.when(step == 0)
    def _():
        if not joined:
            half = own_ref.shape[0]
            stream_ref[pl.ds(pl.multiple_of(where[3] * half, 8), half), :] = own_ref[...]
            stream_ref[pl.ds(pl.multiple_of((1 - where[3]) * half, 8), half), :] = other_ref[...]

        if joined:
            branch = own_ref[...].astype(F32) + other_ref[...].astype(F32)
            stream_ref[...] = base_ref[...] + branch + old_ref[0, 7:8, :]
        unit, _ = norm_parts(stream_ref[...])
        normed[...] = (unit * vec_ref[0, 0:1, :] + vec_ref[0, 1:2, :]).astype(LOW)

    weight = spread.load(w_refs, where, held_weight)
    tokens = where[4]
    head_columns = 3 * HD
    local = qkv_ref.shape[2]
    heads = local // head_columns
    bias = []
    for head in range(heads):
        at = head * HD
        query_bias, value_bias = bias_ref[0, 0, 0, :, at : at + HD], bias_ref[0, 1, 0, :, at : at + HD]
        bias += [query_bias, jnp.zeros_like(query_bias), value_bias]
    bias = jnp.concatenate(bias, axis=1)
    qkv = (cdot(normed[...], weight[:, :local]) + bias).astype(LOW)
    qkv_ref[0] = qkv
    mixed = []
    for head in range(heads):
        at = head * head_columns
        query = qkv[:, at : at + HD]
        key = qkv[:, at + HD : at + 2 * HD]
        value = qkv[:, at + 2 * HD : at + 3 * HD]
        scores = mask_keys(cdot(key, query, 1, 1), tokens)
        top = jnp.max(scores, axis=0, keepdims=True)
        raised = jnp.exp2((scores - top) * POWER)
        weight_sum = jnp.sum(raised, axis=0, keepdims=True)
        mixed.append(cdot(value, raised.astype(LOW), 0, 0) * (1.0 / weight_sum))
        sums_ref[0, head : head + 1, :] = top * POWER + jnp.log2(weight_sum)
    mixed = jnp.concatenate(mixed, axis=0).T.astype(LOW)
    mixed_ref[0] = mixed
    at = local + mixed.shape[1]
    part = cdot(mixed, weight[:, local:at], 1, 1)

    @pl.when(step == 0)
    def _():
        total[...] = part

    @pl.when(step > 0)
    def _():
        total[...] += part

    tail_ref[0] = weight[:, at : at + 2 * tail_units]

    @pl.when(step == pl.num_programs(0) - 1)
    def _():
        part_ref[...] = total[...].astype(LOW)
        turned_ref[...] = normed[...].T


def mlp_forward_kernel(spread, where, *refs):
    count = len(spread.weight_keys)
    base_ref, own_ref, other_ref, vec_ref, bias_ref, tail_ref, tail_bias_ref = refs[:7]
    w_refs = refs[7 : 7 + count]
    (middle_ref, turned_ref, act_ref, slope_ref, act_tail_ref, slope_tail_ref, up_tail_ref, down_tail_ref,
     part_ref, total, held_weight, normed) = refs[7 + count :]
    step = pl.program_id(0)

    @pl.when(step == 0)
    def _():
        branch = own_ref[...].astype(F32) + other_ref[...].astype(F32)
        middle = base_ref[...] + branch + vec_ref[0, 4:5, :]
        middle_ref[...] = middle
        unit, _ = norm_parts(middle)
        normed[...] = (unit * vec_ref[0, 5:6, :] + vec_ref[0, 6:7, :]).astype(LOW)
        steps, _, both = tail_ref.shape
        half = both // 2
        up_tail_ref[...] = jnp.concatenate([tail_ref[t, :, :half] for t in range(steps)], axis=1)
        down_tail_ref[...] = jnp.concatenate([tail_ref[t, :, half:] for t in range(steps)], axis=1)
        act, slope = gelu_both(cdot(normed[...], up_tail_ref[...]) + tail_bias_ref[0, 0])
        act = act.astype(LOW)
        act_tail_ref[...] = act
        slope_tail_ref[...] = slope.astype(LOW)
        total[...] = cdot(act, down_tail_ref[...], 1, 1)

    weight = spread.load(w_refs, where, held_weight)
    units = act_ref.shape[2]
    act, slope = gelu_both(cdot(normed[...], weight[:, :units]) + bias_ref[0, 0, 0])
    act = act.astype(LOW)
    act_ref[0] = act
    slope_ref[0] = slope.astype(LOW)
    total[...] += cdot(act, weight[:, units:], 1, 1)

    @pl.when(step == pl.num_programs(0) - 1)
    def _():
        part_ref[...] = total[...].astype(LOW)
        turned_ref[...] = normed[...].T


def mlp_backward_kernel(spread, where, *refs):
    count = len(spread.weight_keys)
    grad_ref, slope_ref, up_tail_ref, down_tail_ref, slope_tail_ref = refs[:5]
    w_refs = refs[5 : 5 + count]
    (hidden_ref, hidden_tail_ref, sums_ref, sums_tail_ref, part_ref, turned_ref, low, total, held_weight) = refs[
        5 + count :
    ]
    step = pl.program_id(0)

    @pl.when(step == 0)
    def _():
        low[...] = grad_ref[...].astype(LOW)
        hidden = cdot(low[...], down_tail_ref[...]) * slope_tail_ref[...].astype(F32)
        sums_tail_ref[...] = jnp.sum(hidden, axis=0, keepdims=True)
        hidden = hidden.astype(LOW)
        hidden_tail_ref[...] = hidden
        total[...] = cdot(hidden, up_tail_ref[...], 1, 1)

    weight = spread.load(w_refs, where, held_weight)
    units = hidden_ref.shape[2]
    turn_part(low, turned_ref, step)
    hidden = cdot(low[...], weight[:, units:]) * slope_ref[0].astype(F32)
    sums_ref[0] = jnp.sum(hidden, axis=0, keepdims=True)
    hidden = hidden.astype(LOW)
    hidden_ref[0] = hidden
    total[...] += cdot(hidden, weight[:, :units], 1, 1)

    @pl.when(step == pl.num_programs(0) - 1)
    def _():
        part_ref[...] = total[...].astype(LOW)


def mlp_grads_kernel(spread, where, *refs):
    count = len(spread.grad_keys)
    grad_turned, normed_turned, hidden_ref, act_ref, hidden_tail_ref, act_tail_ref = refs[:6]
    out_refs = refs[6 : 6 + count]
    tail_ref, result = refs[6 + count :]
    step = pl.program_id(0)

    @pl.when(step == 0)
    def _():
        up_tail = cdot(normed_turned[...], hidden_tail_ref[...]).astype(LOW)
        down_tail = cdot(grad_turned[...], act_tail_ref[...]).astype(LOW)
        steps, _, both = tail_ref.shape
        half = both // 2
        for t in range(steps):
            at = slice(t * half, (t + 1) * half)
            tail_ref[t] = jnp.concatenate([up_tail[:, at], down_tail[:, at]], axis=1)

    units = hidden_ref.shape[2]
    result[:, :units] = cdot(normed_turned[...], hidden_ref[0]).astype(LOW)
    result[:, units:] = cdot(grad_turned[...], act_ref[0]).astype(LOW)
    spread.store(out_refs, where, result)


def attn_backward_kernel(spread, where, *refs):
    count = len(spread.weight_keys)
    grad_ref, own_ref, other_ref, middle_ref, vec_ref, qkv_ref, sums_ref = refs[:7]
    w_refs = refs[7 : 7 + count]
    dmiddle_ref, norm_sums_ref, dqkv_ref, head_sums_ref, part_ref, low, total, held_weight = refs[7 + count :]
    step = pl.program_id(0)

    @pl.when(step == 0)
    def _():
        grad = grad_ref[...]
        dnormed = own_ref[...].astype(F32) + other_ref[...].astype(F32)
        inner, gain_terms = norm_backward(dnormed, middle_ref[...], vec_ref[0, 5:6, :])
        dmiddle = grad + inner
        dmiddle_ref[...] = dmiddle
        low[...] = dmiddle.astype(LOW)
        for number, terms in enumerate((gain_terms, dnormed, grad, dmiddle)):
            norm_sums_ref[number : number + 1, :] = jnp.sum(terms, axis=0, keepdims=True)

    weight = spread.load(w_refs, where, held_weight)
    tokens = where[4]
    head_columns = 3 * HD
    local = qkv_ref.shape[2]
    heads = local // head_columns
    qkv = qkv_ref[0]
    dmixed = cdot(low[...], weight[:, local : local + heads * HD]).astype(LOW)
    pieces = []
    for head in range(heads):
        at = head * head_columns
        query = qkv[:, at : at + HD]
        key = qkv[:, at + HD : at + 2 * HD]
        value = qkv[:, at + 2 * HD : at + 3 * HD]
        grad = dmixed[:, head * HD : (head + 1) * HD]
        scores = mask_keys(cdot(key, query, 1, 1), tokens)
        probs = jnp.exp2(scores * POWER - sums_ref[0, head : head + 1, :])
        dprobs = cdot(value, grad, 1, 1)
        row_dot = jnp.sum(dprobs * probs, axis=0, keepdims=True)
        dscores = (probs * (dprobs - row_dot)).astype(LOW)
        pieces.append(cdot(key, dscores, 0, 0).T * SCORE)
        pieces.append(cdot(dscores, query) * SCORE)
        pieces.append(cdot(probs.astype(LOW), grad))
    dqkv = jnp.concatenate(pieces, axis=1)
    head_sums_ref[0] = jnp.sum(dqkv, axis=0, keepdims=True)
    dqkv = dqkv.astype(LOW)
    dqkv_ref[0] = dqkv
    part = cdot(dqkv, weight[:, :local], 1, 1)

    @pl.when(step == 0)
    def _():
        total[...] = part

    @pl.when(step > 0)
    def _():
        total[...] += part

    @pl.when(step == pl.num_programs(0) - 1)
    def _():
        part_ref[...] = total[...].astype(LOW)


def attn_grads_kernel(spread, where, *refs):
    count = len(spread.grad_keys)
    dmiddle_ref, normed_turned, dqkv_ref, mixed_ref, tail_ref = refs[:5]
    out_refs = refs[5 : 5 + count]
    result, grad_turned = refs[5 + count :]

    @pl.when(pl.program_id(0) == 0)
    def _():
        grad_turned[...] = dmiddle_ref[...].astype(LOW).T

    parts = [
        cdot(normed_turned[...], dqkv_ref[0]).astype(LOW),
        cdot(grad_turned[...], mixed_ref[0]).astype(LOW),
        tail_ref[0],
    ]
    used = sum(part.shape[1] for part in parts)
    parts.append(jnp.zeros((result.shape[0], result.shape[1] - used), LOW))
    result[...] = jnp.concatenate(parts, axis=1)
    spread.store(out_refs, where, result)


def norm_backward_kernel(where, dmiddle_ref, own_ref, other_ref, stream_ref, vec_ref, out_ref, sums_ref):
    dnormed = own_ref[...].astype(F32) + other_ref[...].astype(F32)
    inner, gain_terms = norm_backward(dnormed, stream_ref[...], vec_ref[0, 0:1, :])
    out_ref[...] = dmiddle_ref[...] + inner

    @pl.when(pl.program_id(0) == 0)
    def _():
        sums_ref[...] = jnp.zeros_like(sums_ref)

    sums_ref[0:1, :] += jnp.sum(gain_terms, axis=0, keepdims=True)
    sums_ref[1:2, :] += jnp.sum(dnormed, axis=0, keepdims=True)


def adam_kernel(units, local, out_local, tail_units, where, *refs):
    attn_own, attn_other, mlp_own, mlp_other = refs[:4]
    states = [refs[4 + 3 * k : 7 + 3 * k] for k in range(4)]
    outs = refs[len(refs) - 16 :]

    def pair(own, other):
        own, other = own[...].astype(F32), other[...].astype(F32)
        low_core = where[3] == 0
        return jnp.where(low_core, own, other), jnp.where(low_core, other, own)

    attn = pair(attn_own, attn_other)
    mlp = pair(mlp_own, mlp_other)
    at = local + out_local
    grads = [
        jnp.concatenate([half[:, :local] for half in attn], axis=1),
        jnp.concatenate([half[:, local:at] for half in attn], axis=1),
        jnp.concatenate(
            [piece for m, n in zip(mlp, attn) for piece in (m[:, :units], n[:, at : at + tail_units])], axis=1
        ),
        jnp.concatenate(
            [
                piece
                for m, n in zip(mlp, attn)
                for piece in (m[:, units:], n[:, at + tail_units : at + 2 * tail_units])
            ],
            axis=1,
        ),
    ]
    for number, grad in enumerate(grads):
        weight, first, second = [ref[0] for ref in states[number]]
        new = adam_step(weight, grad, first, second, RATES[number], DECAY)
        for ref, values in zip(outs[4 * number : 4 * number + 4], (grad, new[1], new[2], new[0])):
            ref[0] = values


def vec_pack_kernel(where, *refs):
    out_ref = refs[-1]
    layers = out_ref.shape[0]
    out_ref[...] = jnp.zeros_like(out_ref)
    for layer in range(layers):
        one_ref, two_ref, head_ref, main_ref, tail_ref = refs[5 * layer : 5 * layer + 5]
        out_ref[layer, 0:2, :] = one_ref[0:2, :]
        out_ref[layer, 2:6, :] = two_ref[0:4, :]
        for t in range(head_ref.shape[0]):
            out_ref[layer, 8 + t : 9 + t, : head_ref.shape[2]] = head_ref[t]
            out_ref[layer, 12 + t : 13 + t, : main_ref.shape[2]] = main_ref[t]
        out_ref[layer, 6:7, : tail_ref.shape[1]] = tail_ref[...]


def vec_kernel(steps, local, units, tail_units, where, own_ref, other_ref, vec_ref, first_ref, second_ref,
               grad_out, first_out, second_out, weight_out):
    low_core = where[3] == 0
    for layer in range(vec_ref.shape[0]):
        own, other = own_ref[layer], other_ref[layer]
        cores = jnp.where(low_core, own, other), jnp.where(low_core, other, own)
        norms = cores[0][0:6]
        heads = local // (3 * HD)

        def head_piece(kind):
            return [
                core[8 + t : 9 + t, (3 * head + kind) * HD : (3 * head + kind + 1) * HD]
                for t in range(steps)
                for core in cores
                for head in range(heads)
            ]

        hidden = [
            piece
            for t in range(steps)
            for core in cores
            for piece in (core[12 + t : 13 + t, :units], core[6:7, t * tail_units : (t + 1) * tail_units])
        ]
        grad = jnp.concatenate(
            [norms[0:1], norms[1:2], *head_piece(0), *head_piece(2),
             norms[5:6], norms[2:3], norms[3:4], norms[4:5], *hidden],
            axis=1,
        )
        at = slice(layer, layer + 1)
        new = adam_step(vec_ref[at, :], grad, first_ref[at, :], second_ref[at, :], RATES[4], 0.0)
        grad_out[at, :] = grad
        first_out[at, :] = new[1]
        second_out[at, :] = new[2]
        weight_out[at, :] = new[0]


def plane_sides(chips):
    side = math.isqrt(chips)
    while chips % side:
        side -= 1
    return side, chips // side


class Place:
    def __init__(self):
        self.nf = lax.axis_size("fsdp")
        self.nt = lax.axis_size("tp")
        self.na, self.nb = plane_sides(self.nf // 2)
        fi = lax.axis_index("fsdp")
        self.core = fi % 2
        self.a = (fi // 2) // self.nb
        self.b = (fi // 2) % self.nb
        self.t = lax.axis_index("tp")
        self.size = {"a": self.na, "b": self.nb, "t": self.nt}
        self.at = {"a": self.a, "b": self.b, "t": self.t}

    def pairs(self, axis, move):
        if axis == "t":
            return [(i, move(i)) for i in range(self.nt)]
        found = []
        for f in range(self.nf):
            place = {"a": f // 2 // self.nb, "b": f // 2 % self.nb, "core": f % 2}
            place[axis] = move(place[axis])
            found.append((f, (place["a"] * self.nb + place["b"]) * 2 + place["core"]))
        return found

    def send(self, values, axis, move):
        return lax.ppermute(values, "tp" if axis == "t" else "fsdp", self.pairs(axis, move))

    def sibling(self, values):
        return self.send(values, "core", lambda i: 1 - i)

    def swap_rows(self, values):
        pairs = []
        for f in range(self.nf):
            for t in range(self.nt):
                if f % 2 != t % 2:
                    sign = 1 if t % 2 else -1
                    pairs.append((f * self.nt + t, (f + sign) * self.nt + t - sign))
        arrived = lax.ppermute(values.astype(LOW), ("fsdp", "tp"), pairs).astype(F32)
        return jnp.where(self.core != self.t % 2, arrived, values)

    def gather_axis(self, block, axis):
        n = self.size[axis]
        return [block] + [self.send(block, axis, lambda i, k=k: (i - k) % n) for k in range(1, n)]

    def scatter_axis(self, parts, axis):
        n = self.size[axis]
        sent = [self.send(parts[k], axis, lambda i, k=k: (i + k) % n) for k in range(1, n)]
        return [parts[0], *sent]


def split_pair(place, first, second):
    return (
        jnp.where(place.core == 0, first, second),
        jnp.where(place.core == 0, second, first),
    )


def sum_kernel(outputs, where, *refs):
    count = sum(size for sizes in outputs for size in sizes)
    ins, outs = refs[:count], refs[count:]
    for out_ref, sizes in zip(outs, outputs):
        for number, size in enumerate(sizes):
            for t in range(out_ref.shape[0]):
                total = ins[0][t, 0].astype(F32)
                for ref in ins[1:size]:
                    total += ref[t, 0].astype(F32)
                out_ref[t, number] = total.astype(LOW)
            ins = ins[size:]


def tie_kernel(where, *refs):
    pass


def tie(where, arrays, after):
    space = pl.BlockSpec(memory_space=pl.ANY)
    return call(
        tie_kernel,
        where,
        1,
        [(space, x) for x in arrays],
        [(space, jax.ShapeDtypeStruct(x.shape, x.dtype)) for x in arrays],
        [],
        aliases={1 + k: k for k in range(len(arrays))},
        after=after,
    )


class Spread:
    def __init__(self, place, rows, columns, middle):
        self.place, self.rows, self.columns = place, rows, columns
        self.middle = middle
        self.direct = rows % 16 == 0
        self.width = place.na * place.nb * 2 * rows
        na, nb = place.na, place.nb
        self.grad_keys = [[(0, a, b) for b in range(nb)] for a in range(na)]
        self.grad_keys += [[(1, a, b) for a in range(na)] for b in range(nb)]
        self.gather_keys = [[(0, 0, 0), (1, 0, 0)]]
        self.gather_keys += [[(0, 0, b), (1, 0, b)] for b in range(1, nb)]
        self.gather_keys += [[(0, a, 0), (1, a, 0)] for a in range(1, na)]
        self.gather_keys += [[(half, a, b)] for half in range(2) for a in range(1, na) for b in range(1, nb)]
        if middle:
            self.gather_keys = self.grad_keys
        self.weight_keys = self.gather_keys
        if not self.direct:
            self.weight_keys = self.grad_keys = [None]

    def shapes(self, keys):
        if not self.direct:
            return [(self.place.nt, self.width, self.columns)]
        return [(self.place.nt, len(blocks), self.rows, self.columns) for blocks in keys]

    def specs(self, keys):
        return [stepped(shape[1:]) for shape in self.shapes(keys)]

    def first_row(self, where, key):
        half, a, b = key
        a = lax.rem(where[0] + a, self.place.na)
        b = lax.rem(where[1] + b, self.place.nb)
        return pl.multiple_of(((a * self.place.nb + b) * 2 + half) * self.rows, 16)

    def load(self, refs, where, scratch):
        if not self.direct:
            return refs[0].at[0]
        for ref, blocks in zip(refs, self.weight_keys):
            for number, key in enumerate(blocks):
                scratch[pl.ds(self.first_row(where, key), self.rows), :] = ref[0, number]
        return scratch

    def store(self, refs, where, scratch):
        if not self.direct:
            refs[0][0] = scratch[...]
            return
        for ref, blocks in zip(refs, self.grad_keys):
            for number, key in enumerate(blocks):
                ref[0, number] = scratch[pl.ds(self.first_row(where, key), self.rows), :]

    def start(self, own, other):
        place = self.place
        halves = split_pair(place, own, other)
        if self.middle:
            return [jnp.stack(place.gather_axis(half, axis)) for half, axis in zip(halves, "ba")]
        return [jnp.stack(halves)]

    def gather(self, where, blocks, after=()):
        place = self.place
        na, nb = place.na, place.nb
        blocks = [lax.all_gather(block, "tp") for block in blocks]
        if self.direct and len(after):
            blocks = tie(where, blocks, after)
        if self.middle:
            arrays = [array for block, axis in zip(blocks, "ab") for array in place.gather_axis(block, axis)]
        else:
            along_b = place.gather_axis(blocks[0], "b")
            along_a = place.gather_axis(blocks[0], "a")
            first = [place.gather_axis(x[:, :1], "a")[1:] for x in along_b[1:]]
            second = [place.gather_axis(x[:, 1:], "b")[1:] for x in along_a[1:]]
            arrays = along_b + along_a[1:]
            arrays += [first[b][a] for a in range(na - 1) for b in range(nb - 1)]
            arrays += [second[a][b] for a in range(na - 1) for b in range(nb - 1)]
        if self.direct:
            return arrays
        found = {
            key: array[:, number]
            for array, keys in zip(arrays, self.gather_keys)
            for number, key in enumerate(keys)
        }
        full = jnp.stack([found[half, a, b] for a in range(na) for b in range(nb) for half in range(2)], axis=1)
        full = full.reshape(place.nt, na, nb, 2, self.rows, self.columns)
        full = self.roll(full, (na - place.a) % na, (nb - place.b) % nb)
        return [full.reshape(place.nt, self.width, self.columns)]

    def roll(self, full, a, b):
        full = lax.dynamic_slice_in_dim(jnp.concatenate([full, full], axis=1), a, self.place.na, 1)
        return lax.dynamic_slice_in_dim(jnp.concatenate([full, full], axis=2), b, self.place.nb, 2)

    def sums(self, where, outputs, after, layer=None):
        place, rows, columns = self.place, self.rows, self.columns

        def block(number):
            return pl.BlockSpec((place.nt, 1, rows, columns), lambda i, s: (0, number, 0, 0))

        shapes = [(place.nt, len(groups), rows, columns) for groups in outputs]
        return call(
            functools.partial(sum_kernel, [[len(group) for group in groups] for groups in outputs]),
            where,
            1,
            [(block(number), x) for groups in outputs for group in groups for x, number in group],
            [(held(shape), low_of(*shape)) for shape in shapes],
            [],
            after=after,
            layer=layer,
        )

    def scatter_last(self, arrays):
        place = self.place
        if not self.direct:
            full = arrays[0].reshape(place.nt, place.na, place.nb, 2, self.rows, self.columns)
            full = self.roll(full, place.a, place.b)
            arrays = [full[:, a, :, 0] for a in range(place.na)] + [full[:, :, b, 1] for b in range(place.nb)]
        return (
            place.scatter_axis(arrays[: place.na], "a"),
            place.scatter_axis(arrays[place.na :], "b"),
        )

    def scatter_first(self, where, halves, after):
        place = self.place
        if self.middle:
            outputs = [[[(x, k) for x in half] for k in range(half[0].shape[1])] for half in halves]
            results = self.sums(where, outputs, after)
            return results[0], [lax.psum_scatter(x, "tp", scatter_dimension=0, tiled=True)[0] for x in results]
        axes = ("b", "a")
        keys = [(half, k) for half in range(2) for k in range(1, place.size[axes[half]])]
        results = self.sums(where, [[[(x, k) for x in halves[half]]] for half, k in keys], after)
        terms = [[(x, 0) for x in arrays] for arrays in halves]
        for (half, k), total in zip(keys, results):
            n = place.size[axes[half]]
            terms[half].append((place.send(total, axes[half], lambda i: (i + k) % n), 0))
        return results[0], terms

    def scatter_tp(self, where, terms, after, layer=None):
        place = self.place
        if self.middle:
            if self.direct:
                terms = tie(where, terms, after)
            done = [
                sum(x.astype(F32) for x in place.scatter_axis(list(half), axis)).astype(LOW)
                for half, axis in zip(terms, "ba")
            ]
            last = after[0]
        else:
            (last,) = self.sums(where, [terms], after, layer)
            done = lax.psum_scatter(last, "tp", scatter_dimension=0, tiled=True)[0]
        mine, other = split_pair(place, done[0], done[1])
        return last, (mine, place.sibling(other))


def body(
    residual_in,
    cotangent,
    slot_tokens,
    qkv_weight,
    out_weight,
    up_weight,
    down_weight,
    vectors,
    qkv_first,
    qkv_second,
    out_first,
    out_second,
    up_first,
    up_second,
    down_first,
    down_second,
    vec_first,
    vec_second,
):
    place = Place()
    layer_count, shard_rows, _ = qkv_weight.shape
    half_rows, width = residual_in.shape
    rows = 2 * half_rows
    nt = place.nt
    local = qkv_weight.shape[2] // 2
    out_local = out_weight.shape[1] // 2
    hidden_local = up_weight.shape[2] // 2
    units = hidden_local // 128 * 128
    tail_units = hidden_local - units
    heads = out_local // HD
    attn_columns = -(-(local + out_local + 2 * tail_units) // 128) * 128
    mlp_columns = 2 * units

    tokens_pair = jnp.concatenate(split_pair(place, slot_tokens, place.sibling(slot_tokens)))
    slot_at = (place.t % 2) * slot_tokens.shape[0] + place.t // 2
    tokens = lax.dynamic_slice_in_dim(tokens_pair, slot_at, 1)
    row_mask = (jnp.arange(rows, dtype=jnp.int32) < tokens[0]).astype(F32)[:, None]
    here = jnp.stack([place.a, place.b, place.t, place.core]).astype(jnp.int32)
    where = jnp.concatenate([here, tokens.astype(jnp.int32)])

    def own_rows(values):
        return lax.dynamic_slice_in_dim(values, place.core * half_rows, half_rows)

    spreads = [
        (
            Spread(place, shard_rows, attn_columns, False),
            Spread(place, shard_rows, mlp_columns, layer > 0),
        )
        for layer in range(layer_count)
    ]

    def turn(arrays):
        qkv, out, up, down = arrays
        return qkv, jnp.swapaxes(out, 1, 2), up, jnp.swapaxes(down, 1, 2)

    weights = turn((qkv_weight, out_weight, up_weight, down_weight))
    firsts = turn((qkv_first, out_first, up_first, down_first))
    seconds = turn((qkv_second, out_second, up_second, down_second))

    def layer_block(array, layer, steps=1):
        block = (1, array.shape[1] // steps, array.shape[2])
        return pl.BlockSpec(block, lambda i, s: (layer, i, 0))

    def pack(layer):
        attn, mlp = (shard_rows, attn_columns), (shard_rows, mlp_columns)
        return call(
            functools.partial(pack_kernel, units),
            here,
            1,
            [(layer_block(w, layer), w) for w in weights],
            [(held(shape), low_of(*shape)) for shape in (attn, attn, mlp, mlp)],
            [],
            bytes_accessed=6 * shard_rows * 13216 // 4,
        )

    starts = []
    for layer in range(layer_count):
        own_attn, other_attn, own_mlp, other_mlp = pack(layer)
        starts.append(
            (
                spreads[layer][0].start(own_attn, place.sibling(other_attn)),
                spreads[layer][1].start(own_mlp, place.sibling(other_mlp)),
            )
        )
    gathered = []
    before = [x for pair in starts[1:] for blocks in pair for x in blocks]
    for layer in range(layer_count):
        attn_full = spreads[layer][0].gather(where, starts[layer][0], before)
        mlp_full = spreads[layer][1].gather(where, starts[layer][1], attn_full[1:3])
        before = mlp_full[1:3]
        gathered.append((attn_full, mlp_full))

    wide = vectors[:, : 8 * width].reshape(layer_count, 8, width)
    head_bias = vectors[:, 2 * width : 4 * width].reshape(layer_count, 2, 2 * nt, 1, out_local)
    hidden_bias = vectors[:, 8 * width :].reshape(layer_count, nt, 2, 1, hidden_local)
    main_bias = hidden_bias[..., :units]
    tail_bias = jnp.moveaxis(hidden_bias[..., units:], 1, 3).reshape(layer_count, 2, 1, nt * tail_units)

    full = whole((rows, width))
    weight_scratch = [
        pltpu.VMEM((width, attn_columns), LOW),
        pltpu.VMEM((width, mlp_columns), LOW),
    ]
    flat = pltpu.VMEM((rows, width), F32)
    flat_low = pltpu.VMEM((rows, width), LOW)
    big = 2 * rows * width

    def wide_of(layer):
        spec = pl.BlockSpec((1, 8, width), lambda i, s: (layer, 0, 0), pipeline_mode=pl.Buffered(1))
        return spec, wide

    def attn_forward(layer, base, own, other):
        spread = spreads[layer][0]
        joined = base is not None
        if joined:
            ins = [(full, base), (full, own), (full, other), wide_of(layer - 1)]
        else:
            half = whole((half_rows, width))
            ins = [(half, own), (half, other)]
        ins.append(wide_of(layer))
        ins.append(
            (
                pl.BlockSpec(
                    (1, 2, 1, 1, out_local), lambda i, s: (layer, 0, 2 * i + s[3], 0, 0)
                ),
                head_bias,
            )
        )
        ins += list(zip(spread.specs(spread.weight_keys), gathered[layer][0]))
        return call(
            functools.partial(attn_forward_kernel, spread, joined, tail_units),
            where,
            nt,
            ins,
            [
                (held((rows, width)), f32_of(rows, width)),
                (held((width, rows)), low_of(width, rows)),
                (stepped((rows, local)), low_of(nt, rows, local)),
                (stepped((rows, out_local)), low_of(nt, rows, out_local)),
                (stepped((heads, rows)), f32_of(nt, heads, rows)),
                (stepped((width, 2 * tail_units)), low_of(nt, width, 2 * tail_units)),
                (held((rows, width)), low_of(rows, width)),
            ],
            [flat, weight_scratch[0], flat_low],
            big * nt * (local + out_local) + 4 * nt * heads * rows * rows * HD,
            rows * width * 12 + nt * width * attn_columns * 2,
            nt * heads * rows * rows,
        )

    def mlp_forward(layer, base, own, other, tails, after=()):
        spread = spreads[layer][1]
        tail = nt * tail_units
        tail_shape = (width, tail)
        ins = [
            (full, base),
            (full, own),
            (full, other),
            wide_of(layer),
            (pl.BlockSpec((1, 1, 1, 1, units), lambda i, s: (layer, i, s[3], 0, 0)), main_bias),
            (whole(tails.shape), tails),
            (pl.BlockSpec((1, 1, 1, tail), lambda i, s: (layer, s[3], 0, 0)), tail_bias),
        ]
        ins += list(zip(spread.specs(spread.weight_keys), gathered[layer][1]))
        return call(
            functools.partial(mlp_forward_kernel, spread),
            where,
            nt,
            ins,
            [
                (held((rows, width)), f32_of(rows, width)),
                (held((width, rows)), low_of(width, rows)),
                (stepped((rows, units)), low_of(nt, rows, units)),
                (stepped((rows, units)), low_of(nt, rows, units)),
                (held((rows, tail)), low_of(rows, tail)),
                (held((rows, tail)), low_of(rows, tail)),
                (held(tail_shape), low_of(*tail_shape)),
                (held(tail_shape), low_of(*tail_shape)),
                (held((rows, width)), low_of(rows, width)),
            ],
            [flat, weight_scratch[1], flat_low],
            2 * big * (nt * units + tail),
            rows * width * 16 + nt * (width + rows) * mlp_columns * 2,
            rows * nt * units,
            after=after,
        )

    def mlp_backward(layer, grad, slope, tails, slope_tail):
        spread = spreads[layer][1]
        tail = nt * tail_units
        ins = [(full, grad), (stepped((rows, units)), slope)]
        ins += [(whole(w.shape), w) for w in (*tails, slope_tail)]
        ins += list(zip(spread.specs(spread.weight_keys), gathered[layer][1]))
        return call(
            functools.partial(mlp_backward_kernel, spread),
            where,
            nt,
            ins,
            [
                (stepped((rows, units)), low_of(nt, rows, units)),
                (held((rows, tail)), low_of(rows, tail)),
                (stepped((1, units)), f32_of(nt, 1, units)),
                (held((1, tail)), f32_of(1, tail)),
                (held((rows, width)), low_of(rows, width)),
                (held((width, rows)), low_of(width, rows)),
            ],
            [flat_low, flat, weight_scratch[1]],
            2 * big * (nt * units + tail),
            rows * width * 6 + nt * (width + rows) * mlp_columns * 2,
        )

    def mlp_grads(layer, grad, normed, hidden, act, hidden_tail, act_tail):
        spread = spreads[layer][1]
        ins = [(whole((width, rows)), grad), (whole((width, rows)), normed)]
        ins += [(stepped((rows, units)), hidden), (stepped((rows, units)), act)]
        ins += [(whole(x.shape), x) for x in (hidden_tail, act_tail)]
        tail_shape = (nt, width, 2 * tail_units)
        outs = [
            (spec, low_of(*shape))
            for spec, shape in zip(spread.specs(spread.grad_keys), spread.shapes(spread.grad_keys))
        ]
        outs.append((held(tail_shape), low_of(*tail_shape)))
        return call(
            functools.partial(mlp_grads_kernel, spread),
            where,
            nt,
            ins,
            outs,
            [weight_scratch[1]],
            2 * big * nt * (units + tail_units),
            rows * width * 6 + nt * (width + rows) * mlp_columns * 2,
        )

    def attn_backward(layer, grad, own, other, middle, qkv, log_sums, after=()):
        spread = spreads[layer][0]
        ins = [(full, grad), (full, own), (full, other), (full, middle), wide_of(layer)]
        ins += [(stepped((rows, local)), qkv), (stepped((heads, rows)), log_sums)]
        ins += list(zip(spread.specs(spread.weight_keys), gathered[layer][0]))
        return call(
            functools.partial(attn_backward_kernel, spread),
            where,
            nt,
            ins,
            [
                (held((rows, width)), f32_of(rows, width)),
                (held((8, width)), f32_of(8, width)),
                (stepped((rows, local)), low_of(nt, rows, local)),
                (stepped((1, local)), f32_of(nt, 1, local)),
                (held((rows, width)), low_of(rows, width)),
            ],
            [flat_low, flat, weight_scratch[0]],
            big * nt * (local + out_local) + 10 * nt * heads * rows * rows * HD,
            rows * width * 20 + nt * width * attn_columns * 2,
            nt * heads * rows * rows,
            after=after,
        )

    def attn_grads(layer, dmiddle, normed, dqkv, mixed, tail_grads):
        spread = spreads[layer][0]
        ins = [(full, dmiddle), (whole((width, rows)), normed)]
        ins += [(stepped((rows, local)), dqkv), (stepped((rows, out_local)), mixed)]
        ins.append((stepped((width, 2 * tail_units)), tail_grads))
        outs = [
            (spec, low_of(*shape))
            for spec, shape in zip(spread.specs(spread.grad_keys), spread.shapes(spread.grad_keys))
        ]
        return call(
            functools.partial(attn_grads_kernel, spread),
            where,
            nt,
            ins,
            outs,
            [weight_scratch[0], pltpu.VMEM((width, rows), LOW)],
            big * nt * (local + out_local),
            rows * width * 6 + nt * (width + rows) * attn_columns * 2,
        )

    def norm_one_backward(layer, dmiddle, own, other, stream, after=()):
        part = pl.BlockSpec((half_rows, width), lambda i, s: (i, 0))
        return call(
            norm_backward_kernel,
            where,
            2,
            [(part, dmiddle), (part, own), (part, other), (part, stream), wide_of(layer)],
            [(part, f32_of(rows, width)), (held((8, width)), f32_of(8, width))],
            [],
            rows * width * 20,
            rows * width * 16,
            after=after,
        )

    grad_stream = None
    mine = place.swap_rows(residual_in)
    base, own, other = None, mine, place.sibling(mine)
    saved = []
    for layer in range(layer_count):
        stream, normed, qkv, mixed, log_sums, tails, part = attn_forward(layer, base, own, other)
        if layer == layer_count - 1:
            (mine,) = tie(where, [place.swap_rows(cotangent)], [qkv])
            grad_stream = jnp.concatenate(split_pair(place, mine, place.sibling(mine)), axis=0) * row_mask
        middle, normed_two, act, slope, act_tail, slope_tail, up_tail, down_tail, part = mlp_forward(
            layer, stream, part, place.sibling(part), tails
        )
        saved.append(
            (stream, normed, qkv, mixed, log_sums, middle, normed_two, act, slope, act_tail, slope_tail,
             (up_tail, down_tail))
        )
        base, own, other = middle, part, place.sibling(part)
    output = own_rows(base) + (own_rows(own).astype(F32) + own_rows(other).astype(F32))
    output = place.swap_rows((output + wide[layer_count - 1, 7:8]) * own_rows(row_mask))


    def adam(layer, attn_pair, mlp_pair, before, after=()):
        steps = 1
        ins = [
            (pl.BlockSpec((shard_rows // steps, x.shape[1]), lambda i, s: (i, 0)), x)
            for x in (*attn_pair, *mlp_pair)
        ]
        for states in zip(weights, firsts, seconds):
            ins += [(layer_block(x, layer, steps), x) for x in states]
        outs = [
            (layer_block(weight, layer, steps), f32_of(*weight.shape)) for weight in weights for _ in range(4)
        ]
        aliases = None
        if before is not None:
            aliases = {1 + len(ins) + k: k for k in range(16)}
            ins += [(pl.BlockSpec(memory_space=pl.ANY), x) for x in before]
        return call(
            functools.partial(adam_kernel, units, local, out_local, tail_units),
            where,
            steps,
            ins,
            outs,
            [],
            bytes_accessed=28 * shard_rows * 13216 // 4,
            aliases=aliases,
            after=after,
        )

    vec_sums = [None] * layer_count
    last = grad_stream
    above = None
    for layer in reversed(range(layer_count)):
        (stream, normed, qkv, mixed, log_sums, middle, normed_two, act, slope, act_tail, slope_tail, tails) = (
            saved[layer]
        )
        spread_attn, spread_mlp = spreads[layer]
        hidden, hidden_tail, hidden_sums, tail_sums, part, grad_turned = mlp_backward(
            layer, grad_stream, slope, tails, slope_tail
        )
        other = place.sibling(part)
        *mlp_grad, tail_grads = mlp_grads(
            layer, grad_turned, normed_two, hidden, act, hidden_tail, act_tail
        )
        last = tail_grads
        mlp_terms = spread_mlp.scatter_last(mlp_grad)
        dmiddle, norm_two_sums, dqkv, head_sums, part = attn_backward(
            layer, grad_stream, part, other, middle, qkv, log_sums, [last]
        )
        other = place.sibling(part)
        attn_grad = attn_grads(layer, dmiddle, normed, dqkv, mixed, tail_grads)
        last = attn_grad[0]
        if above:
            last, attn_terms_above = spreads[above][0].scatter_first(where, attn_terms_above, [last])
        grad_stream, norm_one_sums = norm_one_backward(layer, dmiddle, part, other, stream, [last])
        if layer:
            attn_terms = spread_attn.scatter_last(attn_grad)
        last, mlp_terms = spread_mlp.scatter_first(where, mlp_terms, [norm_one_sums])
        vec_sums[layer] = (norm_one_sums, norm_two_sums, head_sums, hidden_sums, tail_sums)
        if above:
            grad_input = place.swap_rows(own_rows(grad_stream))
            last, attn_pair_one = spreads[above][0].scatter_tp(where, attn_terms_above, [last, grad_input], 1)
            mlp_terms_one = mlp_terms_above
            if spread_attn.direct:
                attn_grad = tie(where, attn_grad, [last])
            attn_terms = spread_attn.scatter_last(attn_grad)
        above, mlp_terms_above, attn_terms_above = layer, mlp_terms, attn_terms
        if layer:
            grad_stream, last = lax.optimization_barrier((grad_stream, last))
    last, mlp_pair_above = spreads[above][1].scatter_tp(where, mlp_terms_above, [last, output])
    _, mlp_pair_one = spreads[1][1].scatter_tp(where, mlp_terms_one, [last])
    last, attn_terms_above = spreads[above][0].scatter_first(where, attn_terms_above, [last])
    updated = adam(1, attn_pair_one, mlp_pair_one, None, [last])
    last, attn_pair_above = spreads[above][0].scatter_tp(where, attn_terms_above, [last, updated[0]])

    flat_sums = [x for sums in vec_sums for x in sums]
    vec_shape = (layer_count, 16, width)
    (vec_total,) = call(
        vec_pack_kernel,
        where,
        1,
        [(whole(x.shape), x) for x in flat_sums],
        [(held(vec_shape), f32_of(*vec_shape))],
        [],
        after=[last, *mlp_pair_above],
    )
    for axis in ("b", "a", "t"):
        step = 1
        while step < place.size[axis]:
            vec_total = vec_total + place.send(vec_total, axis, lambda i: i ^ step)
            step *= 2
    vec_new = call(
        functools.partial(vec_kernel, nt, local, units, tail_units),
        where,
        1,
        [(whole(x.shape), x) for x in (vec_total, place.sibling(vec_total), vectors, vec_first, vec_second)],
        [(held(vectors.shape), f32_of(*vectors.shape)) for _ in range(4)],
        [],
    )
    updated = adam(above, attn_pair_above, mlp_pair_above, updated)
    updated = [
        jnp.swapaxes(x, 1, 2) if number // 4 % 2 else x for number, x in enumerate(updated)
    ]
    return (output, grad_input, *updated, *vec_new)


def solution(mesh):
    rows = P(("fsdp", "tp"), None)
    wide = P(None, "fsdp", "tp")
    tall = P(None, "tp", "fsdp")
    moments = (wide, wide, tall, tall, wide, wide, tall, tall, P(), P())
    return jax.shard_map(
        body,
        mesh=mesh,
        in_specs=(rows, rows, P("fsdp"), wide, tall, wide, tall, P(), *moments),
        out_specs=(rows, rows, *[wide] * 4, *[tall] * 4, *[wide] * 4, *[tall] * 4, *[P()] * 4),
        check_vma=False,
    )
```

```python
import functools
import math

import jax
import jax.numpy as jnp
from jax import lax
from jax.experimental import pallas as pl
from jax.experimental.pallas import tpu as pltpu
from jax.sharding import PartitionSpec as P

HD = 72
IMG_TOK = 729
STEP = 10


EPS_NORM = 1e-06
MASKED = -30000.0
BETA_ONE = 0.9
BETA_TWO = 0.999
ADAM_EPS = 1e-08
DECAY = 0.1
RATES = (0.05, 1.0, 0.05, 0.03, 0.3)
LOW = jnp.bfloat16
F32 = jnp.float32
GELU = math.sqrt(2.0 / math.pi)
SCORE = HD ** (-0.5)
POWER = SCORE / math.log(2.0)
VMEM = 56 * 1024 * 1024
COST = {
    "pack": 4,
    "attn_forward": 26,
    "mlp_forward": 24,
    "mlp_backward": 17,
    "mlp_grads": 16,
    "attn_backward": 33,
    "attn_grads": 13,
    "norm_backward": 9,
    "sum": 5,
    "vec_pack": 0.3,
    "vec": 0.3,
    "adam": 1,
    "tie": 1,
}
SCALE = 2e9


def adam_step(weight, gradient, first_moment, second_moment, step_rate, decay_rate):
    first_new = BETA_ONE * first_moment + (1.0 - BETA_ONE) * gradient
    second_new = BETA_TWO * second_moment + (1.0 - BETA_TWO) * gradient * gradient
    first_hat = first_new / (1.0 - BETA_ONE**STEP)
    second_hat = second_new / (1.0 - BETA_TWO**STEP)
    weight_new = weight - step_rate * (
        first_hat / (jnp.sqrt(second_hat) + ADAM_EPS) + decay_rate * weight
    )
    return (weight_new, first_new, second_new)


def cdot(left, right, left_dim=1, right_dim=0):
    return lax.dot_general(
        left, right, (((left_dim,), (right_dim,)), ((), ())), preferred_element_type=F32
    )


def norm_parts(values):
    centred = values - jnp.mean(values, axis=-1, keepdims=True)
    inverse = lax.rsqrt(jnp.mean(centred * centred, axis=-1, keepdims=True) + EPS_NORM)
    return centred * inverse, inverse


def norm_backward(grad_out, values, gain):
    unit, inverse = norm_parts(values)
    scaled = grad_out * gain
    mean_one = jnp.mean(scaled, axis=-1, keepdims=True)
    mean_two = jnp.mean(scaled * unit, axis=-1, keepdims=True)
    return inverse * (scaled - mean_one - unit * mean_two), grad_out * unit


def gelu_both(inputs):
    square = inputs * inputs
    tanh = jnp.tanh(inputs * (GELU + (0.044715 * GELU) * square))
    half = 0.5 + 0.5 * tanh
    act = inputs * half
    return act, half + act * ((1.0 - tanh) * (GELU + (3 * 0.044715 * GELU) * square))


def mask_keys(scores, tokens):
    rows = scores.shape[0]
    whole = IMG_TOK // 8 * 8
    position = whole + lax.broadcasted_iota(jnp.int32, (rows - whole, 1), 0)
    return jnp.concatenate(
        [scores[:whole], jnp.where(position < tokens, scores[whole:], MASKED / SCORE)], axis=0
    )


def whole(shape):
    return pl.BlockSpec(shape, lambda i, s: (0,) * len(shape), pipeline_mode=pl.Buffered(1))


def held(shape):
    return pl.BlockSpec(shape, lambda i, s: (0,) * len(shape))


def stepped(shape):
    return pl.BlockSpec((1,) + shape, lambda i, s: (i,) + (0,) * len(shape))


def low_of(*shape):
    return jax.ShapeDtypeStruct(shape, LOW)


def f32_of(*shape):
    return jax.ShapeDtypeStruct(shape, F32)


def call(kernel, where, steps, ins, outs, scratch, flops=0, bytes_accessed=0, transcendentals=0, aliases=None,
         after=(), layer=None):
    given = 1 + len(ins)
    name = getattr(kernel, "func", kernel).__name__.removesuffix("_kernel")
    ins = ins + [(pl.BlockSpec(memory_space=pl.ANY), array) for array in after]

    def run(*refs):
        kernel(*refs[:given], *refs[given + len(after) :])

    return pl.pallas_call(
        run,
        name=name,
        grid_spec=pltpu.PrefetchScalarGridSpec(
            num_scalar_prefetch=1,
            grid=(steps,),
            in_specs=[spec for spec, _ in ins],
            out_specs=[spec for spec, _ in outs],
            scratch_shapes=scratch,
        ),
        out_shape=[shape for _, shape in outs],
        input_output_aliases=aliases or {},
        compiler_params=pltpu.CompilerParams(vmem_limit_bytes=VMEM),
        cost_estimate=pl.CostEstimate(
            flops=int(COST.get((name, layer), COST[name]) * SCALE), bytes_accessed=1, transcendentals=0
        ),
    )(where, *[array for _, array in ins])


def turn_part(values, turned, step):
    size = values.shape[1] // 3
    at = pl.ds(pl.multiple_of(jnp.minimum(step, 2) * size, 128), size)
    turned[at, :] = values[:, at].T


def pack_kernel(units, where, qkv_ref, out_ref, up_ref, down_ref, own_attn, other_attn, own_mlp, other_mlp):
    qkv, out = qkv_ref[0].astype(LOW), out_ref[0].astype(LOW)
    up, down = up_ref[0].astype(LOW), down_ref[0].astype(LOW)

    def half(values, number):
        size = values.shape[1] // 2
        return values[:, number * size : (number + 1) * size]

    for number in range(2):
        up_h, down_h = half(up, number), half(down, number)
        attn = [half(qkv, number), half(out, number), up_h[:, units:], down_h[:, units:]]
        used = sum(piece.shape[1] for piece in attn)
        attn.append(jnp.zeros((qkv.shape[0], own_attn.shape[1] - used), LOW))
        attn = jnp.concatenate(attn, axis=1)
        mlp = jnp.concatenate([up_h[:, :units], down_h[:, :units]], axis=1)

        @pl.when(where[3] == number)
        def _():
            own_attn[...] = attn
            own_mlp[...] = mlp

        @pl.when(where[3] != number)
        def _():
            other_attn[...] = attn
            other_mlp[...] = mlp


def attn_forward_kernel(spread, joined, tail_units, where, *refs):
    refs = list(refs)
    count = len(spread.weight_keys)
    if joined:
        base_ref, own_ref, other_ref, old_ref = refs[:4]
        del refs[:4]
    else:
        own_ref, other_ref = refs[:2]
        del refs[:2]
    vec_ref, bias_ref = refs[:2]
    w_refs = refs[2 : 2 + count]
    (stream_ref, turned_ref, qkv_ref, mixed_ref, sums_ref, tail_ref, part_ref, total, held_weight, normed) = refs[
        2 + count :
    ]
    step = pl.program_id(0)

    @pl.when(step == 0)
    def _():
        if not joined:
            half = own_ref.shape[0]
            stream_ref[pl.ds(pl.multiple_of(where[3] * half, 8), half), :] = own_ref[...]
            stream_ref[pl.ds(pl.multiple_of((1 - where[3]) * half, 8), half), :] = other_ref[...]

        if joined:
            branch = own_ref[...].astype(F32) + other_ref[...].astype(F32)
            stream_ref[...] = base_ref[...] + branch + old_ref[0, 7:8, :]
        unit, _ = norm_parts(stream_ref[...])
        normed[...] = (unit * vec_ref[0, 0:1, :] + vec_ref[0, 1:2, :]).astype(LOW)

    weight = spread.load(w_refs, where, held_weight)
    tokens = where[4]
    head_columns = 3 * HD
    local = qkv_ref.shape[2]
    heads = local // head_columns
    bias = []
    for head in range(heads):
        at = head * HD
        query_bias, value_bias = bias_ref[0, 0, 0, :, at : at + HD], bias_ref[0, 1, 0, :, at : at + HD]
        bias += [query_bias, jnp.zeros_like(query_bias), value_bias]
    bias = jnp.concatenate(bias, axis=1)
    qkv = (cdot(normed[...], weight[:, :local]) + bias).astype(LOW)
    qkv_ref[0] = qkv
    mixed = []
    for head in range(heads):
        at = head * head_columns
        query = qkv[:, at : at + HD]
        key = qkv[:, at + HD : at + 2 * HD]
        value = qkv[:, at + 2 * HD : at + 3 * HD]
        scores = mask_keys(cdot(key, query, 1, 1), tokens)
        top = jnp.max(scores, axis=0, keepdims=True)
        raised = jnp.exp2((scores - top) * POWER)
        weight_sum = jnp.sum(raised, axis=0, keepdims=True)
        mixed.append(cdot(value, raised.astype(LOW), 0, 0) * (1.0 / weight_sum))
        sums_ref[0, head : head + 1, :] = top * POWER + jnp.log2(weight_sum)
    mixed = jnp.concatenate(mixed, axis=0).T.astype(LOW)
    mixed_ref[0] = mixed
    at = local + mixed.shape[1]
    part = cdot(mixed, weight[:, local:at], 1, 1)

    @pl.when(step == 0)
    def _():
        total[...] = part

    @pl.when(step > 0)
    def _():
        total[...] += part

    tail_ref[0] = weight[:, at : at + 2 * tail_units]

    @pl.when(step == pl.num_programs(0) - 1)
    def _():
        part_ref[...] = total[...].astype(LOW)
        turned_ref[...] = normed[...].T


def mlp_forward_kernel(spread, where, *refs):
    count = len(spread.weight_keys)
    base_ref, own_ref, other_ref, vec_ref, bias_ref, tail_ref, tail_bias_ref = refs[:7]
    w_refs = refs[7 : 7 + count]
    (middle_ref, turned_ref, act_ref, slope_ref, act_tail_ref, slope_tail_ref, up_tail_ref, down_tail_ref,
     part_ref, total, held_weight, normed) = refs[7 + count :]
    step = pl.program_id(0)

    @pl.when(step == 0)
    def _():
        branch = own_ref[...].astype(F32) + other_ref[...].astype(F32)
        middle = base_ref[...] + branch + vec_ref[0, 4:5, :]
        middle_ref[...] = middle
        unit, _ = norm_parts(middle)
        normed[...] = (unit * vec_ref[0, 5:6, :] + vec_ref[0, 6:7, :]).astype(LOW)
        steps, _, both = tail_ref.shape
        half = both // 2
        up_tail_ref[...] = jnp.concatenate([tail_ref[t, :, :half] for t in range(steps)], axis=1)
        down_tail_ref[...] = jnp.concatenate([tail_ref[t, :, half:] for t in range(steps)], axis=1)
        act, slope = gelu_both(cdot(normed[...], up_tail_ref[...]) + tail_bias_ref[0, 0])
        act = act.astype(LOW)
        act_tail_ref[...] = act
        slope_tail_ref[...] = slope.astype(LOW)
        total[...] = cdot(act, down_tail_ref[...], 1, 1)

    weight = spread.load(w_refs, where, held_weight)
    units = act_ref.shape[2]
    act, slope = gelu_both(cdot(normed[...], weight[:, :units]) + bias_ref[0, 0, 0])
    act = act.astype(LOW)
    act_ref[0] = act
    slope_ref[0] = slope.astype(LOW)
    total[...] += cdot(act, weight[:, units:], 1, 1)

    @pl.when(step == pl.num_programs(0) - 1)
    def _():
        part_ref[...] = total[...].astype(LOW)
        turned_ref[...] = normed[...].T


def mlp_backward_kernel(spread, where, *refs):
    count = len(spread.weight_keys)
    grad_ref, slope_ref, up_tail_ref, down_tail_ref, slope_tail_ref = refs[:5]
    w_refs = refs[5 : 5 + count]
    (hidden_ref, hidden_tail_ref, sums_ref, sums_tail_ref, part_ref, turned_ref, low, total, held_weight) = refs[
        5 + count :
    ]
    step = pl.program_id(0)

    @pl.when(step == 0)
    def _():
        low[...] = grad_ref[...].astype(LOW)
        hidden = cdot(low[...], down_tail_ref[...]) * slope_tail_ref[...].astype(F32)
        sums_tail_ref[...] = jnp.sum(hidden, axis=0, keepdims=True)
        hidden = hidden.astype(LOW)
        hidden_tail_ref[...] = hidden
        total[...] = cdot(hidden, up_tail_ref[...], 1, 1)

    weight = spread.load(w_refs, where, held_weight)
    units = hidden_ref.shape[2]
    turn_part(low, turned_ref, step)
    hidden = cdot(low[...], weight[:, units:]) * slope_ref[0].astype(F32)
    sums_ref[0] = jnp.sum(hidden, axis=0, keepdims=True)
    hidden = hidden.astype(LOW)
    hidden_ref[0] = hidden
    total[...] += cdot(hidden, weight[:, :units], 1, 1)

    @pl.when(step == pl.num_programs(0) - 1)
    def _():
        part_ref[...] = total[...].astype(LOW)


def mlp_grads_kernel(spread, where, *refs):
    count = len(spread.grad_keys)
    grad_turned, normed_turned, hidden_ref, act_ref, hidden_tail_ref, act_tail_ref = refs[:6]
    out_refs = refs[6 : 6 + count]
    tail_ref, result = refs[6 + count :]
    step = pl.program_id(0)

    @pl.when(step == 0)
    def _():
        up_tail = cdot(normed_turned[...], hidden_tail_ref[...]).astype(LOW)
        down_tail = cdot(grad_turned[...], act_tail_ref[...]).astype(LOW)
        steps, _, both = tail_ref.shape
        half = both // 2
        for t in range(steps):
            at = slice(t * half, (t + 1) * half)
            tail_ref[t] = jnp.concatenate([up_tail[:, at], down_tail[:, at]], axis=1)

    units = hidden_ref.shape[2]
    result[:, :units] = cdot(normed_turned[...], hidden_ref[0]).astype(LOW)
    result[:, units:] = cdot(grad_turned[...], act_ref[0]).astype(LOW)
    spread.store(out_refs, where, result)


def attn_backward_kernel(spread, where, *refs):
    count = len(spread.weight_keys)
    grad_ref, own_ref, other_ref, middle_ref, vec_ref, qkv_ref, sums_ref = refs[:7]
    w_refs = refs[7 : 7 + count]
    dmiddle_ref, norm_sums_ref, dqkv_ref, head_sums_ref, part_ref, low, total, held_weight = refs[7 + count :]
    step = pl.program_id(0)

    @pl.when(step == 0)
    def _():
        grad = grad_ref[...]
        dnormed = own_ref[...].astype(F32) + other_ref[...].astype(F32)
        inner, gain_terms = norm_backward(dnormed, middle_ref[...], vec_ref[0, 5:6, :])
        dmiddle = grad + inner
        dmiddle_ref[...] = dmiddle
        low[...] = dmiddle.astype(LOW)
        for number, terms in enumerate((gain_terms, dnormed, grad, dmiddle)):
            norm_sums_ref[number : number + 1, :] = jnp.sum(terms, axis=0, keepdims=True)

    weight = spread.load(w_refs, where, held_weight)
    tokens = where[4]
    head_columns = 3 * HD
    local = qkv_ref.shape[2]
    heads = local // head_columns
    qkv = qkv_ref[0]
    dmixed = cdot(low[...], weight[:, local : local + heads * HD]).astype(LOW)
    pieces = []
    for head in range(heads):
        at = head * head_columns
        query = qkv[:, at : at + HD]
        key = qkv[:, at + HD : at + 2 * HD]
        value = qkv[:, at + 2 * HD : at + 3 * HD]
        grad = dmixed[:, head * HD : (head + 1) * HD]
        scores = mask_keys(cdot(key, query, 1, 1), tokens)
        probs = jnp.exp2(scores * POWER - sums_ref[0, head : head + 1, :])
        dprobs = cdot(value, grad, 1, 1)
        row_dot = jnp.sum(dprobs * probs, axis=0, keepdims=True)
        dscores = (probs * (dprobs - row_dot)).astype(LOW)
        pieces.append(cdot(key, dscores, 0, 0).T * SCORE)
        pieces.append(cdot(dscores, query) * SCORE)
        pieces.append(cdot(probs.astype(LOW), grad))
    dqkv = jnp.concatenate(pieces, axis=1)
    head_sums_ref[0] = jnp.sum(dqkv, axis=0, keepdims=True)
    dqkv = dqkv.astype(LOW)
    dqkv_ref[0] = dqkv
    part = cdot(dqkv, weight[:, :local], 1, 1)

    @pl.when(step == 0)
    def _():
        total[...] = part

    @pl.when(step > 0)
    def _():
        total[...] += part

    @pl.when(step == pl.num_programs(0) - 1)
    def _():
        part_ref[...] = total[...].astype(LOW)


def attn_grads_kernel(spread, where, *refs):
    count = len(spread.grad_keys)
    dmiddle_ref, normed_turned, dqkv_ref, mixed_ref, tail_ref = refs[:5]
    out_refs = refs[5 : 5 + count]
    result, grad_turned = refs[5 + count :]

    @pl.when(pl.program_id(0) == 0)
    def _():
        grad_turned[...] = dmiddle_ref[...].astype(LOW).T

    parts = [
        cdot(normed_turned[...], dqkv_ref[0]).astype(LOW),
        cdot(grad_turned[...], mixed_ref[0]).astype(LOW),
        tail_ref[0],
    ]
    used = sum(part.shape[1] for part in parts)
    parts.append(jnp.zeros((result.shape[0], result.shape[1] - used), LOW))
    result[...] = jnp.concatenate(parts, axis=1)
    spread.store(out_refs, where, result)


def norm_backward_kernel(where, dmiddle_ref, own_ref, other_ref, stream_ref, vec_ref, out_ref, sums_ref):
    dnormed = own_ref[...].astype(F32) + other_ref[...].astype(F32)
    inner, gain_terms = norm_backward(dnormed, stream_ref[...], vec_ref[0, 0:1, :])
    out_ref[...] = dmiddle_ref[...] + inner

    @pl.when(pl.program_id(0) == 0)
    def _():
        sums_ref[...] = jnp.zeros_like(sums_ref)

    sums_ref[0:1, :] += jnp.sum(gain_terms, axis=0, keepdims=True)
    sums_ref[1:2, :] += jnp.sum(dnormed, axis=0, keepdims=True)


def adam_kernel(units, local, out_local, tail_units, where, *refs):
    attn_own, attn_other, mlp_own, mlp_other = refs[:4]
    states = [refs[4 + 3 * k : 7 + 3 * k] for k in range(4)]
    outs = refs[len(refs) - 16 :]

    def pair(own, other):
        own, other = own[...].astype(F32), other[...].astype(F32)
        low_core = where[3] == 0
        return jnp.where(low_core, own, other), jnp.where(low_core, other, own)

    attn = pair(attn_own, attn_other)
    mlp = pair(mlp_own, mlp_other)
    at = local + out_local
    grads = [
        jnp.concatenate([half[:, :local] for half in attn], axis=1),
        jnp.concatenate([half[:, local:at] for half in attn], axis=1),
        jnp.concatenate(
            [piece for m, n in zip(mlp, attn) for piece in (m[:, :units], n[:, at : at + tail_units])], axis=1
        ),
        jnp.concatenate(
            [
                piece
                for m, n in zip(mlp, attn)
                for piece in (m[:, units:], n[:, at + tail_units : at + 2 * tail_units])
            ],
            axis=1,
        ),
    ]
    for number, grad in enumerate(grads):
        weight, first, second = [ref[0] for ref in states[number]]
        new = adam_step(weight, grad, first, second, RATES[number], DECAY)
        for ref, values in zip(outs[4 * number : 4 * number + 4], (grad, new[1], new[2], new[0])):
            ref[0] = values


def vec_pack_kernel(where, *refs):
    out_ref = refs[-1]
    layers = out_ref.shape[0]
    out_ref[...] = jnp.zeros_like(out_ref)
    for layer in range(layers):
        one_ref, two_ref, head_ref, main_ref, tail_ref = refs[5 * layer : 5 * layer + 5]
        out_ref[layer, 0:2, :] = one_ref[0:2, :]
        out_ref[layer, 2:6, :] = two_ref[0:4, :]
        for t in range(head_ref.shape[0]):
            out_ref[layer, 8 + t : 9 + t, : head_ref.shape[2]] = head_ref[t]
            out_ref[layer, 12 + t : 13 + t, : main_ref.shape[2]] = main_ref[t]
        out_ref[layer, 6:7, : tail_ref.shape[1]] = tail_ref[...]


def vec_kernel(steps, local, units, tail_units, where, own_ref, other_ref, vec_ref, first_ref, second_ref,
               grad_out, first_out, second_out, weight_out):
    low_core = where[3] == 0
    for layer in range(vec_ref.shape[0]):
        own, other = own_ref[layer], other_ref[layer]
        cores = jnp.where(low_core, own, other), jnp.where(low_core, other, own)
        norms = cores[0][0:6]
        heads = local // (3 * HD)

        def head_piece(kind):
            return [
                core[8 + t : 9 + t, (3 * head + kind) * HD : (3 * head + kind + 1) * HD]
                for t in range(steps)
                for core in cores
                for head in range(heads)
            ]

        hidden = [
            piece
            for t in range(steps)
            for core in cores
            for piece in (core[12 + t : 13 + t, :units], core[6:7, t * tail_units : (t + 1) * tail_units])
        ]
        grad = jnp.concatenate(
            [norms[0:1], norms[1:2], *head_piece(0), *head_piece(2),
             norms[5:6], norms[2:3], norms[3:4], norms[4:5], *hidden],
            axis=1,
        )
        at = slice(layer, layer + 1)
        new = adam_step(vec_ref[at, :], grad, first_ref[at, :], second_ref[at, :], RATES[4], 0.0)
        grad_out[at, :] = grad
        first_out[at, :] = new[1]
        second_out[at, :] = new[2]
        weight_out[at, :] = new[0]


def plane_sides(chips):
    side = math.isqrt(chips)
    while chips % side:
        side -= 1
    return side, chips // side


class Place:
    def __init__(self):
        self.nf = lax.axis_size("fsdp")
        self.nt = lax.axis_size("tp")
        self.na, self.nb = plane_sides(self.nf // 2)
        fi = lax.axis_index("fsdp")
        self.core = fi % 2
        self.a = (fi // 2) // self.nb
        self.b = (fi // 2) % self.nb
        self.t = lax.axis_index("tp")
        self.size = {"a": self.na, "b": self.nb, "t": self.nt}
        self.at = {"a": self.a, "b": self.b, "t": self.t}

    def pairs(self, axis, move):
        if axis == "t":
            return [(i, move(i)) for i in range(self.nt)]
        found = []
        for f in range(self.nf):
            place = {"a": f // 2 // self.nb, "b": f // 2 % self.nb, "core": f % 2}
            place[axis] = move(place[axis])
            found.append((f, (place["a"] * self.nb + place["b"]) * 2 + place["core"]))
        return found

    def send(self, values, axis, move):
        return lax.ppermute(values, "tp" if axis == "t" else "fsdp", self.pairs(axis, move))

    def sibling(self, values):
        return self.send(values, "core", lambda i: 1 - i)

    def swap_rows(self, values):
        pairs = []
        for f in range(self.nf):
            for t in range(self.nt):
                if f % 2 != t % 2:
                    sign = 1 if t % 2 else -1
                    pairs.append((f * self.nt + t, (f + sign) * self.nt + t - sign))
        arrived = lax.ppermute(values.astype(LOW), ("fsdp", "tp"), pairs).astype(F32)
        return jnp.where(self.core != self.t % 2, arrived, values)

    def gather_axis(self, block, axis):
        n = self.size[axis]
        return [block] + [self.send(block, axis, lambda i, k=k: (i - k) % n) for k in range(1, n)]

    def scatter_axis(self, parts, axis):
        n = self.size[axis]
        sent = [self.send(parts[k], axis, lambda i, k=k: (i + k) % n) for k in range(1, n)]
        return [parts[0], *sent]


def split_pair(place, first, second):
    return (
        jnp.where(place.core == 0, first, second),
        jnp.where(place.core == 0, second, first),
    )


def sum_kernel(outputs, where, *refs):
    count = sum(size for sizes in outputs for size in sizes)
    ins, outs = refs[:count], refs[count:]
    for out_ref, sizes in zip(outs, outputs):
        for number, size in enumerate(sizes):
            for t in range(out_ref.shape[0]):
                total = ins[0][t, 0].astype(F32)
                for ref in ins[1:size]:
                    total += ref[t, 0].astype(F32)
                out_ref[t, number] = total.astype(LOW)
            ins = ins[size:]


def tie_kernel(where, *refs):
    pass


def tie(where, arrays, after):
    space = pl.BlockSpec(memory_space=pl.ANY)
    return call(
        tie_kernel,
        where,
        1,
        [(space, x) for x in arrays],
        [(space, jax.ShapeDtypeStruct(x.shape, x.dtype)) for x in arrays],
        [],
        aliases={1 + k: k for k in range(len(arrays))},
        after=after,
    )


class Spread:
    def __init__(self, place, rows, columns, middle):
        self.place, self.rows, self.columns = place, rows, columns
        self.middle = middle
        self.direct = rows % 16 == 0
        self.width = place.na * place.nb * 2 * rows
        na, nb = place.na, place.nb
        self.grad_keys = [[(0, a, b) for b in range(nb)] for a in range(na)]
        self.grad_keys += [[(1, a, b) for a in range(na)] for b in range(nb)]
        self.gather_keys = [[(0, 0, 0), (1, 0, 0)]]
        self.gather_keys += [[(0, 0, b), (1, 0, b)] for b in range(1, nb)]
        self.gather_keys += [[(0, a, 0), (1, a, 0)] for a in range(1, na)]
        self.gather_keys += [[(half, a, b)] for half in range(2) for a in range(1, na) for b in range(1, nb)]
        if middle:
            self.gather_keys = self.grad_keys
        self.weight_keys = self.gather_keys
        if not self.direct:
            self.weight_keys = self.grad_keys = [None]

    def shapes(self, keys):
        if not self.direct:
            return [(self.place.nt, self.width, self.columns)]
        return [(self.place.nt, len(blocks), self.rows, self.columns) for blocks in keys]

    def specs(self, keys):
        return [stepped(shape[1:]) for shape in self.shapes(keys)]

    def first_row(self, where, key):
        half, a, b = key
        a = lax.rem(where[0] + a, self.place.na)
        b = lax.rem(where[1] + b, self.place.nb)
        return pl.multiple_of(((a * self.place.nb + b) * 2 + half) * self.rows, 16)

    def load(self, refs, where, scratch):
        if not self.direct:
            return refs[0].at[0]
        for ref, blocks in zip(refs, self.weight_keys):
            for number, key in enumerate(blocks):
                scratch[pl.ds(self.first_row(where, key), self.rows), :] = ref[0, number]
        return scratch

    def store(self, refs, where, scratch):
        if not self.direct:
            refs[0][0] = scratch[...]
            return
        for ref, blocks in zip(refs, self.grad_keys):
            for number, key in enumerate(blocks):
                ref[0, number] = scratch[pl.ds(self.first_row(where, key), self.rows), :]

    def start(self, own, other):
        place = self.place
        halves = split_pair(place, own, other)
        if self.middle:
            return [jnp.stack(place.gather_axis(half, axis)) for half, axis in zip(halves, "ba")]
        return [jnp.stack(halves)]

    def gather(self, where, blocks, after=()):
        place = self.place
        na, nb = place.na, place.nb
        blocks = [lax.all_gather(block, "tp") for block in blocks]
        if self.direct and len(after):
            blocks = tie(where, blocks, after)
        if self.middle:
            arrays = [array for block, axis in zip(blocks, "ab") for array in place.gather_axis(block, axis)]
        else:
            along_b = place.gather_axis(blocks[0], "b")
            along_a = place.gather_axis(blocks[0], "a")
            first = [place.gather_axis(x[:, :1], "a")[1:] for x in along_b[1:]]
            second = [place.gather_axis(x[:, 1:], "b")[1:] for x in along_a[1:]]
            arrays = along_b + along_a[1:]
            arrays += [first[b][a] for a in range(na - 1) for b in range(nb - 1)]
            arrays += [second[a][b] for a in range(na - 1) for b in range(nb - 1)]
        if self.direct:
            return arrays
        found = {
            key: array[:, number]
            for array, keys in zip(arrays, self.gather_keys)
            for number, key in enumerate(keys)
        }
        full = jnp.stack([found[half, a, b] for a in range(na) for b in range(nb) for half in range(2)], axis=1)
        full = full.reshape(place.nt, na, nb, 2, self.rows, self.columns)
        full = self.roll(full, (na - place.a) % na, (nb - place.b) % nb)
        return [full.reshape(place.nt, self.width, self.columns)]

    def roll(self, full, a, b):
        full = lax.dynamic_slice_in_dim(jnp.concatenate([full, full], axis=1), a, self.place.na, 1)
        return lax.dynamic_slice_in_dim(jnp.concatenate([full, full], axis=2), b, self.place.nb, 2)

    def sums(self, where, outputs, after, layer=None):
        place, rows, columns = self.place, self.rows, self.columns

        def block(number):
            return pl.BlockSpec((place.nt, 1, rows, columns), lambda i, s: (0, number, 0, 0))

        shapes = [(place.nt, len(groups), rows, columns) for groups in outputs]
        return call(
            functools.partial(sum_kernel, [[len(group) for group in groups] for groups in outputs]),
            where,
            1,
            [(block(number), x) for groups in outputs for group in groups for x, number in group],
            [(held(shape), low_of(*shape)) for shape in shapes],
            [],
            after=after,
            layer=layer,
        )

    def scatter_last(self, arrays):
        place = self.place
        if not self.direct:
            full = arrays[0].reshape(place.nt, place.na, place.nb, 2, self.rows, self.columns)
            full = self.roll(full, place.a, place.b)
            arrays = [full[:, a, :, 0] for a in range(place.na)] + [full[:, :, b, 1] for b in range(place.nb)]
        return (
            place.scatter_axis(arrays[: place.na], "a"),
            place.scatter_axis(arrays[place.na :], "b"),
        )

    def scatter_first(self, where, halves, after):
        place = self.place
        if self.middle:
            outputs = [[[(x, k) for x in half] for k in range(half[0].shape[1])] for half in halves]
            results = self.sums(where, outputs, after)
            return results[0], [lax.psum_scatter(x, "tp", scatter_dimension=0, tiled=True)[0] for x in results]
        axes = ("b", "a")
        keys = [(half, k) for half in range(2) for k in range(1, place.size[axes[half]])]
        results = self.sums(where, [[[(x, k) for x in halves[half]]] for half, k in keys], after)
        terms = [[(x, 0) for x in arrays] for arrays in halves]
        for (half, k), total in zip(keys, results):
            n = place.size[axes[half]]
            terms[half].append((place.send(total, axes[half], lambda i: (i + k) % n), 0))
        return results[0], terms

    def scatter_tp(self, where, terms, after, layer=None):
        place = self.place
        if self.middle:
            if self.direct:
                terms = tie(where, terms, after)
            done = [
                sum(x.astype(F32) for x in place.scatter_axis(list(half), axis)).astype(LOW)
                for half, axis in zip(terms, "ba")
            ]
            last = after[0]
        else:
            (last,) = self.sums(where, [terms], after, layer)
            done = lax.psum_scatter(last, "tp", scatter_dimension=0, tiled=True)[0]
        mine, other = split_pair(place, done[0], done[1])
        return last, (mine, place.sibling(other))


def body(
    residual_in,
    cotangent,
    slot_tokens,
    qkv_weight,
    out_weight,
    up_weight,
    down_weight,
    vectors,
    qkv_first,
    qkv_second,
    out_first,
    out_second,
    up_first,
    up_second,
    down_first,
    down_second,
    vec_first,
    vec_second,
):
    place = Place()
    layer_count, shard_rows, _ = qkv_weight.shape
    half_rows, width = residual_in.shape
    rows = 2 * half_rows
    nt = place.nt
    local = qkv_weight.shape[2] // 2
    out_local = out_weight.shape[1] // 2
    hidden_local = up_weight.shape[2] // 2
    units = hidden_local // 128 * 128
    tail_units = hidden_local - units
    heads = out_local // HD
    attn_columns = -(-(local + out_local + 2 * tail_units) // 128) * 128
    mlp_columns = 2 * units

    tokens_pair = jnp.concatenate(split_pair(place, slot_tokens, place.sibling(slot_tokens)))
    slot_at = (place.t % 2) * slot_tokens.shape[0] + place.t // 2
    tokens = lax.dynamic_slice_in_dim(tokens_pair, slot_at, 1)
    row_mask = (jnp.arange(rows, dtype=jnp.int32) < tokens[0]).astype(F32)[:, None]
    here = jnp.stack([place.a, place.b, place.t, place.core]).astype(jnp.int32)
    where = jnp.concatenate([here, tokens.astype(jnp.int32)])

    def own_rows(values):
        return lax.dynamic_slice_in_dim(values, place.core * half_rows, half_rows)

    spreads = [
        (
            Spread(place, shard_rows, attn_columns, False),
            Spread(place, shard_rows, mlp_columns, layer > 0),
        )
        for layer in range(layer_count)
    ]

    def turn(arrays):
        qkv, out, up, down = arrays
        return qkv, jnp.swapaxes(out, 1, 2), up, jnp.swapaxes(down, 1, 2)

    weights = turn((qkv_weight, out_weight, up_weight, down_weight))
    firsts = turn((qkv_first, out_first, up_first, down_first))
    seconds = turn((qkv_second, out_second, up_second, down_second))

    def layer_block(array, layer, steps=1):
        block = (1, array.shape[1] // steps, array.shape[2])
        return pl.BlockSpec(block, lambda i, s: (layer, i, 0))

    def pack(layer):
        attn, mlp = (shard_rows, attn_columns), (shard_rows, mlp_columns)
        return call(
            functools.partial(pack_kernel, units),
            here,
            1,
            [(layer_block(w, layer), w) for w in weights],
            [(held(shape), low_of(*shape)) for shape in (attn, attn, mlp, mlp)],
            [],
            bytes_accessed=6 * shard_rows * 13216 // 4,
        )

    starts = []
    for layer in range(layer_count):
        own_attn, other_attn, own_mlp, other_mlp = pack(layer)
        starts.append(
            (
                spreads[layer][0].start(own_attn, place.sibling(other_attn)),
                spreads[layer][1].start(own_mlp, place.sibling(other_mlp)),
            )
        )
    gathered = []
    before = [x for pair in starts[1:] for blocks in pair for x in blocks]
    for layer in range(layer_count):
        attn_full = spreads[layer][0].gather(where, starts[layer][0], before)
        mlp_full = spreads[layer][1].gather(where, starts[layer][1], attn_full[1:3])
        before = mlp_full[1:3]
        gathered.append((attn_full, mlp_full))

    wide = vectors[:, : 8 * width].reshape(layer_count, 8, width)
    head_bias = vectors[:, 2 * width : 4 * width].reshape(layer_count, 2, 2 * nt, 1, out_local)
    hidden_bias = vectors[:, 8 * width :].reshape(layer_count, nt, 2, 1, hidden_local)
    main_bias = hidden_bias[..., :units]
    tail_bias = jnp.moveaxis(hidden_bias[..., units:], 1, 3).reshape(layer_count, 2, 1, nt * tail_units)

    full = whole((rows, width))
    weight_scratch = [
        pltpu.VMEM((width, attn_columns), LOW),
        pltpu.VMEM((width, mlp_columns), LOW),
    ]
    flat = pltpu.VMEM((rows, width), F32)
    flat_low = pltpu.VMEM((rows, width), LOW)
    big = 2 * rows * width

    def wide_of(layer):
        spec = pl.BlockSpec((1, 8, width), lambda i, s: (layer, 0, 0), pipeline_mode=pl.Buffered(1))
        return spec, wide

    def attn_forward(layer, base, own, other):
        spread = spreads[layer][0]
        joined = base is not None
        if joined:
            ins = [(full, base), (full, own), (full, other), wide_of(layer - 1)]
        else:
            half = whole((half_rows, width))
            ins = [(half, own), (half, other)]
        ins.append(wide_of(layer))
        ins.append(
            (
                pl.BlockSpec(
                    (1, 2, 1, 1, out_local), lambda i, s: (layer, 0, 2 * i + s[3], 0, 0)
                ),
                head_bias,
            )
        )
        ins += list(zip(spread.specs(spread.weight_keys), gathered[layer][0]))
        return call(
            functools.partial(attn_forward_kernel, spread, joined, tail_units),
            where,
            nt,
            ins,
            [
                (held((rows, width)), f32_of(rows, width)),
                (held((width, rows)), low_of(width, rows)),
                (stepped((rows, local)), low_of(nt, rows, local)),
                (stepped((rows, out_local)), low_of(nt, rows, out_local)),
                (stepped((heads, rows)), f32_of(nt, heads, rows)),
                (stepped((width, 2 * tail_units)), low_of(nt, width, 2 * tail_units)),
                (held((rows, width)), low_of(rows, width)),
            ],
            [flat, weight_scratch[0], flat_low],
            big * nt * (local + out_local) + 4 * nt * heads * rows * rows * HD,
            rows * width * 12 + nt * width * attn_columns * 2,
            nt * heads * rows * rows,
        )

    def mlp_forward(layer, base, own, other, tails, after=()):
        spread = spreads[layer][1]
        tail = nt * tail_units
        tail_shape = (width, tail)
        ins = [
            (full, base),
            (full, own),
            (full, other),
            wide_of(layer),
            (pl.BlockSpec((1, 1, 1, 1, units), lambda i, s: (layer, i, s[3], 0, 0)), main_bias),
            (whole(tails.shape), tails),
            (pl.BlockSpec((1, 1, 1, tail), lambda i, s: (layer, s[3], 0, 0)), tail_bias),
        ]
        ins += list(zip(spread.specs(spread.weight_keys), gathered[layer][1]))
        return call(
            functools.partial(mlp_forward_kernel, spread),
            where,
            nt,
            ins,
            [
                (held((rows, width)), f32_of(rows, width)),
                (held((width, rows)), low_of(width, rows)),
                (stepped((rows, units)), low_of(nt, rows, units)),
                (stepped((rows, units)), low_of(nt, rows, units)),
                (held((rows, tail)), low_of(rows, tail)),
                (held((rows, tail)), low_of(rows, tail)),
                (held(tail_shape), low_of(*tail_shape)),
                (held(tail_shape), low_of(*tail_shape)),
                (held((rows, width)), low_of(rows, width)),
            ],
            [flat, weight_scratch[1], flat_low],
            2 * big * (nt * units + tail),
            rows * width * 16 + nt * (width + rows) * mlp_columns * 2,
            rows * nt * units,
            after=after,
        )

    def mlp_backward(layer, grad, slope, tails, slope_tail):
        spread = spreads[layer][1]
        tail = nt * tail_units
        ins = [(full, grad), (stepped((rows, units)), slope)]
        ins += [(whole(w.shape), w) for w in (*tails, slope_tail)]
        ins += list(zip(spread.specs(spread.weight_keys), gathered[layer][1]))
        return call(
            functools.partial(mlp_backward_kernel, spread),
            where,
            nt,
            ins,
            [
                (stepped((rows, units)), low_of(nt, rows, units)),
                (held((rows, tail)), low_of(rows, tail)),
                (stepped((1, units)), f32_of(nt, 1, units)),
                (held((1, tail)), f32_of(1, tail)),
                (held((rows, width)), low_of(rows, width)),
                (held((width, rows)), low_of(width, rows)),
            ],
            [flat_low, flat, weight_scratch[1]],
            2 * big * (nt * units + tail),
            rows * width * 6 + nt * (width + rows) * mlp_columns * 2,
        )

    def mlp_grads(layer, grad, normed, hidden, act, hidden_tail, act_tail):
        spread = spreads[layer][1]
        ins = [(whole((width, rows)), grad), (whole((width, rows)), normed)]
        ins += [(stepped((rows, units)), hidden), (stepped((rows, units)), act)]
        ins += [(whole(x.shape), x) for x in (hidden_tail, act_tail)]
        tail_shape = (nt, width, 2 * tail_units)
        outs = [
            (spec, low_of(*shape))
            for spec, shape in zip(spread.specs(spread.grad_keys), spread.shapes(spread.grad_keys))
        ]
        outs.append((held(tail_shape), low_of(*tail_shape)))
        return call(
            functools.partial(mlp_grads_kernel, spread),
            where,
            nt,
            ins,
            outs,
            [weight_scratch[1]],
            2 * big * nt * (units + tail_units),
            rows * width * 6 + nt * (width + rows) * mlp_columns * 2,
        )

    def attn_backward(layer, grad, own, other, middle, qkv, log_sums, after=()):
        spread = spreads[layer][0]
        ins = [(full, grad), (full, own), (full, other), (full, middle), wide_of(layer)]
        ins += [(stepped((rows, local)), qkv), (stepped((heads, rows)), log_sums)]
        ins += list(zip(spread.specs(spread.weight_keys), gathered[layer][0]))
        return call(
            functools.partial(attn_backward_kernel, spread),
            where,
            nt,
            ins,
            [
                (held((rows, width)), f32_of(rows, width)),
                (held((8, width)), f32_of(8, width)),
                (stepped((rows, local)), low_of(nt, rows, local)),
                (stepped((1, local)), f32_of(nt, 1, local)),
                (held((rows, width)), low_of(rows, width)),
            ],
            [flat_low, flat, weight_scratch[0]],
            big * nt * (local + out_local) + 10 * nt * heads * rows * rows * HD,
            rows * width * 20 + nt * width * attn_columns * 2,
            nt * heads * rows * rows,
            after=after,
        )

    def attn_grads(layer, dmiddle, normed, dqkv, mixed, tail_grads):
        spread = spreads[layer][0]
        ins = [(full, dmiddle), (whole((width, rows)), normed)]
        ins += [(stepped((rows, local)), dqkv), (stepped((rows, out_local)), mixed)]
        ins.append((stepped((width, 2 * tail_units)), tail_grads))
        outs = [
            (spec, low_of(*shape))
            for spec, shape in zip(spread.specs(spread.grad_keys), spread.shapes(spread.grad_keys))
        ]
        return call(
            functools.partial(attn_grads_kernel, spread),
            where,
            nt,
            ins,
            outs,
            [weight_scratch[0], pltpu.VMEM((width, rows), LOW)],
            big * nt * (local + out_local),
            rows * width * 6 + nt * (width + rows) * attn_columns * 2,
        )

    def norm_one_backward(layer, dmiddle, own, other, stream, after=()):
        part = pl.BlockSpec((half_rows, width), lambda i, s: (i, 0))
        return call(
            norm_backward_kernel,
            where,
            2,
            [(part, dmiddle), (part, own), (part, other), (part, stream), wide_of(layer)],
            [(part, f32_of(rows, width)), (held((8, width)), f32_of(8, width))],
            [],
            rows * width * 20,
            rows * width * 16,
            after=after,
        )

    grad_stream = None
    mine = place.swap_rows(residual_in)
    base, own, other = None, mine, place.sibling(mine)
    saved = []
    for layer in range(layer_count):
        stream, normed, qkv, mixed, log_sums, tails, part = attn_forward(layer, base, own, other)
        if layer == layer_count - 1:
            (mine,) = tie(where, [place.swap_rows(cotangent)], [qkv])
            grad_stream = jnp.concatenate(split_pair(place, mine, place.sibling(mine)), axis=0) * row_mask
        middle, normed_two, act, slope, act_tail, slope_tail, up_tail, down_tail, part = mlp_forward(
            layer, stream, part, place.sibling(part), tails
        )
        saved.append(
            (stream, normed, qkv, mixed, log_sums, middle, normed_two, act, slope, act_tail, slope_tail,
             (up_tail, down_tail))
        )
        base, own, other = middle, part, place.sibling(part)
    output = own_rows(base) + (own_rows(own).astype(F32) + own_rows(other).astype(F32))
    output = place.swap_rows((output + wide[layer_count - 1, 7:8]) * own_rows(row_mask))


    def adam(layer, attn_pair, mlp_pair, before, after=()):
        steps = 1
        ins = [
            (pl.BlockSpec((shard_rows // steps, x.shape[1]), lambda i, s: (i, 0)), x)
            for x in (*attn_pair, *mlp_pair)
        ]
        for states in zip(weights, firsts, seconds):
            ins += [(layer_block(x, layer, steps), x) for x in states]
        outs = [
            (layer_block(weight, layer, steps), f32_of(*weight.shape)) for weight in weights for _ in range(4)
        ]
        aliases = None
        if before is not None:
            aliases = {1 + len(ins) + k: k for k in range(16)}
            ins += [(pl.BlockSpec(memory_space=pl.ANY), x) for x in before]
        return call(
            functools.partial(adam_kernel, units, local, out_local, tail_units),
            where,
            steps,
            ins,
            outs,
            [],
            bytes_accessed=28 * shard_rows * 13216 // 4,
            aliases=aliases,
            after=after,
        )

    vec_sums = [None] * layer_count
    last = grad_stream
    above = None
    for layer in reversed(range(layer_count)):
        (stream, normed, qkv, mixed, log_sums, middle, normed_two, act, slope, act_tail, slope_tail, tails) = (
            saved[layer]
        )
        spread_attn, spread_mlp = spreads[layer]
        hidden, hidden_tail, hidden_sums, tail_sums, part, grad_turned = mlp_backward(
            layer, grad_stream, slope, tails, slope_tail
        )
        other = place.sibling(part)
        *mlp_grad, tail_grads = mlp_grads(
            layer, grad_turned, normed_two, hidden, act, hidden_tail, act_tail
        )
        last = tail_grads
        arrived = [x for half in attn_terms_above for x in half[1:]] if above else []
        mlp_terms = spread_mlp.scatter_last(mlp_grad)
        dmiddle, norm_two_sums, dqkv, head_sums, part = attn_backward(
            layer, grad_stream, part, other, middle, qkv, log_sums, [last, *arrived]
        )
        other = place.sibling(part)
        attn_grad = attn_grads(layer, dmiddle, normed, dqkv, mixed, tail_grads)
        last = attn_grad[0]
        if above:
            last, attn_terms_above = spreads[above][0].scatter_first(where, attn_terms_above, [last, output])
        grad_stream, norm_one_sums = norm_one_backward(layer, dmiddle, part, other, stream, [last])
        if layer:
            attn_terms = spread_attn.scatter_last(attn_grad)
        last, mlp_terms = spread_mlp.scatter_first(where, mlp_terms, [norm_one_sums])
        vec_sums[layer] = (norm_one_sums, norm_two_sums, head_sums, hidden_sums, tail_sums)
        if above:
            grad_input = place.swap_rows(own_rows(grad_stream))
            last, attn_pair_one = spreads[above][0].scatter_tp(where, attn_terms_above, [last, grad_input], 1)
            mlp_terms_one = mlp_terms_above
            if spread_attn.direct:
                attn_grad = tie(where, attn_grad, [last])
            attn_terms = spread_attn.scatter_last(attn_grad)
        above, mlp_terms_above, attn_terms_above = layer, mlp_terms, attn_terms
        if layer:
            grad_stream, last = lax.optimization_barrier((grad_stream, last))
    last, mlp_pair_above = spreads[above][1].scatter_tp(where, mlp_terms_above, [last])
    _, mlp_pair_one = spreads[1][1].scatter_tp(where, mlp_terms_one, [last])
    last, attn_terms_above = spreads[above][0].scatter_first(where, attn_terms_above, [last])
    updated = adam(1, attn_pair_one, mlp_pair_one, None, [last])
    last, attn_pair_above = spreads[above][0].scatter_tp(where, attn_terms_above, [last, updated[0]])

    flat_sums = [x for sums in vec_sums for x in sums]
    vec_shape = (layer_count, 16, width)
    (vec_total,) = call(
        vec_pack_kernel,
        where,
        1,
        [(whole(x.shape), x) for x in flat_sums],
        [(held(vec_shape), f32_of(*vec_shape))],
        [],
        after=[last, *mlp_pair_above],
    )
    for axis in ("b", "a", "t"):
        step = 1
        while step < place.size[axis]:
            vec_total = vec_total + place.send(vec_total, axis, lambda i: i ^ step)
            step *= 2
    vec_new = call(
        functools.partial(vec_kernel, nt, local, units, tail_units),
        where,
        1,
        [(whole(x.shape), x) for x in (vec_total, place.sibling(vec_total), vectors, vec_first, vec_second)],
        [(held(vectors.shape), f32_of(*vectors.shape)) for _ in range(4)],
        [],
    )
    updated = adam(above, attn_pair_above, mlp_pair_above, updated)
    updated = [
        jnp.swapaxes(x, 1, 2) if number // 4 % 2 else x for number, x in enumerate(updated)
    ]
    return (output, grad_input, *updated, *vec_new)


def solution(mesh):
    rows = P(("fsdp", "tp"), None)
    wide = P(None, "fsdp", "tp")
    tall = P(None, "tp", "fsdp")
    moments = (wide, wide, tall, tall, wide, wide, tall, tall, P(), P())
    return jax.shard_map(
        body,
        mesh=mesh,
        in_specs=(rows, rows, P("fsdp"), wide, tall, wide, tall, P(), *moments),
        out_specs=(rows, rows, *[wide] * 4, *[tall] * 4, *[wide] * 4, *[tall] * 4, *[P()] * 4),
        check_vma=False,
    )
```

```python
import functools
import math

import jax
import jax.numpy as jnp
from jax import lax
from jax.experimental import pallas as pl
from jax.experimental.pallas import tpu as pltpu
from jax.sharding import PartitionSpec as P

HD = 72
IMG_TOK = 729
STEP = 10


EPS_NORM = 1e-06
MASKED = -30000.0
BETA_ONE = 0.9
BETA_TWO = 0.999
ADAM_EPS = 1e-08
DECAY = 0.1
RATES = (0.05, 1.0, 0.05, 0.03, 0.3)
LOW = jnp.bfloat16
F32 = jnp.float32
GELU = math.sqrt(2.0 / math.pi)
SCORE = HD ** (-0.5)
POWER = SCORE / math.log(2.0)
VMEM = 56 * 1024 * 1024
COST = {
    "pack": 4,
    "attn_forward": 26,
    "mlp_forward": 24,
    "mlp_backward": 17,
    "mlp_grads": 16,
    "attn_backward": 33,
    "attn_grads": 13,
    "norm_backward": 9,
    "sum": 5,
    "vec_pack": 0.3,
    "vec": 0.3,
    "adam": 1,
    "tie": 1,
}
SCALE = 2e9


def adam_step(weight, gradient, first_moment, second_moment, step_rate, decay_rate):
    first_new = BETA_ONE * first_moment + (1.0 - BETA_ONE) * gradient
    second_new = BETA_TWO * second_moment + (1.0 - BETA_TWO) * gradient * gradient
    first_hat = first_new / (1.0 - BETA_ONE**STEP)
    second_hat = second_new / (1.0 - BETA_TWO**STEP)
    weight_new = weight - step_rate * (
        first_hat / (jnp.sqrt(second_hat) + ADAM_EPS) + decay_rate * weight
    )
    return (weight_new, first_new, second_new)


def cdot(left, right, left_dim=1, right_dim=0):
    return lax.dot_general(
        left, right, (((left_dim,), (right_dim,)), ((), ())), preferred_element_type=F32
    )


def norm_parts(values):
    centred = values - jnp.mean(values, axis=-1, keepdims=True)
    inverse = lax.rsqrt(jnp.mean(centred * centred, axis=-1, keepdims=True) + EPS_NORM)
    return centred * inverse, inverse


def norm_backward(grad_out, values, gain):
    unit, inverse = norm_parts(values)
    scaled = grad_out * gain
    mean_one = jnp.mean(scaled, axis=-1, keepdims=True)
    mean_two = jnp.mean(scaled * unit, axis=-1, keepdims=True)
    return inverse * (scaled - mean_one - unit * mean_two), grad_out * unit


def gelu_both(inputs):
    square = inputs * inputs
    tanh = jnp.tanh(inputs * (GELU + (0.044715 * GELU) * square))
    half = 0.5 + 0.5 * tanh
    act = inputs * half
    return act, half + act * ((1.0 - tanh) * (GELU + (3 * 0.044715 * GELU) * square))


def mask_keys(scores, tokens):
    rows = scores.shape[0]
    whole = IMG_TOK // 8 * 8
    position = whole + lax.broadcasted_iota(jnp.int32, (rows - whole, 1), 0)
    return jnp.concatenate(
        [scores[:whole], jnp.where(position < tokens, scores[whole:], MASKED / SCORE)], axis=0
    )


def whole(shape):
    return pl.BlockSpec(shape, lambda i, s: (0,) * len(shape), pipeline_mode=pl.Buffered(1))


def held(shape):
    return pl.BlockSpec(shape, lambda i, s: (0,) * len(shape))


def stepped(shape):
    return pl.BlockSpec((1,) + shape, lambda i, s: (i,) + (0,) * len(shape))


def low_of(*shape):
    return jax.ShapeDtypeStruct(shape, LOW)


def f32_of(*shape):
    return jax.ShapeDtypeStruct(shape, F32)


def call(kernel, where, steps, ins, outs, scratch, flops=0, bytes_accessed=0, transcendentals=0, aliases=None,
         after=(), layer=None):
    given = 1 + len(ins)
    name = getattr(kernel, "func", kernel).__name__.removesuffix("_kernel")
    ins = ins + [(pl.BlockSpec(memory_space=pl.ANY), array) for array in after]

    def run(*refs):
        kernel(*refs[:given], *refs[given + len(after) :])

    return pl.pallas_call(
        run,
        name=name,
        grid_spec=pltpu.PrefetchScalarGridSpec(
            num_scalar_prefetch=1,
            grid=(steps,),
            in_specs=[spec for spec, _ in ins],
            out_specs=[spec for spec, _ in outs],
            scratch_shapes=scratch,
        ),
        out_shape=[shape for _, shape in outs],
        input_output_aliases=aliases or {},
        compiler_params=pltpu.CompilerParams(vmem_limit_bytes=VMEM),
        cost_estimate=pl.CostEstimate(
            flops=int(COST.get((name, layer), COST[name]) * SCALE), bytes_accessed=1, transcendentals=0
        ),
    )(where, *[array for _, array in ins])


def turn_part(values, turned, step):
    size = values.shape[1] // 3
    at = pl.ds(pl.multiple_of(jnp.minimum(step, 2) * size, 128), size)
    turned[at, :] = values[:, at].T


def pack_kernel(units, where, qkv_ref, out_ref, up_ref, down_ref, own_attn, other_attn, own_mlp, other_mlp):
    qkv, out = qkv_ref[0].astype(LOW), out_ref[0].astype(LOW)
    up, down = up_ref[0].astype(LOW), down_ref[0].astype(LOW)

    def half(values, number):
        size = values.shape[1] // 2
        return values[:, number * size : (number + 1) * size]

    for number in range(2):
        up_h, down_h = half(up, number), half(down, number)
        attn = [half(qkv, number), half(out, number), up_h[:, units:], down_h[:, units:]]
        used = sum(piece.shape[1] for piece in attn)
        attn.append(jnp.zeros((qkv.shape[0], own_attn.shape[1] - used), LOW))
        attn = jnp.concatenate(attn, axis=1)
        mlp = jnp.concatenate([up_h[:, :units], down_h[:, :units]], axis=1)

        @pl.when(where[3] == number)
        def _():
            own_attn[...] = attn
            own_mlp[...] = mlp

        @pl.when(where[3] != number)
        def _():
            other_attn[...] = attn
            other_mlp[...] = mlp


def attn_forward_kernel(spread, joined, tail_units, where, *refs):
    refs = list(refs)
    count = len(spread.weight_keys)
    if joined:
        base_ref, own_ref, other_ref, old_ref = refs[:4]
        del refs[:4]
    else:
        own_ref, other_ref = refs[:2]
        del refs[:2]
    vec_ref, bias_ref = refs[:2]
    w_refs = refs[2 : 2 + count]
    (stream_ref, turned_ref, qkv_ref, mixed_ref, sums_ref, tail_ref, part_ref, total, held_weight, normed) = refs[
        2 + count :
    ]
    step = pl.program_id(0)

    @pl.when(step == 0)
    def _():
        if not joined:
            half = own_ref.shape[0]
            stream_ref[pl.ds(pl.multiple_of(where[3] * half, 8), half), :] = own_ref[...]
            stream_ref[pl.ds(pl.multiple_of((1 - where[3]) * half, 8), half), :] = other_ref[...]

        if joined:
            branch = own_ref[...].astype(F32) + other_ref[...].astype(F32)
            stream_ref[...] = base_ref[...] + branch + old_ref[0, 7:8, :]
        unit, _ = norm_parts(stream_ref[...])
        normed[...] = (unit * vec_ref[0, 0:1, :] + vec_ref[0, 1:2, :]).astype(LOW)

    weight = spread.load(w_refs, where, held_weight)
    tokens = where[4]
    head_columns = 3 * HD
    local = qkv_ref.shape[2]
    heads = local // head_columns
    bias = []
    for head in range(heads):
        at = head * HD
        query_bias, value_bias = bias_ref[0, 0, 0, :, at : at + HD], bias_ref[0, 1, 0, :, at : at + HD]
        bias += [query_bias, jnp.zeros_like(query_bias), value_bias]
    bias = jnp.concatenate(bias, axis=1)
    qkv = (cdot(normed[...], weight[:, :local]) + bias).astype(LOW)
    qkv_ref[0] = qkv
    mixed = []
    for head in range(heads):
        at = head * head_columns
        query = qkv[:, at : at + HD]
        key = qkv[:, at + HD : at + 2 * HD]
        value = qkv[:, at + 2 * HD : at + 3 * HD]
        scores = mask_keys(cdot(key, query, 1, 1), tokens)
        top = jnp.max(scores, axis=0, keepdims=True)
        raised = jnp.exp2((scores - top) * POWER)
        weight_sum = jnp.sum(raised, axis=0, keepdims=True)
        mixed.append(cdot(value, raised.astype(LOW), 0, 0) * (1.0 / weight_sum))
        sums_ref[0, head : head + 1, :] = top * POWER + jnp.log2(weight_sum)
    mixed = jnp.concatenate(mixed, axis=0).T.astype(LOW)
    mixed_ref[0] = mixed
    at = local + mixed.shape[1]
    part = cdot(mixed, weight[:, local:at], 1, 1)

    @pl.when(step == 0)
    def _():
        total[...] = part

    @pl.when(step > 0)
    def _():
        total[...] += part

    tail_ref[0] = weight[:, at : at + 2 * tail_units]

    @pl.when(step == pl.num_programs(0) - 1)
    def _():
        part_ref[...] = total[...].astype(LOW)
        turned_ref[...] = normed[...].T


def mlp_forward_kernel(spread, where, *refs):
    count = len(spread.weight_keys)
    base_ref, own_ref, other_ref, vec_ref, bias_ref, tail_ref, tail_bias_ref = refs[:7]
    w_refs = refs[7 : 7 + count]
    (middle_ref, turned_ref, act_ref, slope_ref, act_tail_ref, slope_tail_ref, up_tail_ref, down_tail_ref,
     part_ref, total, held_weight, normed) = refs[7 + count :]
    step = pl.program_id(0)

    @pl.when(step == 0)
    def _():
        branch = own_ref[...].astype(F32) + other_ref[...].astype(F32)
        middle = base_ref[...] + branch + vec_ref[0, 4:5, :]
        middle_ref[...] = middle
        unit, _ = norm_parts(middle)
        normed[...] = (unit * vec_ref[0, 5:6, :] + vec_ref[0, 6:7, :]).astype(LOW)
        steps, _, both = tail_ref.shape
        half = both // 2
        up_tail_ref[...] = jnp.concatenate([tail_ref[t, :, :half] for t in range(steps)], axis=1)
        down_tail_ref[...] = jnp.concatenate([tail_ref[t, :, half:] for t in range(steps)], axis=1)
        act, slope = gelu_both(cdot(normed[...], up_tail_ref[...]) + tail_bias_ref[0, 0])
        act = act.astype(LOW)
        act_tail_ref[...] = act
        slope_tail_ref[...] = slope.astype(LOW)
        total[...] = cdot(act, down_tail_ref[...], 1, 1)

    weight = spread.load(w_refs, where, held_weight)
    units = act_ref.shape[2]
    act, slope = gelu_both(cdot(normed[...], weight[:, :units]) + bias_ref[0, 0, 0])
    act = act.astype(LOW)
    act_ref[0] = act
    slope_ref[0] = slope.astype(LOW)
    total[...] += cdot(act, weight[:, units:], 1, 1)

    @pl.when(step == pl.num_programs(0) - 1)
    def _():
        part_ref[...] = total[...].astype(LOW)
        turned_ref[...] = normed[...].T


def mlp_backward_kernel(spread, where, *refs):
    count = len(spread.weight_keys)
    grad_ref, slope_ref, up_tail_ref, down_tail_ref, slope_tail_ref = refs[:5]
    w_refs = refs[5 : 5 + count]
    (hidden_ref, hidden_tail_ref, sums_ref, sums_tail_ref, part_ref, turned_ref, low, total, held_weight) = refs[
        5 + count :
    ]
    step = pl.program_id(0)

    @pl.when(step == 0)
    def _():
        low[...] = grad_ref[...].astype(LOW)
        hidden = cdot(low[...], down_tail_ref[...]) * slope_tail_ref[...].astype(F32)
        sums_tail_ref[...] = jnp.sum(hidden, axis=0, keepdims=True)
        hidden = hidden.astype(LOW)
        hidden_tail_ref[...] = hidden
        total[...] = cdot(hidden, up_tail_ref[...], 1, 1)

    weight = spread.load(w_refs, where, held_weight)
    units = hidden_ref.shape[2]
    turn_part(low, turned_ref, step)
    hidden = cdot(low[...], weight[:, units:]) * slope_ref[0].astype(F32)
    sums_ref[0] = jnp.sum(hidden, axis=0, keepdims=True)
    hidden = hidden.astype(LOW)
    hidden_ref[0] = hidden
    total[...] += cdot(hidden, weight[:, :units], 1, 1)

    @pl.when(step == pl.num_programs(0) - 1)
    def _():
        part_ref[...] = total[...].astype(LOW)


def mlp_grads_kernel(spread, where, *refs):
    count = len(spread.grad_keys)
    grad_turned, normed_turned, hidden_ref, act_ref, hidden_tail_ref, act_tail_ref = refs[:6]
    out_refs = refs[6 : 6 + count]
    tail_ref, result = refs[6 + count :]
    step = pl.program_id(0)

    @pl.when(step == 0)
    def _():
        up_tail = cdot(normed_turned[...], hidden_tail_ref[...]).astype(LOW)
        down_tail = cdot(grad_turned[...], act_tail_ref[...]).astype(LOW)
        steps, _, both = tail_ref.shape
        half = both // 2
        for t in range(steps):
            at = slice(t * half, (t + 1) * half)
            tail_ref[t] = jnp.concatenate([up_tail[:, at], down_tail[:, at]], axis=1)

    units = hidden_ref.shape[2]
    result[:, :units] = cdot(normed_turned[...], hidden_ref[0]).astype(LOW)
    result[:, units:] = cdot(grad_turned[...], act_ref[0]).astype(LOW)
    spread.store(out_refs, where, result)


def attn_backward_kernel(spread, where, *refs):
    count = len(spread.weight_keys)
    grad_ref, own_ref, other_ref, middle_ref, vec_ref, qkv_ref, sums_ref = refs[:7]
    w_refs = refs[7 : 7 + count]
    dmiddle_ref, norm_sums_ref, dqkv_ref, head_sums_ref, part_ref, low, total, held_weight = refs[7 + count :]
    step = pl.program_id(0)

    @pl.when(step == 0)
    def _():
        grad = grad_ref[...]
        dnormed = own_ref[...].astype(F32) + other_ref[...].astype(F32)
        inner, gain_terms = norm_backward(dnormed, middle_ref[...], vec_ref[0, 5:6, :])
        dmiddle = grad + inner
        dmiddle_ref[...] = dmiddle
        low[...] = dmiddle.astype(LOW)
        for number, terms in enumerate((gain_terms, dnormed, grad, dmiddle)):
            norm_sums_ref[number : number + 1, :] = jnp.sum(terms, axis=0, keepdims=True)

    weight = spread.load(w_refs, where, held_weight)
    tokens = where[4]
    head_columns = 3 * HD
    local = qkv_ref.shape[2]
    heads = local // head_columns
    qkv = qkv_ref[0]
    dmixed = cdot(low[...], weight[:, local : local + heads * HD]).astype(LOW)
    pieces = []
    for head in range(heads):
        at = head * head_columns
        query = qkv[:, at : at + HD]
        key = qkv[:, at + HD : at + 2 * HD]
        value = qkv[:, at + 2 * HD : at + 3 * HD]
        grad = dmixed[:, head * HD : (head + 1) * HD]
        scores = mask_keys(cdot(key, query, 1, 1), tokens)
        probs = jnp.exp2(scores * POWER - sums_ref[0, head : head + 1, :])
        dprobs = cdot(value, grad, 1, 1)
        row_dot = jnp.sum(dprobs * probs, axis=0, keepdims=True)
        dscores = (probs * (dprobs - row_dot)).astype(LOW)
        pieces.append(cdot(key, dscores, 0, 0).T * SCORE)
        pieces.append(cdot(dscores, query) * SCORE)
        pieces.append(cdot(probs.astype(LOW), grad))
    dqkv = jnp.concatenate(pieces, axis=1)
    head_sums_ref[0] = jnp.sum(dqkv, axis=0, keepdims=True)
    dqkv = dqkv.astype(LOW)
    dqkv_ref[0] = dqkv
    part = cdot(dqkv, weight[:, :local], 1, 1)

    @pl.when(step == 0)
    def _():
        total[...] = part

    @pl.when(step > 0)
    def _():
        total[...] += part

    @pl.when(step == pl.num_programs(0) - 1)
    def _():
        part_ref[...] = total[...].astype(LOW)


def attn_grads_kernel(spread, where, *refs):
    count = len(spread.grad_keys)
    dmiddle_ref, normed_turned, dqkv_ref, mixed_ref, tail_ref = refs[:5]
    out_refs = refs[5 : 5 + count]
    result, grad_turned = refs[5 + count :]

    @pl.when(pl.program_id(0) == 0)
    def _():
        grad_turned[...] = dmiddle_ref[...].astype(LOW).T

    parts = [
        cdot(normed_turned[...], dqkv_ref[0]).astype(LOW),
        cdot(grad_turned[...], mixed_ref[0]).astype(LOW),
        tail_ref[0],
    ]
    used = sum(part.shape[1] for part in parts)
    parts.append(jnp.zeros((result.shape[0], result.shape[1] - used), LOW))
    result[...] = jnp.concatenate(parts, axis=1)
    spread.store(out_refs, where, result)


def norm_backward_kernel(where, dmiddle_ref, own_ref, other_ref, stream_ref, vec_ref, out_ref, sums_ref):
    dnormed = own_ref[...].astype(F32) + other_ref[...].astype(F32)
    inner, gain_terms = norm_backward(dnormed, stream_ref[...], vec_ref[0, 0:1, :])
    out_ref[...] = dmiddle_ref[...] + inner

    @pl.when(pl.program_id(0) == 0)
    def _():
        sums_ref[...] = jnp.zeros_like(sums_ref)

    sums_ref[0:1, :] += jnp.sum(gain_terms, axis=0, keepdims=True)
    sums_ref[1:2, :] += jnp.sum(dnormed, axis=0, keepdims=True)


def adam_kernel(units, local, out_local, tail_units, where, *refs):
    attn_own, attn_other, mlp_own, mlp_other = refs[:4]
    states = [refs[4 + 3 * k : 7 + 3 * k] for k in range(4)]
    outs = refs[len(refs) - 16 :]

    def pair(own, other):
        own, other = own[...].astype(F32), other[...].astype(F32)
        low_core = where[3] == 0
        return jnp.where(low_core, own, other), jnp.where(low_core, other, own)

    attn = pair(attn_own, attn_other)
    mlp = pair(mlp_own, mlp_other)
    at = local + out_local
    grads = [
        jnp.concatenate([half[:, :local] for half in attn], axis=1),
        jnp.concatenate([half[:, local:at] for half in attn], axis=1),
        jnp.concatenate(
            [piece for m, n in zip(mlp, attn) for piece in (m[:, :units], n[:, at : at + tail_units])], axis=1
        ),
        jnp.concatenate(
            [
                piece
                for m, n in zip(mlp, attn)
                for piece in (m[:, units:], n[:, at + tail_units : at + 2 * tail_units])
            ],
            axis=1,
        ),
    ]
    for number, grad in enumerate(grads):
        weight, first, second = [ref[0] for ref in states[number]]
        new = adam_step(weight, grad, first, second, RATES[number], DECAY)
        for ref, values in zip(outs[4 * number : 4 * number + 4], (grad, new[1], new[2], new[0])):
            ref[0] = values


def vec_pack_kernel(where, *refs):
    out_ref = refs[-1]
    layers = out_ref.shape[0]
    out_ref[...] = jnp.zeros_like(out_ref)
    for layer in range(layers):
        one_ref, two_ref, head_ref, main_ref, tail_ref = refs[5 * layer : 5 * layer + 5]
        out_ref[layer, 0:2, :] = one_ref[0:2, :]
        out_ref[layer, 2:6, :] = two_ref[0:4, :]
        for t in range(head_ref.shape[0]):
            out_ref[layer, 8 + t : 9 + t, : head_ref.shape[2]] = head_ref[t]
            out_ref[layer, 12 + t : 13 + t, : main_ref.shape[2]] = main_ref[t]
        out_ref[layer, 6:7, : tail_ref.shape[1]] = tail_ref[...]


def vec_kernel(steps, local, units, tail_units, where, own_ref, other_ref, vec_ref, first_ref, second_ref,
               grad_out, first_out, second_out, weight_out):
    low_core = where[3] == 0
    for layer in range(vec_ref.shape[0]):
        own, other = own_ref[layer], other_ref[layer]
        cores = jnp.where(low_core, own, other), jnp.where(low_core, other, own)
        norms = cores[0][0:6]
        heads = local // (3 * HD)

        def head_piece(kind):
            return [
                core[8 + t : 9 + t, (3 * head + kind) * HD : (3 * head + kind + 1) * HD]
                for t in range(steps)
                for core in cores
                for head in range(heads)
            ]

        hidden = [
            piece
            for t in range(steps)
            for core in cores
            for piece in (core[12 + t : 13 + t, :units], core[6:7, t * tail_units : (t + 1) * tail_units])
        ]
        grad = jnp.concatenate(
            [norms[0:1], norms[1:2], *head_piece(0), *head_piece(2),
             norms[5:6], norms[2:3], norms[3:4], norms[4:5], *hidden],
            axis=1,
        )
        at = slice(layer, layer + 1)
        new = adam_step(vec_ref[at, :], grad, first_ref[at, :], second_ref[at, :], RATES[4], 0.0)
        grad_out[at, :] = grad
        first_out[at, :] = new[1]
        second_out[at, :] = new[2]
        weight_out[at, :] = new[0]


def plane_sides(chips):
    side = math.isqrt(chips)
    while chips % side:
        side -= 1
    return side, chips // side


class Place:
    def __init__(self):
        self.nf = lax.axis_size("fsdp")
        self.nt = lax.axis_size("tp")
        self.na, self.nb = plane_sides(self.nf // 2)
        fi = lax.axis_index("fsdp")
        self.core = fi % 2
        self.a = (fi // 2) // self.nb
        self.b = (fi // 2) % self.nb
        self.t = lax.axis_index("tp")
        self.size = {"a": self.na, "b": self.nb, "t": self.nt}
        self.at = {"a": self.a, "b": self.b, "t": self.t}

    def pairs(self, axis, move):
        if axis == "t":
            return [(i, move(i)) for i in range(self.nt)]
        found = []
        for f in range(self.nf):
            place = {"a": f // 2 // self.nb, "b": f // 2 % self.nb, "core": f % 2}
            place[axis] = move(place[axis])
            found.append((f, (place["a"] * self.nb + place["b"]) * 2 + place["core"]))
        return found

    def send(self, values, axis, move):
        return lax.ppermute(values, "tp" if axis == "t" else "fsdp", self.pairs(axis, move))

    def sibling(self, values):
        return self.send(values, "core", lambda i: 1 - i)

    def swap_rows(self, values):
        pairs = []
        for f in range(self.nf):
            for t in range(self.nt):
                if f % 2 != t % 2:
                    sign = 1 if t % 2 else -1
                    pairs.append((f * self.nt + t, (f + sign) * self.nt + t - sign))
        arrived = lax.ppermute(values.astype(LOW), ("fsdp", "tp"), pairs).astype(F32)
        return jnp.where(self.core != self.t % 2, arrived, values)

    def sum_all(self, values):
        def flips(axes):
            moved = [()]
            for axis in axes:
                moved = [(*kept, k) for k in range(self.size[axis]) for kept in moved]
            return moved

        def add(values, axes):
            terms = []
            for flip in flips(axes):
                if not any(flip):
                    terms.append(values)
                elif axes == ("t",):
                    terms.append(self.send(values, "t", lambda i, k=flip[0]: i ^ k))
                else:
                    pairs = []
                    for f in range(self.nf):
                        a, b = f // 2 // self.nb, f // 2 % self.nb
                        for axis, k in zip(axes, flip):
                            a, b = (a ^ k, b) if axis == "a" else (a, b ^ k)
                        pairs.append((f, (a * self.nb + b) * 2 + f % 2))
                    terms.append(lax.ppermute(values, "fsdp", pairs))
            while len(terms) > 1:
                terms = [terms[k] + terms[k + 1] for k in range(0, len(terms), 2)]
            return terms[0]

        if self.na * self.nb <= 4:
            values = add(values, ("b", "a"))
        else:
            values = add(add(values, ("b",)), ("a",))
        return add(values, ("t",))

    def gather_axis(self, block, axis):
        n = self.size[axis]
        return [block] + [self.send(block, axis, lambda i, k=k: (i - k) % n) for k in range(1, n)]

    def scatter_axis(self, parts, axis):
        n = self.size[axis]
        sent = [self.send(parts[k], axis, lambda i, k=k: (i + k) % n) for k in range(1, n)]
        return [parts[0], *sent]


def split_pair(place, first, second):
    return (
        jnp.where(place.core == 0, first, second),
        jnp.where(place.core == 0, second, first),
    )


def sum_kernel(outputs, where, *refs):
    count = sum(size for sizes in outputs for size in sizes)
    ins, outs = refs[:count], refs[count:]
    for out_ref, sizes in zip(outs, outputs):
        for number, size in enumerate(sizes):
            for t in range(out_ref.shape[0]):
                total = ins[0][t, 0].astype(F32)
                for ref in ins[1:size]:
                    total += ref[t, 0].astype(F32)
                out_ref[t, number] = total.astype(LOW)
            ins = ins[size:]


def tie_kernel(where, *refs):
    pass


def tie(where, arrays, after):
    space = pl.BlockSpec(memory_space=pl.ANY)
    return call(
        tie_kernel,
        where,
        1,
        [(space, x) for x in arrays],
        [(space, jax.ShapeDtypeStruct(x.shape, x.dtype)) for x in arrays],
        [],
        aliases={1 + k: k for k in range(len(arrays))},
        after=after,
    )


class Spread:
    def __init__(self, place, rows, columns, middle):
        self.place, self.rows, self.columns = place, rows, columns
        self.middle = middle
        self.direct = rows % 16 == 0
        self.width = place.na * place.nb * 2 * rows
        na, nb = place.na, place.nb
        self.grad_keys = [[(0, a, b) for b in range(nb)] for a in range(na)]
        self.grad_keys += [[(1, a, b) for a in range(na)] for b in range(nb)]
        self.gather_keys = [[(0, 0, 0), (1, 0, 0)]]
        self.gather_keys += [[(0, 0, b), (1, 0, b)] for b in range(1, nb)]
        self.gather_keys += [[(0, a, 0), (1, a, 0)] for a in range(1, na)]
        self.gather_keys += [[(half, a, b)] for half in range(2) for a in range(1, na) for b in range(1, nb)]
        if middle:
            self.gather_keys = self.grad_keys
        self.weight_keys = self.gather_keys
        if not self.direct:
            self.weight_keys = self.grad_keys = [None]

    def shapes(self, keys):
        if not self.direct:
            return [(self.place.nt, self.width, self.columns)]
        return [(self.place.nt, len(blocks), self.rows, self.columns) for blocks in keys]

    def specs(self, keys):
        return [stepped(shape[1:]) for shape in self.shapes(keys)]

    def first_row(self, where, key):
        half, a, b = key
        a = lax.rem(where[0] + a, self.place.na)
        b = lax.rem(where[1] + b, self.place.nb)
        return pl.multiple_of(((a * self.place.nb + b) * 2 + half) * self.rows, 16)

    def load(self, refs, where, scratch):
        if not self.direct:
            return refs[0].at[0]
        for ref, blocks in zip(refs, self.weight_keys):
            for number, key in enumerate(blocks):
                scratch[pl.ds(self.first_row(where, key), self.rows), :] = ref[0, number]
        return scratch

    def store(self, refs, where, scratch):
        if not self.direct:
            refs[0][0] = scratch[...]
            return
        for ref, blocks in zip(refs, self.grad_keys):
            for number, key in enumerate(blocks):
                ref[0, number] = scratch[pl.ds(self.first_row(where, key), self.rows), :]

    def start(self, own, other):
        place = self.place
        halves = split_pair(place, own, other)
        if self.middle:
            return [jnp.stack(place.gather_axis(half, axis)) for half, axis in zip(halves, "ba")]
        return [jnp.stack(halves)]

    def gather(self, where, blocks, after=()):
        place = self.place
        na, nb = place.na, place.nb
        blocks = [lax.all_gather(block, "tp") for block in blocks]
        if self.direct and len(after):
            blocks = tie(where, blocks, after)
        if self.middle:
            arrays = [array for block, axis in zip(blocks, "ab") for array in place.gather_axis(block, axis)]
        else:
            along_b = place.gather_axis(blocks[0], "b")
            along_a = place.gather_axis(blocks[0], "a")
            first = [place.gather_axis(x[:, :1], "a")[1:] for x in along_b[1:]]
            second = [place.gather_axis(x[:, 1:], "b")[1:] for x in along_a[1:]]
            arrays = along_b + along_a[1:]
            arrays += [first[b][a] for a in range(na - 1) for b in range(nb - 1)]
            arrays += [second[a][b] for a in range(na - 1) for b in range(nb - 1)]
        if self.direct:
            return arrays
        found = {
            key: array[:, number]
            for array, keys in zip(arrays, self.gather_keys)
            for number, key in enumerate(keys)
        }
        full = jnp.stack([found[half, a, b] for a in range(na) for b in range(nb) for half in range(2)], axis=1)
        full = full.reshape(place.nt, na, nb, 2, self.rows, self.columns)
        full = self.roll(full, (na - place.a) % na, (nb - place.b) % nb)
        return [full.reshape(place.nt, self.width, self.columns)]

    def roll(self, full, a, b):
        full = lax.dynamic_slice_in_dim(jnp.concatenate([full, full], axis=1), a, self.place.na, 1)
        return lax.dynamic_slice_in_dim(jnp.concatenate([full, full], axis=2), b, self.place.nb, 2)

    def sums(self, where, outputs, after, layer=None):
        place, rows, columns = self.place, self.rows, self.columns

        def block(number):
            return pl.BlockSpec((place.nt, 1, rows, columns), lambda i, s: (0, number, 0, 0))

        shapes = [(place.nt, len(groups), rows, columns) for groups in outputs]
        return call(
            functools.partial(sum_kernel, [[len(group) for group in groups] for groups in outputs]),
            where,
            1,
            [(block(number), x) for groups in outputs for group in groups for x, number in group],
            [(held(shape), low_of(*shape)) for shape in shapes],
            [],
            after=after,
            layer=layer,
        )

    def scatter_last(self, arrays):
        place = self.place
        if not self.direct:
            full = arrays[0].reshape(place.nt, place.na, place.nb, 2, self.rows, self.columns)
            full = self.roll(full, place.a, place.b)
            arrays = [full[:, a, :, 0] for a in range(place.na)] + [full[:, :, b, 1] for b in range(place.nb)]
        return (
            place.scatter_axis(arrays[: place.na], "a"),
            place.scatter_axis(arrays[place.na :], "b"),
        )

    def scatter_first(self, where, halves, after):
        place = self.place
        if self.middle:
            outputs = [[[(x, k) for x in half] for k in range(half[0].shape[1])] for half in halves]
            results = self.sums(where, outputs, after)
            return results[0], [lax.psum_scatter(x, "tp", scatter_dimension=0, tiled=True)[0] for x in results]
        axes = ("b", "a")
        keys = [(half, k) for half in range(2) for k in range(1, place.size[axes[half]])]
        results = self.sums(where, [[[(x, k) for x in halves[half]]] for half, k in keys], after)
        terms = [[(x, 0) for x in arrays] for arrays in halves]
        for (half, k), total in zip(keys, results):
            n = place.size[axes[half]]
            terms[half].append((place.send(total, axes[half], lambda i: (i + k) % n), 0))
        return results[0], terms

    def scatter_tp(self, where, terms, after, layer=None):
        place = self.place
        (last,) = self.sums(where, [terms], after, layer)
        done = lax.psum_scatter(last, "tp", scatter_dimension=0, tiled=True)[0]
        return last, self.pair(done)

    def pair(self, done):
        mine, other = split_pair(self.place, done[0], done[1])
        return mine, self.place.sibling(other)

    def last_moves(self, where, terms, after):
        if self.direct:
            terms = tie(where, terms, after)
        return [self.place.scatter_axis(list(half), axis) for half, axis in zip(terms, "ba")]

    def last_sums(self, where, moved, after):
        if self.direct:
            arrived = tie(where, [x for half in moved for x in half[1:]], after)
            counts = [len(half) - 1 for half in moved]
            moved = [[moved[0][0], *arrived[: counts[0]]], [moved[1][0], *arrived[counts[0] :]]]
        return self.pair([sum(x.astype(F32) for x in half).astype(LOW) for half in moved])


def body(
    residual_in,
    cotangent,
    slot_tokens,
    qkv_weight,
    out_weight,
    up_weight,
    down_weight,
    vectors,
    qkv_first,
    qkv_second,
    out_first,
    out_second,
    up_first,
    up_second,
    down_first,
    down_second,
    vec_first,
    vec_second,
):
    place = Place()
    layer_count, shard_rows, _ = qkv_weight.shape
    half_rows, width = residual_in.shape
    rows = 2 * half_rows
    nt = place.nt
    local = qkv_weight.shape[2] // 2
    out_local = out_weight.shape[1] // 2
    hidden_local = up_weight.shape[2] // 2
    units = hidden_local // 128 * 128
    tail_units = hidden_local - units
    heads = out_local // HD
    attn_columns = -(-(local + out_local + 2 * tail_units) // 128) * 128
    mlp_columns = 2 * units

    tokens_pair = jnp.concatenate(split_pair(place, slot_tokens, place.sibling(slot_tokens)))
    slot_at = (place.t % 2) * slot_tokens.shape[0] + place.t // 2
    tokens = lax.dynamic_slice_in_dim(tokens_pair, slot_at, 1)
    row_mask = (jnp.arange(rows, dtype=jnp.int32) < tokens[0]).astype(F32)[:, None]
    here = jnp.stack([place.a, place.b, place.t, place.core]).astype(jnp.int32)
    where = jnp.concatenate([here, tokens.astype(jnp.int32)])

    def own_rows(values):
        return lax.dynamic_slice_in_dim(values, place.core * half_rows, half_rows)

    spreads = [
        (
            Spread(place, shard_rows, attn_columns, False),
            Spread(place, shard_rows, mlp_columns, layer > 0),
        )
        for layer in range(layer_count)
    ]

    def turn(arrays):
        qkv, out, up, down = arrays
        return qkv, jnp.swapaxes(out, 1, 2), up, jnp.swapaxes(down, 1, 2)

    weights = turn((qkv_weight, out_weight, up_weight, down_weight))
    firsts = turn((qkv_first, out_first, up_first, down_first))
    seconds = turn((qkv_second, out_second, up_second, down_second))

    def layer_block(array, layer, steps=1):
        block = (1, array.shape[1] // steps, array.shape[2])
        return pl.BlockSpec(block, lambda i, s: (layer, i, 0))

    def pack(layer):
        attn, mlp = (shard_rows, attn_columns), (shard_rows, mlp_columns)
        return call(
            functools.partial(pack_kernel, units),
            here,
            1,
            [(layer_block(w, layer), w) for w in weights],
            [(held(shape), low_of(*shape)) for shape in (attn, attn, mlp, mlp)],
            [],
            bytes_accessed=6 * shard_rows * 13216 // 4,
        )

    starts = []
    for layer in range(layer_count):
        own_attn, other_attn, own_mlp, other_mlp = pack(layer)
        starts.append(
            (
                spreads[layer][0].start(own_attn, place.sibling(other_attn)),
                spreads[layer][1].start(own_mlp, place.sibling(other_mlp)),
            )
        )
    gathered = []
    before = [x for pair in starts[1:] for blocks in pair for x in blocks]
    for layer in range(layer_count):
        attn_full = spreads[layer][0].gather(where, starts[layer][0], before)
        mlp_full = spreads[layer][1].gather(where, starts[layer][1], attn_full[1:3])
        before = mlp_full[1:3]
        gathered.append((attn_full, mlp_full))

    wide = vectors[:, : 8 * width].reshape(layer_count, 8, width)
    head_bias = vectors[:, 2 * width : 4 * width].reshape(layer_count, 2, 2 * nt, 1, out_local)
    hidden_bias = vectors[:, 8 * width :].reshape(layer_count, nt, 2, 1, hidden_local)
    main_bias = hidden_bias[..., :units]
    tail_bias = jnp.moveaxis(hidden_bias[..., units:], 1, 3).reshape(layer_count, 2, 1, nt * tail_units)

    full = whole((rows, width))
    weight_scratch = [
        pltpu.VMEM((width, attn_columns), LOW),
        pltpu.VMEM((width, mlp_columns), LOW),
    ]
    flat = pltpu.VMEM((rows, width), F32)
    flat_low = pltpu.VMEM((rows, width), LOW)
    big = 2 * rows * width

    def wide_of(layer):
        spec = pl.BlockSpec((1, 8, width), lambda i, s: (layer, 0, 0), pipeline_mode=pl.Buffered(1))
        return spec, wide

    def attn_forward(layer, base, own, other):
        spread = spreads[layer][0]
        joined = base is not None
        if joined:
            ins = [(full, base), (full, own), (full, other), wide_of(layer - 1)]
        else:
            half = whole((half_rows, width))
            ins = [(half, own), (half, other)]
        ins.append(wide_of(layer))
        ins.append(
            (
                pl.BlockSpec(
                    (1, 2, 1, 1, out_local), lambda i, s: (layer, 0, 2 * i + s[3], 0, 0)
                ),
                head_bias,
            )
        )
        ins += list(zip(spread.specs(spread.weight_keys), gathered[layer][0]))
        return call(
            functools.partial(attn_forward_kernel, spread, joined, tail_units),
            where,
            nt,
            ins,
            [
                (held((rows, width)), f32_of(rows, width)),
                (held((width, rows)), low_of(width, rows)),
                (stepped((rows, local)), low_of(nt, rows, local)),
                (stepped((rows, out_local)), low_of(nt, rows, out_local)),
                (stepped((heads, rows)), f32_of(nt, heads, rows)),
                (stepped((width, 2 * tail_units)), low_of(nt, width, 2 * tail_units)),
                (held((rows, width)), low_of(rows, width)),
            ],
            [flat, weight_scratch[0], flat_low],
            big * nt * (local + out_local) + 4 * nt * heads * rows * rows * HD,
            rows * width * 12 + nt * width * attn_columns * 2,
            nt * heads * rows * rows,
        )

    def mlp_forward(layer, base, own, other, tails, after=()):
        spread = spreads[layer][1]
        tail = nt * tail_units
        tail_shape = (width, tail)
        ins = [
            (full, base),
            (full, own),
            (full, other),
            wide_of(layer),
            (pl.BlockSpec((1, 1, 1, 1, units), lambda i, s: (layer, i, s[3], 0, 0)), main_bias),
            (whole(tails.shape), tails),
            (pl.BlockSpec((1, 1, 1, tail), lambda i, s: (layer, s[3], 0, 0)), tail_bias),
        ]
        ins += list(zip(spread.specs(spread.weight_keys), gathered[layer][1]))
        return call(
            functools.partial(mlp_forward_kernel, spread),
            where,
            nt,
            ins,
            [
                (held((rows, width)), f32_of(rows, width)),
                (held((width, rows)), low_of(width, rows)),
                (stepped((rows, units)), low_of(nt, rows, units)),
                (stepped((rows, units)), low_of(nt, rows, units)),
                (held((rows, tail)), low_of(rows, tail)),
                (held((rows, tail)), low_of(rows, tail)),
                (held(tail_shape), low_of(*tail_shape)),
                (held(tail_shape), low_of(*tail_shape)),
                (held((rows, width)), low_of(rows, width)),
            ],
            [flat, weight_scratch[1], flat_low],
            2 * big * (nt * units + tail),
            rows * width * 16 + nt * (width + rows) * mlp_columns * 2,
            rows * nt * units,
            after=after,
        )

    def mlp_backward(layer, grad, slope, tails, slope_tail):
        spread = spreads[layer][1]
        tail = nt * tail_units
        ins = [(full, grad), (stepped((rows, units)), slope)]
        ins += [(whole(w.shape), w) for w in (*tails, slope_tail)]
        ins += list(zip(spread.specs(spread.weight_keys), gathered[layer][1]))
        return call(
            functools.partial(mlp_backward_kernel, spread),
            where,
            nt,
            ins,
            [
                (stepped((rows, units)), low_of(nt, rows, units)),
                (held((rows, tail)), low_of(rows, tail)),
                (stepped((1, units)), f32_of(nt, 1, units)),
                (held((1, tail)), f32_of(1, tail)),
                (held((rows, width)), low_of(rows, width)),
                (held((width, rows)), low_of(width, rows)),
            ],
            [flat_low, flat, weight_scratch[1]],
            2 * big * (nt * units + tail),
            rows * width * 6 + nt * (width + rows) * mlp_columns * 2,
        )

    def mlp_grads(layer, grad, normed, hidden, act, hidden_tail, act_tail):
        spread = spreads[layer][1]
        ins = [(whole((width, rows)), grad), (whole((width, rows)), normed)]
        ins += [(stepped((rows, units)), hidden), (stepped((rows, units)), act)]
        ins += [(whole(x.shape), x) for x in (hidden_tail, act_tail)]
        tail_shape = (nt, width, 2 * tail_units)
        outs = [
            (spec, low_of(*shape))
            for spec, shape in zip(spread.specs(spread.grad_keys), spread.shapes(spread.grad_keys))
        ]
        outs.append((held(tail_shape), low_of(*tail_shape)))
        return call(
            functools.partial(mlp_grads_kernel, spread),
            where,
            nt,
            ins,
            outs,
            [weight_scratch[1]],
            2 * big * nt * (units + tail_units),
            rows * width * 6 + nt * (width + rows) * mlp_columns * 2,
        )

    def attn_backward(layer, grad, own, other, middle, qkv, log_sums, after=()):
        spread = spreads[layer][0]
        ins = [(full, grad), (full, own), (full, other), (full, middle), wide_of(layer)]
        ins += [(stepped((rows, local)), qkv), (stepped((heads, rows)), log_sums)]
        ins += list(zip(spread.specs(spread.weight_keys), gathered[layer][0]))
        return call(
            functools.partial(attn_backward_kernel, spread),
            where,
            nt,
            ins,
            [
                (held((rows, width)), f32_of(rows, width)),
                (held((8, width)), f32_of(8, width)),
                (stepped((rows, local)), low_of(nt, rows, local)),
                (stepped((1, local)), f32_of(nt, 1, local)),
                (held((rows, width)), low_of(rows, width)),
            ],
            [flat_low, flat, weight_scratch[0]],
            big * nt * (local + out_local) + 10 * nt * heads * rows * rows * HD,
            rows * width * 20 + nt * width * attn_columns * 2,
            nt * heads * rows * rows,
            after=after,
        )

    def attn_grads(layer, dmiddle, normed, dqkv, mixed, tail_grads):
        spread = spreads[layer][0]
        ins = [(full, dmiddle), (whole((width, rows)), normed)]
        ins += [(stepped((rows, local)), dqkv), (stepped((rows, out_local)), mixed)]
        ins.append((stepped((width, 2 * tail_units)), tail_grads))
        outs = [
            (spec, low_of(*shape))
            for spec, shape in zip(spread.specs(spread.grad_keys), spread.shapes(spread.grad_keys))
        ]
        return call(
            functools.partial(attn_grads_kernel, spread),
            where,
            nt,
            ins,
            outs,
            [weight_scratch[0], pltpu.VMEM((width, rows), LOW)],
            big * nt * (local + out_local),
            rows * width * 6 + nt * (width + rows) * attn_columns * 2,
        )

    def norm_one_backward(layer, dmiddle, own, other, stream, after=()):
        part = pl.BlockSpec((half_rows, width), lambda i, s: (i, 0))
        return call(
            norm_backward_kernel,
            where,
            2,
            [(part, dmiddle), (part, own), (part, other), (part, stream), wide_of(layer)],
            [(part, f32_of(rows, width)), (held((8, width)), f32_of(8, width))],
            [],
            rows * width * 20,
            rows * width * 16,
            after=after,
        )

    grad_stream = None
    mine = place.swap_rows(residual_in)
    base, own, other = None, mine, place.sibling(mine)
    saved = []
    for layer in range(layer_count):
        stream, normed, qkv, mixed, log_sums, tails, part = attn_forward(layer, base, own, other)
        if layer == layer_count - 1:
            (mine,) = tie(where, [place.swap_rows(cotangent)], [qkv])
            grad_stream = jnp.concatenate(split_pair(place, mine, place.sibling(mine)), axis=0) * row_mask
        middle, normed_two, act, slope, act_tail, slope_tail, up_tail, down_tail, part = mlp_forward(
            layer, stream, part, place.sibling(part), tails
        )
        saved.append(
            (stream, normed, qkv, mixed, log_sums, middle, normed_two, act, slope, act_tail, slope_tail,
             (up_tail, down_tail))
        )
        base, own, other = middle, part, place.sibling(part)
    output = own_rows(base) + (own_rows(own).astype(F32) + own_rows(other).astype(F32))
    output = place.swap_rows((output + wide[layer_count - 1, 7:8]) * own_rows(row_mask))


    def adam(layer, attn_pair, mlp_pair, before, after=()):
        steps = 1
        ins = [
            (pl.BlockSpec((shard_rows // steps, x.shape[1]), lambda i, s: (i, 0)), x)
            for x in (*attn_pair, *mlp_pair)
        ]
        for states in zip(weights, firsts, seconds):
            ins += [(layer_block(x, layer, steps), x) for x in states]
        outs = [
            (layer_block(weight, layer, steps), f32_of(*weight.shape)) for weight in weights for _ in range(4)
        ]
        aliases = None
        if before is not None:
            aliases = {1 + len(ins) + k: k for k in range(16)}
            ins += [(pl.BlockSpec(memory_space=pl.ANY), x) for x in before]
        return call(
            functools.partial(adam_kernel, units, local, out_local, tail_units),
            where,
            steps,
            ins,
            outs,
            [],
            bytes_accessed=28 * shard_rows * 13216 // 4,
            aliases=aliases,
            after=after,
        )

    vec_sums = [None] * layer_count
    last = grad_stream
    above = None
    for layer in reversed(range(layer_count)):
        (stream, normed, qkv, mixed, log_sums, middle, normed_two, act, slope, act_tail, slope_tail, tails) = (
            saved[layer]
        )
        spread_attn, spread_mlp = spreads[layer]
        hidden, hidden_tail, hidden_sums, tail_sums, part, grad_turned = mlp_backward(
            layer, grad_stream, slope, tails, slope_tail
        )
        other = place.sibling(part)
        *mlp_grad, tail_grads = mlp_grads(
            layer, grad_turned, normed_two, hidden, act, hidden_tail, act_tail
        )
        last = tail_grads
        arrived = [x for half in attn_terms_above for x in half[1:]] if above else []
        mlp_terms = spread_mlp.scatter_last(mlp_grad)
        dmiddle, norm_two_sums, dqkv, head_sums, part = attn_backward(
            layer, grad_stream, part, other, middle, qkv, log_sums, [last, *arrived]
        )
        other = place.sibling(part)
        attn_grad = attn_grads(layer, dmiddle, normed, dqkv, mixed, tail_grads)
        last = attn_grad[0]
        if above:
            last, attn_terms_above = spreads[above][0].scatter_first(where, attn_terms_above, [last, output])
        grad_stream, norm_one_sums = norm_one_backward(layer, dmiddle, part, other, stream, [last])
        if layer:
            attn_terms = spread_attn.scatter_last(attn_grad)
        last, mlp_terms = spread_mlp.scatter_first(where, mlp_terms, [norm_one_sums])
        vec_sums[layer] = (norm_one_sums, norm_two_sums, head_sums, hidden_sums, tail_sums)
        if above:
            grad_input = place.swap_rows(own_rows(grad_stream))
            last, attn_pair_one = spreads[above][0].scatter_tp(where, attn_terms_above, [last, grad_input], 1)
            mlp_terms_one = mlp_terms_above
            if spread_attn.direct:
                attn_grad = tie(where, attn_grad, [last])
            attn_terms = spread_attn.scatter_last(attn_grad)
        above, mlp_terms_above, attn_terms_above = layer, mlp_terms, attn_terms
        if layer:
            grad_stream, last = lax.optimization_barrier((grad_stream, last))
    last, mlp_pair_above = spreads[above][1].scatter_tp(where, mlp_terms_above, [last])
    moved_one = spreads[1][1].last_moves(where, mlp_terms_one, [last])
    last, attn_terms_above = spreads[above][0].scatter_first(where, attn_terms_above, [last])
    mlp_pair_one = spreads[1][1].last_sums(where, moved_one, [last])
    updated = adam(1, attn_pair_one, mlp_pair_one, None, [last])
    last, attn_pair_above = spreads[above][0].scatter_tp(where, attn_terms_above, [last, updated[0]])

    flat_sums = [x for sums in vec_sums for x in sums]
    vec_shape = (layer_count, 16, width)
    (vec_total,) = call(
        vec_pack_kernel,
        where,
        1,
        [(whole(x.shape), x) for x in flat_sums],
        [(held(vec_shape), f32_of(*vec_shape))],
        [],
        after=[last, *mlp_pair_above],
    )
    vec_total = place.sum_all(vec_total)
    vec_new = call(
        functools.partial(vec_kernel, nt, local, units, tail_units),
        where,
        1,
        [(whole(x.shape), x) for x in (vec_total, place.sibling(vec_total), vectors, vec_first, vec_second)],
        [(held(vectors.shape), f32_of(*vectors.shape)) for _ in range(4)],
        [],
    )
    updated = adam(above, attn_pair_above, mlp_pair_above, updated)
    updated = [
        jnp.swapaxes(x, 1, 2) if number // 4 % 2 else x for number, x in enumerate(updated)
    ]
    return (output, grad_input, *updated, *vec_new)


def solution(mesh):
    rows = P(("fsdp", "tp"), None)
    wide = P(None, "fsdp", "tp")
    tall = P(None, "tp", "fsdp")
    moments = (wide, wide, tall, tall, wide, wide, tall, tall, P(), P())
    return jax.shard_map(
        body,
        mesh=mesh,
        in_specs=(rows, rows, P("fsdp"), wide, tall, wide, tall, P(), *moments),
        out_specs=(rows, rows, *[wide] * 4, *[tall] * 4, *[wide] * 4, *[tall] * 4, *[P()] * 4),
        check_vma=False,
    )
```

```python
import functools
import math

import jax
import jax.numpy as jnp
from jax import lax
from jax.experimental import pallas as pl
from jax.experimental.pallas import tpu as pltpu
from jax.sharding import PartitionSpec as P

HD = 72
IMG_TOK = 729
STEP = 10


EPS_NORM = 1e-06
MASKED = -30000.0
BETA_ONE = 0.9
BETA_TWO = 0.999
ADAM_EPS = 1e-08
DECAY = 0.1
RATES = (0.05, 1.0, 0.05, 0.03, 0.3)
LOW = jnp.bfloat16
F32 = jnp.float32
GELU = math.sqrt(2.0 / math.pi)
SCORE = HD ** (-0.5)
POWER = SCORE / math.log(2.0)
VMEM = 56 * 1024 * 1024
COST = {
    "pack": 4,
    "attn_forward": 26,
    "mlp_forward": 24,
    "mlp_backward": 17,
    "mlp_grads": 16,
    "attn_backward": 33,
    "attn_grads": 13,
    "norm_backward": 9,
    "sum": 5,
    "vec_pack": 0.3,
    "vec": 0.3,
    "adam": 1,
    "tie": 0.01,
}
SCALE = 3e9


def adam_step(weight, gradient, first_moment, second_moment, step_rate, decay_rate):
    first_new = BETA_ONE * first_moment + (1.0 - BETA_ONE) * gradient
    second_new = BETA_TWO * second_moment + (1.0 - BETA_TWO) * gradient * gradient
    first_hat = first_new / (1.0 - BETA_ONE**STEP)
    second_hat = second_new / (1.0 - BETA_TWO**STEP)
    weight_new = weight - step_rate * (
        first_hat / (jnp.sqrt(second_hat) + ADAM_EPS) + decay_rate * weight
    )
    return (weight_new, first_new, second_new)


def cdot(left, right, left_dim=1, right_dim=0):
    return lax.dot_general(
        left, right, (((left_dim,), (right_dim,)), ((), ())), preferred_element_type=F32
    )


def norm_parts(values):
    centred = values - jnp.mean(values, axis=-1, keepdims=True)
    inverse = lax.rsqrt(jnp.mean(centred * centred, axis=-1, keepdims=True) + EPS_NORM)
    return centred * inverse, inverse


def norm_backward(grad_out, values, gain):
    unit, inverse = norm_parts(values)
    scaled = grad_out * gain
    mean_one = jnp.mean(scaled, axis=-1, keepdims=True)
    mean_two = jnp.mean(scaled * unit, axis=-1, keepdims=True)
    return inverse * (scaled - mean_one - unit * mean_two), grad_out * unit


def gelu_both(inputs):
    square = inputs * inputs
    tanh = jnp.tanh(inputs * (GELU + (0.044715 * GELU) * square))
    half = 0.5 + 0.5 * tanh
    act = inputs * half
    return act, half + act * ((1.0 - tanh) * (GELU + (3 * 0.044715 * GELU) * square))


def mask_keys(scores, tokens):
    rows = scores.shape[0]
    whole = IMG_TOK // 8 * 8
    position = whole + lax.broadcasted_iota(jnp.int32, (rows - whole, 1), 0)
    return jnp.concatenate(
        [scores[:whole], jnp.where(position < tokens, scores[whole:], MASKED / SCORE)], axis=0
    )


def whole(shape):
    return pl.BlockSpec(shape, lambda i, s: (0,) * len(shape), pipeline_mode=pl.Buffered(1))


def held(shape):
    return pl.BlockSpec(shape, lambda i, s: (0,) * len(shape))


def stepped(shape):
    return pl.BlockSpec((1,) + shape, lambda i, s: (i,) + (0,) * len(shape))


def low_of(*shape):
    return jax.ShapeDtypeStruct(shape, LOW)


def f32_of(*shape):
    return jax.ShapeDtypeStruct(shape, F32)


def call(kernel, where, steps, ins, outs, scratch, flops=0, bytes_accessed=0, transcendentals=0, aliases=None,
         after=(), layer=None):
    given = 1 + len(ins)
    name = getattr(kernel, "func", kernel).__name__.removesuffix("_kernel")
    ins = ins + [(pl.BlockSpec(memory_space=pl.ANY), array) for array in after]

    def run(*refs):
        kernel(*refs[:given], *refs[given + len(after) :])

    return pl.pallas_call(
        run,
        name=name,
        grid_spec=pltpu.PrefetchScalarGridSpec(
            num_scalar_prefetch=1,
            grid=(steps,),
            in_specs=[spec for spec, _ in ins],
            out_specs=[spec for spec, _ in outs],
            scratch_shapes=scratch,
        ),
        out_shape=[shape for _, shape in outs],
        input_output_aliases=aliases or {},
        compiler_params=pltpu.CompilerParams(vmem_limit_bytes=VMEM),
        cost_estimate=pl.CostEstimate(
            flops=int(COST.get((name, layer), COST[name]) * SCALE), bytes_accessed=1, transcendentals=0
        ),
    )(where, *[array for _, array in ins])


def turn_part(values, turned, step):
    size = values.shape[1] // 3
    at = pl.ds(pl.multiple_of(jnp.minimum(step, 2) * size, 128), size)
    turned[at, :] = values[:, at].T


def pack_kernel(units, where, qkv_ref, out_ref, up_ref, down_ref, own_attn, other_attn, own_mlp, other_mlp):
    qkv, out = qkv_ref[0].astype(LOW), out_ref[0].astype(LOW)
    up, down = up_ref[0].astype(LOW), down_ref[0].astype(LOW)

    def half(values, number):
        size = values.shape[1] // 2
        return values[:, number * size : (number + 1) * size]

    for number in range(2):
        up_h, down_h = half(up, number), half(down, number)
        attn = [half(qkv, number), half(out, number), up_h[:, units:], down_h[:, units:]]
        used = sum(piece.shape[1] for piece in attn)
        attn.append(jnp.zeros((qkv.shape[0], own_attn.shape[1] - used), LOW))
        attn = jnp.concatenate(attn, axis=1)
        mlp = jnp.concatenate([up_h[:, :units], down_h[:, :units]], axis=1)

        @pl.when(where[3] == number)
        def _():
            own_attn[...] = attn
            own_mlp[...] = mlp

        @pl.when(where[3] != number)
        def _():
            other_attn[...] = attn
            other_mlp[...] = mlp


def attn_forward_kernel(spread, joined, tail_units, where, *refs):
    refs = list(refs)
    count = len(spread.weight_keys)
    if joined:
        base_ref, own_ref, other_ref, old_ref = refs[:4]
        del refs[:4]
    else:
        own_ref, other_ref = refs[:2]
        del refs[:2]
    vec_ref, bias_ref = refs[:2]
    w_refs = refs[2 : 2 + count]
    (stream_ref, turned_ref, qkv_ref, mixed_ref, sums_ref, tail_ref, part_ref, total, held_weight, normed) = refs[
        2 + count :
    ]
    step = pl.program_id(0)

    @pl.when(step == 0)
    def _():
        if not joined:
            half = own_ref.shape[0]
            stream_ref[pl.ds(pl.multiple_of(where[3] * half, 8), half), :] = own_ref[...]
            stream_ref[pl.ds(pl.multiple_of((1 - where[3]) * half, 8), half), :] = other_ref[...]

        if joined:
            branch = own_ref[...].astype(F32) + other_ref[...].astype(F32)
            stream_ref[...] = base_ref[...] + branch + old_ref[0, 7:8, :]
        unit, _ = norm_parts(stream_ref[...])
        normed[...] = (unit * vec_ref[0, 0:1, :] + vec_ref[0, 1:2, :]).astype(LOW)

    weight = spread.load(w_refs, where, held_weight)
    tokens = where[4]
    head_columns = 3 * HD
    local = qkv_ref.shape[2]
    heads = local // head_columns
    bias = []
    for head in range(heads):
        at = head * HD
        query_bias, value_bias = bias_ref[0, 0, 0, :, at : at + HD], bias_ref[0, 1, 0, :, at : at + HD]
        bias += [query_bias, jnp.zeros_like(query_bias), value_bias]
    bias = jnp.concatenate(bias, axis=1)
    qkv = (cdot(normed[...], weight[:, :local]) + bias).astype(LOW)
    qkv_ref[0] = qkv
    mixed = []
    for head in range(heads):
        at = head * head_columns
        query = qkv[:, at : at + HD]
        key = qkv[:, at + HD : at + 2 * HD]
        value = qkv[:, at + 2 * HD : at + 3 * HD]
        scores = mask_keys(cdot(key, query, 1, 1), tokens)
        top = jnp.max(scores, axis=0, keepdims=True)
        raised = jnp.exp2((scores - top) * POWER)
        weight_sum = jnp.sum(raised, axis=0, keepdims=True)
        mixed.append(cdot(value, raised.astype(LOW), 0, 0) * (1.0 / weight_sum))
        sums_ref[0, head : head + 1, :] = top * POWER + jnp.log2(weight_sum)
    mixed = jnp.concatenate(mixed, axis=0).T.astype(LOW)
    mixed_ref[0] = mixed
    at = local + mixed.shape[1]
    part = cdot(mixed, weight[:, local:at], 1, 1)

    @pl.when(step == 0)
    def _():
        total[...] = part

    @pl.when(step > 0)
    def _():
        total[...] += part

    tail_ref[0] = weight[:, at : at + 2 * tail_units]

    @pl.when(step == pl.num_programs(0) - 1)
    def _():
        part_ref[...] = total[...].astype(LOW)
        turned_ref[...] = normed[...].T


def mlp_forward_kernel(spread, where, *refs):
    count = len(spread.weight_keys)
    base_ref, own_ref, other_ref, vec_ref, bias_ref, tail_ref, tail_bias_ref = refs[:7]
    w_refs = refs[7 : 7 + count]
    (middle_ref, turned_ref, act_ref, slope_ref, act_tail_ref, slope_tail_ref, up_tail_ref, down_tail_ref,
     part_ref, total, held_weight, normed) = refs[7 + count :]
    step = pl.program_id(0)

    @pl.when(step == 0)
    def _():
        branch = own_ref[...].astype(F32) + other_ref[...].astype(F32)
        middle = base_ref[...] + branch + vec_ref[0, 4:5, :]
        middle_ref[...] = middle
        unit, _ = norm_parts(middle)
        normed[...] = (unit * vec_ref[0, 5:6, :] + vec_ref[0, 6:7, :]).astype(LOW)
        steps, _, both = tail_ref.shape
        half = both // 2
        up_tail_ref[...] = jnp.concatenate([tail_ref[t, :, :half] for t in range(steps)], axis=1)
        down_tail_ref[...] = jnp.concatenate([tail_ref[t, :, half:] for t in range(steps)], axis=1)
        act, slope = gelu_both(cdot(normed[...], up_tail_ref[...]) + tail_bias_ref[0, 0])
        act = act.astype(LOW)
        act_tail_ref[...] = act
        slope_tail_ref[...] = slope.astype(LOW)
        total[...] = cdot(act, down_tail_ref[...], 1, 1)

    weight = spread.load(w_refs, where, held_weight)
    units = act_ref.shape[2]
    act, slope = gelu_both(cdot(normed[...], weight[:, :units]) + bias_ref[0, 0, 0])
    act = act.astype(LOW)
    act_ref[0] = act
    slope_ref[0] = slope.astype(LOW)
    total[...] += cdot(act, weight[:, units:], 1, 1)

    @pl.when(step == pl.num_programs(0) - 1)
    def _():
        part_ref[...] = total[...].astype(LOW)
        turned_ref[...] = normed[...].T


def mlp_backward_kernel(spread, where, *refs):
    count = len(spread.weight_keys)
    grad_ref, slope_ref, up_tail_ref, down_tail_ref, slope_tail_ref = refs[:5]
    w_refs = refs[5 : 5 + count]
    (hidden_ref, hidden_tail_ref, sums_ref, sums_tail_ref, part_ref, turned_ref, low, total, held_weight) = refs[
        5 + count :
    ]
    step = pl.program_id(0)

    @pl.when(step == 0)
    def _():
        low[...] = grad_ref[...].astype(LOW)
        hidden = cdot(low[...], down_tail_ref[...]) * slope_tail_ref[...].astype(F32)
        sums_tail_ref[...] = jnp.sum(hidden, axis=0, keepdims=True)
        hidden = hidden.astype(LOW)
        hidden_tail_ref[...] = hidden
        total[...] = cdot(hidden, up_tail_ref[...], 1, 1)

    weight = spread.load(w_refs, where, held_weight)
    units = hidden_ref.shape[2]
    turn_part(low, turned_ref, step)
    hidden = cdot(low[...], weight[:, units:]) * slope_ref[0].astype(F32)
    sums_ref[0] = jnp.sum(hidden, axis=0, keepdims=True)
    hidden = hidden.astype(LOW)
    hidden_ref[0] = hidden
    total[...] += cdot(hidden, weight[:, :units], 1, 1)

    @pl.when(step == pl.num_programs(0) - 1)
    def _():
        part_ref[...] = total[...].astype(LOW)


def mlp_grads_kernel(spread, where, *refs):
    count = len(spread.grad_keys)
    grad_turned, normed_turned, hidden_ref, act_ref, hidden_tail_ref, act_tail_ref = refs[:6]
    out_refs = refs[6 : 6 + count]
    tail_ref, result = refs[6 + count :]
    step = pl.program_id(0)

    @pl.when(step == 0)
    def _():
        up_tail = cdot(normed_turned[...], hidden_tail_ref[...]).astype(LOW)
        down_tail = cdot(grad_turned[...], act_tail_ref[...]).astype(LOW)
        steps, _, both = tail_ref.shape
        half = both // 2
        for t in range(steps):
            at = slice(t * half, (t + 1) * half)
            tail_ref[t] = jnp.concatenate([up_tail[:, at], down_tail[:, at]], axis=1)

    units = hidden_ref.shape[2]
    result[:, :units] = cdot(normed_turned[...], hidden_ref[0]).astype(LOW)
    result[:, units:] = cdot(grad_turned[...], act_ref[0]).astype(LOW)
    spread.store(out_refs, where, result)


def attn_backward_kernel(spread, where, *refs):
    count = len(spread.weight_keys)
    grad_ref, own_ref, other_ref, middle_ref, vec_ref, qkv_ref, sums_ref = refs[:7]
    w_refs = refs[7 : 7 + count]
    dmiddle_ref, norm_sums_ref, dqkv_ref, head_sums_ref, part_ref, low, total, held_weight = refs[7 + count :]
    step = pl.program_id(0)

    @pl.when(step == 0)
    def _():
        grad = grad_ref[...]
        dnormed = own_ref[...].astype(F32) + other_ref[...].astype(F32)
        inner, gain_terms = norm_backward(dnormed, middle_ref[...], vec_ref[0, 5:6, :])
        dmiddle = grad + inner
        dmiddle_ref[...] = dmiddle
        low[...] = dmiddle.astype(LOW)
        for number, terms in enumerate((gain_terms, dnormed, grad, dmiddle)):
            norm_sums_ref[number : number + 1, :] = jnp.sum(terms, axis=0, keepdims=True)

    weight = spread.load(w_refs, where, held_weight)
    tokens = where[4]
    head_columns = 3 * HD
    local = qkv_ref.shape[2]
    heads = local // head_columns
    qkv = qkv_ref[0]
    dmixed = cdot(low[...], weight[:, local : local + heads * HD]).astype(LOW)
    pieces = []
    for head in range(heads):
        at = head * head_columns
        query = qkv[:, at : at + HD]
        key = qkv[:, at + HD : at + 2 * HD]
        value = qkv[:, at + 2 * HD : at + 3 * HD]
        grad = dmixed[:, head * HD : (head + 1) * HD]
        scores = mask_keys(cdot(key, query, 1, 1), tokens)
        probs = jnp.exp2(scores * POWER - sums_ref[0, head : head + 1, :])
        dprobs = cdot(value, grad, 1, 1)
        row_dot = jnp.sum(dprobs * probs, axis=0, keepdims=True)
        dscores = (probs * (dprobs - row_dot)).astype(LOW)
        pieces.append(cdot(key, dscores, 0, 0).T * SCORE)
        pieces.append(cdot(dscores, query) * SCORE)
        pieces.append(cdot(probs.astype(LOW), grad))
    dqkv = jnp.concatenate(pieces, axis=1)
    head_sums_ref[0] = jnp.sum(dqkv, axis=0, keepdims=True)
    dqkv = dqkv.astype(LOW)
    dqkv_ref[0] = dqkv
    part = cdot(dqkv, weight[:, :local], 1, 1)

    @pl.when(step == 0)
    def _():
        total[...] = part

    @pl.when(step > 0)
    def _():
        total[...] += part

    @pl.when(step == pl.num_programs(0) - 1)
    def _():
        part_ref[...] = total[...].astype(LOW)


def attn_grads_kernel(spread, where, *refs):
    count = len(spread.grad_keys)
    dmiddle_ref, normed_turned, dqkv_ref, mixed_ref, tail_ref = refs[:5]
    out_refs = refs[5 : 5 + count]
    result, grad_turned = refs[5 + count :]

    @pl.when(pl.program_id(0) == 0)
    def _():
        grad_turned[...] = dmiddle_ref[...].astype(LOW).T

    parts = [
        cdot(normed_turned[...], dqkv_ref[0]).astype(LOW),
        cdot(grad_turned[...], mixed_ref[0]).astype(LOW),
        tail_ref[0],
    ]
    used = sum(part.shape[1] for part in parts)
    parts.append(jnp.zeros((result.shape[0], result.shape[1] - used), LOW))
    result[...] = jnp.concatenate(parts, axis=1)
    spread.store(out_refs, where, result)


def norm_backward_kernel(where, dmiddle_ref, own_ref, other_ref, stream_ref, vec_ref, out_ref, sums_ref):
    dnormed = own_ref[...].astype(F32) + other_ref[...].astype(F32)
    inner, gain_terms = norm_backward(dnormed, stream_ref[...], vec_ref[0, 0:1, :])
    out_ref[...] = dmiddle_ref[...] + inner

    @pl.when(pl.program_id(0) == 0)
    def _():
        sums_ref[...] = jnp.zeros_like(sums_ref)

    sums_ref[0:1, :] += jnp.sum(gain_terms, axis=0, keepdims=True)
    sums_ref[1:2, :] += jnp.sum(dnormed, axis=0, keepdims=True)


def adam_kernel(units, local, out_local, tail_units, where, *refs):
    attn_own, attn_other, mlp_own, mlp_other = refs[:4]
    states = [refs[4 + 3 * k : 7 + 3 * k] for k in range(4)]
    outs = refs[len(refs) - 16 :]

    def pair(own, other):
        own, other = own[...].astype(F32), other[...].astype(F32)
        low_core = where[3] == 0
        return jnp.where(low_core, own, other), jnp.where(low_core, other, own)

    attn = pair(attn_own, attn_other)
    mlp = pair(mlp_own, mlp_other)
    at = local + out_local
    grads = [
        jnp.concatenate([half[:, :local] for half in attn], axis=1),
        jnp.concatenate([half[:, local:at] for half in attn], axis=1),
        jnp.concatenate(
            [piece for m, n in zip(mlp, attn) for piece in (m[:, :units], n[:, at : at + tail_units])], axis=1
        ),
        jnp.concatenate(
            [
                piece
                for m, n in zip(mlp, attn)
                for piece in (m[:, units:], n[:, at + tail_units : at + 2 * tail_units])
            ],
            axis=1,
        ),
    ]
    for number, grad in enumerate(grads):
        weight, first, second = [ref[0] for ref in states[number]]
        new = adam_step(weight, grad, first, second, RATES[number], DECAY)
        for ref, values in zip(outs[4 * number : 4 * number + 4], (grad, new[1], new[2], new[0])):
            ref[0] = values


def vec_pack_kernel(where, *refs):
    out_ref = refs[-1]
    layers = out_ref.shape[0]
    out_ref[...] = jnp.zeros_like(out_ref)
    for layer in range(layers):
        one_ref, two_ref, head_ref, main_ref, tail_ref = refs[5 * layer : 5 * layer + 5]
        out_ref[layer, 0:2, :] = one_ref[0:2, :]
        out_ref[layer, 2:6, :] = two_ref[0:4, :]
        for t in range(head_ref.shape[0]):
            out_ref[layer, 8 + t : 9 + t, : head_ref.shape[2]] = head_ref[t]
            out_ref[layer, 12 + t : 13 + t, : main_ref.shape[2]] = main_ref[t]
        out_ref[layer, 6:7, : tail_ref.shape[1]] = tail_ref[...]


def vec_kernel(steps, local, units, tail_units, where, own_ref, other_ref, vec_ref, first_ref, second_ref,
               grad_out, first_out, second_out, weight_out):
    low_core = where[3] == 0
    for layer in range(vec_ref.shape[0]):
        own, other = own_ref[layer], other_ref[layer]
        cores = jnp.where(low_core, own, other), jnp.where(low_core, other, own)
        norms = cores[0][0:6]
        heads = local // (3 * HD)

        def head_piece(kind):
            return [
                core[8 + t : 9 + t, (3 * head + kind) * HD : (3 * head + kind + 1) * HD]
                for t in range(steps)
                for core in cores
                for head in range(heads)
            ]

        hidden = [
            piece
            for t in range(steps)
            for core in cores
            for piece in (core[12 + t : 13 + t, :units], core[6:7, t * tail_units : (t + 1) * tail_units])
        ]
        grad = jnp.concatenate(
            [norms[0:1], norms[1:2], *head_piece(0), *head_piece(2),
             norms[5:6], norms[2:3], norms[3:4], norms[4:5], *hidden],
            axis=1,
        )
        at = slice(layer, layer + 1)
        new = adam_step(vec_ref[at, :], grad, first_ref[at, :], second_ref[at, :], RATES[4], 0.0)
        grad_out[at, :] = grad
        first_out[at, :] = new[1]
        second_out[at, :] = new[2]
        weight_out[at, :] = new[0]


def plane_sides(chips):
    side = math.isqrt(chips)
    while chips % side:
        side -= 1
    return side, chips // side


class Place:
    def __init__(self):
        self.nf = lax.axis_size("fsdp")
        self.nt = lax.axis_size("tp")
        self.na, self.nb = plane_sides(self.nf // 2)
        fi = lax.axis_index("fsdp")
        self.core = fi % 2
        self.a = (fi // 2) // self.nb
        self.b = (fi // 2) % self.nb
        self.t = lax.axis_index("tp")
        self.size = {"a": self.na, "b": self.nb, "t": self.nt}
        self.at = {"a": self.a, "b": self.b, "t": self.t}

    def pairs(self, axis, move):
        if axis == "t":
            return [(i, move(i)) for i in range(self.nt)]
        found = []
        for f in range(self.nf):
            place = {"a": f // 2 // self.nb, "b": f // 2 % self.nb, "core": f % 2}
            place[axis] = move(place[axis])
            found.append((f, (place["a"] * self.nb + place["b"]) * 2 + place["core"]))
        return found

    def send(self, values, axis, move):
        return lax.ppermute(values, "tp" if axis == "t" else "fsdp", self.pairs(axis, move))

    def sibling(self, values):
        return self.send(values, "core", lambda i: 1 - i)

    def swap_rows(self, values):
        pairs = []
        for f in range(self.nf):
            for t in range(self.nt):
                if f % 2 != t % 2:
                    sign = 1 if t % 2 else -1
                    pairs.append((f * self.nt + t, (f + sign) * self.nt + t - sign))
        arrived = lax.ppermute(values.astype(LOW), ("fsdp", "tp"), pairs).astype(F32)
        return jnp.where(self.core != self.t % 2, arrived, values)

    def gather_axis(self, block, axis):
        n = self.size[axis]
        return [block] + [self.send(block, axis, lambda i, k=k: (i - k) % n) for k in range(1, n)]

    def scatter_axis(self, parts, axis):
        n = self.size[axis]
        sent = [self.send(parts[k], axis, lambda i, k=k: (i + k) % n) for k in range(1, n)]
        return [parts[0], *sent]


def split_pair(place, first, second):
    return (
        jnp.where(place.core == 0, first, second),
        jnp.where(place.core == 0, second, first),
    )


def sum_kernel(outputs, where, *refs):
    count = sum(size for sizes in outputs for size in sizes)
    ins, outs = refs[:count], refs[count:]
    for out_ref, sizes in zip(outs, outputs):
        for number, size in enumerate(sizes):
            for t in range(out_ref.shape[0]):
                total = ins[0][t, 0].astype(F32)
                for ref in ins[1:size]:
                    total += ref[t, 0].astype(F32)
                out_ref[t, number] = total.astype(LOW)
            ins = ins[size:]


def tie_kernel(where, *refs):
    pass


def tie(where, arrays, after):
    space = pl.BlockSpec(memory_space=pl.ANY)
    return call(
        tie_kernel,
        where,
        1,
        [(space, x) for x in arrays],
        [(space, jax.ShapeDtypeStruct(x.shape, x.dtype)) for x in arrays],
        [],
        aliases={1 + k: k for k in range(len(arrays))},
        after=after,
    )


class Spread:
    def __init__(self, place, rows, columns, middle):
        self.place, self.rows, self.columns = place, rows, columns
        self.middle = middle
        self.direct = rows % 16 == 0
        self.width = place.na * place.nb * 2 * rows
        na, nb = place.na, place.nb
        self.grad_keys = [[(0, a, b) for b in range(nb)] for a in range(na)]
        self.grad_keys += [[(1, a, b) for a in range(na)] for b in range(nb)]
        self.gather_keys = [[(0, 0, 0), (1, 0, 0)]]
        self.gather_keys += [[(0, 0, b), (1, 0, b)] for b in range(1, nb)]
        self.gather_keys += [[(0, a, 0), (1, a, 0)] for a in range(1, na)]
        self.gather_keys += [[(half, a, b)] for half in range(2) for a in range(1, na) for b in range(1, nb)]
        if middle:
            self.gather_keys = self.grad_keys
        self.weight_keys = self.gather_keys
        if not self.direct:
            self.weight_keys = self.grad_keys = [None]

    def shapes(self, keys):
        if not self.direct:
            return [(self.place.nt, self.width, self.columns)]
        return [(self.place.nt, len(blocks), self.rows, self.columns) for blocks in keys]

    def specs(self, keys):
        return [stepped(shape[1:]) for shape in self.shapes(keys)]

    def first_row(self, where, key):
        half, a, b = key
        a = lax.rem(where[0] + a, self.place.na)
        b = lax.rem(where[1] + b, self.place.nb)
        return pl.multiple_of(((a * self.place.nb + b) * 2 + half) * self.rows, 16)

    def load(self, refs, where, scratch):
        if not self.direct:
            return refs[0].at[0]
        for ref, blocks in zip(refs, self.weight_keys):
            for number, key in enumerate(blocks):
                scratch[pl.ds(self.first_row(where, key), self.rows), :] = ref[0, number]
        return scratch

    def store(self, refs, where, scratch):
        if not self.direct:
            refs[0][0] = scratch[...]
            return
        for ref, blocks in zip(refs, self.grad_keys):
            for number, key in enumerate(blocks):
                ref[0, number] = scratch[pl.ds(self.first_row(where, key), self.rows), :]

    def start(self, own, other):
        place = self.place
        halves = split_pair(place, own, other)
        if self.middle:
            return [jnp.stack(place.gather_axis(half, axis)) for half, axis in zip(halves, "ba")]
        return [jnp.stack(halves)]

    def gather(self, where, blocks, after=()):
        place = self.place
        na, nb = place.na, place.nb
        blocks = [lax.all_gather(block, "tp") for block in blocks]
        if self.direct and len(after):
            blocks = tie(where, blocks, after)
        if self.middle:
            arrays = [array for block, axis in zip(blocks, "ab") for array in place.gather_axis(block, axis)]
        else:
            along_b = place.gather_axis(blocks[0], "b")
            along_a = place.gather_axis(blocks[0], "a")
            first = [place.gather_axis(x[:, :1], "a")[1:] for x in along_b[1:]]
            second = [place.gather_axis(x[:, 1:], "b")[1:] for x in along_a[1:]]
            arrays = along_b + along_a[1:]
            arrays += [first[b][a] for a in range(na - 1) for b in range(nb - 1)]
            arrays += [second[a][b] for a in range(na - 1) for b in range(nb - 1)]
        if self.direct:
            return arrays
        found = {
            key: array[:, number]
            for array, keys in zip(arrays, self.gather_keys)
            for number, key in enumerate(keys)
        }
        full = jnp.stack([found[half, a, b] for a in range(na) for b in range(nb) for half in range(2)], axis=1)
        full = full.reshape(place.nt, na, nb, 2, self.rows, self.columns)
        full = self.roll(full, (na - place.a) % na, (nb - place.b) % nb)
        return [full.reshape(place.nt, self.width, self.columns)]

    def roll(self, full, a, b):
        full = lax.dynamic_slice_in_dim(jnp.concatenate([full, full], axis=1), a, self.place.na, 1)
        return lax.dynamic_slice_in_dim(jnp.concatenate([full, full], axis=2), b, self.place.nb, 2)

    def sums(self, where, outputs, after, layer=None):
        place, rows, columns = self.place, self.rows, self.columns

        def block(number):
            return pl.BlockSpec((place.nt, 1, rows, columns), lambda i, s: (0, number, 0, 0))

        shapes = [(place.nt, len(groups), rows, columns) for groups in outputs]
        return call(
            functools.partial(sum_kernel, [[len(group) for group in groups] for groups in outputs]),
            where,
            1,
            [(block(number), x) for groups in outputs for group in groups for x, number in group],
            [(held(shape), low_of(*shape)) for shape in shapes],
            [],
            after=after,
            layer=layer,
        )

    def scatter_last(self, arrays):
        place = self.place
        if not self.direct:
            full = arrays[0].reshape(place.nt, place.na, place.nb, 2, self.rows, self.columns)
            full = self.roll(full, place.a, place.b)
            arrays = [full[:, a, :, 0] for a in range(place.na)] + [full[:, :, b, 1] for b in range(place.nb)]
        return (
            place.scatter_axis(arrays[: place.na], "a"),
            place.scatter_axis(arrays[place.na :], "b"),
        )

    def scatter_first(self, where, halves, after):
        place = self.place
        if self.middle:
            outputs = [[[(x, k) for x in half] for k in range(half[0].shape[1])] for half in halves]
            results = self.sums(where, outputs, after)
            return results[0], [lax.psum_scatter(x, "tp", scatter_dimension=0, tiled=True)[0] for x in results]
        axes = ("b", "a")
        keys = [(half, k) for half in range(2) for k in range(1, place.size[axes[half]])]
        results = self.sums(where, [[[(x, k) for x in halves[half]]] for half, k in keys], after)
        terms = [[(x, 0) for x in arrays] for arrays in halves]
        for (half, k), total in zip(keys, results):
            n = place.size[axes[half]]
            terms[half].append((place.send(total, axes[half], lambda i: (i + k) % n), 0))
        return results[0], terms

    def scatter_tp(self, where, terms, after, layer=None):
        place = self.place
        if self.middle:
            if self.direct:
                terms = tie(where, terms, after)
            done = [
                sum(x.astype(F32) for x in place.scatter_axis(list(half), axis)).astype(LOW)
                for half, axis in zip(terms, "ba")
            ]
            last = after[0]
        else:
            (last,) = self.sums(where, [terms], after, layer)
            done = lax.psum_scatter(last, "tp", scatter_dimension=0, tiled=True)[0]
        mine, other = split_pair(place, done[0], done[1])
        return last, (mine, place.sibling(other))


def body(
    residual_in,
    cotangent,
    slot_tokens,
    qkv_weight,
    out_weight,
    up_weight,
    down_weight,
    vectors,
    qkv_first,
    qkv_second,
    out_first,
    out_second,
    up_first,
    up_second,
    down_first,
    down_second,
    vec_first,
    vec_second,
):
    place = Place()
    layer_count, shard_rows, _ = qkv_weight.shape
    half_rows, width = residual_in.shape
    rows = 2 * half_rows
    nt = place.nt
    local = qkv_weight.shape[2] // 2
    out_local = out_weight.shape[1] // 2
    hidden_local = up_weight.shape[2] // 2
    units = hidden_local // 128 * 128
    tail_units = hidden_local - units
    heads = out_local // HD
    attn_columns = -(-(local + out_local + 2 * tail_units) // 128) * 128
    mlp_columns = 2 * units

    tokens_pair = jnp.concatenate(split_pair(place, slot_tokens, place.sibling(slot_tokens)))
    slot_at = (place.t % 2) * slot_tokens.shape[0] + place.t // 2
    tokens = lax.dynamic_slice_in_dim(tokens_pair, slot_at, 1)
    row_mask = (jnp.arange(rows, dtype=jnp.int32) < tokens[0]).astype(F32)[:, None]
    here = jnp.stack([place.a, place.b, place.t, place.core]).astype(jnp.int32)
    where = jnp.concatenate([here, tokens.astype(jnp.int32)])

    def own_rows(values):
        return lax.dynamic_slice_in_dim(values, place.core * half_rows, half_rows)

    spreads = [
        (
            Spread(place, shard_rows, attn_columns, False),
            Spread(place, shard_rows, mlp_columns, layer > 0),
        )
        for layer in range(layer_count)
    ]

    def turn(arrays):
        qkv, out, up, down = arrays
        return qkv, jnp.swapaxes(out, 1, 2), up, jnp.swapaxes(down, 1, 2)

    weights = turn((qkv_weight, out_weight, up_weight, down_weight))
    firsts = turn((qkv_first, out_first, up_first, down_first))
    seconds = turn((qkv_second, out_second, up_second, down_second))

    def layer_block(array, layer, steps=1):
        block = (1, array.shape[1] // steps, array.shape[2])
        return pl.BlockSpec(block, lambda i, s: (layer, i, 0))

    def pack(layer):
        attn, mlp = (shard_rows, attn_columns), (shard_rows, mlp_columns)
        return call(
            functools.partial(pack_kernel, units),
            here,
            1,
            [(layer_block(w, layer), w) for w in weights],
            [(held(shape), low_of(*shape)) for shape in (attn, attn, mlp, mlp)],
            [],
            bytes_accessed=6 * shard_rows * 13216 // 4,
        )

    starts = []
    for layer in range(layer_count):
        own_attn, other_attn, own_mlp, other_mlp = pack(layer)
        starts.append(
            (
                spreads[layer][0].start(own_attn, place.sibling(other_attn)),
                spreads[layer][1].start(own_mlp, place.sibling(other_mlp)),
            )
        )
    gathered = []
    before = [x for pair in starts[1:] for blocks in pair for x in blocks]
    for layer in range(layer_count):
        attn_full = spreads[layer][0].gather(where, starts[layer][0], before)
        mlp_full = spreads[layer][1].gather(where, starts[layer][1], attn_full[1:3])
        before = mlp_full[1:3]
        gathered.append((attn_full, mlp_full))

    wide = vectors[:, : 8 * width].reshape(layer_count, 8, width)
    head_bias = vectors[:, 2 * width : 4 * width].reshape(layer_count, 2, 2 * nt, 1, out_local)
    hidden_bias = vectors[:, 8 * width :].reshape(layer_count, nt, 2, 1, hidden_local)
    main_bias = hidden_bias[..., :units]
    tail_bias = jnp.moveaxis(hidden_bias[..., units:], 1, 3).reshape(layer_count, 2, 1, nt * tail_units)

    full = whole((rows, width))
    weight_scratch = [
        pltpu.VMEM((width, attn_columns), LOW),
        pltpu.VMEM((width, mlp_columns), LOW),
    ]
    flat = pltpu.VMEM((rows, width), F32)
    flat_low = pltpu.VMEM((rows, width), LOW)
    big = 2 * rows * width

    def wide_of(layer):
        spec = pl.BlockSpec((1, 8, width), lambda i, s: (layer, 0, 0), pipeline_mode=pl.Buffered(1))
        return spec, wide

    def attn_forward(layer, base, own, other):
        spread = spreads[layer][0]
        joined = base is not None
        if joined:
            ins = [(full, base), (full, own), (full, other), wide_of(layer - 1)]
        else:
            half = whole((half_rows, width))
            ins = [(half, own), (half, other)]
        ins.append(wide_of(layer))
        ins.append(
            (
                pl.BlockSpec(
                    (1, 2, 1, 1, out_local), lambda i, s: (layer, 0, 2 * i + s[3], 0, 0)
                ),
                head_bias,
            )
        )
        ins += list(zip(spread.specs(spread.weight_keys), gathered[layer][0]))
        return call(
            functools.partial(attn_forward_kernel, spread, joined, tail_units),
            where,
            nt,
            ins,
            [
                (held((rows, width)), f32_of(rows, width)),
                (held((width, rows)), low_of(width, rows)),
                (stepped((rows, local)), low_of(nt, rows, local)),
                (stepped((rows, out_local)), low_of(nt, rows, out_local)),
                (stepped((heads, rows)), f32_of(nt, heads, rows)),
                (stepped((width, 2 * tail_units)), low_of(nt, width, 2 * tail_units)),
                (held((rows, width)), low_of(rows, width)),
            ],
            [flat, weight_scratch[0], flat_low],
            big * nt * (local + out_local) + 4 * nt * heads * rows * rows * HD,
            rows * width * 12 + nt * width * attn_columns * 2,
            nt * heads * rows * rows,
        )

    def mlp_forward(layer, base, own, other, tails, after=()):
        spread = spreads[layer][1]
        tail = nt * tail_units
        tail_shape = (width, tail)
        ins = [
            (full, base),
            (full, own),
            (full, other),
            wide_of(layer),
            (pl.BlockSpec((1, 1, 1, 1, units), lambda i, s: (layer, i, s[3], 0, 0)), main_bias),
            (whole(tails.shape), tails),
            (pl.BlockSpec((1, 1, 1, tail), lambda i, s: (layer, s[3], 0, 0)), tail_bias),
        ]
        ins += list(zip(spread.specs(spread.weight_keys), gathered[layer][1]))
        return call(
            functools.partial(mlp_forward_kernel, spread),
            where,
            nt,
            ins,
            [
                (held((rows, width)), f32_of(rows, width)),
                (held((width, rows)), low_of(width, rows)),
                (stepped((rows, units)), low_of(nt, rows, units)),
                (stepped((rows, units)), low_of(nt, rows, units)),
                (held((rows, tail)), low_of(rows, tail)),
                (held((rows, tail)), low_of(rows, tail)),
                (held(tail_shape), low_of(*tail_shape)),
                (held(tail_shape), low_of(*tail_shape)),
                (held((rows, width)), low_of(rows, width)),
            ],
            [flat, weight_scratch[1], flat_low],
            2 * big * (nt * units + tail),
            rows * width * 16 + nt * (width + rows) * mlp_columns * 2,
            rows * nt * units,
            after=after,
        )

    def mlp_backward(layer, grad, slope, tails, slope_tail):
        spread = spreads[layer][1]
        tail = nt * tail_units
        ins = [(full, grad), (stepped((rows, units)), slope)]
        ins += [(whole(w.shape), w) for w in (*tails, slope_tail)]
        ins += list(zip(spread.specs(spread.weight_keys), gathered[layer][1]))
        return call(
            functools.partial(mlp_backward_kernel, spread),
            where,
            nt,
            ins,
            [
                (stepped((rows, units)), low_of(nt, rows, units)),
                (held((rows, tail)), low_of(rows, tail)),
                (stepped((1, units)), f32_of(nt, 1, units)),
                (held((1, tail)), f32_of(1, tail)),
                (held((rows, width)), low_of(rows, width)),
                (held((width, rows)), low_of(width, rows)),
            ],
            [flat_low, flat, weight_scratch[1]],
            2 * big * (nt * units + tail),
            rows * width * 6 + nt * (width + rows) * mlp_columns * 2,
        )

    def mlp_grads(layer, grad, normed, hidden, act, hidden_tail, act_tail):
        spread = spreads[layer][1]
        ins = [(whole((width, rows)), grad), (whole((width, rows)), normed)]
        ins += [(stepped((rows, units)), hidden), (stepped((rows, units)), act)]
        ins += [(whole(x.shape), x) for x in (hidden_tail, act_tail)]
        tail_shape = (nt, width, 2 * tail_units)
        outs = [
            (spec, low_of(*shape))
            for spec, shape in zip(spread.specs(spread.grad_keys), spread.shapes(spread.grad_keys))
        ]
        outs.append((held(tail_shape), low_of(*tail_shape)))
        return call(
            functools.partial(mlp_grads_kernel, spread),
            where,
            nt,
            ins,
            outs,
            [weight_scratch[1]],
            2 * big * nt * (units + tail_units),
            rows * width * 6 + nt * (width + rows) * mlp_columns * 2,
        )

    def attn_backward(layer, grad, own, other, middle, qkv, log_sums, after=()):
        spread = spreads[layer][0]
        ins = [(full, grad), (full, own), (full, other), (full, middle), wide_of(layer)]
        ins += [(stepped((rows, local)), qkv), (stepped((heads, rows)), log_sums)]
        ins += list(zip(spread.specs(spread.weight_keys), gathered[layer][0]))
        return call(
            functools.partial(attn_backward_kernel, spread),
            where,
            nt,
            ins,
            [
                (held((rows, width)), f32_of(rows, width)),
                (held((8, width)), f32_of(8, width)),
                (stepped((rows, local)), low_of(nt, rows, local)),
                (stepped((1, local)), f32_of(nt, 1, local)),
                (held((rows, width)), low_of(rows, width)),
            ],
            [flat_low, flat, weight_scratch[0]],
            big * nt * (local + out_local) + 10 * nt * heads * rows * rows * HD,
            rows * width * 20 + nt * width * attn_columns * 2,
            nt * heads * rows * rows,
            after=after,
        )

    def attn_grads(layer, dmiddle, normed, dqkv, mixed, tail_grads):
        spread = spreads[layer][0]
        ins = [(full, dmiddle), (whole((width, rows)), normed)]
        ins += [(stepped((rows, local)), dqkv), (stepped((rows, out_local)), mixed)]
        ins.append((stepped((width, 2 * tail_units)), tail_grads))
        outs = [
            (spec, low_of(*shape))
            for spec, shape in zip(spread.specs(spread.grad_keys), spread.shapes(spread.grad_keys))
        ]
        return call(
            functools.partial(attn_grads_kernel, spread),
            where,
            nt,
            ins,
            outs,
            [weight_scratch[0], pltpu.VMEM((width, rows), LOW)],
            big * nt * (local + out_local),
            rows * width * 6 + nt * (width + rows) * attn_columns * 2,
        )

    def norm_one_backward(layer, dmiddle, own, other, stream, after=()):
        part = pl.BlockSpec((half_rows, width), lambda i, s: (i, 0))
        return call(
            norm_backward_kernel,
            where,
            2,
            [(part, dmiddle), (part, own), (part, other), (part, stream), wide_of(layer)],
            [(part, f32_of(rows, width)), (held((8, width)), f32_of(8, width))],
            [],
            rows * width * 20,
            rows * width * 16,
            after=after,
        )

    grad_stream = None
    mine = place.swap_rows(residual_in)
    base, own, other = None, mine, place.sibling(mine)
    saved = []
    for layer in range(layer_count):
        stream, normed, qkv, mixed, log_sums, tails, part = attn_forward(layer, base, own, other)
        if layer == layer_count - 1:
            (mine,) = tie(where, [place.swap_rows(cotangent)], [qkv])
            grad_stream = jnp.concatenate(split_pair(place, mine, place.sibling(mine)), axis=0) * row_mask
        middle, normed_two, act, slope, act_tail, slope_tail, up_tail, down_tail, part = mlp_forward(
            layer, stream, part, place.sibling(part), tails
        )
        saved.append(
            (stream, normed, qkv, mixed, log_sums, middle, normed_two, act, slope, act_tail, slope_tail,
             (up_tail, down_tail))
        )
        base, own, other = middle, part, place.sibling(part)
    output = own_rows(base) + (own_rows(own).astype(F32) + own_rows(other).astype(F32))
    output = place.swap_rows((output + wide[layer_count - 1, 7:8]) * own_rows(row_mask))


    def adam(layer, attn_pair, mlp_pair, before, after=()):
        steps = 1
        ins = [
            (pl.BlockSpec((shard_rows // steps, x.shape[1]), lambda i, s: (i, 0)), x)
            for x in (*attn_pair, *mlp_pair)
        ]
        for states in zip(weights, firsts, seconds):
            ins += [(layer_block(x, layer, steps), x) for x in states]
        outs = [
            (layer_block(weight, layer, steps), f32_of(*weight.shape)) for weight in weights for _ in range(4)
        ]
        aliases = None
        if before is not None:
            aliases = {1 + len(ins) + k: k for k in range(16)}
            ins += [(pl.BlockSpec(memory_space=pl.ANY), x) for x in before]
        return call(
            functools.partial(adam_kernel, units, local, out_local, tail_units),
            where,
            steps,
            ins,
            outs,
            [],
            bytes_accessed=28 * shard_rows * 13216 // 4,
            aliases=aliases,
            after=after,
        )

    vec_sums = [None] * layer_count
    last = grad_stream
    above = None
    for layer in reversed(range(layer_count)):
        (stream, normed, qkv, mixed, log_sums, middle, normed_two, act, slope, act_tail, slope_tail, tails) = (
            saved[layer]
        )
        spread_attn, spread_mlp = spreads[layer]
        hidden, hidden_tail, hidden_sums, tail_sums, part, grad_turned = mlp_backward(
            layer, grad_stream, slope, tails, slope_tail
        )
        other = place.sibling(part)
        *mlp_grad, tail_grads = mlp_grads(
            layer, grad_turned, normed_two, hidden, act, hidden_tail, act_tail
        )
        last = tail_grads
        arrived = [x for half in attn_terms_above for x in half[1:]] if above else []
        mlp_terms = spread_mlp.scatter_last(mlp_grad)
        dmiddle, norm_two_sums, dqkv, head_sums, part = attn_backward(
            layer, grad_stream, part, other, middle, qkv, log_sums, [last, *arrived]
        )
        other = place.sibling(part)
        attn_grad = attn_grads(layer, dmiddle, normed, dqkv, mixed, tail_grads)
        last = attn_grad[0]
        if above:
            last, attn_terms_above = spreads[above][0].scatter_first(where, attn_terms_above, [last, output])
        grad_stream, norm_one_sums = norm_one_backward(layer, dmiddle, part, other, stream, [last])
        if layer:
            attn_terms = spread_attn.scatter_last(attn_grad)
        last, mlp_terms = spread_mlp.scatter_first(where, mlp_terms, [norm_one_sums])
        vec_sums[layer] = (norm_one_sums, norm_two_sums, head_sums, hidden_sums, tail_sums)
        if above:
            grad_input = place.swap_rows(own_rows(grad_stream))
            last, attn_pair_one = spreads[above][0].scatter_tp(where, attn_terms_above, [last, grad_input], 1)
            mlp_terms_one = mlp_terms_above
            if spread_attn.direct:
                attn_grad = tie(where, attn_grad, [last])
            attn_terms = spread_attn.scatter_last(attn_grad)
        above, mlp_terms_above, attn_terms_above = layer, mlp_terms, attn_terms
        if layer:
            grad_stream, last = lax.optimization_barrier((grad_stream, last))
    last, mlp_pair_above = spreads[above][1].scatter_tp(where, mlp_terms_above, [last, attn_grad[0]])
    _, mlp_pair_one = spreads[1][1].scatter_tp(where, mlp_terms_one, [last])
    last, attn_terms_above = spreads[above][0].scatter_first(where, attn_terms_above, [last])
    updated = adam(1, attn_pair_one, mlp_pair_one, None, [last])
    last, attn_pair_above = spreads[above][0].scatter_tp(where, attn_terms_above, [last, updated[0]])

    flat_sums = [x for sums in vec_sums for x in sums]
    vec_shape = (layer_count, 16, width)
    (vec_total,) = call(
        vec_pack_kernel,
        where,
        1,
        [(whole(x.shape), x) for x in flat_sums],
        [(held(vec_shape), f32_of(*vec_shape))],
        [],
        after=[last, *mlp_pair_above],
    )
    for axis in ("b", "a", "t"):
        step = 1
        while step < place.size[axis]:
            vec_total = vec_total + place.send(vec_total, axis, lambda i: i ^ step)
            step *= 2
    updated = adam(above, attn_pair_above, mlp_pair_above, updated)
    vec_new = call(
        functools.partial(vec_kernel, nt, local, units, tail_units),
        where,
        1,
        [(whole(x.shape), x) for x in (vec_total, place.sibling(vec_total), vectors, vec_first, vec_second)],
        [(held(vectors.shape), f32_of(*vectors.shape)) for _ in range(4)],
        [],
    )
    updated = [
        jnp.swapaxes(x, 1, 2) if number // 4 % 2 else x for number, x in enumerate(updated)
    ]
    return (output, grad_input, *updated, *vec_new)


def solution(mesh):
    rows = P(("fsdp", "tp"), None)
    wide = P(None, "fsdp", "tp")
    tall = P(None, "tp", "fsdp")
    moments = (wide, wide, tall, tall, wide, wide, tall, tall, P(), P())
    return jax.shard_map(
        body,
        mesh=mesh,
        in_specs=(rows, rows, P("fsdp"), wide, tall, wide, tall, P(), *moments),
        out_specs=(rows, rows, *[wide] * 4, *[tall] * 4, *[wide] * 4, *[tall] * 4, *[P()] * 4),
        check_vma=False,
    )
```

```python
import functools
import math

import jax
import jax.numpy as jnp
from jax import lax
from jax.experimental import pallas as pl
from jax.experimental.pallas import tpu as pltpu
from jax.sharding import PartitionSpec as P

HD = 72
IMG_TOK = 729
STEP = 10


EPS_NORM = 1e-06
MASKED = -30000.0
BETA_ONE = 0.9
BETA_TWO = 0.999
ADAM_EPS = 1e-08
DECAY = 0.1
RATES = (0.05, 1.0, 0.05, 0.03, 0.3)
LOW = jnp.bfloat16
F32 = jnp.float32
GELU = math.sqrt(2.0 / math.pi)
SCORE = HD ** (-0.5)
POWER = SCORE / math.log(2.0)
VMEM = 56 * 1024 * 1024
COST = {
    "pack": 4,
    "attn_forward": 26,
    "mlp_forward": 24,
    "mlp_backward": 17,
    "mlp_grads": 16,
    "attn_backward": 33,
    "attn_grads": 13,
    "norm_backward": 9,
    "sum": 5,
    "vec_pack": 0.3,
    "vec": 0.3,
    "adam": 1,
    "tie": 0.01,
}
SCALE = 3e9


def adam_step(weight, gradient, first_moment, second_moment, step_rate, decay_rate):
    first_new = BETA_ONE * first_moment + (1.0 - BETA_ONE) * gradient
    second_new = BETA_TWO * second_moment + (1.0 - BETA_TWO) * gradient * gradient
    first_hat = first_new / (1.0 - BETA_ONE**STEP)
    second_hat = second_new / (1.0 - BETA_TWO**STEP)
    weight_new = weight - step_rate * (
        first_hat / (jnp.sqrt(second_hat) + ADAM_EPS) + decay_rate * weight
    )
    return (weight_new, first_new, second_new)


def cdot(left, right, left_dim=1, right_dim=0):
    return lax.dot_general(
        left, right, (((left_dim,), (right_dim,)), ((), ())), preferred_element_type=F32
    )


def norm_parts(values):
    centred = values - jnp.mean(values, axis=-1, keepdims=True)
    inverse = lax.rsqrt(jnp.mean(centred * centred, axis=-1, keepdims=True) + EPS_NORM)
    return centred * inverse, inverse


def norm_backward(grad_out, values, gain):
    unit, inverse = norm_parts(values)
    scaled = grad_out * gain
    mean_one = jnp.mean(scaled, axis=-1, keepdims=True)
    mean_two = jnp.mean(scaled * unit, axis=-1, keepdims=True)
    return inverse * (scaled - mean_one - unit * mean_two), grad_out * unit


def gelu_both(inputs):
    square = inputs * inputs
    tanh = jnp.tanh(inputs * (GELU + (0.044715 * GELU) * square))
    half = 0.5 + 0.5 * tanh
    act = inputs * half
    return act, half + act * ((1.0 - tanh) * (GELU + (3 * 0.044715 * GELU) * square))


def mask_keys(scores, tokens):
    rows = scores.shape[0]
    whole = IMG_TOK // 8 * 8
    position = whole + lax.broadcasted_iota(jnp.int32, (rows - whole, 1), 0)
    return jnp.concatenate(
        [scores[:whole], jnp.where(position < tokens, scores[whole:], MASKED / SCORE)], axis=0
    )


def whole(shape):
    return pl.BlockSpec(shape, lambda i, s: (0,) * len(shape), pipeline_mode=pl.Buffered(1))


def held(shape):
    return pl.BlockSpec(shape, lambda i, s: (0,) * len(shape))


def stepped(shape):
    return pl.BlockSpec((1,) + shape, lambda i, s: (i,) + (0,) * len(shape))


def low_of(*shape):
    return jax.ShapeDtypeStruct(shape, LOW)


def f32_of(*shape):
    return jax.ShapeDtypeStruct(shape, F32)


def call(kernel, where, steps, ins, outs, scratch, flops=0, bytes_accessed=0, transcendentals=0, aliases=None,
         after=(), layer=None):
    given = 1 + len(ins)
    name = getattr(kernel, "func", kernel).__name__.removesuffix("_kernel")
    ins = ins + [(pl.BlockSpec(memory_space=pl.ANY), array) for array in after]

    def run(*refs):
        kernel(*refs[:given], *refs[given + len(after) :])

    return pl.pallas_call(
        run,
        name=name,
        grid_spec=pltpu.PrefetchScalarGridSpec(
            num_scalar_prefetch=1,
            grid=(steps,),
            in_specs=[spec for spec, _ in ins],
            out_specs=[spec for spec, _ in outs],
            scratch_shapes=scratch,
        ),
        out_shape=[shape for _, shape in outs],
        input_output_aliases=aliases or {},
        compiler_params=pltpu.CompilerParams(vmem_limit_bytes=VMEM),
        cost_estimate=pl.CostEstimate(
            flops=int(COST.get((name, layer), COST[name]) * SCALE), bytes_accessed=1, transcendentals=0
        ),
    )(where, *[array for _, array in ins])


def turn_part(values, turned, step):
    size = values.shape[1] // 3
    at = pl.ds(pl.multiple_of(jnp.minimum(step, 2) * size, 128), size)
    turned[at, :] = values[:, at].T


def pack_kernel(units, where, qkv_ref, out_ref, up_ref, down_ref, own_attn, other_attn, own_mlp, other_mlp):
    qkv, out = qkv_ref[0].astype(LOW), out_ref[0].astype(LOW)
    up, down = up_ref[0].astype(LOW), down_ref[0].astype(LOW)

    def half(values, number):
        size = values.shape[1] // 2
        return values[:, number * size : (number + 1) * size]

    for number in range(2):
        up_h, down_h = half(up, number), half(down, number)
        attn = [half(qkv, number), half(out, number), up_h[:, units:], down_h[:, units:]]
        used = sum(piece.shape[1] for piece in attn)
        attn.append(jnp.zeros((qkv.shape[0], own_attn.shape[1] - used), LOW))
        attn = jnp.concatenate(attn, axis=1)
        mlp = jnp.concatenate([up_h[:, :units], down_h[:, :units]], axis=1)

        @pl.when(where[3] == number)
        def _():
            own_attn[...] = attn
            own_mlp[...] = mlp

        @pl.when(where[3] != number)
        def _():
            other_attn[...] = attn
            other_mlp[...] = mlp


def attn_forward_kernel(spread, joined, tail_units, where, *refs):
    refs = list(refs)
    count = len(spread.weight_keys)
    if joined:
        base_ref, own_ref, other_ref, old_ref = refs[:4]
        del refs[:4]
    else:
        own_ref, other_ref = refs[:2]
        del refs[:2]
    vec_ref, bias_ref = refs[:2]
    w_refs = refs[2 : 2 + count]
    (stream_ref, turned_ref, qkv_ref, mixed_ref, sums_ref, tail_ref, part_ref, total, held_weight, normed) = refs[
        2 + count :
    ]
    step = pl.program_id(0)

    @pl.when(step == 0)
    def _():
        if not joined:
            half = own_ref.shape[0]
            stream_ref[pl.ds(pl.multiple_of(where[3] * half, 8), half), :] = own_ref[...]
            stream_ref[pl.ds(pl.multiple_of((1 - where[3]) * half, 8), half), :] = other_ref[...]

        if joined:
            branch = own_ref[...].astype(F32) + other_ref[...].astype(F32)
            stream_ref[...] = base_ref[...] + branch + old_ref[0, 7:8, :]
        unit, _ = norm_parts(stream_ref[...])
        normed[...] = (unit * vec_ref[0, 0:1, :] + vec_ref[0, 1:2, :]).astype(LOW)

    weight = spread.load(w_refs, where, held_weight)
    tokens = where[4]
    head_columns = 3 * HD
    local = qkv_ref.shape[2]
    heads = local // head_columns
    bias = []
    for head in range(heads):
        at = head * HD
        query_bias, value_bias = bias_ref[0, 0, 0, :, at : at + HD], bias_ref[0, 1, 0, :, at : at + HD]
        bias += [query_bias, jnp.zeros_like(query_bias), value_bias]
    bias = jnp.concatenate(bias, axis=1)
    qkv = (cdot(normed[...], weight[:, :local]) + bias).astype(LOW)
    qkv_ref[0] = qkv
    mixed = []
    for head in range(heads):
        at = head * head_columns
        query = qkv[:, at : at + HD]
        key = qkv[:, at + HD : at + 2 * HD]
        value = qkv[:, at + 2 * HD : at + 3 * HD]
        scores = mask_keys(cdot(key, query, 1, 1), tokens)
        top = jnp.max(scores, axis=0, keepdims=True)
        raised = jnp.exp2((scores - top) * POWER)
        weight_sum = jnp.sum(raised, axis=0, keepdims=True)
        mixed.append(cdot(value, raised.astype(LOW), 0, 0) * (1.0 / weight_sum))
        sums_ref[0, head : head + 1, :] = top * POWER + jnp.log2(weight_sum)
    mixed = jnp.concatenate(mixed, axis=0).T.astype(LOW)
    mixed_ref[0] = mixed
    at = local + mixed.shape[1]
    part = cdot(mixed, weight[:, local:at], 1, 1)

    @pl.when(step == 0)
    def _():
        total[...] = part

    @pl.when(step > 0)
    def _():
        total[...] += part

    tail_ref[0] = weight[:, at : at + 2 * tail_units]

    @pl.when(step == pl.num_programs(0) - 1)
    def _():
        part_ref[...] = total[...].astype(LOW)
        turned_ref[...] = normed[...].T


def mlp_forward_kernel(spread, where, *refs):
    count = len(spread.weight_keys)
    base_ref, own_ref, other_ref, vec_ref, bias_ref, tail_ref, tail_bias_ref = refs[:7]
    w_refs = refs[7 : 7 + count]
    (middle_ref, turned_ref, act_ref, slope_ref, act_tail_ref, slope_tail_ref, up_tail_ref, down_tail_ref,
     part_ref, total, held_weight, normed) = refs[7 + count :]
    step = pl.program_id(0)

    @pl.when(step == 0)
    def _():
        branch = own_ref[...].astype(F32) + other_ref[...].astype(F32)
        middle = base_ref[...] + branch + vec_ref[0, 4:5, :]
        middle_ref[...] = middle
        unit, _ = norm_parts(middle)
        normed[...] = (unit * vec_ref[0, 5:6, :] + vec_ref[0, 6:7, :]).astype(LOW)
        steps, _, both = tail_ref.shape
        half = both // 2
        up_tail_ref[...] = jnp.concatenate([tail_ref[t, :, :half] for t in range(steps)], axis=1)
        down_tail_ref[...] = jnp.concatenate([tail_ref[t, :, half:] for t in range(steps)], axis=1)
        act, slope = gelu_both(cdot(normed[...], up_tail_ref[...]) + tail_bias_ref[0, 0])
        act = act.astype(LOW)
        act_tail_ref[...] = act
        slope_tail_ref[...] = slope.astype(LOW)
        total[...] = cdot(act, down_tail_ref[...], 1, 1)

    weight = spread.load(w_refs, where, held_weight)
    units = act_ref.shape[2]
    act, slope = gelu_both(cdot(normed[...], weight[:, :units]) + bias_ref[0, 0, 0])
    act = act.astype(LOW)
    act_ref[0] = act
    slope_ref[0] = slope.astype(LOW)
    total[...] += cdot(act, weight[:, units:], 1, 1)

    @pl.when(step == pl.num_programs(0) - 1)
    def _():
        part_ref[...] = total[...].astype(LOW)
        turned_ref[...] = normed[...].T


def mlp_backward_kernel(spread, where, *refs):
    count = len(spread.weight_keys)
    grad_ref, slope_ref, up_tail_ref, down_tail_ref, slope_tail_ref = refs[:5]
    w_refs = refs[5 : 5 + count]
    (hidden_ref, hidden_tail_ref, sums_ref, sums_tail_ref, part_ref, turned_ref, low, total, held_weight) = refs[
        5 + count :
    ]
    step = pl.program_id(0)

    @pl.when(step == 0)
    def _():
        low[...] = grad_ref[...].astype(LOW)
        hidden = cdot(low[...], down_tail_ref[...]) * slope_tail_ref[...].astype(F32)
        sums_tail_ref[...] = jnp.sum(hidden, axis=0, keepdims=True)
        hidden = hidden.astype(LOW)
        hidden_tail_ref[...] = hidden
        total[...] = cdot(hidden, up_tail_ref[...], 1, 1)

    weight = spread.load(w_refs, where, held_weight)
    units = hidden_ref.shape[2]
    turn_part(low, turned_ref, step)
    hidden = cdot(low[...], weight[:, units:]) * slope_ref[0].astype(F32)
    sums_ref[0] = jnp.sum(hidden, axis=0, keepdims=True)
    hidden = hidden.astype(LOW)
    hidden_ref[0] = hidden
    total[...] += cdot(hidden, weight[:, :units], 1, 1)

    @pl.when(step == pl.num_programs(0) - 1)
    def _():
        part_ref[...] = total[...].astype(LOW)


def mlp_grads_kernel(spread, where, *refs):
    count = len(spread.grad_keys)
    grad_turned, normed_turned, hidden_ref, act_ref, hidden_tail_ref, act_tail_ref = refs[:6]
    out_refs = refs[6 : 6 + count]
    tail_ref, result = refs[6 + count :]
    step = pl.program_id(0)

    @pl.when(step == 0)
    def _():
        up_tail = cdot(normed_turned[...], hidden_tail_ref[...]).astype(LOW)
        down_tail = cdot(grad_turned[...], act_tail_ref[...]).astype(LOW)
        steps, _, both = tail_ref.shape
        half = both // 2
        for t in range(steps):
            at = slice(t * half, (t + 1) * half)
            tail_ref[t] = jnp.concatenate([up_tail[:, at], down_tail[:, at]], axis=1)

    units = hidden_ref.shape[2]
    result[:, :units] = cdot(normed_turned[...], hidden_ref[0]).astype(LOW)
    result[:, units:] = cdot(grad_turned[...], act_ref[0]).astype(LOW)
    spread.store(out_refs, where, result)


def attn_backward_kernel(spread, where, *refs):
    count = len(spread.weight_keys)
    grad_ref, own_ref, other_ref, middle_ref, vec_ref, qkv_ref, sums_ref = refs[:7]
    w_refs = refs[7 : 7 + count]
    dmiddle_ref, norm_sums_ref, dqkv_ref, head_sums_ref, part_ref, low, total, held_weight = refs[7 + count :]
    step = pl.program_id(0)

    @pl.when(step == 0)
    def _():
        grad = grad_ref[...]
        dnormed = own_ref[...].astype(F32) + other_ref[...].astype(F32)
        inner, gain_terms = norm_backward(dnormed, middle_ref[...], vec_ref[0, 5:6, :])
        dmiddle = grad + inner
        dmiddle_ref[...] = dmiddle
        low[...] = dmiddle.astype(LOW)
        for number, terms in enumerate((gain_terms, dnormed, grad, dmiddle)):
            norm_sums_ref[number : number + 1, :] = jnp.sum(terms, axis=0, keepdims=True)

    weight = spread.load(w_refs, where, held_weight)
    tokens = where[4]
    head_columns = 3 * HD
    local = qkv_ref.shape[2]
    heads = local // head_columns
    qkv = qkv_ref[0]
    dmixed = cdot(low[...], weight[:, local : local + heads * HD]).astype(LOW)
    pieces = []
    for head in range(heads):
        at = head * head_columns
        query = qkv[:, at : at + HD]
        key = qkv[:, at + HD : at + 2 * HD]
        value = qkv[:, at + 2 * HD : at + 3 * HD]
        grad = dmixed[:, head * HD : (head + 1) * HD]
        scores = mask_keys(cdot(key, query, 1, 1), tokens)
        probs = jnp.exp2(scores * POWER - sums_ref[0, head : head + 1, :])
        dprobs = cdot(value, grad, 1, 1)
        row_dot = jnp.sum(dprobs * probs, axis=0, keepdims=True)
        dscores = (probs * (dprobs - row_dot)).astype(LOW)
        pieces.append(cdot(key, dscores, 0, 0).T * SCORE)
        pieces.append(cdot(dscores, query) * SCORE)
        pieces.append(cdot(probs.astype(LOW), grad))
    dqkv = jnp.concatenate(pieces, axis=1)
    head_sums_ref[0] = jnp.sum(dqkv, axis=0, keepdims=True)
    dqkv = dqkv.astype(LOW)
    dqkv_ref[0] = dqkv
    part = cdot(dqkv, weight[:, :local], 1, 1)

    @pl.when(step == 0)
    def _():
        total[...] = part

    @pl.when(step > 0)
    def _():
        total[...] += part

    @pl.when(step == pl.num_programs(0) - 1)
    def _():
        part_ref[...] = total[...].astype(LOW)


def attn_grads_kernel(spread, where, *refs):
    count = len(spread.grad_keys)
    dmiddle_ref, normed_turned, dqkv_ref, mixed_ref, tail_ref = refs[:5]
    out_refs = refs[5 : 5 + count]
    result, grad_turned = refs[5 + count :]

    @pl.when(pl.program_id(0) == 0)
    def _():
        grad_turned[...] = dmiddle_ref[...].astype(LOW).T

    parts = [
        cdot(normed_turned[...], dqkv_ref[0]).astype(LOW),
        cdot(grad_turned[...], mixed_ref[0]).astype(LOW),
        tail_ref[0],
    ]
    used = sum(part.shape[1] for part in parts)
    parts.append(jnp.zeros((result.shape[0], result.shape[1] - used), LOW))
    result[...] = jnp.concatenate(parts, axis=1)
    spread.store(out_refs, where, result)


def norm_backward_kernel(where, dmiddle_ref, own_ref, other_ref, stream_ref, vec_ref, out_ref, sums_ref):
    dnormed = own_ref[...].astype(F32) + other_ref[...].astype(F32)
    inner, gain_terms = norm_backward(dnormed, stream_ref[...], vec_ref[0, 0:1, :])
    out_ref[...] = dmiddle_ref[...] + inner

    @pl.when(pl.program_id(0) == 0)
    def _():
        sums_ref[...] = jnp.zeros_like(sums_ref)

    sums_ref[0:1, :] += jnp.sum(gain_terms, axis=0, keepdims=True)
    sums_ref[1:2, :] += jnp.sum(dnormed, axis=0, keepdims=True)


def adam_kernel(units, local, out_local, tail_units, where, *refs):
    attn_own, attn_other, mlp_own, mlp_other = refs[:4]
    states = [refs[4 + 3 * k : 7 + 3 * k] for k in range(4)]
    outs = refs[len(refs) - 16 :]

    def pair(own, other):
        own, other = own[...].astype(F32), other[...].astype(F32)
        low_core = where[3] == 0
        return jnp.where(low_core, own, other), jnp.where(low_core, other, own)

    attn = pair(attn_own, attn_other)
    mlp = pair(mlp_own, mlp_other)
    at = local + out_local
    grads = [
        jnp.concatenate([half[:, :local] for half in attn], axis=1),
        jnp.concatenate([half[:, local:at] for half in attn], axis=1),
        jnp.concatenate(
            [piece for m, n in zip(mlp, attn) for piece in (m[:, :units], n[:, at : at + tail_units])], axis=1
        ),
        jnp.concatenate(
            [
                piece
                for m, n in zip(mlp, attn)
                for piece in (m[:, units:], n[:, at + tail_units : at + 2 * tail_units])
            ],
            axis=1,
        ),
    ]
    for number, grad in enumerate(grads):
        weight, first, second = [ref[0] for ref in states[number]]
        new = adam_step(weight, grad, first, second, RATES[number], DECAY)
        for ref, values in zip(outs[4 * number : 4 * number + 4], (grad, new[1], new[2], new[0])):
            ref[0] = values


def vec_pack_kernel(where, *refs):
    out_ref = refs[-1]
    layers = out_ref.shape[0]
    out_ref[...] = jnp.zeros_like(out_ref)
    for layer in range(layers):
        one_ref, two_ref, head_ref, main_ref, tail_ref = refs[5 * layer : 5 * layer + 5]
        out_ref[layer, 0:2, :] = one_ref[0:2, :]
        out_ref[layer, 2:6, :] = two_ref[0:4, :]
        for t in range(head_ref.shape[0]):
            out_ref[layer, 8 + t : 9 + t, : head_ref.shape[2]] = head_ref[t]
            out_ref[layer, 12 + t : 13 + t, : main_ref.shape[2]] = main_ref[t]
        out_ref[layer, 6:7, : tail_ref.shape[1]] = tail_ref[...]


def vec_kernel(steps, local, units, tail_units, where, own_ref, other_ref, vec_ref, first_ref, second_ref,
               grad_out, first_out, second_out, weight_out):
    low_core = where[3] == 0
    for layer in range(vec_ref.shape[0]):
        own, other = own_ref[layer], other_ref[layer]
        cores = jnp.where(low_core, own, other), jnp.where(low_core, other, own)
        norms = cores[0][0:6]
        heads = local // (3 * HD)

        def head_piece(kind):
            return [
                core[8 + t : 9 + t, (3 * head + kind) * HD : (3 * head + kind + 1) * HD]
                for t in range(steps)
                for core in cores
                for head in range(heads)
            ]

        hidden = [
            piece
            for t in range(steps)
            for core in cores
            for piece in (core[12 + t : 13 + t, :units], core[6:7, t * tail_units : (t + 1) * tail_units])
        ]
        grad = jnp.concatenate(
            [norms[0:1], norms[1:2], *head_piece(0), *head_piece(2),
             norms[5:6], norms[2:3], norms[3:4], norms[4:5], *hidden],
            axis=1,
        )
        at = slice(layer, layer + 1)
        new = adam_step(vec_ref[at, :], grad, first_ref[at, :], second_ref[at, :], RATES[4], 0.0)
        grad_out[at, :] = grad
        first_out[at, :] = new[1]
        second_out[at, :] = new[2]
        weight_out[at, :] = new[0]


def plane_sides(chips):
    side = math.isqrt(chips)
    while chips % side:
        side -= 1
    return side, chips // side


class Place:
    def __init__(self):
        self.nf = lax.axis_size("fsdp")
        self.nt = lax.axis_size("tp")
        self.na, self.nb = plane_sides(self.nf // 2)
        fi = lax.axis_index("fsdp")
        self.core = fi % 2
        self.a = (fi // 2) // self.nb
        self.b = (fi // 2) % self.nb
        self.t = lax.axis_index("tp")
        self.size = {"a": self.na, "b": self.nb, "t": self.nt}
        self.at = {"a": self.a, "b": self.b, "t": self.t}

    def pairs(self, axis, move):
        if axis == "t":
            return [(i, move(i)) for i in range(self.nt)]
        found = []
        for f in range(self.nf):
            place = {"a": f // 2 // self.nb, "b": f // 2 % self.nb, "core": f % 2}
            place[axis] = move(place[axis])
            found.append((f, (place["a"] * self.nb + place["b"]) * 2 + place["core"]))
        return found

    def send(self, values, axis, move):
        return lax.ppermute(values, "tp" if axis == "t" else "fsdp", self.pairs(axis, move))

    def sibling(self, values):
        return self.send(values, "core", lambda i: 1 - i)

    def swap_rows(self, values):
        pairs = []
        for f in range(self.nf):
            for t in range(self.nt):
                if f % 2 != t % 2:
                    sign = 1 if t % 2 else -1
                    pairs.append((f * self.nt + t, (f + sign) * self.nt + t - sign))
        arrived = lax.ppermute(values.astype(LOW), ("fsdp", "tp"), pairs).astype(F32)
        return jnp.where(self.core != self.t % 2, arrived, values)

    def gather_axis(self, block, axis):
        n = self.size[axis]
        return [block] + [self.send(block, axis, lambda i, k=k: (i - k) % n) for k in range(1, n)]

    def scatter_axis(self, parts, axis):
        n = self.size[axis]
        sent = [self.send(parts[k], axis, lambda i, k=k: (i + k) % n) for k in range(1, n)]
        return [parts[0], *sent]


def split_pair(place, first, second):
    return (
        jnp.where(place.core == 0, first, second),
        jnp.where(place.core == 0, second, first),
    )


def sum_kernel(outputs, where, *refs):
    count = sum(size for sizes in outputs for size in sizes)
    ins, outs = refs[:count], refs[count:]
    for out_ref, sizes in zip(outs, outputs):
        for number, size in enumerate(sizes):
            for t in range(out_ref.shape[0]):
                total = ins[0][t, 0].astype(F32)
                for ref in ins[1:size]:
                    total += ref[t, 0].astype(F32)
                out_ref[t, number] = total.astype(LOW)
            ins = ins[size:]


def tie_kernel(where, *refs):
    pass


def tie(where, arrays, after):
    space = pl.BlockSpec(memory_space=pl.ANY)
    return call(
        tie_kernel,
        where,
        1,
        [(space, x) for x in arrays],
        [(space, jax.ShapeDtypeStruct(x.shape, x.dtype)) for x in arrays],
        [],
        aliases={1 + k: k for k in range(len(arrays))},
        after=after,
    )


class Spread:
    def __init__(self, place, rows, columns, middle):
        self.place, self.rows, self.columns = place, rows, columns
        self.middle = middle
        self.direct = rows % 16 == 0
        self.width = place.na * place.nb * 2 * rows
        na, nb = place.na, place.nb
        self.grad_keys = [[(0, a, b) for b in range(nb)] for a in range(na)]
        self.grad_keys += [[(1, a, b) for a in range(na)] for b in range(nb)]
        self.gather_keys = [[(0, 0, 0), (1, 0, 0)]]
        self.gather_keys += [[(0, 0, b), (1, 0, b)] for b in range(1, nb)]
        self.gather_keys += [[(0, a, 0), (1, a, 0)] for a in range(1, na)]
        self.gather_keys += [[(half, a, b)] for half in range(2) for a in range(1, na) for b in range(1, nb)]
        if middle:
            self.gather_keys = self.grad_keys
        self.weight_keys = self.gather_keys
        if not self.direct:
            self.weight_keys = self.grad_keys = [None]

    def shapes(self, keys):
        if not self.direct:
            return [(self.place.nt, self.width, self.columns)]
        return [(self.place.nt, len(blocks), self.rows, self.columns) for blocks in keys]

    def specs(self, keys):
        return [stepped(shape[1:]) for shape in self.shapes(keys)]

    def first_row(self, where, key):
        half, a, b = key
        a = lax.rem(where[0] + a, self.place.na)
        b = lax.rem(where[1] + b, self.place.nb)
        return pl.multiple_of(((a * self.place.nb + b) * 2 + half) * self.rows, 16)

    def load(self, refs, where, scratch):
        if not self.direct:
            return refs[0].at[0]
        for ref, blocks in zip(refs, self.weight_keys):
            for number, key in enumerate(blocks):
                scratch[pl.ds(self.first_row(where, key), self.rows), :] = ref[0, number]
        return scratch

    def store(self, refs, where, scratch):
        if not self.direct:
            refs[0][0] = scratch[...]
            return
        for ref, blocks in zip(refs, self.grad_keys):
            for number, key in enumerate(blocks):
                ref[0, number] = scratch[pl.ds(self.first_row(where, key), self.rows), :]

    def start(self, own, other):
        place = self.place
        halves = split_pair(place, own, other)
        if self.middle:
            return [jnp.stack(place.gather_axis(half, axis)) for half, axis in zip(halves, "ba")]
        return [jnp.stack(halves)]

    def gather(self, where, blocks, after=()):
        place = self.place
        na, nb = place.na, place.nb
        blocks = [lax.all_gather(block, "tp") for block in blocks]
        if self.direct and len(after):
            blocks = tie(where, blocks, after)
        if self.middle:
            arrays = [array for block, axis in zip(blocks, "ab") for array in place.gather_axis(block, axis)]
        else:
            along_b = place.gather_axis(blocks[0], "b")
            along_a = place.gather_axis(blocks[0], "a")
            first = [place.gather_axis(x[:, :1], "a")[1:] for x in along_b[1:]]
            second = [place.gather_axis(x[:, 1:], "b")[1:] for x in along_a[1:]]
            arrays = along_b + along_a[1:]
            arrays += [first[b][a] for a in range(na - 1) for b in range(nb - 1)]
            arrays += [second[a][b] for a in range(na - 1) for b in range(nb - 1)]
        if self.direct:
            return arrays
        found = {
            key: array[:, number]
            for array, keys in zip(arrays, self.gather_keys)
            for number, key in enumerate(keys)
        }
        full = jnp.stack([found[half, a, b] for a in range(na) for b in range(nb) for half in range(2)], axis=1)
        full = full.reshape(place.nt, na, nb, 2, self.rows, self.columns)
        full = self.roll(full, (na - place.a) % na, (nb - place.b) % nb)
        return [full.reshape(place.nt, self.width, self.columns)]

    def roll(self, full, a, b):
        full = lax.dynamic_slice_in_dim(jnp.concatenate([full, full], axis=1), a, self.place.na, 1)
        return lax.dynamic_slice_in_dim(jnp.concatenate([full, full], axis=2), b, self.place.nb, 2)

    def sums(self, where, outputs, after, layer=None):
        place, rows, columns = self.place, self.rows, self.columns

        def block(number):
            return pl.BlockSpec((place.nt, 1, rows, columns), lambda i, s: (0, number, 0, 0))

        shapes = [(place.nt, len(groups), rows, columns) for groups in outputs]
        return call(
            functools.partial(sum_kernel, [[len(group) for group in groups] for groups in outputs]),
            where,
            1,
            [(block(number), x) for groups in outputs for group in groups for x, number in group],
            [(held(shape), low_of(*shape)) for shape in shapes],
            [],
            after=after,
            layer=layer,
        )

    def scatter_last(self, arrays):
        place = self.place
        if not self.direct:
            full = arrays[0].reshape(place.nt, place.na, place.nb, 2, self.rows, self.columns)
            full = self.roll(full, place.a, place.b)
            arrays = [full[:, a, :, 0] for a in range(place.na)] + [full[:, :, b, 1] for b in range(place.nb)]
        return (
            place.scatter_axis(arrays[: place.na], "a"),
            place.scatter_axis(arrays[place.na :], "b"),
        )

    def scatter_first(self, where, halves, after):
        place = self.place
        if self.middle:
            outputs = [[[(x, k) for x in half] for k in range(half[0].shape[1])] for half in halves]
            results = self.sums(where, outputs, after)
            return results[0], [lax.psum_scatter(x, "tp", scatter_dimension=0, tiled=True)[0] for x in results]
        axes = ("b", "a")
        keys = [(half, k) for half in range(2) for k in range(1, place.size[axes[half]])]
        results = self.sums(where, [[[(x, k) for x in halves[half]]] for half, k in keys], after)
        terms = [[(x, 0) for x in arrays] for arrays in halves]
        for (half, k), total in zip(keys, results):
            n = place.size[axes[half]]
            terms[half].append((place.send(total, axes[half], lambda i: (i + k) % n), 0))
        return results[0], terms

    def scatter_tp(self, where, terms, after, layer=None):
        place = self.place
        if self.middle:
            if self.direct:
                terms = tie(where, terms, after)
            done = [
                sum(x.astype(F32) for x in place.scatter_axis(list(half), axis)).astype(LOW)
                for half, axis in zip(terms, "ba")
            ]
            last = after[0]
        else:
            (last,) = self.sums(where, [terms], after, layer)
            done = lax.psum_scatter(last, "tp", scatter_dimension=0, tiled=True)[0]
        mine, other = split_pair(place, done[0], done[1])
        return last, (mine, place.sibling(other))


def body(
    residual_in,
    cotangent,
    slot_tokens,
    qkv_weight,
    out_weight,
    up_weight,
    down_weight,
    vectors,
    qkv_first,
    qkv_second,
    out_first,
    out_second,
    up_first,
    up_second,
    down_first,
    down_second,
    vec_first,
    vec_second,
):
    place = Place()
    layer_count, shard_rows, _ = qkv_weight.shape
    half_rows, width = residual_in.shape
    rows = 2 * half_rows
    nt = place.nt
    local = qkv_weight.shape[2] // 2
    out_local = out_weight.shape[1] // 2
    hidden_local = up_weight.shape[2] // 2
    units = hidden_local // 128 * 128
    tail_units = hidden_local - units
    heads = out_local // HD
    attn_columns = -(-(local + out_local + 2 * tail_units) // 128) * 128
    mlp_columns = 2 * units

    tokens_pair = jnp.concatenate(split_pair(place, slot_tokens, place.sibling(slot_tokens)))
    slot_at = (place.t % 2) * slot_tokens.shape[0] + place.t // 2
    tokens = lax.dynamic_slice_in_dim(tokens_pair, slot_at, 1)
    row_mask = (jnp.arange(rows, dtype=jnp.int32) < tokens[0]).astype(F32)[:, None]
    here = jnp.stack([place.a, place.b, place.t, place.core]).astype(jnp.int32)
    where = jnp.concatenate([here, tokens.astype(jnp.int32)])

    def own_rows(values):
        return lax.dynamic_slice_in_dim(values, place.core * half_rows, half_rows)

    spreads = [
        (
            Spread(place, shard_rows, attn_columns, False),
            Spread(place, shard_rows, mlp_columns, layer > 0),
        )
        for layer in range(layer_count)
    ]

    def turn(arrays):
        qkv, out, up, down = arrays
        return qkv, jnp.swapaxes(out, 1, 2), up, jnp.swapaxes(down, 1, 2)

    weights = turn((qkv_weight, out_weight, up_weight, down_weight))
    firsts = turn((qkv_first, out_first, up_first, down_first))
    seconds = turn((qkv_second, out_second, up_second, down_second))

    def layer_block(array, layer, steps=1):
        block = (1, array.shape[1] // steps, array.shape[2])
        return pl.BlockSpec(block, lambda i, s: (layer, i, 0))

    def pack(layer):
        attn, mlp = (shard_rows, attn_columns), (shard_rows, mlp_columns)
        return call(
            functools.partial(pack_kernel, units),
            here,
            1,
            [(layer_block(w, layer), w) for w in weights],
            [(held(shape), low_of(*shape)) for shape in (attn, attn, mlp, mlp)],
            [],
            bytes_accessed=6 * shard_rows * 13216 // 4,
        )

    starts = []
    for layer in range(layer_count):
        own_attn, other_attn, own_mlp, other_mlp = pack(layer)
        starts.append(
            (
                spreads[layer][0].start(own_attn, place.sibling(other_attn)),
                spreads[layer][1].start(own_mlp, place.sibling(other_mlp)),
            )
        )
    gathered = []
    before = [x for pair in starts[1:] for blocks in pair for x in blocks]
    for layer in range(layer_count):
        attn_full = spreads[layer][0].gather(where, starts[layer][0], before)
        mlp_full = spreads[layer][1].gather(where, starts[layer][1], attn_full[1:3])
        before = mlp_full[1:3]
        gathered.append((attn_full, mlp_full))

    wide = vectors[:, : 8 * width].reshape(layer_count, 8, width)
    head_bias = vectors[:, 2 * width : 4 * width].reshape(layer_count, 2, 2 * nt, 1, out_local)
    hidden_bias = vectors[:, 8 * width :].reshape(layer_count, nt, 2, 1, hidden_local)
    main_bias = hidden_bias[..., :units]
    tail_bias = jnp.moveaxis(hidden_bias[..., units:], 1, 3).reshape(layer_count, 2, 1, nt * tail_units)

    full = whole((rows, width))
    weight_scratch = [
        pltpu.VMEM((width, attn_columns), LOW),
        pltpu.VMEM((width, mlp_columns), LOW),
    ]
    flat = pltpu.VMEM((rows, width), F32)
    flat_low = pltpu.VMEM((rows, width), LOW)
    big = 2 * rows * width

    def wide_of(layer):
        spec = pl.BlockSpec((1, 8, width), lambda i, s: (layer, 0, 0), pipeline_mode=pl.Buffered(1))
        return spec, wide

    def attn_forward(layer, base, own, other):
        spread = spreads[layer][0]
        joined = base is not None
        if joined:
            ins = [(full, base), (full, own), (full, other), wide_of(layer - 1)]
        else:
            half = whole((half_rows, width))
            ins = [(half, own), (half, other)]
        ins.append(wide_of(layer))
        ins.append(
            (
                pl.BlockSpec(
                    (1, 2, 1, 1, out_local), lambda i, s: (layer, 0, 2 * i + s[3], 0, 0)
                ),
                head_bias,
            )
        )
        ins += list(zip(spread.specs(spread.weight_keys), gathered[layer][0]))
        return call(
            functools.partial(attn_forward_kernel, spread, joined, tail_units),
            where,
            nt,
            ins,
            [
                (held((rows, width)), f32_of(rows, width)),
                (held((width, rows)), low_of(width, rows)),
                (stepped((rows, local)), low_of(nt, rows, local)),
                (stepped((rows, out_local)), low_of(nt, rows, out_local)),
                (stepped((heads, rows)), f32_of(nt, heads, rows)),
                (stepped((width, 2 * tail_units)), low_of(nt, width, 2 * tail_units)),
                (held((rows, width)), low_of(rows, width)),
            ],
            [flat, weight_scratch[0], flat_low],
            big * nt * (local + out_local) + 4 * nt * heads * rows * rows * HD,
            rows * width * 12 + nt * width * attn_columns * 2,
            nt * heads * rows * rows,
        )

    def mlp_forward(layer, base, own, other, tails, after=()):
        spread = spreads[layer][1]
        tail = nt * tail_units
        tail_shape = (width, tail)
        ins = [
            (full, base),
            (full, own),
            (full, other),
            wide_of(layer),
            (pl.BlockSpec((1, 1, 1, 1, units), lambda i, s: (layer, i, s[3], 0, 0)), main_bias),
            (whole(tails.shape), tails),
            (pl.BlockSpec((1, 1, 1, tail), lambda i, s: (layer, s[3], 0, 0)), tail_bias),
        ]
        ins += list(zip(spread.specs(spread.weight_keys), gathered[layer][1]))
        return call(
            functools.partial(mlp_forward_kernel, spread),
            where,
            nt,
            ins,
            [
                (held((rows, width)), f32_of(rows, width)),
                (held((width, rows)), low_of(width, rows)),
                (stepped((rows, units)), low_of(nt, rows, units)),
                (stepped((rows, units)), low_of(nt, rows, units)),
                (held((rows, tail)), low_of(rows, tail)),
                (held((rows, tail)), low_of(rows, tail)),
                (held(tail_shape), low_of(*tail_shape)),
                (held(tail_shape), low_of(*tail_shape)),
                (held((rows, width)), low_of(rows, width)),
            ],
            [flat, weight_scratch[1], flat_low],
            2 * big * (nt * units + tail),
            rows * width * 16 + nt * (width + rows) * mlp_columns * 2,
            rows * nt * units,
            after=after,
        )

    def mlp_backward(layer, grad, slope, tails, slope_tail):
        spread = spreads[layer][1]
        tail = nt * tail_units
        ins = [(full, grad), (stepped((rows, units)), slope)]
        ins += [(whole(w.shape), w) for w in (*tails, slope_tail)]
        ins += list(zip(spread.specs(spread.weight_keys), gathered[layer][1]))
        return call(
            functools.partial(mlp_backward_kernel, spread),
            where,
            nt,
            ins,
            [
                (stepped((rows, units)), low_of(nt, rows, units)),
                (held((rows, tail)), low_of(rows, tail)),
                (stepped((1, units)), f32_of(nt, 1, units)),
                (held((1, tail)), f32_of(1, tail)),
                (held((rows, width)), low_of(rows, width)),
                (held((width, rows)), low_of(width, rows)),
            ],
            [flat_low, flat, weight_scratch[1]],
            2 * big * (nt * units + tail),
            rows * width * 6 + nt * (width + rows) * mlp_columns * 2,
        )

    def mlp_grads(layer, grad, normed, hidden, act, hidden_tail, act_tail):
        spread = spreads[layer][1]
        ins = [(whole((width, rows)), grad), (whole((width, rows)), normed)]
        ins += [(stepped((rows, units)), hidden), (stepped((rows, units)), act)]
        ins += [(whole(x.shape), x) for x in (hidden_tail, act_tail)]
        tail_shape = (nt, width, 2 * tail_units)
        outs = [
            (spec, low_of(*shape))
            for spec, shape in zip(spread.specs(spread.grad_keys), spread.shapes(spread.grad_keys))
        ]
        outs.append((held(tail_shape), low_of(*tail_shape)))
        return call(
            functools.partial(mlp_grads_kernel, spread),
            where,
            nt,
            ins,
            outs,
            [weight_scratch[1]],
            2 * big * nt * (units + tail_units),
            rows * width * 6 + nt * (width + rows) * mlp_columns * 2,
        )

    def attn_backward(layer, grad, own, other, middle, qkv, log_sums, after=()):
        spread = spreads[layer][0]
        ins = [(full, grad), (full, own), (full, other), (full, middle), wide_of(layer)]
        ins += [(stepped((rows, local)), qkv), (stepped((heads, rows)), log_sums)]
        ins += list(zip(spread.specs(spread.weight_keys), gathered[layer][0]))
        return call(
            functools.partial(attn_backward_kernel, spread),
            where,
            nt,
            ins,
            [
                (held((rows, width)), f32_of(rows, width)),
                (held((8, width)), f32_of(8, width)),
                (stepped((rows, local)), low_of(nt, rows, local)),
                (stepped((1, local)), f32_of(nt, 1, local)),
                (held((rows, width)), low_of(rows, width)),
            ],
            [flat_low, flat, weight_scratch[0]],
            big * nt * (local + out_local) + 10 * nt * heads * rows * rows * HD,
            rows * width * 20 + nt * width * attn_columns * 2,
            nt * heads * rows * rows,
            after=after,
        )

    def attn_grads(layer, dmiddle, normed, dqkv, mixed, tail_grads):
        spread = spreads[layer][0]
        ins = [(full, dmiddle), (whole((width, rows)), normed)]
        ins += [(stepped((rows, local)), dqkv), (stepped((rows, out_local)), mixed)]
        ins.append((stepped((width, 2 * tail_units)), tail_grads))
        outs = [
            (spec, low_of(*shape))
            for spec, shape in zip(spread.specs(spread.grad_keys), spread.shapes(spread.grad_keys))
        ]
        return call(
            functools.partial(attn_grads_kernel, spread),
            where,
            nt,
            ins,
            outs,
            [weight_scratch[0], pltpu.VMEM((width, rows), LOW)],
            big * nt * (local + out_local),
            rows * width * 6 + nt * (width + rows) * attn_columns * 2,
        )

    def norm_one_backward(layer, dmiddle, own, other, stream, after=()):
        part = pl.BlockSpec((half_rows, width), lambda i, s: (i, 0))
        return call(
            norm_backward_kernel,
            where,
            2,
            [(part, dmiddle), (part, own), (part, other), (part, stream), wide_of(layer)],
            [(part, f32_of(rows, width)), (held((8, width)), f32_of(8, width))],
            [],
            rows * width * 20,
            rows * width * 16,
            after=after,
        )

    grad_stream = None
    mine = place.swap_rows(residual_in)
    base, own, other = None, mine, place.sibling(mine)
    saved = []
    for layer in range(layer_count):
        stream, normed, qkv, mixed, log_sums, tails, part = attn_forward(layer, base, own, other)
        if layer == layer_count - 1:
            (mine,) = tie(where, [place.swap_rows(cotangent)], [qkv])
            grad_stream = jnp.concatenate(split_pair(place, mine, place.sibling(mine)), axis=0) * row_mask
        middle, normed_two, act, slope, act_tail, slope_tail, up_tail, down_tail, part = mlp_forward(
            layer, stream, part, place.sibling(part), tails
        )
        saved.append(
            (stream, normed, qkv, mixed, log_sums, middle, normed_two, act, slope, act_tail, slope_tail,
             (up_tail, down_tail))
        )
        base, own, other = middle, part, place.sibling(part)
    output = own_rows(base) + (own_rows(own).astype(F32) + own_rows(other).astype(F32))
    output = place.swap_rows((output + wide[layer_count - 1, 7:8]) * own_rows(row_mask))


    def adam(layer, attn_pair, mlp_pair, before, after=()):
        steps = 1
        ins = [
            (pl.BlockSpec((shard_rows // steps, x.shape[1]), lambda i, s: (i, 0)), x)
            for x in (*attn_pair, *mlp_pair)
        ]
        for states in zip(weights, firsts, seconds):
            ins += [(layer_block(x, layer, steps), x) for x in states]
        outs = [
            (layer_block(weight, layer, steps), f32_of(*weight.shape)) for weight in weights for _ in range(4)
        ]
        aliases = None
        if before is not None:
            aliases = {1 + len(ins) + k: k for k in range(16)}
            ins += [(pl.BlockSpec(memory_space=pl.ANY), x) for x in before]
        return call(
            functools.partial(adam_kernel, units, local, out_local, tail_units),
            where,
            steps,
            ins,
            outs,
            [],
            bytes_accessed=28 * shard_rows * 13216 // 4,
            aliases=aliases,
            after=after,
        )

    vec_sums = [None] * layer_count
    last = grad_stream
    above = None
    for layer in reversed(range(layer_count)):
        (stream, normed, qkv, mixed, log_sums, middle, normed_two, act, slope, act_tail, slope_tail, tails) = (
            saved[layer]
        )
        spread_attn, spread_mlp = spreads[layer]
        hidden, hidden_tail, hidden_sums, tail_sums, part, grad_turned = mlp_backward(
            layer, grad_stream, slope, tails, slope_tail
        )
        other = place.sibling(part)
        *mlp_grad, tail_grads = mlp_grads(
            layer, grad_turned, normed_two, hidden, act, hidden_tail, act_tail
        )
        last = tail_grads
        arrived = [x for half in attn_terms_above for x in half[1:]] if above else []
        mlp_terms = spread_mlp.scatter_last(mlp_grad)
        dmiddle, norm_two_sums, dqkv, head_sums, part = attn_backward(
            layer, grad_stream, part, other, middle, qkv, log_sums, [last, *arrived]
        )
        other = place.sibling(part)
        attn_grad = attn_grads(layer, dmiddle, normed, dqkv, mixed, tail_grads)
        last = attn_grad[0]
        if above:
            last, attn_terms_above = spreads[above][0].scatter_first(where, attn_terms_above, [last, output])
        grad_stream, norm_one_sums = norm_one_backward(layer, dmiddle, part, other, stream, [last])
        if layer:
            attn_terms = spread_attn.scatter_last(attn_grad)
        last, mlp_terms = spread_mlp.scatter_first(where, mlp_terms, [norm_one_sums])
        vec_sums[layer] = (norm_one_sums, norm_two_sums, head_sums, hidden_sums, tail_sums)
        if above:
            grad_input = place.swap_rows(own_rows(grad_stream))
            last, attn_pair_one = spreads[above][0].scatter_tp(where, attn_terms_above, [last, grad_input], 1)
            mlp_terms_one = mlp_terms_above
            if spread_attn.direct:
                attn_grad = tie(where, attn_grad, [last])
            attn_terms = spread_attn.scatter_last(attn_grad)
        above, mlp_terms_above, attn_terms_above = layer, mlp_terms, attn_terms
        if layer:
            grad_stream, last = lax.optimization_barrier((grad_stream, last))
    last, mlp_pair_above = spreads[above][1].scatter_tp(where, mlp_terms_above, [last, attn_grad[0]])
    _, mlp_pair_one = spreads[1][1].scatter_tp(where, mlp_terms_one, [last])
    last, attn_terms_above = spreads[above][0].scatter_first(where, attn_terms_above, [last])
    updated = adam(1, attn_pair_one, mlp_pair_one, None, [last])
    last, attn_pair_above = spreads[above][0].scatter_tp(where, attn_terms_above, [last, updated[0]])

    flat_sums = [x for sums in vec_sums for x in sums]
    vec_shape = (layer_count, 16, width)
    (vec_total,) = call(
        vec_pack_kernel,
        where,
        1,
        [(whole(x.shape), x) for x in flat_sums],
        [(held(vec_shape), f32_of(*vec_shape))],
        [],
        after=[last],
    )
    for axis in ("b", "a", "t"):
        if axis == "t":
            (vec_total,) = tie(where, [vec_total], mlp_pair_above)
        step = 1
        while step < place.size[axis]:
            vec_total = vec_total + place.send(vec_total, axis, lambda i: i ^ step)
            step *= 2
    updated = adam(above, attn_pair_above, mlp_pair_above, updated)
    vec_new = call(
        functools.partial(vec_kernel, nt, local, units, tail_units),
        where,
        1,
        [(whole(x.shape), x) for x in (vec_total, place.sibling(vec_total), vectors, vec_first, vec_second)],
        [(held(vectors.shape), f32_of(*vectors.shape)) for _ in range(4)],
        [],
    )
    updated = [
        jnp.swapaxes(x, 1, 2) if number // 4 % 2 else x for number, x in enumerate(updated)
    ]
    return (output, grad_input, *updated, *vec_new)


def solution(mesh):
    rows = P(("fsdp", "tp"), None)
    wide = P(None, "fsdp", "tp")
    tall = P(None, "tp", "fsdp")
    moments = (wide, wide, tall, tall, wide, wide, tall, tall, P(), P())
    return jax.shard_map(
        body,
        mesh=mesh,
        in_specs=(rows, rows, P("fsdp"), wide, tall, wide, tall, P(), *moments),
        out_specs=(rows, rows, *[wide] * 4, *[tall] * 4, *[wide] * 4, *[tall] * 4, *[P()] * 4),
        check_vma=False,
    )
```

```python
import functools
import math

import jax
import jax.numpy as jnp
from jax import lax
from jax.experimental import pallas as pl
from jax.experimental.pallas import tpu as pltpu
from jax.sharding import PartitionSpec as P

HD = 72
IMG_TOK = 729
STEP = 10


EPS_NORM = 1e-06
MASKED = -30000.0
BETA_ONE = 0.9
BETA_TWO = 0.999
ADAM_EPS = 1e-08
DECAY = 0.1
RATES = (0.05, 1.0, 0.05, 0.03, 0.3)
LOW = jnp.bfloat16
F32 = jnp.float32
GELU = math.sqrt(2.0 / math.pi)
SCORE = HD ** (-0.5)
POWER = SCORE / math.log(2.0)
VMEM = 56 * 1024 * 1024
COST = {
    "pack": 4,
    "attn_forward": 26,
    "mlp_forward": 24,
    "mlp_backward": 17,
    "mlp_grads": 16,
    "attn_backward": 33,
    "attn_grads": 13,
    "norm_backward": 9,
    "sum": 5,
    "vec_pack": 0.3,
    "vec": 0.3,
    "adam": 1,
    "tie": 0.01,
}
SCALE = 3e9


def adam_step(weight, gradient, first_moment, second_moment, step_rate, decay_rate):
    first_new = BETA_ONE * first_moment + (1.0 - BETA_ONE) * gradient
    second_new = BETA_TWO * second_moment + (1.0 - BETA_TWO) * gradient * gradient
    first_hat = first_new / (1.0 - BETA_ONE**STEP)
    second_hat = second_new / (1.0 - BETA_TWO**STEP)
    weight_new = weight - step_rate * (
        first_hat / (jnp.sqrt(second_hat) + ADAM_EPS) + decay_rate * weight
    )
    return (weight_new, first_new, second_new)


def cdot(left, right, left_dim=1, right_dim=0):
    return lax.dot_general(
        left, right, (((left_dim,), (right_dim,)), ((), ())), preferred_element_type=F32
    )


def norm_parts(values):
    centred = values - jnp.mean(values, axis=-1, keepdims=True)
    inverse = lax.rsqrt(jnp.mean(centred * centred, axis=-1, keepdims=True) + EPS_NORM)
    return centred * inverse, inverse


def norm_backward(grad_out, values, gain):
    unit, inverse = norm_parts(values)
    scaled = grad_out * gain
    mean_one = jnp.mean(scaled, axis=-1, keepdims=True)
    mean_two = jnp.mean(scaled * unit, axis=-1, keepdims=True)
    return inverse * (scaled - mean_one - unit * mean_two), grad_out * unit


def gelu_both(inputs):
    square = inputs * inputs
    tanh = jnp.tanh(inputs * (GELU + (0.044715 * GELU) * square))
    half = 0.5 + 0.5 * tanh
    act = inputs * half
    return act, half + act * ((1.0 - tanh) * (GELU + (3 * 0.044715 * GELU) * square))


def mask_keys(scores, tokens):
    rows = scores.shape[0]
    whole = IMG_TOK // 8 * 8
    position = whole + lax.broadcasted_iota(jnp.int32, (rows - whole, 1), 0)
    return jnp.concatenate(
        [scores[:whole], jnp.where(position < tokens, scores[whole:], MASKED / SCORE)], axis=0
    )


def whole(shape):
    return pl.BlockSpec(shape, lambda i, s: (0,) * len(shape), pipeline_mode=pl.Buffered(1))


def held(shape):
    return pl.BlockSpec(shape, lambda i, s: (0,) * len(shape))


def stepped(shape):
    return pl.BlockSpec((1,) + shape, lambda i, s: (i,) + (0,) * len(shape))


def low_of(*shape):
    return jax.ShapeDtypeStruct(shape, LOW)


def f32_of(*shape):
    return jax.ShapeDtypeStruct(shape, F32)


def call(kernel, where, steps, ins, outs, scratch, flops=0, bytes_accessed=0, transcendentals=0, aliases=None,
         after=(), layer=None):
    given = 1 + len(ins)
    name = getattr(kernel, "func", kernel).__name__.removesuffix("_kernel")
    ins = ins + [(pl.BlockSpec(memory_space=pl.ANY), array) for array in after]

    def run(*refs):
        kernel(*refs[:given], *refs[given + len(after) :])

    return pl.pallas_call(
        run,
        name=name,
        grid_spec=pltpu.PrefetchScalarGridSpec(
            num_scalar_prefetch=1,
            grid=(steps,),
            in_specs=[spec for spec, _ in ins],
            out_specs=[spec for spec, _ in outs],
            scratch_shapes=scratch,
        ),
        out_shape=[shape for _, shape in outs],
        input_output_aliases=aliases or {},
        compiler_params=pltpu.CompilerParams(vmem_limit_bytes=VMEM),
        cost_estimate=pl.CostEstimate(
            flops=int(COST.get((name, layer), COST[name]) * SCALE), bytes_accessed=1, transcendentals=0
        ),
    )(where, *[array for _, array in ins])


def turn_part(values, turned, step):
    size = values.shape[1] // 3
    at = pl.ds(pl.multiple_of(jnp.minimum(step, 2) * size, 128), size)
    turned[at, :] = values[:, at].T


def pack_kernel(units, where, qkv_ref, out_ref, up_ref, down_ref, own_attn, other_attn, own_mlp, other_mlp):
    qkv, out = qkv_ref[0].astype(LOW), out_ref[0].astype(LOW)
    up, down = up_ref[0].astype(LOW), down_ref[0].astype(LOW)

    def half(values, number):
        size = values.shape[1] // 2
        return values[:, number * size : (number + 1) * size]

    for number in range(2):
        up_h, down_h = half(up, number), half(down, number)
        attn = [half(qkv, number), half(out, number), up_h[:, units:], down_h[:, units:]]
        used = sum(piece.shape[1] for piece in attn)
        attn.append(jnp.zeros((qkv.shape[0], own_attn.shape[1] - used), LOW))
        attn = jnp.concatenate(attn, axis=1)
        mlp = jnp.concatenate([up_h[:, :units], down_h[:, :units]], axis=1)

        @pl.when(where[3] == number)
        def _():
            own_attn[...] = attn
            own_mlp[...] = mlp

        @pl.when(where[3] != number)
        def _():
            other_attn[...] = attn
            other_mlp[...] = mlp


def attn_forward_kernel(spread, joined, tail_units, where, *refs):
    refs = list(refs)
    count = len(spread.weight_keys)
    if joined:
        base_ref, own_ref, other_ref, old_ref = refs[:4]
        del refs[:4]
    else:
        own_ref, other_ref = refs[:2]
        del refs[:2]
    vec_ref, bias_ref = refs[:2]
    w_refs = refs[2 : 2 + count]
    (stream_ref, turned_ref, qkv_ref, mixed_ref, sums_ref, tail_ref, part_ref, total, held_weight, normed) = refs[
        2 + count :
    ]
    step = pl.program_id(0)

    @pl.when(step == 0)
    def _():
        if not joined:
            half = own_ref.shape[0]
            stream_ref[pl.ds(pl.multiple_of(where[3] * half, 8), half), :] = own_ref[...]
            stream_ref[pl.ds(pl.multiple_of((1 - where[3]) * half, 8), half), :] = other_ref[...]

        if joined:
            branch = own_ref[...].astype(F32) + other_ref[...].astype(F32)
            stream_ref[...] = base_ref[...] + branch + old_ref[0, 7:8, :]
        unit, _ = norm_parts(stream_ref[...])
        normed[...] = (unit * vec_ref[0, 0:1, :] + vec_ref[0, 1:2, :]).astype(LOW)

    weight = spread.load(w_refs, where, held_weight)
    tokens = where[4]
    head_columns = 3 * HD
    local = qkv_ref.shape[2]
    heads = local // head_columns
    bias = []
    for head in range(heads):
        at = head * HD
        query_bias, value_bias = bias_ref[0, 0, 0, :, at : at + HD], bias_ref[0, 1, 0, :, at : at + HD]
        bias += [query_bias, jnp.zeros_like(query_bias), value_bias]
    bias = jnp.concatenate(bias, axis=1)
    qkv = (cdot(normed[...], weight[:, :local]) + bias).astype(LOW)
    qkv_ref[0] = qkv
    mixed = []
    for head in range(heads):
        at = head * head_columns
        query = qkv[:, at : at + HD]
        key = qkv[:, at + HD : at + 2 * HD]
        value = qkv[:, at + 2 * HD : at + 3 * HD]
        scores = mask_keys(cdot(key, query, 1, 1), tokens)
        top = jnp.max(scores, axis=0, keepdims=True)
        raised = jnp.exp2((scores - top) * POWER)
        weight_sum = jnp.sum(raised, axis=0, keepdims=True)
        mixed.append(cdot(value, raised.astype(LOW), 0, 0) * (1.0 / weight_sum))
        sums_ref[0, head : head + 1, :] = top * POWER + jnp.log2(weight_sum)
    mixed = jnp.concatenate(mixed, axis=0).T.astype(LOW)
    mixed_ref[0] = mixed
    at = local + mixed.shape[1]
    part = cdot(mixed, weight[:, local:at], 1, 1)

    @pl.when(step == 0)
    def _():
        total[...] = part

    @pl.when(step > 0)
    def _():
        total[...] += part

    tail_ref[0] = weight[:, at : at + 2 * tail_units]

    @pl.when(step == pl.num_programs(0) - 1)
    def _():
        part_ref[...] = total[...].astype(LOW)
        turned_ref[...] = normed[...].T


def mlp_forward_kernel(spread, where, *refs):
    count = len(spread.weight_keys)
    base_ref, own_ref, other_ref, vec_ref, bias_ref, tail_ref, tail_bias_ref = refs[:7]
    w_refs = refs[7 : 7 + count]
    (middle_ref, turned_ref, act_ref, slope_ref, act_tail_ref, slope_tail_ref, up_tail_ref, down_tail_ref,
     part_ref, total, held_weight, normed) = refs[7 + count :]
    step = pl.program_id(0)

    @pl.when(step == 0)
    def _():
        branch = own_ref[...].astype(F32) + other_ref[...].astype(F32)
        middle = base_ref[...] + branch + vec_ref[0, 4:5, :]
        middle_ref[...] = middle
        unit, _ = norm_parts(middle)
        normed[...] = (unit * vec_ref[0, 5:6, :] + vec_ref[0, 6:7, :]).astype(LOW)
        steps, _, both = tail_ref.shape
        half = both // 2
        up_tail_ref[...] = jnp.concatenate([tail_ref[t, :, :half] for t in range(steps)], axis=1)
        down_tail_ref[...] = jnp.concatenate([tail_ref[t, :, half:] for t in range(steps)], axis=1)
        act, slope = gelu_both(cdot(normed[...], up_tail_ref[...]) + tail_bias_ref[0, 0])
        act = act.astype(LOW)
        act_tail_ref[...] = act
        slope_tail_ref[...] = slope.astype(LOW)
        total[...] = cdot(act, down_tail_ref[...], 1, 1)

    weight = spread.load(w_refs, where, held_weight)
    units = act_ref.shape[2]
    act, slope = gelu_both(cdot(normed[...], weight[:, :units]) + bias_ref[0, 0, 0])
    act = act.astype(LOW)
    act_ref[0] = act
    slope_ref[0] = slope.astype(LOW)
    total[...] += cdot(act, weight[:, units:], 1, 1)

    @pl.when(step == pl.num_programs(0) - 1)
    def _():
        part_ref[...] = total[...].astype(LOW)
        turned_ref[...] = normed[...].T


def mlp_backward_kernel(spread, where, *refs):
    count = len(spread.weight_keys)
    grad_ref, slope_ref, up_tail_ref, down_tail_ref, slope_tail_ref = refs[:5]
    w_refs = refs[5 : 5 + count]
    (hidden_ref, hidden_tail_ref, sums_ref, sums_tail_ref, part_ref, turned_ref, low, total, held_weight) = refs[
        5 + count :
    ]
    step = pl.program_id(0)

    @pl.when(step == 0)
    def _():
        low[...] = grad_ref[...].astype(LOW)
        hidden = cdot(low[...], down_tail_ref[...]) * slope_tail_ref[...].astype(F32)
        sums_tail_ref[...] = jnp.sum(hidden, axis=0, keepdims=True)
        hidden = hidden.astype(LOW)
        hidden_tail_ref[...] = hidden
        total[...] = cdot(hidden, up_tail_ref[...], 1, 1)

    weight = spread.load(w_refs, where, held_weight)
    units = hidden_ref.shape[2]
    turn_part(low, turned_ref, step)
    hidden = cdot(low[...], weight[:, units:]) * slope_ref[0].astype(F32)
    sums_ref[0] = jnp.sum(hidden, axis=0, keepdims=True)
    hidden = hidden.astype(LOW)
    hidden_ref[0] = hidden
    total[...] += cdot(hidden, weight[:, :units], 1, 1)

    @pl.when(step == pl.num_programs(0) - 1)
    def _():
        part_ref[...] = total[...].astype(LOW)


def mlp_grads_kernel(spread, where, *refs):
    count = len(spread.grad_keys)
    grad_turned, normed_turned, hidden_ref, act_ref, hidden_tail_ref, act_tail_ref = refs[:6]
    out_refs = refs[6 : 6 + count]
    tail_ref, result = refs[6 + count :]
    step = pl.program_id(0)

    @pl.when(step == 0)
    def _():
        up_tail = cdot(normed_turned[...], hidden_tail_ref[...]).astype(LOW)
        down_tail = cdot(grad_turned[...], act_tail_ref[...]).astype(LOW)
        steps, _, both = tail_ref.shape
        half = both // 2
        for t in range(steps):
            at = slice(t * half, (t + 1) * half)
            tail_ref[t] = jnp.concatenate([up_tail[:, at], down_tail[:, at]], axis=1)

    units = hidden_ref.shape[2]
    result[:, :units] = cdot(normed_turned[...], hidden_ref[0]).astype(LOW)
    result[:, units:] = cdot(grad_turned[...], act_ref[0]).astype(LOW)
    spread.store(out_refs, where, result)


def attn_backward_kernel(spread, where, *refs):
    count = len(spread.weight_keys)
    grad_ref, own_ref, other_ref, middle_ref, vec_ref, qkv_ref, sums_ref = refs[:7]
    w_refs = refs[7 : 7 + count]
    dmiddle_ref, norm_sums_ref, dqkv_ref, head_sums_ref, part_ref, low, total, held_weight = refs[7 + count :]
    step = pl.program_id(0)

    @pl.when(step == 0)
    def _():
        grad = grad_ref[...]
        dnormed = own_ref[...].astype(F32) + other_ref[...].astype(F32)
        inner, gain_terms = norm_backward(dnormed, middle_ref[...], vec_ref[0, 5:6, :])
        dmiddle = grad + inner
        dmiddle_ref[...] = dmiddle
        low[...] = dmiddle.astype(LOW)
        for number, terms in enumerate((gain_terms, dnormed, grad, dmiddle)):
            norm_sums_ref[number : number + 1, :] = jnp.sum(terms, axis=0, keepdims=True)

    weight = spread.load(w_refs, where, held_weight)
    tokens = where[4]
    head_columns = 3 * HD
    local = qkv_ref.shape[2]
    heads = local // head_columns
    qkv = qkv_ref[0]
    dmixed = cdot(low[...], weight[:, local : local + heads * HD]).astype(LOW)
    pieces = []
    for head in range(heads):
        at = head * head_columns
        query = qkv[:, at : at + HD]
        key = qkv[:, at + HD : at + 2 * HD]
        value = qkv[:, at + 2 * HD : at + 3 * HD]
        grad = dmixed[:, head * HD : (head + 1) * HD]
        scores = mask_keys(cdot(key, query, 1, 1), tokens)
        probs = jnp.exp2(scores * POWER - sums_ref[0, head : head + 1, :])
        dprobs = cdot(value, grad, 1, 1)
        row_dot = jnp.sum(dprobs * probs, axis=0, keepdims=True)
        dscores = (probs * (dprobs - row_dot)).astype(LOW)
        pieces.append(cdot(key, dscores, 0, 0).T * SCORE)
        pieces.append(cdot(dscores, query) * SCORE)
        pieces.append(cdot(probs.astype(LOW), grad))
    dqkv = jnp.concatenate(pieces, axis=1)
    head_sums_ref[0] = jnp.sum(dqkv, axis=0, keepdims=True)
    dqkv = dqkv.astype(LOW)
    dqkv_ref[0] = dqkv
    part = cdot(dqkv, weight[:, :local], 1, 1)

    @pl.when(step == 0)
    def _():
        total[...] = part

    @pl.when(step > 0)
    def _():
        total[...] += part

    @pl.when(step == pl.num_programs(0) - 1)
    def _():
        part_ref[...] = total[...].astype(LOW)


def attn_grads_kernel(spread, where, *refs):
    count = len(spread.grad_keys)
    dmiddle_ref, normed_turned, dqkv_ref, mixed_ref, tail_ref = refs[:5]
    out_refs = refs[5 : 5 + count]
    result, grad_turned = refs[5 + count :]

    @pl.when(pl.program_id(0) == 0)
    def _():
        grad_turned[...] = dmiddle_ref[...].astype(LOW).T

    parts = [
        cdot(normed_turned[...], dqkv_ref[0]).astype(LOW),
        cdot(grad_turned[...], mixed_ref[0]).astype(LOW),
        tail_ref[0],
    ]
    used = sum(part.shape[1] for part in parts)
    parts.append(jnp.zeros((result.shape[0], result.shape[1] - used), LOW))
    result[...] = jnp.concatenate(parts, axis=1)
    spread.store(out_refs, where, result)


def norm_backward_kernel(where, dmiddle_ref, own_ref, other_ref, stream_ref, vec_ref, out_ref, sums_ref):
    dnormed = own_ref[...].astype(F32) + other_ref[...].astype(F32)
    inner, gain_terms = norm_backward(dnormed, stream_ref[...], vec_ref[0, 0:1, :])
    out_ref[...] = dmiddle_ref[...] + inner

    @pl.when(pl.program_id(0) == 0)
    def _():
        sums_ref[...] = jnp.zeros_like(sums_ref)

    sums_ref[0:1, :] += jnp.sum(gain_terms, axis=0, keepdims=True)
    sums_ref[1:2, :] += jnp.sum(dnormed, axis=0, keepdims=True)


def adam_kernel(units, local, out_local, tail_units, where, *refs):
    attn_own, attn_other, mlp_own, mlp_other = refs[:4]
    states = [refs[4 + 3 * k : 7 + 3 * k] for k in range(4)]
    outs = refs[len(refs) - 16 :]

    def pair(own, other):
        own, other = own[...].astype(F32), other[...].astype(F32)
        low_core = where[3] == 0
        return jnp.where(low_core, own, other), jnp.where(low_core, other, own)

    attn = pair(attn_own, attn_other)
    mlp = pair(mlp_own, mlp_other)
    at = local + out_local
    grads = [
        jnp.concatenate([half[:, :local] for half in attn], axis=1),
        jnp.concatenate([half[:, local:at] for half in attn], axis=1),
        jnp.concatenate(
            [piece for m, n in zip(mlp, attn) for piece in (m[:, :units], n[:, at : at + tail_units])], axis=1
        ),
        jnp.concatenate(
            [
                piece
                for m, n in zip(mlp, attn)
                for piece in (m[:, units:], n[:, at + tail_units : at + 2 * tail_units])
            ],
            axis=1,
        ),
    ]
    for number, grad in enumerate(grads):
        weight, first, second = [ref[0] for ref in states[number]]
        new = adam_step(weight, grad, first, second, RATES[number], DECAY)
        for ref, values in zip(outs[4 * number : 4 * number + 4], (grad, new[1], new[2], new[0])):
            ref[0] = values


VEC_ROWS = 11


def vec_pack_kernel(where, *refs):
    out_ref = refs[-1]
    out_ref[...] = jnp.zeros_like(out_ref)
    for layer in range(len(refs) // 5):
        one_ref, two_ref, head_ref, main_ref, tail_ref = refs[5 * layer : 5 * layer + 5]
        row = VEC_ROWS * layer
        out_ref[row : row + 2, :] = one_ref[0:2, :]
        out_ref[row + 2 : row + 6, :] = two_ref[0:4, :]
        out_ref[row + 6 : row + 7, : tail_ref.shape[1]] = tail_ref[...]
        units = main_ref.shape[2]
        for t in range(head_ref.shape[0]):
            out_ref[row + 7 + t : row + 8 + t, : head_ref.shape[2]] = head_ref[t]
            out_ref[row + 7 + t : row + 8 + t, units : 2 * units] = main_ref[t]


def vec_kernel(steps, local, units, tail_units, where, own_ref, other_ref, vec_ref, first_ref, second_ref,
               grad_out, first_out, second_out, weight_out):
    low_core = where[3] == 0
    for layer in range(vec_ref.shape[0]):
        rows = slice(VEC_ROWS * layer, VEC_ROWS * (layer + 1))
        own, other = own_ref[rows, :], other_ref[rows, :]
        cores = jnp.where(low_core, own, other), jnp.where(low_core, other, own)
        norms = cores[0][0:6]
        heads = local // (3 * HD)

        def head_piece(kind):
            return [
                core[7 + t : 8 + t, (3 * head + kind) * HD : (3 * head + kind + 1) * HD]
                for t in range(steps)
                for core in cores
                for head in range(heads)
            ]

        hidden = [
            piece
            for t in range(steps)
            for core in cores
            for piece in (core[7 + t : 8 + t, units : 2 * units], core[6:7, t * tail_units : (t + 1) * tail_units])
        ]
        grad = jnp.concatenate(
            [norms[0:1], norms[1:2], *head_piece(0), *head_piece(2),
             norms[5:6], norms[2:3], norms[3:4], norms[4:5], *hidden],
            axis=1,
        )
        at = slice(layer, layer + 1)
        new = adam_step(vec_ref[at, :], grad, first_ref[at, :], second_ref[at, :], RATES[4], 0.0)
        grad_out[at, :] = grad
        first_out[at, :] = new[1]
        second_out[at, :] = new[2]
        weight_out[at, :] = new[0]


def plane_sides(chips):
    side = math.isqrt(chips)
    while chips % side:
        side -= 1
    return side, chips // side


class Place:
    def __init__(self):
        self.nf = lax.axis_size("fsdp")
        self.nt = lax.axis_size("tp")
        self.na, self.nb = plane_sides(self.nf // 2)
        fi = lax.axis_index("fsdp")
        self.core = fi % 2
        self.a = (fi // 2) // self.nb
        self.b = (fi // 2) % self.nb
        self.t = lax.axis_index("tp")
        self.size = {"a": self.na, "b": self.nb, "t": self.nt}
        self.at = {"a": self.a, "b": self.b, "t": self.t}

    def pairs(self, axis, move):
        if axis == "t":
            return [(i, move(i)) for i in range(self.nt)]
        found = []
        for f in range(self.nf):
            place = {"a": f // 2 // self.nb, "b": f // 2 % self.nb, "core": f % 2}
            place[axis] = move(place[axis])
            found.append((f, (place["a"] * self.nb + place["b"]) * 2 + place["core"]))
        return found

    def send(self, values, axis, move):
        return lax.ppermute(values, "tp" if axis == "t" else "fsdp", self.pairs(axis, move))

    def sibling(self, values):
        return self.send(values, "core", lambda i: 1 - i)

    def swap_rows(self, values):
        pairs = []
        for f in range(self.nf):
            for t in range(self.nt):
                if f % 2 != t % 2:
                    sign = 1 if t % 2 else -1
                    pairs.append((f * self.nt + t, (f + sign) * self.nt + t - sign))
        arrived = lax.ppermute(values.astype(LOW), ("fsdp", "tp"), pairs).astype(F32)
        return jnp.where(self.core != self.t % 2, arrived, values)

    def gather_axis(self, block, axis):
        n = self.size[axis]
        return [block] + [self.send(block, axis, lambda i, k=k: (i - k) % n) for k in range(1, n)]

    def scatter_axis(self, parts, axis):
        n = self.size[axis]
        sent = [self.send(parts[k], axis, lambda i, k=k: (i + k) % n) for k in range(1, n)]
        return [parts[0], *sent]


def split_pair(place, first, second):
    return (
        jnp.where(place.core == 0, first, second),
        jnp.where(place.core == 0, second, first),
    )


def sum_kernel(outputs, where, *refs):
    count = sum(size for sizes in outputs for size in sizes)
    ins, outs = refs[:count], refs[count:]
    for out_ref, sizes in zip(outs, outputs):
        for number, size in enumerate(sizes):
            for t in range(out_ref.shape[0]):
                total = ins[0][t, 0].astype(F32)
                for ref in ins[1:size]:
                    total += ref[t, 0].astype(F32)
                out_ref[t, number] = total.astype(LOW)
            ins = ins[size:]


def tie_kernel(where, *refs):
    pass


def tie(where, arrays, after):
    space = pl.BlockSpec(memory_space=pl.ANY)
    return call(
        tie_kernel,
        where,
        1,
        [(space, x) for x in arrays],
        [(space, jax.ShapeDtypeStruct(x.shape, x.dtype)) for x in arrays],
        [],
        aliases={1 + k: k for k in range(len(arrays))},
        after=after,
    )


class Spread:
    def __init__(self, place, rows, columns, middle):
        self.place, self.rows, self.columns = place, rows, columns
        self.middle = middle
        self.direct = rows % 16 == 0
        self.width = place.na * place.nb * 2 * rows
        na, nb = place.na, place.nb
        self.grad_keys = [[(0, a, b) for b in range(nb)] for a in range(na)]
        self.grad_keys += [[(1, a, b) for a in range(na)] for b in range(nb)]
        self.gather_keys = [[(0, 0, 0), (1, 0, 0)]]
        self.gather_keys += [[(0, 0, b), (1, 0, b)] for b in range(1, nb)]
        self.gather_keys += [[(0, a, 0), (1, a, 0)] for a in range(1, na)]
        self.gather_keys += [[(half, a, b)] for half in range(2) for a in range(1, na) for b in range(1, nb)]
        if middle:
            self.gather_keys = self.grad_keys
        self.weight_keys = self.gather_keys
        if not self.direct:
            self.weight_keys = self.grad_keys = [None]

    def shapes(self, keys):
        if not self.direct:
            return [(self.place.nt, self.width, self.columns)]
        return [(self.place.nt, len(blocks), self.rows, self.columns) for blocks in keys]

    def specs(self, keys):
        return [stepped(shape[1:]) for shape in self.shapes(keys)]

    def first_row(self, where, key):
        half, a, b = key
        a = lax.rem(where[0] + a, self.place.na)
        b = lax.rem(where[1] + b, self.place.nb)
        return pl.multiple_of(((a * self.place.nb + b) * 2 + half) * self.rows, 16)

    def load(self, refs, where, scratch):
        if not self.direct:
            return refs[0].at[0]
        for ref, blocks in zip(refs, self.weight_keys):
            for number, key in enumerate(blocks):
                scratch[pl.ds(self.first_row(where, key), self.rows), :] = ref[0, number]
        return scratch

    def store(self, refs, where, scratch):
        if not self.direct:
            refs[0][0] = scratch[...]
            return
        for ref, blocks in zip(refs, self.grad_keys):
            for number, key in enumerate(blocks):
                ref[0, number] = scratch[pl.ds(self.first_row(where, key), self.rows), :]

    def start(self, own, other):
        place = self.place
        halves = split_pair(place, own, other)
        if self.middle:
            return [jnp.stack(place.gather_axis(half, axis)) for half, axis in zip(halves, "ba")]
        return [jnp.stack(halves)]

    def gather(self, where, blocks, after=()):
        place = self.place
        na, nb = place.na, place.nb
        blocks = [lax.all_gather(block, "tp") for block in blocks]
        if self.direct and len(after):
            blocks = tie(where, blocks, after)
        if self.middle:
            arrays = [array for block, axis in zip(blocks, "ab") for array in place.gather_axis(block, axis)]
        else:
            along_b = place.gather_axis(blocks[0], "b")
            along_a = place.gather_axis(blocks[0], "a")
            first = [place.gather_axis(x[:, :1], "a")[1:] for x in along_b[1:]]
            second = [place.gather_axis(x[:, 1:], "b")[1:] for x in along_a[1:]]
            arrays = along_b + along_a[1:]
            arrays += [first[b][a] for a in range(na - 1) for b in range(nb - 1)]
            arrays += [second[a][b] for a in range(na - 1) for b in range(nb - 1)]
        if self.direct:
            return arrays
        found = {
            key: array[:, number]
            for array, keys in zip(arrays, self.gather_keys)
            for number, key in enumerate(keys)
        }
        full = jnp.stack([found[half, a, b] for a in range(na) for b in range(nb) for half in range(2)], axis=1)
        full = full.reshape(place.nt, na, nb, 2, self.rows, self.columns)
        full = self.roll(full, (na - place.a) % na, (nb - place.b) % nb)
        return [full.reshape(place.nt, self.width, self.columns)]

    def roll(self, full, a, b):
        full = lax.dynamic_slice_in_dim(jnp.concatenate([full, full], axis=1), a, self.place.na, 1)
        return lax.dynamic_slice_in_dim(jnp.concatenate([full, full], axis=2), b, self.place.nb, 2)

    def sums(self, where, outputs, after, layer=None):
        place, rows, columns = self.place, self.rows, self.columns

        def block(number):
            return pl.BlockSpec((place.nt, 1, rows, columns), lambda i, s: (0, number, 0, 0))

        shapes = [(place.nt, len(groups), rows, columns) for groups in outputs]
        return call(
            functools.partial(sum_kernel, [[len(group) for group in groups] for groups in outputs]),
            where,
            1,
            [(block(number), x) for groups in outputs for group in groups for x, number in group],
            [(held(shape), low_of(*shape)) for shape in shapes],
            [],
            after=after,
            layer=layer,
        )

    def scatter_last(self, arrays):
        place = self.place
        if not self.direct:
            full = arrays[0].reshape(place.nt, place.na, place.nb, 2, self.rows, self.columns)
            full = self.roll(full, place.a, place.b)
            arrays = [full[:, a, :, 0] for a in range(place.na)] + [full[:, :, b, 1] for b in range(place.nb)]
        return (
            place.scatter_axis(arrays[: place.na], "a"),
            place.scatter_axis(arrays[place.na :], "b"),
        )

    def scatter_first(self, where, halves, after):
        place = self.place
        if self.middle:
            outputs = [[[(x, k) for x in half] for k in range(half[0].shape[1])] for half in halves]
            results = self.sums(where, outputs, after)
            return results[0], [lax.psum_scatter(x, "tp", scatter_dimension=0, tiled=True)[0] for x in results]
        axes = ("b", "a")
        keys = [(half, k) for half in range(2) for k in range(1, place.size[axes[half]])]
        results = self.sums(where, [[[(x, k) for x in halves[half]]] for half, k in keys], after)
        terms = [[(x, 0) for x in arrays] for arrays in halves]
        for (half, k), total in zip(keys, results):
            n = place.size[axes[half]]
            terms[half].append((place.send(total, axes[half], lambda i: (i + k) % n), 0))
        return results[0], terms

    def scatter_tp(self, where, terms, after, layer=None):
        place = self.place
        if self.middle:
            if self.direct:
                terms = tie(where, terms, after)
            done = [
                sum(x.astype(F32) for x in place.scatter_axis(list(half), axis)).astype(LOW)
                for half, axis in zip(terms, "ba")
            ]
            last = after[0]
        else:
            (last,) = self.sums(where, [terms], after, layer)
            done = lax.psum_scatter(last, "tp", scatter_dimension=0, tiled=True)[0]
        mine, other = split_pair(place, done[0], done[1])
        return last, (mine, place.sibling(other))


def body(
    residual_in,
    cotangent,
    slot_tokens,
    qkv_weight,
    out_weight,
    up_weight,
    down_weight,
    vectors,
    qkv_first,
    qkv_second,
    out_first,
    out_second,
    up_first,
    up_second,
    down_first,
    down_second,
    vec_first,
    vec_second,
):
    place = Place()
    layer_count, shard_rows, _ = qkv_weight.shape
    half_rows, width = residual_in.shape
    rows = 2 * half_rows
    nt = place.nt
    local = qkv_weight.shape[2] // 2
    out_local = out_weight.shape[1] // 2
    hidden_local = up_weight.shape[2] // 2
    units = hidden_local // 128 * 128
    tail_units = hidden_local - units
    heads = out_local // HD
    attn_columns = -(-(local + out_local + 2 * tail_units) // 128) * 128
    mlp_columns = 2 * units

    tokens_pair = jnp.concatenate(split_pair(place, slot_tokens, place.sibling(slot_tokens)))
    slot_at = (place.t % 2) * slot_tokens.shape[0] + place.t // 2
    tokens = lax.dynamic_slice_in_dim(tokens_pair, slot_at, 1)
    row_mask = (jnp.arange(rows, dtype=jnp.int32) < tokens[0]).astype(F32)[:, None]
    here = jnp.stack([place.a, place.b, place.t, place.core]).astype(jnp.int32)
    where = jnp.concatenate([here, tokens.astype(jnp.int32)])

    def own_rows(values):
        return lax.dynamic_slice_in_dim(values, place.core * half_rows, half_rows)

    spreads = [
        (
            Spread(place, shard_rows, attn_columns, False),
            Spread(place, shard_rows, mlp_columns, layer > 0),
        )
        for layer in range(layer_count)
    ]

    def turn(arrays):
        qkv, out, up, down = arrays
        return qkv, jnp.swapaxes(out, 1, 2), up, jnp.swapaxes(down, 1, 2)

    weights = turn((qkv_weight, out_weight, up_weight, down_weight))
    firsts = turn((qkv_first, out_first, up_first, down_first))
    seconds = turn((qkv_second, out_second, up_second, down_second))

    def layer_block(array, layer, steps=1):
        block = (1, array.shape[1] // steps, array.shape[2])
        return pl.BlockSpec(block, lambda i, s: (layer, i, 0))

    def pack(layer):
        attn, mlp = (shard_rows, attn_columns), (shard_rows, mlp_columns)
        return call(
            functools.partial(pack_kernel, units),
            here,
            1,
            [(layer_block(w, layer), w) for w in weights],
            [(held(shape), low_of(*shape)) for shape in (attn, attn, mlp, mlp)],
            [],
            bytes_accessed=6 * shard_rows * 13216 // 4,
        )

    starts = []
    for layer in range(layer_count):
        own_attn, other_attn, own_mlp, other_mlp = pack(layer)
        starts.append(
            (
                spreads[layer][0].start(own_attn, place.sibling(other_attn)),
                spreads[layer][1].start(own_mlp, place.sibling(other_mlp)),
            )
        )
    gathered = []
    before = [x for pair in starts[1:] for blocks in pair for x in blocks]
    for layer in range(layer_count):
        attn_full = spreads[layer][0].gather(where, starts[layer][0], before)
        mlp_full = spreads[layer][1].gather(where, starts[layer][1], attn_full[1:3])
        before = mlp_full[1:3]
        gathered.append((attn_full, mlp_full))

    wide = vectors[:, : 8 * width].reshape(layer_count, 8, width)
    head_bias = vectors[:, 2 * width : 4 * width].reshape(layer_count, 2, 2 * nt, 1, out_local)
    hidden_bias = vectors[:, 8 * width :].reshape(layer_count, nt, 2, 1, hidden_local)
    main_bias = hidden_bias[..., :units]
    tail_bias = jnp.moveaxis(hidden_bias[..., units:], 1, 3).reshape(layer_count, 2, 1, nt * tail_units)

    full = whole((rows, width))
    weight_scratch = [
        pltpu.VMEM((width, attn_columns), LOW),
        pltpu.VMEM((width, mlp_columns), LOW),
    ]
    flat = pltpu.VMEM((rows, width), F32)
    flat_low = pltpu.VMEM((rows, width), LOW)
    big = 2 * rows * width

    def wide_of(layer):
        spec = pl.BlockSpec((1, 8, width), lambda i, s: (layer, 0, 0), pipeline_mode=pl.Buffered(1))
        return spec, wide

    def attn_forward(layer, base, own, other):
        spread = spreads[layer][0]
        joined = base is not None
        if joined:
            ins = [(full, base), (full, own), (full, other), wide_of(layer - 1)]
        else:
            half = whole((half_rows, width))
            ins = [(half, own), (half, other)]
        ins.append(wide_of(layer))
        ins.append(
            (
                pl.BlockSpec(
                    (1, 2, 1, 1, out_local), lambda i, s: (layer, 0, 2 * i + s[3], 0, 0)
                ),
                head_bias,
            )
        )
        ins += list(zip(spread.specs(spread.weight_keys), gathered[layer][0]))
        return call(
            functools.partial(attn_forward_kernel, spread, joined, tail_units),
            where,
            nt,
            ins,
            [
                (held((rows, width)), f32_of(rows, width)),
                (held((width, rows)), low_of(width, rows)),
                (stepped((rows, local)), low_of(nt, rows, local)),
                (stepped((rows, out_local)), low_of(nt, rows, out_local)),
                (stepped((heads, rows)), f32_of(nt, heads, rows)),
                (stepped((width, 2 * tail_units)), low_of(nt, width, 2 * tail_units)),
                (held((rows, width)), low_of(rows, width)),
            ],
            [flat, weight_scratch[0], flat_low],
            big * nt * (local + out_local) + 4 * nt * heads * rows * rows * HD,
            rows * width * 12 + nt * width * attn_columns * 2,
            nt * heads * rows * rows,
        )

    def mlp_forward(layer, base, own, other, tails, after=()):
        spread = spreads[layer][1]
        tail = nt * tail_units
        tail_shape = (width, tail)
        ins = [
            (full, base),
            (full, own),
            (full, other),
            wide_of(layer),
            (pl.BlockSpec((1, 1, 1, 1, units), lambda i, s: (layer, i, s[3], 0, 0)), main_bias),
            (whole(tails.shape), tails),
            (pl.BlockSpec((1, 1, 1, tail), lambda i, s: (layer, s[3], 0, 0)), tail_bias),
        ]
        ins += list(zip(spread.specs(spread.weight_keys), gathered[layer][1]))
        return call(
            functools.partial(mlp_forward_kernel, spread),
            where,
            nt,
            ins,
            [
                (held((rows, width)), f32_of(rows, width)),
                (held((width, rows)), low_of(width, rows)),
                (stepped((rows, units)), low_of(nt, rows, units)),
                (stepped((rows, units)), low_of(nt, rows, units)),
                (held((rows, tail)), low_of(rows, tail)),
                (held((rows, tail)), low_of(rows, tail)),
                (held(tail_shape), low_of(*tail_shape)),
                (held(tail_shape), low_of(*tail_shape)),
                (held((rows, width)), low_of(rows, width)),
            ],
            [flat, weight_scratch[1], flat_low],
            2 * big * (nt * units + tail),
            rows * width * 16 + nt * (width + rows) * mlp_columns * 2,
            rows * nt * units,
            after=after,
        )

    def mlp_backward(layer, grad, slope, tails, slope_tail):
        spread = spreads[layer][1]
        tail = nt * tail_units
        ins = [(full, grad), (stepped((rows, units)), slope)]
        ins += [(whole(w.shape), w) for w in (*tails, slope_tail)]
        ins += list(zip(spread.specs(spread.weight_keys), gathered[layer][1]))
        return call(
            functools.partial(mlp_backward_kernel, spread),
            where,
            nt,
            ins,
            [
                (stepped((rows, units)), low_of(nt, rows, units)),
                (held((rows, tail)), low_of(rows, tail)),
                (stepped((1, units)), f32_of(nt, 1, units)),
                (held((1, tail)), f32_of(1, tail)),
                (held((rows, width)), low_of(rows, width)),
                (held((width, rows)), low_of(width, rows)),
            ],
            [flat_low, flat, weight_scratch[1]],
            2 * big * (nt * units + tail),
            rows * width * 6 + nt * (width + rows) * mlp_columns * 2,
        )

    def mlp_grads(layer, grad, normed, hidden, act, hidden_tail, act_tail):
        spread = spreads[layer][1]
        ins = [(whole((width, rows)), grad), (whole((width, rows)), normed)]
        ins += [(stepped((rows, units)), hidden), (stepped((rows, units)), act)]
        ins += [(whole(x.shape), x) for x in (hidden_tail, act_tail)]
        tail_shape = (nt, width, 2 * tail_units)
        outs = [
            (spec, low_of(*shape))
            for spec, shape in zip(spread.specs(spread.grad_keys), spread.shapes(spread.grad_keys))
        ]
        outs.append((held(tail_shape), low_of(*tail_shape)))
        return call(
            functools.partial(mlp_grads_kernel, spread),
            where,
            nt,
            ins,
            outs,
            [weight_scratch[1]],
            2 * big * nt * (units + tail_units),
            rows * width * 6 + nt * (width + rows) * mlp_columns * 2,
        )

    def attn_backward(layer, grad, own, other, middle, qkv, log_sums, after=()):
        spread = spreads[layer][0]
        ins = [(full, grad), (full, own), (full, other), (full, middle), wide_of(layer)]
        ins += [(stepped((rows, local)), qkv), (stepped((heads, rows)), log_sums)]
        ins += list(zip(spread.specs(spread.weight_keys), gathered[layer][0]))
        return call(
            functools.partial(attn_backward_kernel, spread),
            where,
            nt,
            ins,
            [
                (held((rows, width)), f32_of(rows, width)),
                (held((8, width)), f32_of(8, width)),
                (stepped((rows, local)), low_of(nt, rows, local)),
                (stepped((1, local)), f32_of(nt, 1, local)),
                (held((rows, width)), low_of(rows, width)),
            ],
            [flat_low, flat, weight_scratch[0]],
            big * nt * (local + out_local) + 10 * nt * heads * rows * rows * HD,
            rows * width * 20 + nt * width * attn_columns * 2,
            nt * heads * rows * rows,
            after=after,
        )

    def attn_grads(layer, dmiddle, normed, dqkv, mixed, tail_grads):
        spread = spreads[layer][0]
        ins = [(full, dmiddle), (whole((width, rows)), normed)]
        ins += [(stepped((rows, local)), dqkv), (stepped((rows, out_local)), mixed)]
        ins.append((stepped((width, 2 * tail_units)), tail_grads))
        outs = [
            (spec, low_of(*shape))
            for spec, shape in zip(spread.specs(spread.grad_keys), spread.shapes(spread.grad_keys))
        ]
        return call(
            functools.partial(attn_grads_kernel, spread),
            where,
            nt,
            ins,
            outs,
            [weight_scratch[0], pltpu.VMEM((width, rows), LOW)],
            big * nt * (local + out_local),
            rows * width * 6 + nt * (width + rows) * attn_columns * 2,
        )

    def norm_one_backward(layer, dmiddle, own, other, stream, after=()):
        part = pl.BlockSpec((half_rows, width), lambda i, s: (i, 0))
        return call(
            norm_backward_kernel,
            where,
            2,
            [(part, dmiddle), (part, own), (part, other), (part, stream), wide_of(layer)],
            [(part, f32_of(rows, width)), (held((8, width)), f32_of(8, width))],
            [],
            rows * width * 20,
            rows * width * 16,
            after=after,
        )

    grad_stream = None
    mine = place.swap_rows(residual_in)
    base, own, other = None, mine, place.sibling(mine)
    saved = []
    for layer in range(layer_count):
        stream, normed, qkv, mixed, log_sums, tails, part = attn_forward(layer, base, own, other)
        if layer == layer_count - 1:
            (mine,) = tie(where, [place.swap_rows(cotangent)], [qkv])
            grad_stream = jnp.concatenate(split_pair(place, mine, place.sibling(mine)), axis=0) * row_mask
        middle, normed_two, act, slope, act_tail, slope_tail, up_tail, down_tail, part = mlp_forward(
            layer, stream, part, place.sibling(part), tails
        )
        saved.append(
            (stream, normed, qkv, mixed, log_sums, middle, normed_two, act, slope, act_tail, slope_tail,
             (up_tail, down_tail))
        )
        base, own, other = middle, part, place.sibling(part)
    output = own_rows(base) + (own_rows(own).astype(F32) + own_rows(other).astype(F32))
    output = place.swap_rows((output + wide[layer_count - 1, 7:8]) * own_rows(row_mask))


    def adam(layer, attn_pair, mlp_pair, before, after=()):
        steps = 1
        ins = [
            (pl.BlockSpec((shard_rows // steps, x.shape[1]), lambda i, s: (i, 0)), x)
            for x in (*attn_pair, *mlp_pair)
        ]
        for states in zip(weights, firsts, seconds):
            ins += [(layer_block(x, layer, steps), x) for x in states]
        outs = [
            (layer_block(weight, layer, steps), f32_of(*weight.shape)) for weight in weights for _ in range(4)
        ]
        aliases = None
        if before is not None:
            aliases = {1 + len(ins) + k: k for k in range(16)}
            ins += [(pl.BlockSpec(memory_space=pl.ANY), x) for x in before]
        return call(
            functools.partial(adam_kernel, units, local, out_local, tail_units),
            where,
            steps,
            ins,
            outs,
            [],
            bytes_accessed=28 * shard_rows * 13216 // 4,
            aliases=aliases,
            after=after,
        )

    vec_sums = [None] * layer_count
    last = grad_stream
    above = None
    for layer in reversed(range(layer_count)):
        (stream, normed, qkv, mixed, log_sums, middle, normed_two, act, slope, act_tail, slope_tail, tails) = (
            saved[layer]
        )
        spread_attn, spread_mlp = spreads[layer]
        hidden, hidden_tail, hidden_sums, tail_sums, part, grad_turned = mlp_backward(
            layer, grad_stream, slope, tails, slope_tail
        )
        other = place.sibling(part)
        *mlp_grad, tail_grads = mlp_grads(
            layer, grad_turned, normed_two, hidden, act, hidden_tail, act_tail
        )
        last = tail_grads
        arrived = [x for half in attn_terms_above for x in half[1:]] if above else []
        mlp_terms = spread_mlp.scatter_last(mlp_grad)
        dmiddle, norm_two_sums, dqkv, head_sums, part = attn_backward(
            layer, grad_stream, part, other, middle, qkv, log_sums, [last, *arrived]
        )
        other = place.sibling(part)
        attn_grad = attn_grads(layer, dmiddle, normed, dqkv, mixed, tail_grads)
        last = attn_grad[0]
        if above:
            last, attn_terms_above = spreads[above][0].scatter_first(where, attn_terms_above, [last, output])
        grad_stream, norm_one_sums = norm_one_backward(layer, dmiddle, part, other, stream, [last])
        if layer:
            attn_terms = spread_attn.scatter_last(attn_grad)
        last, mlp_terms = spread_mlp.scatter_first(where, mlp_terms, [norm_one_sums])
        vec_sums[layer] = (norm_one_sums, norm_two_sums, head_sums, hidden_sums, tail_sums)
        if above:
            grad_input = place.swap_rows(own_rows(grad_stream))
            last, attn_pair_one = spreads[above][0].scatter_tp(where, attn_terms_above, [last, grad_input], 1)
            mlp_terms_one = mlp_terms_above
            if spread_attn.direct:
                attn_grad = tie(where, attn_grad, [last])
            attn_terms = spread_attn.scatter_last(attn_grad)
        above, mlp_terms_above, attn_terms_above = layer, mlp_terms, attn_terms
        if layer:
            grad_stream, last = lax.optimization_barrier((grad_stream, last))
    last, mlp_pair_above = spreads[above][1].scatter_tp(where, mlp_terms_above, [last, attn_grad[0]])
    _, mlp_pair_one = spreads[1][1].scatter_tp(where, mlp_terms_one, [last])
    last, attn_terms_above = spreads[above][0].scatter_first(where, attn_terms_above, [last])
    updated = adam(1, attn_pair_one, mlp_pair_one, None, [last])
    last, attn_pair_above = spreads[above][0].scatter_tp(where, attn_terms_above, [last, updated[0]])

    flat_sums = [x for sums in vec_sums for x in sums]
    vec_shape = (-(-VEC_ROWS * layer_count // 8) * 8, width)
    (vec_total,) = call(
        vec_pack_kernel,
        where,
        1,
        [(whole(x.shape), x) for x in flat_sums],
        [(held(vec_shape), f32_of(*vec_shape))],
        [],
        after=[last],
    )
    for axis in ("b", "a", "t"):
        if axis == "t":
            (vec_total,) = tie(where, [vec_total], mlp_pair_above)
        step = 1
        while step < place.size[axis]:
            vec_total = vec_total + place.send(vec_total, axis, lambda i: i ^ step)
            step *= 2
    updated = adam(above, attn_pair_above, mlp_pair_above, updated)
    vec_new = call(
        functools.partial(vec_kernel, nt, local, units, tail_units),
        where,
        1,
        [(whole(x.shape), x) for x in (vec_total, place.sibling(vec_total), vectors, vec_first, vec_second)],
        [(held(vectors.shape), f32_of(*vectors.shape)) for _ in range(4)],
        [],
    )
    updated = [
        jnp.swapaxes(x, 1, 2) if number // 4 % 2 else x for number, x in enumerate(updated)
    ]
    return (output, grad_input, *updated, *vec_new)


def solution(mesh):
    rows = P(("fsdp", "tp"), None)
    wide = P(None, "fsdp", "tp")
    tall = P(None, "tp", "fsdp")
    moments = (wide, wide, tall, tall, wide, wide, tall, tall, P(), P())
    return jax.shard_map(
        body,
        mesh=mesh,
        in_specs=(rows, rows, P("fsdp"), wide, tall, wide, tall, P(), *moments),
        out_specs=(rows, rows, *[wide] * 4, *[tall] * 4, *[wide] * 4, *[tall] * 4, *[P()] * 4),
        check_vma=False,
    )
```
